32 devices in a mesh: groups: 2 (over y), particle: 16 (over z, x, core).
Axes of the slice: x: 2, y: 2, z: 4, core: 2. Of those that a mesh axis runs over, the one named last changes fastest.
Arguments:
- images: bfloat16 [1024, 32768], P(('groups', 'particle')), parts along dimension 0, may hold values from -6 to 6
- noise_precision: float32 [1024], P(('groups', 'particle')), parts along dimension 0, may hold values from 0.3 to 4.05
- assigned_class: int32 [1024], P(('groups', 'particle')), parts along dimension 0, may hold values from 0 to 7
- class_refs: bfloat16 [4, 8, 2, 32768], P('groups'), parts along dimension 0, may hold values from -6 to 6
- interp_index: int32 [16, 16384], P('particle'), may hold values from 0 to 32766
- interp_frac: float32 [16, 16384], P('particle'), may hold values from 0 to 1
- shift_grid: int32 [8, 2], replicated, may hold values from -6 to 6
Outputs:
- back_slices: float32 [32, 32768], P(('groups', 'particle')), parts along dimension 0
- class_weight: float32 [16], P('groups'), parts along dimension 0
The draws below stay inside these ranges and needn't reach their ends.
There are 2 independent parts, one for each index of `groups`. The reference program is written for one: setup_inputs(seed, part) draws one part's arguments, and reference() takes and returns one part's arrays. A program takes and returns all parts, laid end to end along the dimension named above; an argument that names none is the same for every part. Nothing has to cross between parts.
All inputs are finite; a program needn't handle non-finite values.
Results may differ from the reference program's by a relative error of at most 0.0089.
Values may be sent and summed in bfloat16 or wider, within the bound.
No kernel may reach another device: no remote copies, remote signals or barrier semaphores. Data moves between devices by JAX's collectives and lax.ppermute only.
A program may use at most 128 MiB of HBM per device.

```python
import math
import jax
import jax.numpy as jnp
from jax import lax

KY = 128
PIX = 16384
BOX = 256
CLASSES = 8
VOX = 32768
SHIFTS = 8
LOWK = 16
PART_DEV = 32
PARTICLES = 512
ORIENT = 8


def draw_noise_precision(key, part):
    key = jax.random.fold_in(key, 11)
    ramp = 1.0 + 2.0 * jnp.arange(PARTICLES, dtype=jnp.float32) / (PARTICLES - 1)
    base_value = jnp.exp(jax.random.uniform(key, (PARTICLES,), jnp.float32, math.log(0.3), math.log(1.35)))
    return base_value * ramp


def draw_class_refs(key, part):
    key = jax.random.fold_in(key, 23)
    shape = (2, CLASSES, 2, VOX)
    values = jnp.clip(jax.random.normal(key, shape, jnp.float32), -6.0, 6.0)
    return values.astype(jnp.bfloat16)


def draw_interp_frac(key, part):
    key = jax.random.fold_in(key, 37)
    shape = (2 * ORIENT, PIX)
    values = jax.random.uniform(key, shape, jnp.float32)
    return values


def with_ends(entries, own_key, least, largest):
    extent = entries.shape
    spot = [jax.random.randint(jax.random.fold_in(own_key, axis), (), 0, extent[axis]) for axis in range(len(extent))]
    entries = entries.at[tuple(spot)].set(least)
    longest = extent.index(max(extent))
    spot[longest] = (spot[longest] + 1) % extent[longest]
    return entries.at[tuple(spot)].set(largest)


def levels(own_key, dims, cuts, low, top_value):
    gain, own = 1.0, jax.random.fold_in(own_key, 6)
    for position, blocks in cuts:
        draws = jnp.exp(jax.random.uniform(jax.random.fold_in(own, position), (blocks,), jnp.float32, low / len(cuts), top_value / len(cuts)))
        gain = gain * jnp.repeat(draws, dims[position] // blocks).reshape([-1 if axis == position else 1 for axis in range(len(dims))])
    return gain


def noise(key, extent, scale, reach, shards=(), kind=jnp.bfloat16):
    factor_of = levels(key, extent, shards, -0.22, 0.18) if shards else 1.0
    values = jax.random.normal(key, extent, jnp.float32) * scale * factor_of
    return jnp.minimum(jnp.maximum(values, -reach), reach).astype(kind)


def setup_inputs(seed: int = 0, part: int = 0) -> dict:
    key_list = jax.random.split(jax.random.key(seed), 8)
    part_keys = jax.random.split(jax.random.fold_in(key_list[7], part), 8)
    return {
        "images": noise(part_keys[0], (PARTICLES, 2 * PIX), 1.0, 6.0, ((0, 16),)),
        "noise_precision": draw_noise_precision(jax.random.fold_in(jax.random.fold_in(key_list[7], part), 71), part),
        "assigned_class": with_ends(jax.random.randint(part_keys[2], (PARTICLES,), 0, CLASSES), jax.random.fold_in(part_keys[2], 1), 0, CLASSES - 1).astype(jnp.int32),
        "class_refs": draw_class_refs(jax.random.fold_in(jax.random.fold_in(key_list[7], part), 71), part),
        "interp_index": with_ends(jax.random.randint(key_list[4], (2 * ORIENT, PIX), 0, VOX - 1), jax.random.fold_in(key_list[4], 1), 0, (VOX - 1) - 1).astype(jnp.int32),
        "interp_frac": draw_interp_frac(jax.random.fold_in(key_list[7], 71), part),
        "shift_grid": with_ends(jax.random.randint(key_list[6], (SHIFTS, 2), -6, 7), jax.random.fold_in(key_list[6], 1), -6, 6).astype(jnp.int32),
    }


PRIOR_REWARD = 1.0

def phase_tables(shift_grid, pixel_count):
    pixel_ids = jnp.arange(pixel_count, dtype=jnp.int32)
    freq_x = pixel_ids // KY
    freq_y = pixel_ids % KY - KY // 2
    phase_turns = jnp.mod(freq_x[None, :] * shift_grid[:, 0:1] + freq_y[None, :] * shift_grid[:, 1:2], BOX)
    angles = phase_turns.astype(jnp.float32) * (2.0 * math.pi / BOX)
    return (jnp.cos(angles), jnp.sin(angles))

def shift_images(images, cos_table, sin_table, pixel_count):
    real_part = images[:, :pixel_count].astype(jnp.float32)[None]
    imag_part = images[:, pixel_count:].astype(jnp.float32)[None]
    cos_b = cos_table[:, None, :]
    sin_b = sin_table[:, None, :]
    return jnp.concatenate([real_part * cos_b + imag_part * sin_b, imag_part * cos_b - real_part * sin_b], axis=2).astype(jnp.bfloat16)

def project_rows(ref_table, interp_index, interp_frac):
    row_count, pixel_count = interp_index.shape
    wide_index = jnp.broadcast_to(interp_index[:, None, :], (row_count, 2, pixel_count)).astype(jnp.int32)
    low_value = jnp.take_along_axis(ref_table, wide_index, axis=2).astype(jnp.float32)
    high_value = jnp.take_along_axis(ref_table, wide_index + 1, axis=2).astype(jnp.float32)
    frac_wide = interp_frac[:, None, :]
    blended = (1.0 - frac_wide) * low_value + frac_wide * high_value
    return blended.reshape(row_count, 2 * pixel_count).astype(jnp.bfloat16)

def reference(images, noise_precision, assigned_class, class_refs, interp_index, interp_frac, shift_grid):
    cos_table, sin_table = phase_tables(shift_grid, PIX)
    row_ids = jnp.arange(2 * ORIENT, dtype=jnp.int32)
    half_ids = row_ids // 2 % 2
    orient_ids = 2 * (row_ids // 4) + row_ids % 2
    class_ids = orient_ids // (ORIENT // CLASSES)
    ref_table = class_refs[half_ids, class_ids]
    proj = project_rows(ref_table, interp_index, interp_frac)
    proj_groups = proj.reshape(ORIENT // 2, 2, 2, 2 * PIX)
    class_of_row = jnp.arange(ORIENT, dtype=jnp.int32) // (ORIENT // CLASSES)
    total_blocks = PARTICLES // PART_DEV
    all_images = images.reshape(total_blocks // 4, 2, 2, PART_DEV, 2 * PIX)
    all_prec = noise_precision.reshape(total_blocks // 4, 2, 2, PART_DEV)
    all_assign = assigned_class.reshape(total_blocks // 4, 2, 2, PART_DEV)
    likelihood_scale = 1.0 / math.sqrt(2 * PIX)
    class_mass = jnp.zeros((CLASSES,), jnp.float32)
    half_terms = []
    for half_idx in range(2):
        own_rows = proj_groups[:, half_idx].reshape(ORIENT, 2 * PIX)
        projection_power = lax.optimization_barrier(jnp.sum(jnp.square(own_rows.astype(jnp.float32)), axis=1))
        image_blocks = all_images[:, half_idx].reshape(total_blocks // 2, PART_DEV, 2 * PIX)
        prec_blocks = all_prec[:, half_idx].reshape(total_blocks // 2, PART_DEV)
        assign_blocks = all_assign[:, half_idx].reshape(total_blocks // 2, PART_DEV)

        def step(acc_state, item):
            back_term, mass_now = acc_state
            image_block, precision_block, assign_block = item
            stacked = shift_images(image_block, cos_table, sin_table, PIX)
            flat_stack = stacked.reshape(SHIFTS * PART_DEV, 2 * PIX)
            cross_correlation = jnp.dot(flat_stack, own_rows.T, preferred_element_type=jnp.float32).reshape(SHIFTS, PART_DEV, ORIENT)
            match_scores = (class_of_row[None, None, :] == assign_block[None, :, None]).astype(jnp.float32)
            log_likelihoods = precision_block[None, :, None] * (cross_correlation - 0.5 * projection_power[None, None, :]) * likelihood_scale + PRIOR_REWARD * match_scores
            peak_score = lax.optimization_barrier(jnp.max(log_likelihoods, axis=(0, 2), keepdims=True))
            exp_terms = jnp.exp(log_likelihoods - peak_score)
            posterior = exp_terms / lax.optimization_barrier(jnp.sum(exp_terms, axis=(0, 2), keepdims=True))
            weights = posterior.astype(jnp.bfloat16)
            weight_rows = weights.transpose(2, 0, 1).reshape(ORIENT, SHIFTS * PART_DEV)
            back_term = back_term + jnp.dot(weight_rows, flat_stack, preferred_element_type=jnp.float32)
            class_share = lax.optimization_barrier(jnp.sum(posterior, axis=0)).reshape(PART_DEV, CLASSES, ORIENT // CLASSES).sum(axis=2)
            mass_now = mass_now + lax.optimization_barrier(jnp.sum(precision_block[:, None] * class_share, axis=0))
            return ((back_term, mass_now), None)
        start_term = jnp.zeros((ORIENT, 2 * PIX), jnp.float32)
        (back_term, class_mass), _ = lax.scan(step, (start_term, class_mass), (image_blocks, prec_blocks, assign_blocks))
        half_terms.append(back_term / math.sqrt(PART_DEV))
    col_ids = jnp.arange(2 * PIX, dtype=jnp.int32)
    low_mask = col_ids % PIX < LOWK * KY
    averaged = (half_terms[0] + half_terms[1]) * 0.5
    first_half = jnp.where(low_mask[None, :], averaged, half_terms[0]).reshape(ORIENT // 2, 2, 2 * PIX)
    second = jnp.where(low_mask[None, :], averaged, half_terms[1]).reshape(ORIENT // 2, 2, 2 * PIX)
    back_slices = jnp.stack([first_half, second], axis=1).reshape(2 * ORIENT, 2 * PIX)
    class_weight = class_mass * (CLASSES / PARTICLES)
    return (back_slices, class_weight)
```

```python
import functools
import math

import jax
import jax.numpy as jnp
from jax import lax
from jax.experimental import pallas as pl
from jax.experimental.pallas import tpu as pltpu
from jax.sharding import PartitionSpec as P

KY = 128
BOX = 256
CLASSES = 8
LOWK = 16
LANES = 128
PRIOR_REWARD = 1.0
MASS_ROWS = 16
MIB = 1 << 20


def exchange(value, mask):
    pairs = [(source, source ^ mask) for source in range(lax.axis_size("particle"))]
    return lax.ppermute(value, "particle", pairs)


def whole_vmem(count):
    return [pl.BlockSpec(memory_space=pltpu.VMEM)] * count


def project_kernel(pick_ref, table_ref, index_ref, frac_ref, out_ref, flat, table, blended, *, chunk):
    highs = flat.shape[1]
    pixels = index_ref.shape[1]
    stride = table.shape[0] // 2

    def unfold(step, carry):
        piece = table_ref[0, 0, :, pl.ds(step * 8 * LANES, 8 * LANES)].astype(jnp.float32)
        for k in range(8):
            for comp in range(2):
                flat[comp, pl.ds(step * 8 + k, 1), :] = piece[comp : comp + 1, k * LANES : (k + 1) * LANES]
        return carry

    lax.fori_loop(0, highs // 8, unfold, 0)
    for comp in range(2):
        turned = flat[comp].T
        following = jnp.broadcast_to(pltpu.roll(turned[0:8], highs - 1, 1)[0:1], (16, highs))
        table[comp * stride : comp * stride + LANES, :] = turned.astype(jnp.bfloat16)
        table[comp * stride + LANES : (comp + 1) * stride, :] = following.astype(jnp.bfloat16)

    def body(step, carry):
        where = pl.ds(step * chunk, chunk)
        index = index_ref[:, where]
        frac = frac_ref[:, where]
        high = index // LANES
        low = index % LANES
        high_ids = lax.broadcasted_iota(jnp.int32, (highs, chunk), 0)
        one_hot = jnp.where(high_ids == high, 1.0, 0.0).astype(jnp.bfloat16)
        rows = jnp.dot(table[...], one_hot, preferred_element_type=jnp.float32)
        low_ids = lax.broadcasted_iota(jnp.int32, (LANES + 8, chunk), 0)
        weight = jnp.where(low_ids == low, 1.0 - frac, jnp.where(low_ids == low + 1, frac, 0.0))
        for comp in range(2):
            value = jnp.sum(
                rows[comp * stride : comp * stride + LANES + 8] * weight, axis=0, keepdims=True
            )
            for k in range(chunk // LANES):
                row = comp * (pixels // LANES) + step * (chunk // LANES) + k
                blended[pl.ds(row, 1), :] = value[:, k * LANES : (k + 1) * LANES]
        return carry

    lax.fori_loop(0, pixels // chunk, body, 0)
    out_ref[...] = blended[...].astype(jnp.bfloat16)


def project_row(class_refs, pick, interp_index, interp_frac):
    vox = class_refs.shape[3]
    pixels = interp_index.shape[1]
    highs = vox // LANES
    out_rows = 2 * pixels // LANES
    grid_spec = pltpu.PrefetchScalarGridSpec(
        num_scalar_prefetch=1,
        grid=(1,),
        in_specs=[
            pl.BlockSpec((1, 1, 2, vox), lambda i, pick: (pick[0], pick[1], 0, 0)),
            pl.BlockSpec((1, pixels), lambda i, pick: (0, 0)),
            pl.BlockSpec((1, pixels), lambda i, pick: (0, 0)),
        ],
        out_specs=pl.BlockSpec((out_rows, LANES), lambda i, pick: (0, 0)),
        scratch_shapes=[
            pltpu.VMEM((2, highs, LANES), jnp.float32),
            pltpu.VMEM((2 * (LANES + 16), highs), jnp.bfloat16),
            pltpu.VMEM((out_rows, LANES), jnp.float32),
        ],
    )
    return pl.pallas_call(
        functools.partial(project_kernel, chunk=1024),
        grid_spec=grid_spec,
        out_shape=jax.ShapeDtypeStruct((out_rows, LANES), jnp.bfloat16),
        compiler_params=pltpu.CompilerParams(vmem_limit_bytes=16 * MIB),
        name="project_row",
    )(pick, class_refs, interp_index, interp_frac)


def slot_rows(device, slots):
    ids = lax.broadcasted_iota(jnp.int32, (slots, 1), 0)
    flips, core_flip = ids % (slots // 2), ids // (slots // 2)
    return 2 * ((device // 4) ^ flips) + ((device % 2) ^ core_flip)


def split_mass(mass_row):
    ids = lax.broadcasted_iota(jnp.int32, (MASS_ROWS, LANES), 0)
    upper = mass_row.astype(jnp.bfloat16).astype(jnp.float32)
    lower = mass_row - upper
    return jnp.where(ids == 0, upper, jnp.where(ids == 1, lower, 0.0)).astype(jnp.bfloat16)


def joined_mass(block):
    return jnp.sum(block.astype(jnp.float32), axis=0, keepdims=True)


def expect_kernel(*refs, slots, chunk):
    device_ref, images, precision_ref, assigned_ref, shift_ref = refs[:5]
    row_refs = refs[5 : 5 + slots]
    keep, to_core, to_half, to_both, own_mass = refs[5 + slots : 10 + slots]
    proj, sums, cos_ref, sin_ref = refs[10 + slots :]
    device = device_ref[0]
    shifts = shift_ref.shape[0]
    parts = images.shape[0]
    pixels = images.shape[1] // 2
    tiles = pixels // LANES
    per_row = 2 * tiles
    half = slots // 2

    grid_x = shift_ref[:, 0:1]
    grid_y = shift_ref[:, 1:2]
    lane = lax.broadcasted_iota(jnp.int32, (shifts, KY), 1)
    turn_x = (lane * grid_x) & (BOX - 1)
    turn_y = ((lane - KY // 2) * grid_y) & (BOX - 1)
    angle_x = turn_x.astype(jnp.float32) * (2.0 * math.pi / BOX)
    angle_y = turn_y.astype(jnp.float32) * (2.0 * math.pi / BOX)
    cos_x, sin_x = jnp.cos(angle_x), jnp.sin(angle_x)
    cos_y, sin_y = jnp.cos(angle_y), jnp.sin(angle_y)
    for j in range(tiles):
        where = slice(j * LANES, (j + 1) * LANES)
        cos_j, sin_j = cos_x[:, j : j + 1], sin_x[:, j : j + 1]
        cos_ref[:, where] = cos_j * cos_y - sin_j * sin_y
        sin_ref[:, where] = sin_j * cos_y + cos_j * sin_y
    for slot in range(slots):
        proj[slot * per_row : (slot + 1) * per_row, :] = row_refs[slot][...].astype(jnp.float32)

    chunk_tiles = chunk // LANES
    contract_lanes = (((1,), (1,)), ((), ()))

    def correlate(step, carry):
        total, power = carry
        first = step * chunk_tiles
        real = jnp.concatenate(
            [proj[pl.ds(first + k, slots, stride=per_row), :] for k in range(chunk_tiles)], axis=1
        )
        imag = jnp.concatenate(
            [proj[pl.ds(tiles + first + k, slots, stride=per_row), :] for k in range(chunk_tiles)],
            axis=1,
        )
        where = pl.ds(pl.multiple_of(step * chunk, chunk), chunk)
        reals, imags = [], []
        for s in range(shifts):
            cos_s, sin_s = cos_ref[s : s + 1, where], sin_ref[s : s + 1, where]
            reals.append(real * cos_s - imag * sin_s)
            imags.append(real * sin_s + imag * cos_s)
        turned_real = jnp.concatenate(reals, axis=0).astype(jnp.bfloat16)
        turned_imag = jnp.concatenate(imags, axis=0).astype(jnp.bfloat16)
        image_real = images[:, where]
        image_imag = images[:, pl.ds(pl.multiple_of(pixels + step * chunk, chunk), chunk)]
        total = total + lax.dot_general(
            turned_real, image_real, contract_lanes, preferred_element_type=jnp.float32
        )
        total = total + lax.dot_general(
            turned_imag, image_imag, contract_lanes, preferred_element_type=jnp.float32
        )
        squares = real * real + imag * imag
        for k in range(chunk_tiles):
            power = power + squares[:, k * LANES : (k + 1) * LANES]
        return total, power

    total, power = lax.fori_loop(
        0,
        pixels // chunk,
        correlate,
        (
            jnp.zeros((shifts * slots, parts), jnp.float32),
            jnp.zeros((slots, LANES), jnp.float32),
        ),
    )
    power = jnp.sum(power, axis=1, keepdims=True)
    slot_class = slot_rows(device, slots) // (slots // CLASSES)
    match = (slot_class == assigned_ref[...]).astype(jnp.float32) * PRIOR_REWARD
    precision = precision_ref[...]
    likelihood_scale = 1.0 / math.sqrt(2 * pixels)
    logits = [
        precision * (total[s * slots : (s + 1) * slots] - 0.5 * power) * likelihood_scale + match
        for s in range(shifts)
    ]
    peak = functools.reduce(jnp.maximum, logits)
    peak = jnp.max(peak, axis=0, keepdims=True)
    terms = [jnp.exp(value - peak) for value in logits]
    mass = functools.reduce(jnp.add, terms)
    norm = jnp.sum(mass, axis=0, keepdims=True)
    weights = jnp.concatenate([term / norm for term in terms], axis=0).astype(jnp.bfloat16)
    slot_mass = jnp.sum(mass / norm * precision, axis=1, keepdims=True)
    class_lane = lax.broadcasted_iota(jnp.int32, (slots, LANES), 1)
    mass_row = jnp.sum(
        jnp.where(class_lane == slot_class, slot_mass, 0.0), axis=0, keepdims=True
    )

    def backproject(step, carry):
        where = pl.ds(pl.multiple_of(step * chunk, chunk), chunk)
        image_real = images[:, where]
        image_imag = images[:, pl.ds(pl.multiple_of(pixels + step * chunk, chunk), chunk)]
        from_real = jnp.dot(weights, image_real, preferred_element_type=jnp.float32)
        from_imag = jnp.dot(weights, image_imag, preferred_element_type=jnp.float32)
        real = jnp.zeros((slots, chunk), jnp.float32)
        imag = jnp.zeros((slots, chunk), jnp.float32)
        for s in range(shifts):
            cos_s, sin_s = cos_ref[s : s + 1, where], sin_ref[s : s + 1, where]
            part_real = from_real[s * slots : (s + 1) * slots]
            part_imag = from_imag[s * slots : (s + 1) * slots]
            real = real + (part_real * cos_s + part_imag * sin_s)
            imag = imag + (part_imag * cos_s - part_real * sin_s)
        first = step * chunk_tiles
        for k in range(chunk_tiles):
            piece = slice(k * LANES, (k + 1) * LANES)
            sums[pl.ds(first + k, slots, stride=per_row), :] = real[:, piece]
            sums[pl.ds(tiles + first + k, slots, stride=per_row), :] = imag[:, piece]
        return carry

    lax.fori_loop(0, pixels // chunk, backproject, 0)

    body = half * per_row
    low_rows = LOWK * KY // LANES
    mass_block = split_mass(mass_row)
    keep[...] = sums[0:body, :]
    to_core[0:body, :] = sums[body : 2 * body, :].astype(jnp.bfloat16)
    to_core[body:, :] = mass_block
    for target, start in ((to_half, 0), (to_both, half)):
        for m in range(half):
            for comp in range(2):
                source = (start + m) * per_row + comp * tiles
                dest = (2 * m + comp) * low_rows
                target[dest : dest + low_rows, :] = sums[source : source + low_rows, :].astype(
                    jnp.bfloat16
                )
        target[2 * half * low_rows :, :] = mass_block
    own_mass[...] = jnp.broadcast_to(mass_row, own_mass.shape)


def expect(device, images, precision, assigned, shift_grid, rows):
    slots = len(rows)
    half = slots // 2
    pixels = images.shape[1] // 2
    per_row = 2 * pixels // LANES
    shifts = shift_grid.shape[0]
    low = 2 * half * (LOWK * KY // LANES) + MASS_ROWS
    limit = (12 + 2 * slots) * MIB
    return pl.pallas_call(
        functools.partial(expect_kernel, slots=slots, chunk=512),
        in_specs=[pl.BlockSpec(memory_space=pltpu.SMEM)] + whole_vmem(4 + slots),
        out_specs=whole_vmem(5),
        out_shape=[
            jax.ShapeDtypeStruct((half * per_row, LANES), jnp.float32),
            jax.ShapeDtypeStruct((half * per_row + MASS_ROWS, LANES), jnp.bfloat16),
            jax.ShapeDtypeStruct((low, LANES), jnp.bfloat16),
            jax.ShapeDtypeStruct((low, LANES), jnp.bfloat16),
            jax.ShapeDtypeStruct((8, LANES), jnp.float32),
        ],
        scratch_shapes=[
            pltpu.VMEM((slots * per_row, LANES), jnp.float32),
            pltpu.VMEM((slots * per_row, LANES), jnp.float32),
            pltpu.VMEM((shifts, pixels), jnp.float32),
            pltpu.VMEM((shifts, pixels), jnp.float32),
        ],
        compiler_params=pltpu.CompilerParams(vmem_limit_bytes=limit),
        name="expect",
    )(device, images, precision, assigned, shift_grid, *rows)


def merge_kernel(keep, from_core, from_half, from_both, mass, *outs, half):
    own, own_mass, sends = outs[0], outs[1], outs[2:]
    per_row = own.shape[0]
    tiles = per_row // 2
    low_rows = LOWK * KY // LANES
    body = half * per_row
    low_body = 2 * half * low_rows
    total_mass = (
        mass[0:1, :]
        + joined_mass(from_core[body:, :])
        + joined_mass(from_half[low_body:, :])
        + joined_mass(from_both[low_body:, :])
    )
    mass_block = split_mass(total_mass)
    own_mass[...] = jnp.broadcast_to(total_mass, own_mass.shape)
    for m in range(half):
        target = own if m == 0 else sends[m - 1]
        for comp in range(2):
            start = comp * tiles
            source = m * per_row + start
            low = (2 * m + comp) * low_rows
            own_low = keep[source : source + low_rows, :] + from_core[
                source : source + low_rows, :
            ].astype(jnp.float32)
            other_low = from_half[low : low + low_rows, :].astype(jnp.float32) + from_both[
                low : low + low_rows, :
            ].astype(jnp.float32)
            target[start : start + low_rows, :] = ((own_low + other_low) * 0.5).astype(target.dtype)
            rest = slice(source + low_rows, source + tiles)
            target[start + low_rows : start + tiles, :] = (
                keep[rest, :] + from_core[rest, :].astype(jnp.float32)
            ).astype(target.dtype)
        if m > 0:
            target[per_row:, :] = mass_block


def merge(keep, from_core, from_half, from_both, mass, half):
    per_row = keep.shape[0] // half
    return pl.pallas_call(
        functools.partial(merge_kernel, half=half),
        in_specs=whole_vmem(5),
        out_specs=whole_vmem(1 + half),
        out_shape=[
            jax.ShapeDtypeStruct((per_row, LANES), jnp.float32),
            jax.ShapeDtypeStruct((8, LANES), jnp.float32),
        ]
        + [jax.ShapeDtypeStruct((per_row + MASS_ROWS, LANES), jnp.bfloat16)] * (half - 1),
        compiler_params=pltpu.CompilerParams(vmem_limit_bytes=(12 + 2 * half) * MIB),
        name="merge",
    )(keep, from_core, from_half, from_both, mass)


def finish_kernel(*refs, scale, mass_scale):
    own, mass = refs[0], refs[1]
    received, (out, mass_out) = refs[2:-2], refs[-2:]
    per_row = own.shape[0]
    total = own[...]
    total_mass = mass[0:1, :]
    for ref in received:
        total = total + ref[0:per_row, :].astype(jnp.float32)
        total_mass = total_mass + joined_mass(ref[per_row:, :])
    out[...] = total * scale
    mass_out[...] = jnp.broadcast_to(total_mass * mass_scale, mass_out.shape)


def finish(own, mass, received, scale, mass_scale):
    return pl.pallas_call(
        functools.partial(finish_kernel, scale=scale, mass_scale=mass_scale),
        in_specs=whole_vmem(2 + len(received)),
        out_specs=whole_vmem(2),
        out_shape=[
            jax.ShapeDtypeStruct(own.shape, jnp.float32),
            jax.ShapeDtypeStruct(mass.shape, jnp.float32),
        ],
        compiler_params=pltpu.CompilerParams(vmem_limit_bytes=16 * MIB),
        name="finish",
    )(own, mass, *received)


def local(
    images, noise_precision, assigned_class, class_refs, interp_index, interp_frac, shift_grid
):
    dev_count = lax.axis_size("particle")
    device = lax.axis_index("particle").astype(jnp.int32)
    orient_count = dev_count // 2
    half = dev_count // 4
    part_count = images.shape[0]
    half_set = device // 2 % 2
    class_id = (2 * (device // 4) + device % 2) // (orient_count // CLASSES)
    own_row = project_row(
        class_refs, jnp.stack([half_set, class_id]), interp_index, interp_frac
    )
    same_core = [own_row] + [exchange(own_row, 4 * m) for m in range(1, half)]
    rows = same_core + [exchange(row, 1) for row in same_core]
    keep, to_core, to_half, to_both, mass = expect(
        device.reshape(1),
        images,
        noise_precision.reshape(1, part_count),
        assigned_class.reshape(1, part_count),
        shift_grid,
        rows,
    )
    merged = merge(
        keep, exchange(to_core, 1), exchange(to_half, 2), exchange(to_both, 3), mass, half
    )
    own, mass, sends = merged[0], merged[1], merged[2:]
    received = [exchange(send, 4 * (m + 1)) for m, send in enumerate(sends)]
    back, class_mass = finish(
        own,
        mass,
        received,
        1.0 / math.sqrt(part_count),
        CLASSES / (part_count * dev_count),
    )
    return back.reshape(1, images.shape[1]), class_mass[0, :CLASSES]


def solution(mesh):
    in_specs = (
        P(("groups", "particle"), None),
        P(("groups", "particle")),
        P(("groups", "particle")),
        P("groups", None, None, None),
        P("particle", None),
        P("particle", None),
        P(),
    )
    out_specs = (P(("groups", "particle"), None), P("groups"))
    return jax.shard_map(local, mesh=mesh, in_specs=in_specs, out_specs=out_specs, check_vma=False)
```

```python
import functools
import math

import jax
import jax.numpy as jnp
from jax import lax
from jax.experimental import pallas as pl
from jax.experimental.pallas import tpu as pltpu
from jax.sharding import PartitionSpec as P

KY = 128
BOX = 256
CLASSES = 8
LOWK = 16
LANES = 128
PRIOR_REWARD = 1.0
MASS_ROWS = 16
MIB = 1 << 20


def exchange(value, mask):
    pairs = [(source, source ^ mask) for source in range(lax.axis_size("particle"))]
    return lax.ppermute(value, "particle", pairs)


def across_z(value):
    count = lax.axis_size("particle")
    groups = [list(range(first, count, 4)) for first in range(4)]
    return lax.all_to_all(
        value, "particle", split_axis=0, concat_axis=0, axis_index_groups=groups, tiled=True
    )


def whole_vmem(count):
    return [pl.BlockSpec(memory_space=pltpu.VMEM)] * count


def project_kernel(pick_ref, table_ref, index_ref, frac_ref, out_ref, flat, table, blended, *, chunk):
    highs = flat.shape[1]
    pixels = index_ref.shape[1]
    stride = table.shape[0] // 2

    def unfold(step, carry):
        piece = table_ref[0, 0, :, pl.ds(step * 8 * LANES, 8 * LANES)].astype(jnp.float32)
        for k in range(8):
            for comp in range(2):
                flat[comp, pl.ds(step * 8 + k, 1), :] = piece[comp : comp + 1, k * LANES : (k + 1) * LANES]
        return carry

    lax.fori_loop(0, highs // 8, unfold, 0)
    for comp in range(2):
        turned = flat[comp].T
        following = jnp.broadcast_to(pltpu.roll(turned[0:8], highs - 1, 1)[0:1], (16, highs))
        table[comp * stride : comp * stride + LANES, :] = turned.astype(jnp.bfloat16)
        table[comp * stride + LANES : (comp + 1) * stride, :] = following.astype(jnp.bfloat16)

    def body(step, carry):
        where = pl.ds(step * chunk, chunk)
        index = index_ref[:, where]
        frac = frac_ref[:, where]
        high = index // LANES
        low = index % LANES
        high_ids = lax.broadcasted_iota(jnp.int32, (highs, chunk), 0)
        one_hot = jnp.where(high_ids == high, 1.0, 0.0).astype(jnp.bfloat16)
        rows = jnp.dot(table[...], one_hot, preferred_element_type=jnp.float32)
        low_ids = lax.broadcasted_iota(jnp.int32, (LANES + 8, chunk), 0)
        weight = jnp.where(low_ids == low, 1.0 - frac, jnp.where(low_ids == low + 1, frac, 0.0))
        for comp in range(2):
            value = jnp.sum(
                rows[comp * stride : comp * stride + LANES + 8] * weight, axis=0, keepdims=True
            )
            for k in range(chunk // LANES):
                row = comp * (pixels // LANES) + step * (chunk // LANES) + k
                blended[pl.ds(row, 1), :] = value[:, k * LANES : (k + 1) * LANES]
        return carry

    lax.fori_loop(0, pixels // chunk, body, 0)
    row = blended[...].astype(jnp.bfloat16)
    for m in range(out_ref.shape[0]):
        out_ref[m] = row


def project_row(class_refs, pick, interp_index, interp_frac, copies):
    vox = class_refs.shape[3]
    pixels = interp_index.shape[1]
    highs = vox // LANES
    out_rows = 2 * pixels // LANES
    grid_spec = pltpu.PrefetchScalarGridSpec(
        num_scalar_prefetch=1,
        grid=(1,),
        in_specs=[
            pl.BlockSpec((1, 1, 2, vox), lambda i, pick: (pick[0], pick[1], 0, 0)),
            pl.BlockSpec((1, pixels), lambda i, pick: (0, 0)),
            pl.BlockSpec((1, pixels), lambda i, pick: (0, 0)),
        ],
        out_specs=pl.BlockSpec((copies, out_rows, LANES), lambda i, pick: (0, 0, 0)),
        scratch_shapes=[
            pltpu.VMEM((2, highs, LANES), jnp.float32),
            pltpu.VMEM((2 * (LANES + 16), highs), jnp.bfloat16),
            pltpu.VMEM((out_rows, LANES), jnp.float32),
        ],
    )
    return pl.pallas_call(
        functools.partial(project_kernel, chunk=1024),
        grid_spec=grid_spec,
        out_shape=jax.ShapeDtypeStruct((copies, out_rows, LANES), jnp.bfloat16),
        compiler_params=pltpu.CompilerParams(vmem_limit_bytes=56 * MIB),
        name="project_row",
    )(pick, class_refs, interp_index, interp_frac)


def slot_rows(device, slots):
    ids = lax.broadcasted_iota(jnp.int32, (slots, 1), 0)
    place, core_flip = ids % (slots // 2), ids // (slots // 2)
    return 2 * place + ((device % 2) ^ core_flip)


def split_mass(mass_row):
    ids = lax.broadcasted_iota(jnp.int32, (MASS_ROWS, LANES), 0)
    upper = mass_row.astype(jnp.bfloat16).astype(jnp.float32)
    lower = mass_row - upper
    return jnp.where(ids == 0, upper, jnp.where(ids == 1, lower, 0.0)).astype(jnp.bfloat16)


def joined_mass(block):
    return jnp.sum(block.astype(jnp.float32), axis=0, keepdims=True)


def table_kernel(shift_ref, cos_ref, sin_ref):
    shifts, pixels = cos_ref.shape
    grid_x = shift_ref[:, 0:1]
    grid_y = shift_ref[:, 1:2]
    lane = lax.broadcasted_iota(jnp.int32, (shifts, KY), 1)
    turn_x = (lane * grid_x) & (BOX - 1)
    turn_y = ((lane - KY // 2) * grid_y) & (BOX - 1)
    angle_x = turn_x.astype(jnp.float32) * (2.0 * math.pi / BOX)
    angle_y = turn_y.astype(jnp.float32) * (2.0 * math.pi / BOX)
    cos_x, sin_x = jnp.cos(angle_x), jnp.sin(angle_x)
    cos_y, sin_y = jnp.cos(angle_y), jnp.sin(angle_y)
    for j in range(pixels // LANES):
        where = slice(j * LANES, (j + 1) * LANES)
        cos_j, sin_j = cos_x[:, j : j + 1], sin_x[:, j : j + 1]
        cos_ref[:, where] = cos_j * cos_y - sin_j * sin_y
        sin_ref[:, where] = sin_j * cos_y + cos_j * sin_y


def phase_tables(shift_grid, pixels):
    shape = jax.ShapeDtypeStruct((shift_grid.shape[0], pixels), jnp.float32)
    return pl.pallas_call(
        table_kernel,
        in_specs=whole_vmem(1),
        out_specs=whole_vmem(2),
        out_shape=[shape, shape],
        compiler_params=pltpu.CompilerParams(vmem_limit_bytes=16 * MIB),
        cost_estimate=pl.CostEstimate(flops=2000000, bytes_accessed=2000000, transcendentals=0),
        name="phase_tables",
    )(shift_grid)


def rotate_back(weights, images, cos_ref, sin_ref, where, imag_where, slots):
    from_real = jnp.dot(weights, images[:, where], preferred_element_type=jnp.float32)
    from_imag = jnp.dot(weights, images[:, imag_where], preferred_element_type=jnp.float32)
    real = imag = None
    for s in range(cos_ref.shape[0]):
        cos_s, sin_s = cos_ref[s : s + 1, where], sin_ref[s : s + 1, where]
        part_real = from_real[s * slots : (s + 1) * slots]
        part_imag = from_imag[s * slots : (s + 1) * slots]
        real_s = part_real * cos_s + part_imag * sin_s
        imag_s = part_imag * cos_s - part_real * sin_s
        real = real_s if real is None else real + real_s
        imag = imag_s if imag is None else imag + imag_s
    return real, imag


def expect_kernel(
    device_ref, images, precision_ref, assigned_ref, cos_ref, sin_ref, row_ref, other_ref,
    weight_ref, low_ref, low_send, own_mass, proj, *, slots, chunk
):
    device = device_ref[0]
    shifts = cos_ref.shape[0]
    parts = images.shape[0]
    pixels = images.shape[1] // 2
    tiles = pixels // LANES
    per_row = 2 * tiles
    half = slots // 2
    for m in range(half):
        proj[m * per_row : (m + 1) * per_row, :] = row_ref[m].astype(jnp.float32)
        proj[(half + m) * per_row : (half + m + 1) * per_row, :] = other_ref[m].astype(jnp.float32)

    chunk_tiles = chunk // LANES
    contract_lanes = (((1,), (1,)), ((), ()))

    def correlate(step, carry):
        total, power = carry
        first = step * chunk_tiles
        real = jnp.concatenate(
            [proj[pl.ds(first + k, slots, stride=per_row), :] for k in range(chunk_tiles)], axis=1
        )
        imag = jnp.concatenate(
            [proj[pl.ds(tiles + first + k, slots, stride=per_row), :] for k in range(chunk_tiles)],
            axis=1,
        )
        where = pl.ds(pl.multiple_of(step * chunk, chunk), chunk)
        reals, imags = [], []
        for s in range(shifts):
            cos_s, sin_s = cos_ref[s : s + 1, where], sin_ref[s : s + 1, where]
            reals.append(real * cos_s - imag * sin_s)
            imags.append(real * sin_s + imag * cos_s)
        turned_real = jnp.concatenate(reals, axis=0).astype(jnp.bfloat16)
        turned_imag = jnp.concatenate(imags, axis=0).astype(jnp.bfloat16)
        image_real = images[:, where]
        image_imag = images[:, pl.ds(pl.multiple_of(pixels + step * chunk, chunk), chunk)]
        total = total + lax.dot_general(
            turned_real, image_real, contract_lanes, preferred_element_type=jnp.float32
        )
        total = total + lax.dot_general(
            turned_imag, image_imag, contract_lanes, preferred_element_type=jnp.float32
        )
        squares = real * real + imag * imag
        for k in range(chunk_tiles):
            power = power + squares[:, k * LANES : (k + 1) * LANES]
        return total, power

    total, power = lax.fori_loop(
        0,
        pixels // chunk,
        correlate,
        (
            jnp.zeros((shifts * slots, parts), jnp.float32),
            jnp.zeros((slots, LANES), jnp.float32),
        ),
    )
    power = jnp.sum(power, axis=1, keepdims=True)
    slot_class = slot_rows(device, slots) // (slots // CLASSES)
    match = (slot_class == assigned_ref[...]).astype(jnp.float32) * PRIOR_REWARD
    precision = precision_ref[...]
    likelihood_scale = 1.0 / math.sqrt(2 * pixels)
    logits = [
        precision * (total[s * slots : (s + 1) * slots] - 0.5 * power) * likelihood_scale + match
        for s in range(shifts)
    ]
    peak = functools.reduce(jnp.maximum, logits)
    peak = jnp.max(peak, axis=0, keepdims=True)
    terms = [jnp.exp(value - peak) for value in logits]
    mass = functools.reduce(jnp.add, terms)
    norm = jnp.sum(mass, axis=0, keepdims=True)
    weights = jnp.concatenate([term / norm for term in terms], axis=0).astype(jnp.bfloat16)
    weight_ref[...] = weights
    slot_mass = jnp.sum(mass / norm * precision, axis=1, keepdims=True)
    class_lane = lax.broadcasted_iota(jnp.int32, (slots, LANES), 1)
    mass_row = jnp.sum(
        jnp.where(class_lane == slot_class, slot_mass, 0.0), axis=0, keepdims=True
    )
    own_mass[...] = jnp.broadcast_to(mass_row, own_mass.shape)

    low_rows = LOWK * KY // LANES
    low_width = LOWK * KY
    real, imag = rotate_back(
        weights, images, cos_ref, sin_ref, slice(0, low_width), slice(pixels, pixels + low_width), slots
    )
    for k in range(low_rows):
        piece = slice(k * LANES, (k + 1) * LANES)
        low_ref[pl.ds(k, slots, stride=2 * low_rows), :] = real[:, piece]
        low_ref[pl.ds(low_rows + k, slots, stride=2 * low_rows), :] = imag[:, piece]
    low_body = low_ref.shape[0]
    low_send[0:low_body, :] = low_ref[...].astype(jnp.bfloat16)
    low_send[low_body:, :] = split_mass(mass_row)


def expect(device, images, precision, assigned, cos_table, sin_table, rows, others):
    slots = 2 * rows.shape[0]
    pixels = images.shape[1] // 2
    per_row = 2 * pixels // LANES
    shifts = cos_table.shape[0]
    low = slots * 2 * (LOWK * KY // LANES)
    return pl.pallas_call(
        functools.partial(expect_kernel, slots=slots, chunk=2048),
        in_specs=[pl.BlockSpec(memory_space=pltpu.SMEM)] + whole_vmem(7),
        out_specs=whole_vmem(4),
        out_shape=[
            jax.ShapeDtypeStruct((shifts * slots, images.shape[0]), jnp.bfloat16),
            jax.ShapeDtypeStruct((low, LANES), jnp.float32),
            jax.ShapeDtypeStruct((low + MASS_ROWS, LANES), jnp.bfloat16),
            jax.ShapeDtypeStruct((8, LANES), jnp.float32),
        ],
        scratch_shapes=[pltpu.VMEM((slots * per_row, LANES), jnp.float32)],
        compiler_params=pltpu.CompilerParams(vmem_limit_bytes=(14 + slots // 2) * MIB),
        name="expect",
    )(device, images, precision, assigned, cos_table, sin_table, rows, others)


def backproject_kernel(weight_ref, images, cos_ref, sin_ref, sums, *, slots, chunk):
    pixels = images.shape[1] // 2
    tiles = pixels // LANES
    per_row = 2 * tiles
    chunk_tiles = chunk // LANES
    weights = weight_ref[...]

    def body(step, carry):
        where = pl.ds(pl.multiple_of(step * chunk, chunk), chunk)
        imag_where = pl.ds(pl.multiple_of(pixels + step * chunk, chunk), chunk)
        real, imag = rotate_back(weights, images, cos_ref, sin_ref, where, imag_where, slots)
        first = step * chunk_tiles
        for k in range(chunk_tiles):
            piece = slice(k * LANES, (k + 1) * LANES)
            sums[pl.ds(first + k, slots, stride=per_row), :] = real[:, piece]
            sums[pl.ds(tiles + first + k, slots, stride=per_row), :] = imag[:, piece]
        return carry

    lax.fori_loop(LOWK * KY // chunk, pixels // chunk, body, 0)


def backproject(weights, images, cos_table, sin_table, slots):
    per_row = images.shape[1] // LANES
    return pl.pallas_call(
        functools.partial(backproject_kernel, slots=slots, chunk=2048),
        in_specs=whole_vmem(4),
        out_specs=pl.BlockSpec(memory_space=pltpu.VMEM),
        out_shape=jax.ShapeDtypeStruct((slots * per_row, LANES), jnp.float32),
        compiler_params=pltpu.CompilerParams(vmem_limit_bytes=(14 + slots // 2) * MIB),
        cost_estimate=pl.CostEstimate(flops=20000000, bytes_accessed=20000000, transcendentals=0),
        name="backproject",
    )(weights, images, cos_table, sin_table)


def fold_kernel(sums_in, low_ref, low_received, mass, keep, to_core, total_mass, *, slots):
    per_row = sums_in.shape[0] // slots
    tiles = per_row // 2
    low_rows = LOWK * KY // LANES
    half = slots // 2
    low_body = low_ref.shape[0]
    folded = mass[0:1, :] + joined_mass(low_received[low_body:, :])
    total_mass[...] = jnp.broadcast_to(folded, total_mass.shape)
    for slot in range(slots):
        target = keep if slot < half else to_core
        for comp in range(2):
            low = slice((2 * slot + comp) * low_rows, (2 * slot + comp + 1) * low_rows)
            start = slot * per_row + comp * tiles
            dest = (slot % half) * per_row + comp * tiles
            value = (low_ref[low, :] + low_received[low, :].astype(jnp.float32)) * 0.5
            target[dest : dest + low_rows, :] = value.astype(target.dtype)
            target[dest + low_rows : dest + tiles, :] = sums_in[
                start + low_rows : start + tiles, :
            ].astype(target.dtype)
    to_core[half * per_row :, :] = split_mass(folded)


def fold(sums, low, low_received, mass, slots):
    half_rows = sums.shape[0] // 2
    return pl.pallas_call(
        functools.partial(fold_kernel, slots=slots),
        in_specs=whole_vmem(4),
        out_specs=whole_vmem(3),
        out_shape=[
            jax.ShapeDtypeStruct((half_rows, LANES), jnp.float32),
            jax.ShapeDtypeStruct((half_rows + MASS_ROWS, LANES), jnp.bfloat16),
            jax.ShapeDtypeStruct((8, LANES), jnp.float32),
        ],
        compiler_params=pltpu.CompilerParams(vmem_limit_bytes=(10 + slots // 2) * MIB),
        name="fold",
    )(sums, low, low_received, mass)


def merge_kernel(keep, from_core, mass, out, *, half):
    per_row = keep.shape[0] // half
    total_mass = mass[0:1, :] + joined_mass(from_core[half * per_row :, :])
    block = split_mass(total_mass)
    for m in range(half):
        rows = slice(m * per_row, (m + 1) * per_row)
        out[m, 0:per_row, :] = (keep[rows, :] + from_core[rows, :].astype(jnp.float32)).astype(
            jnp.bfloat16
        )
        out[m, per_row:, :] = block


def merge(keep, from_core, mass, half):
    per_row = keep.shape[0] // half
    return pl.pallas_call(
        functools.partial(merge_kernel, half=half),
        in_specs=whole_vmem(3),
        out_specs=pl.BlockSpec(memory_space=pltpu.VMEM),
        out_shape=jax.ShapeDtypeStruct((half, per_row + MASS_ROWS, LANES), jnp.bfloat16),
        compiler_params=pltpu.CompilerParams(vmem_limit_bytes=(12 + half) * MIB),
        name="merge",
    )(keep, from_core, mass)


def finish_kernel(received, out, mass_out, *, scale, mass_scale):
    per_row = out.shape[0]
    total, total_mass = None, None
    for m in range(received.shape[0]):
        value = received[m, 0:per_row, :].astype(jnp.float32)
        mass = joined_mass(received[m, per_row:, :])
        total = value if total is None else total + value
        total_mass = mass if total_mass is None else total_mass + mass
    out[...] = total * scale
    mass_out[...] = total_mass[0, :CLASSES] * mass_scale


def finish(received, scale, mass_scale):
    return pl.pallas_call(
        functools.partial(finish_kernel, scale=scale, mass_scale=mass_scale),
        in_specs=whole_vmem(1),
        out_specs=whole_vmem(2),
        out_shape=[
            jax.ShapeDtypeStruct((received.shape[1] - MASS_ROWS, LANES), jnp.float32),
            jax.ShapeDtypeStruct((CLASSES,), jnp.float32),
        ],
        compiler_params=pltpu.CompilerParams(vmem_limit_bytes=16 * MIB),
        name="finish",
    )(received)


def local(
    images, noise_precision, assigned_class, class_refs, interp_index, interp_frac, shift_grid
):
    dev_count = lax.axis_size("particle")
    device = lax.axis_index("particle").astype(jnp.int32)
    slots = dev_count // 2
    part_count = images.shape[0]
    half_set = device // 2 % 2
    class_id = (2 * (device // 4) + device % 2) // (slots // CLASSES)
    copies = project_row(
        class_refs, jnp.stack([half_set, class_id]), interp_index, interp_frac, slots // 2
    )
    rows = across_z(copies)
    cos_table, sin_table = phase_tables(shift_grid, images.shape[1] // 2)
    weights, low, low_send, mass = expect(
        device.reshape(1),
        images,
        noise_precision.reshape(1, part_count),
        assigned_class.reshape(1, part_count),
        cos_table,
        sin_table,
        rows,
        exchange(rows, 1),
    )
    low_received = exchange(low_send, 2)
    sums = backproject(weights, images, cos_table, sin_table, slots)
    keep, to_core, mass = fold(sums, low, low_received, mass, slots)
    received = across_z(merge(keep, exchange(to_core, 1), mass, slots // 2))
    back, class_mass = finish(
        received, 1.0 / math.sqrt(part_count), CLASSES / (part_count * dev_count)
    )
    return back.reshape(1, images.shape[1]), class_mass


def solution(mesh):
    in_specs = (
        P(("groups", "particle"), None),
        P(("groups", "particle")),
        P(("groups", "particle")),
        P("groups", None, None, None),
        P("particle", None),
        P("particle", None),
        P(),
    )
    out_specs = (P(("groups", "particle"), None), P("groups"))
    return jax.shard_map(local, mesh=mesh, in_specs=in_specs, out_specs=out_specs, check_vma=False)
```

```python
import functools
import math

import jax
import jax.numpy as jnp
from jax import lax
from jax.experimental import pallas as pl
from jax.experimental.pallas import tpu as pltpu
from jax.sharding import PartitionSpec as P

KY = 128
BOX = 256
CLASSES = 8
LOWK = 16
LANES = 128
PRIOR_REWARD = 1.0
MASS_ROWS = 16
MIB = 1 << 20


def exchange(value, mask):
    pairs = [(source, source ^ mask) for source in range(lax.axis_size("particle"))]
    return lax.ppermute(value, "particle", pairs)


def in_hbm(value):
    return pltpu.with_memory_space_constraint(value, pltpu.HBM)


def whole_vmem(count):
    return [pl.BlockSpec(memory_space=pltpu.VMEM)] * count


def tree_select(values, masks):
    for mask in masks:
        values = [
            jnp.where(mask, values[i + 1], values[i]) if i + 1 < len(values) else values[i]
            for i in range(0, len(values), 2)
        ]
    return values[0]


def project_kernel(
    table_hbm, index_hbm, frac_hbm, out_ref,
    table_in, index_ref, frac_ref, flat, wide, table, blended, sems, *, chunk
):
    device = lax.axis_index("particle")
    row_count = lax.axis_size("particle") // 2
    half_set = device // 2 % 2
    class_id = (2 * (device // 4) + device % 2) // (row_count // CLASSES)
    copies = [
        pltpu.make_async_copy(
            table_hbm.at[pl.ds(half_set, 1), pl.ds(class_id, 1)], table_in, sems.at[0]
        ),
        pltpu.make_async_copy(index_hbm, index_ref, sems.at[1]),
        pltpu.make_async_copy(frac_hbm, frac_ref, sems.at[2]),
    ]
    for copy in copies:
        copy.start()
    copies[0].wait()
    highs = flat.shape[1]
    pixels = index_ref.shape[1]
    groups = table.shape[0] // 16
    stride = 8 * groups

    def unfold(step, carry):
        piece = table_in[0, 0, :, pl.ds(step * 8 * LANES, 8 * LANES)].astype(jnp.float32)
        for k in range(8):
            for comp in range(2):
                flat[comp, pl.ds(step * 8 + k, 1), :] = piece[comp : comp + 1, k * LANES : (k + 1) * LANES]
        return carry

    lax.fori_loop(0, highs // 8, unfold, 0, unroll=4)
    picked = []
    for comp in range(2):
        turned = flat[comp].T
        wide[0:LANES, :] = turned
        wide[LANES : LANES + 8, :] = pltpu.roll(turned[0:8], highs - 1, 1)
        picked += [wide[7 * g : 7 * g + 8, :] for g in range(groups)]
    for pair in range(groups):
        table[16 * pair : 16 * (pair + 1), :] = jnp.concatenate(
            picked[2 * pair : 2 * pair + 2], axis=0
        ).astype(jnp.bfloat16)
    copies[1].wait()
    copies[2].wait()

    def body(step, carry):
        where = pl.ds(pl.multiple_of(step * chunk, chunk), chunk)
        index = index_ref[:, where]
        frac = frac_ref[:, where]
        high = index >> 7
        low = index & (LANES - 1)
        group = (low * 147) >> 10
        first = low - 7 * group
        high_ids = lax.broadcasted_iota(jnp.int32, (highs, chunk), 0)
        one_hot = jnp.where(high_ids == high, 1.0, 0.0).astype(jnp.bfloat16)
        rows = jnp.dot(table[...], one_hot, preferred_element_type=jnp.float32)
        group = jnp.broadcast_to(group, (8, chunk))
        masks = [(group & (1 << bit)) != 0 for bit in range((groups - 1).bit_length())]
        ids = lax.broadcasted_iota(jnp.int32, (8, chunk), 0)
        weight = jnp.where(ids == first, 1.0 - frac, jnp.where(ids == first + 1, frac, 0.0))
        for comp in range(2):
            start = comp * stride
            picked = tree_select([rows[start + 8 * g : start + 8 * g + 8] for g in range(groups)], masks)
            value = jnp.sum(picked * weight, axis=0, keepdims=True)
            for k in range(chunk // LANES):
                row = comp * (pixels // LANES) + step * (chunk // LANES) + k
                blended[pl.ds(row, 1), :] = value[:, k * LANES : (k + 1) * LANES]
        return carry

    lax.fori_loop(0, pixels // chunk, body, 0, unroll=2)
    out_ref[...] = blended[...].astype(jnp.bfloat16)


def project_row(class_refs, interp_index, interp_frac):
    vox = class_refs.shape[3]
    pixels = interp_index.shape[1]
    highs = vox // LANES
    out_rows = 2 * pixels // LANES
    groups = -(-LANES // 7)
    return pl.pallas_call(
        functools.partial(project_kernel, chunk=1024),
        in_specs=[pl.BlockSpec(memory_space=pltpu.HBM)] * 3,
        out_specs=pl.BlockSpec(memory_space=pltpu.VMEM),
        out_shape=jax.ShapeDtypeStruct((out_rows, LANES), jnp.bfloat16),
        scratch_shapes=[
            pltpu.VMEM((1, 1, 2, vox), jnp.bfloat16),
            pltpu.VMEM((1, pixels), jnp.int32),
            pltpu.VMEM((1, pixels), jnp.float32),
            pltpu.VMEM((2, highs, LANES), jnp.float32),
            pltpu.VMEM((LANES + 8, highs), jnp.float32),
            pltpu.VMEM((16 * groups, highs), jnp.bfloat16),
            pltpu.VMEM((out_rows, LANES), jnp.float32),
            pltpu.SemaphoreType.DMA((3,)),
        ],
        compiler_params=pltpu.CompilerParams(vmem_limit_bytes=16 * MIB),
        name="project_row",
    )(*(in_hbm(value) for value in (class_refs, interp_index, interp_frac)))


def slot_rows(device, slots):
    ids = lax.broadcasted_iota(jnp.int32, (slots, 1), 0)
    flips, core_flip = ids % (slots // 2), ids // (slots // 2)
    return 2 * ((device // 4) ^ flips) + ((device % 2) ^ core_flip)


def split_mass(mass_row):
    ids = lax.broadcasted_iota(jnp.int32, (MASS_ROWS, LANES), 0)
    upper = mass_row.astype(jnp.bfloat16).astype(jnp.float32)
    lower = mass_row - upper
    return jnp.where(ids == 0, upper, jnp.where(ids == 1, lower, 0.0)).astype(jnp.bfloat16)


def joined_mass(block):
    return jnp.sum(block.astype(jnp.float32), axis=0, keepdims=True)


def table_kernel(shift_ref, cos_ref, sin_ref):
    shifts, pixels = cos_ref.shape
    grid_x = shift_ref[:, 0:1]
    grid_y = shift_ref[:, 1:2]
    lane = lax.broadcasted_iota(jnp.int32, (shifts, KY), 1)
    turn_x = (lane * grid_x) & (BOX - 1)
    turn_y = ((lane - KY // 2) * grid_y) & (BOX - 1)
    angle_x = turn_x.astype(jnp.float32) * (2.0 * math.pi / BOX)
    angle_y = turn_y.astype(jnp.float32) * (2.0 * math.pi / BOX)
    cos_x, sin_x = jnp.cos(angle_x), jnp.sin(angle_x)
    cos_y, sin_y = jnp.cos(angle_y), jnp.sin(angle_y)
    for j in range(pixels // LANES):
        where = slice(j * LANES, (j + 1) * LANES)
        cos_j, sin_j = cos_x[:, j : j + 1], sin_x[:, j : j + 1]
        cos_ref[:, where] = cos_j * cos_y - sin_j * sin_y
        sin_ref[:, where] = sin_j * cos_y + cos_j * sin_y


def phase_tables(shift_grid, pixels):
    shape = jax.ShapeDtypeStruct((shift_grid.shape[0], pixels), jnp.float32)
    return pl.pallas_call(
        table_kernel,
        in_specs=whole_vmem(1),
        out_specs=whole_vmem(2),
        out_shape=[shape, shape],
        compiler_params=pltpu.CompilerParams(vmem_limit_bytes=16 * MIB),
        cost_estimate=pl.CostEstimate(flops=2000000, bytes_accessed=2000000, transcendentals=0),
        name="phase_tables",
    )(shift_grid)


def rotate_back(weights, images, cos_ref, sin_ref, where, imag_where, slots):
    from_real = jnp.dot(weights, images[:, where], preferred_element_type=jnp.float32)
    from_imag = jnp.dot(weights, images[:, imag_where], preferred_element_type=jnp.float32)
    real = imag = None
    for s in range(cos_ref.shape[0]):
        cos_s, sin_s = cos_ref[s : s + 1, where], sin_ref[s : s + 1, where]
        part_real = from_real[s * slots : (s + 1) * slots]
        part_imag = from_imag[s * slots : (s + 1) * slots]
        real_s = part_real * cos_s + part_imag * sin_s
        imag_s = part_imag * cos_s - part_real * sin_s
        real = real_s if real is None else real + real_s
        imag = imag_s if imag is None else imag + imag_s
    return real, imag


def expect_kernel(images, precision_ref, assigned_ref, cos_ref, sin_ref, *refs, slots, chunk):
    row_refs, (weight_ref, low_ref, low_send, own_mass, proj) = refs[:slots], refs[slots:]
    device = lax.axis_index("particle")
    shifts = cos_ref.shape[0]
    parts = images.shape[0]
    pixels = images.shape[1] // 2
    tiles = pixels // LANES
    per_row = 2 * tiles
    for slot in range(slots):
        proj[slot * per_row : (slot + 1) * per_row, :] = row_refs[slot][...].astype(jnp.float32)

    chunk_tiles = chunk // LANES
    contract_lanes = (((1,), (1,)), ((), ()))

    def correlate(step, carry):
        total, power = carry
        first = step * chunk_tiles
        real = jnp.concatenate(
            [proj[pl.ds(first + k, slots, stride=per_row), :] for k in range(chunk_tiles)], axis=1
        )
        imag = jnp.concatenate(
            [proj[pl.ds(tiles + first + k, slots, stride=per_row), :] for k in range(chunk_tiles)],
            axis=1,
        )
        where = pl.ds(pl.multiple_of(step * chunk, chunk), chunk)
        reals, imags = [], []
        for s in range(shifts):
            cos_s, sin_s = cos_ref[s : s + 1, where], sin_ref[s : s + 1, where]
            reals.append(real * cos_s - imag * sin_s)
            imags.append(real * sin_s + imag * cos_s)
        turned_real = jnp.concatenate(reals, axis=0).astype(jnp.bfloat16)
        turned_imag = jnp.concatenate(imags, axis=0).astype(jnp.bfloat16)
        image_real = images[:, where]
        image_imag = images[:, pl.ds(pl.multiple_of(pixels + step * chunk, chunk), chunk)]
        total = total + lax.dot_general(
            turned_real, image_real, contract_lanes, preferred_element_type=jnp.float32
        )
        total = total + lax.dot_general(
            turned_imag, image_imag, contract_lanes, preferred_element_type=jnp.float32
        )
        squares = real * real + imag * imag
        for k in range(chunk_tiles):
            power = power + squares[:, k * LANES : (k + 1) * LANES]
        return total, power

    total, power = lax.fori_loop(
        0,
        pixels // chunk,
        correlate,
        (
            jnp.zeros((shifts * slots, parts), jnp.float32),
            jnp.zeros((slots, LANES), jnp.float32),
        ),
    )
    power = jnp.sum(power, axis=1, keepdims=True)
    slot_class = slot_rows(device, slots) // (slots // CLASSES)
    match = (slot_class == assigned_ref[...]).astype(jnp.float32) * PRIOR_REWARD
    precision = precision_ref[...]
    likelihood_scale = 1.0 / math.sqrt(2 * pixels)
    logits = [
        precision * (total[s * slots : (s + 1) * slots] - 0.5 * power) * likelihood_scale + match
        for s in range(shifts)
    ]
    peak = functools.reduce(jnp.maximum, logits)
    peak = jnp.max(peak, axis=0, keepdims=True)
    terms = [jnp.exp(value - peak) for value in logits]
    mass = functools.reduce(jnp.add, terms)
    norm = jnp.sum(mass, axis=0, keepdims=True)
    weights = jnp.concatenate([term / norm for term in terms], axis=0).astype(jnp.bfloat16)
    weight_ref[...] = weights
    slot_mass = jnp.sum(mass / norm * precision, axis=1, keepdims=True)
    class_lane = lax.broadcasted_iota(jnp.int32, (slots, LANES), 1)
    mass_row = jnp.sum(
        jnp.where(class_lane == slot_class, slot_mass, 0.0), axis=0, keepdims=True
    )
    own_mass[...] = jnp.broadcast_to(mass_row, own_mass.shape)

    low_rows = LOWK * KY // LANES
    low_width = LOWK * KY
    real, imag = rotate_back(
        weights, images, cos_ref, sin_ref, slice(0, low_width), slice(pixels, pixels + low_width), slots
    )
    for k in range(low_rows):
        piece = slice(k * LANES, (k + 1) * LANES)
        low_ref[pl.ds(k, slots, stride=2 * low_rows), :] = real[:, piece]
        low_ref[pl.ds(low_rows + k, slots, stride=2 * low_rows), :] = imag[:, piece]
    low_body = low_ref.shape[0]
    low_send[0:low_body, :] = low_ref[...].astype(jnp.bfloat16)
    low_send[low_body:, :] = split_mass(mass_row)


def expect(images, precision, assigned, cos_table, sin_table, rows):
    slots = len(rows)
    pixels = images.shape[1] // 2
    per_row = 2 * pixels // LANES
    shifts = cos_table.shape[0]
    low = slots * 2 * (LOWK * KY // LANES)
    return pl.pallas_call(
        functools.partial(expect_kernel, slots=slots, chunk=2048),
        in_specs=whole_vmem(5 + slots),
        out_specs=whole_vmem(4),
        out_shape=[
            jax.ShapeDtypeStruct((shifts * slots, images.shape[0]), jnp.bfloat16),
            jax.ShapeDtypeStruct((low, LANES), jnp.float32),
            jax.ShapeDtypeStruct((low + MASS_ROWS, LANES), jnp.bfloat16),
            jax.ShapeDtypeStruct((8, LANES), jnp.float32),
        ],
        scratch_shapes=[pltpu.VMEM((slots * per_row, LANES), jnp.float32)],
        compiler_params=pltpu.CompilerParams(vmem_limit_bytes=(14 + slots // 2) * MIB),
        name="expect",
    )(images, precision, assigned, cos_table, sin_table, *rows)


def backproject_kernel(weight_ref, images, cos_ref, sin_ref, sums, *, slots, chunk):
    pixels = images.shape[1] // 2
    tiles = pixels // LANES
    per_row = 2 * tiles
    chunk_tiles = chunk // LANES
    weights = weight_ref[...]

    def body(step, carry):
        where = pl.ds(pl.multiple_of(step * chunk, chunk), chunk)
        imag_where = pl.ds(pl.multiple_of(pixels + step * chunk, chunk), chunk)
        real, imag = rotate_back(weights, images, cos_ref, sin_ref, where, imag_where, slots)
        first = step * chunk_tiles
        for k in range(chunk_tiles):
            piece = slice(k * LANES, (k + 1) * LANES)
            sums[pl.ds(first + k, slots, stride=per_row), :] = real[:, piece]
            sums[pl.ds(tiles + first + k, slots, stride=per_row), :] = imag[:, piece]
        return carry

    lax.fori_loop(LOWK * KY // chunk, pixels // chunk, body, 0)


def backproject(weights, images, cos_table, sin_table, slots):
    per_row = images.shape[1] // LANES
    return pl.pallas_call(
        functools.partial(backproject_kernel, slots=slots, chunk=2048),
        in_specs=whole_vmem(4),
        out_specs=pl.BlockSpec(memory_space=pltpu.VMEM),
        out_shape=jax.ShapeDtypeStruct((slots * per_row, LANES), jnp.float32),
        compiler_params=pltpu.CompilerParams(vmem_limit_bytes=(14 + slots // 2) * MIB),
        cost_estimate=pl.CostEstimate(flops=20000000, bytes_accessed=20000000, transcendentals=0),
        name="backproject",
    )(weights, images, cos_table, sin_table)


def fold_kernel(sums_in, low_ref, low_received, mass, keep, to_core, total_mass, *, slots):
    per_row = sums_in.shape[0] // slots
    tiles = per_row // 2
    low_rows = LOWK * KY // LANES
    half = slots // 2
    low_body = low_ref.shape[0]
    folded = mass[0:1, :] + joined_mass(low_received[low_body:, :])
    total_mass[...] = jnp.broadcast_to(folded, total_mass.shape)
    for slot in range(slots):
        target = keep if slot < half else to_core
        for comp in range(2):
            low = slice((2 * slot + comp) * low_rows, (2 * slot + comp + 1) * low_rows)
            start = slot * per_row + comp * tiles
            dest = (slot % half) * per_row + comp * tiles
            value = (low_ref[low, :] + low_received[low, :].astype(jnp.float32)) * 0.5
            target[dest : dest + low_rows, :] = value.astype(target.dtype)
            target[dest + low_rows : dest + tiles, :] = sums_in[
                start + low_rows : start + tiles, :
            ].astype(target.dtype)
    to_core[half * per_row :, :] = split_mass(folded)


def fold(sums, low, low_received, mass, slots):
    half_rows = sums.shape[0] // 2
    return pl.pallas_call(
        functools.partial(fold_kernel, slots=slots),
        in_specs=whole_vmem(4),
        out_specs=whole_vmem(3),
        out_shape=[
            jax.ShapeDtypeStruct((half_rows, LANES), jnp.float32),
            jax.ShapeDtypeStruct((half_rows + MASS_ROWS, LANES), jnp.bfloat16),
            jax.ShapeDtypeStruct((8, LANES), jnp.float32),
        ],
        compiler_params=pltpu.CompilerParams(vmem_limit_bytes=(10 + slots // 2) * MIB),
        name="fold",
    )(sums, low, low_received, mass)


def merge_kernel(keep, from_core, mass, own, own_mass, *sends, half):
    per_row = keep.shape[0] // half
    total_mass = mass[0:1, :] + joined_mass(from_core[half * per_row :, :])
    block = split_mass(total_mass)
    own_mass[...] = jnp.broadcast_to(total_mass, own_mass.shape)
    for m in range(half):
        rows = slice(m * per_row, (m + 1) * per_row)
        value = keep[rows, :] + from_core[rows, :].astype(jnp.float32)
        if m == 0:
            own[...] = value
        else:
            sends[m - 1][0:per_row, :] = value.astype(jnp.bfloat16)
            sends[m - 1][per_row:, :] = block


def merge(keep, from_core, mass, half):
    per_row = keep.shape[0] // half
    return pl.pallas_call(
        functools.partial(merge_kernel, half=half),
        in_specs=whole_vmem(3),
        out_specs=whole_vmem(1 + half),
        out_shape=[
            jax.ShapeDtypeStruct((per_row, LANES), jnp.float32),
            jax.ShapeDtypeStruct((8, LANES), jnp.float32),
        ]
        + [jax.ShapeDtypeStruct((per_row + MASS_ROWS, LANES), jnp.bfloat16)] * (half - 1),
        compiler_params=pltpu.CompilerParams(vmem_limit_bytes=(12 + half) * MIB),
        name="merge",
    )(keep, from_core, mass)


def finish_kernel(own, mass, *refs, scale, mass_scale):
    received, (out, mass_out) = refs[:-2], refs[-2:]
    per_row = own.shape[0]
    total = own[...]
    total_mass = mass[0:1, :]
    for ref in received:
        total = total + ref[0:per_row, :].astype(jnp.float32)
        total_mass = total_mass + joined_mass(ref[per_row:, :])
    out[...] = total * scale
    mass_out[...] = total_mass[0, :CLASSES] * mass_scale


def finish(own, mass, received, scale, mass_scale):
    return pl.pallas_call(
        functools.partial(finish_kernel, scale=scale, mass_scale=mass_scale),
        in_specs=whole_vmem(2 + len(received)),
        out_specs=whole_vmem(2),
        out_shape=[
            jax.ShapeDtypeStruct(own.shape, jnp.float32),
            jax.ShapeDtypeStruct((CLASSES,), jnp.float32),
        ],
        compiler_params=pltpu.CompilerParams(vmem_limit_bytes=16 * MIB),
        name="finish",
    )(own, mass, *received)


def local(
    images, noise_precision, assigned_class, class_refs, interp_index, interp_frac, shift_grid
):
    dev_count = lax.axis_size("particle")
    slots = dev_count // 2
    half = slots // 2
    part_count = images.shape[0]
    own_row = project_row(class_refs, interp_index, interp_frac)
    same_core = [own_row] + [exchange(own_row, 4 * m) for m in range(1, half)]
    rows = same_core + [exchange(row, 1) for row in same_core]
    cos_table, sin_table = phase_tables(shift_grid, images.shape[1] // 2)
    weights, low, low_send, mass = expect(
        images,
        noise_precision.reshape(1, part_count),
        assigned_class.reshape(1, part_count),
        cos_table,
        sin_table,
        rows,
    )
    low_received = exchange(low_send, 2)
    sums = backproject(weights, images, cos_table, sin_table, slots)
    keep, to_core, mass = fold(sums, low, low_received, mass, slots)
    merged = merge(keep, exchange(to_core, 1), mass, half)
    own, mass, sends = merged[0], merged[1], merged[2:]
    received = [exchange(sends[m - 1], 4 * m) for m in range(half - 1, 0, -1)]
    back, class_mass = finish(
        own, mass, received, 1.0 / math.sqrt(part_count), CLASSES / (part_count * dev_count)
    )
    return back.reshape(1, images.shape[1]), class_mass


def solution(mesh):
    in_specs = (
        P(("groups", "particle"), None),
        P(("groups", "particle")),
        P(("groups", "particle")),
        P("groups", None, None, None),
        P("particle", None),
        P("particle", None),
        P(),
    )
    out_specs = (P(("groups", "particle"), None), P("groups"))
    return jax.shard_map(local, mesh=mesh, in_specs=in_specs, out_specs=out_specs, check_vma=False)
```

```python
import functools
import math

import jax
import jax.numpy as jnp
from jax import lax
from jax.experimental import pallas as pl
from jax.experimental.pallas import tpu as pltpu
from jax.sharding import PartitionSpec as P

KY = 128
BOX = 256
CLASSES = 8
LOWK = 16
LANES = 128
PRIOR_REWARD = 1.0
MASS_ROWS = 16
BLOCK = 8
LOW_TILES = LOWK * KY // LANES // 2
MIB = 1 << 20


def exchange(value, mask):
    pairs = [(source, source ^ mask) for source in range(lax.axis_size("particle"))]
    return lax.ppermute(value, "particle", pairs)


def in_hbm(value):
    return pltpu.with_memory_space_constraint(value, pltpu.HBM)


def whole_vmem(count):
    return [pl.BlockSpec(memory_space=pltpu.VMEM)] * count


def own_half():
    return lax.axis_index("particle") % 2


def tree_select(values, masks):
    for mask in masks:
        values = [
            jnp.where(mask, values[i + 1], values[i]) if i + 1 < len(values) else values[i]
            for i in range(0, len(values), 2)
        ]
    return values[0]


def project_half(table, index_ref, frac_ref, half, blended):
    pixels = index_ref.shape[1]
    highs = table.shape[1]
    groups = table.shape[0] // 16
    stride = 8 * groups
    chunk = BLOCK * LANES
    blocks = pixels // (2 * chunk)

    def body(step, carry):
        where = pl.ds(pl.multiple_of((2 * step + half) * chunk, chunk), chunk)
        index = index_ref[:, where]
        frac = frac_ref[:, where]
        high = index >> 7
        low = index & (LANES - 1)
        group = (low * 147) >> 10
        first = low - 7 * group
        high_ids = lax.broadcasted_iota(jnp.int32, (highs, chunk), 0)
        one_hot = jnp.where(high_ids == high, 1.0, 0.0).astype(jnp.bfloat16)
        rows = jnp.dot(table[...], one_hot, preferred_element_type=jnp.float32)
        group = jnp.broadcast_to(group, (8, chunk))
        masks = [(group & (1 << bit)) != 0 for bit in range((groups - 1).bit_length())]
        ids = lax.broadcasted_iota(jnp.int32, (8, chunk), 0)
        weight = jnp.where(ids == first, 1.0 - frac, jnp.where(ids == first + 1, frac, 0.0))
        for comp in range(2):
            start = comp * stride
            picked = tree_select([rows[start + 8 * g : start + 8 * g + 8] for g in range(groups)], masks)
            value = jnp.sum(picked * weight, axis=0, keepdims=True)
            for k in range(BLOCK):
                row = (comp * blocks + step) * BLOCK + k
                blended[pl.ds(row, 1), :] = value[:, k * LANES : (k + 1) * LANES]
        return carry

    lax.fori_loop(0, blocks, body, 0, unroll=2)


def project_other_kernel(
    table_hbm, index_hbm, frac_hbm, out_ref, table, index_ref, frac_ref,
    table_in, flat, wide, blended, sems
):
    device = lax.axis_index("particle")
    row_count = lax.axis_size("particle") // 2
    half_set = device // 2 % 2
    class_id = (2 * (device // 4) + device % 2) // (row_count // CLASSES)
    copies = [
        pltpu.make_async_copy(
            table_hbm.at[pl.ds(half_set, 1), pl.ds(class_id, 1)], table_in, sems.at[0]
        ),
        pltpu.make_async_copy(index_hbm, index_ref, sems.at[1]),
        pltpu.make_async_copy(frac_hbm, frac_ref, sems.at[2]),
    ]
    for copy in copies:
        copy.start()
    copies[0].wait()
    highs = flat.shape[1]
    groups = table.shape[0] // 16

    def unfold(step, carry):
        piece = table_in[0, 0, :, pl.ds(step * 8 * LANES, 8 * LANES)].astype(jnp.float32)
        for k in range(8):
            for comp in range(2):
                flat[comp, pl.ds(step * 8 + k, 1), :] = piece[comp : comp + 1, k * LANES : (k + 1) * LANES]
        return carry

    lax.fori_loop(0, highs // 8, unfold, 0, unroll=4)
    picked = []
    for comp in range(2):
        turned = flat[comp].T
        wide[0:LANES, :] = turned
        wide[LANES : LANES + 8, :] = pltpu.roll(turned[0:8], highs - 1, 1)
        picked += [wide[7 * g : 7 * g + 8, :] for g in range(groups)]
    for pair in range(groups):
        table[16 * pair : 16 * (pair + 1), :] = jnp.concatenate(
            picked[2 * pair : 2 * pair + 2], axis=0
        ).astype(jnp.bfloat16)
    copies[1].wait()
    copies[2].wait()
    project_half(table, index_ref, frac_ref, 1 - own_half(), blended)
    out_ref[...] = blended[...].astype(jnp.bfloat16)


def project_other(class_refs, interp_index, interp_frac):
    vox = class_refs.shape[3]
    pixels = interp_index.shape[1]
    highs = vox // LANES
    half_rows = pixels // LANES
    groups = -(-LANES // 7)
    return pl.pallas_call(
        project_other_kernel,
        in_specs=[pl.BlockSpec(memory_space=pltpu.HBM)] * 3,
        out_specs=whole_vmem(4),
        out_shape=[
            jax.ShapeDtypeStruct((half_rows, LANES), jnp.bfloat16),
            jax.ShapeDtypeStruct((16 * groups, highs), jnp.bfloat16),
            jax.ShapeDtypeStruct((1, pixels), jnp.int32),
            jax.ShapeDtypeStruct((1, pixels), jnp.float32),
        ],
        scratch_shapes=[
            pltpu.VMEM((1, 1, 2, vox), jnp.bfloat16),
            pltpu.VMEM((2, highs, LANES), jnp.float32),
            pltpu.VMEM((LANES + 8, highs), jnp.float32),
            pltpu.VMEM((half_rows, LANES), jnp.float32),
            pltpu.SemaphoreType.DMA((3,)),
        ],
        compiler_params=pltpu.CompilerParams(vmem_limit_bytes=16 * MIB),
        name="project_other",
    )(*(in_hbm(value) for value in (class_refs, interp_index, interp_frac)))


def project_own_kernel(
    table, index_ref, frac_ref, images_hbm, out_ref, own_images, other_images, blended, sems
):
    pixels = index_ref.shape[1]
    chunk = BLOCK * LANES
    blocks = pixels // (2 * chunk)
    copies = []
    for target, half in ((other_images, 1 - own_half()), (own_images, own_half())):
        for comp in range(2):
            for step in range(blocks):
                source = pl.multiple_of(comp * pixels + (2 * step + half) * chunk, chunk)
                dest = (comp * blocks + step) * chunk
                copies.append(
                    pltpu.make_async_copy(
                        images_hbm.at[:, pl.ds(source, chunk)],
                        target.at[:, pl.ds(dest, chunk)],
                        sems.at[len(copies)],
                    )
                )
    for copy in copies:
        copy.start()
    project_half(table, index_ref, frac_ref, own_half(), blended)
    out_ref[...] = blended[...].astype(jnp.bfloat16)
    for copy in copies:
        copy.wait()


def project_own(table, index, frac, images):
    parts, width = images.shape
    half_rows = index.shape[1] // LANES
    half_images = jax.ShapeDtypeStruct((parts, width // 2), jnp.bfloat16)
    return pl.pallas_call(
        project_own_kernel,
        in_specs=whole_vmem(3) + [pl.BlockSpec(memory_space=pltpu.HBM)],
        out_specs=whole_vmem(3),
        out_shape=[
            jax.ShapeDtypeStruct((half_rows, LANES), jnp.bfloat16),
            half_images,
            half_images,
        ],
        scratch_shapes=[
            pltpu.VMEM((half_rows, LANES), jnp.float32),
            pltpu.SemaphoreType.DMA((2 * width // (2 * BLOCK * LANES),)),
        ],
        compiler_params=pltpu.CompilerParams(vmem_limit_bytes=16 * MIB),
        cost_estimate=pl.CostEstimate(flops=2000000000, bytes_accessed=8000000, transcendentals=0),
        name="project_own",
    )(table, index, frac, in_hbm(images))


def pair_kernel(own, other, out_ref):
    count = own.shape[0]
    core = own_half()
    out_ref[pl.ds(pl.multiple_of(core * count, count), count), :] = own[...]
    out_ref[pl.ds(pl.multiple_of((1 - core) * count, count), count), :] = other[...]


def pair_rows(own, other):
    return pl.pallas_call(
        pair_kernel,
        in_specs=whole_vmem(2),
        out_specs=pl.BlockSpec(memory_space=pltpu.VMEM),
        out_shape=jax.ShapeDtypeStruct((2 * own.shape[0], LANES), own.dtype),
        compiler_params=pltpu.CompilerParams(vmem_limit_bytes=16 * MIB),
        name="pair_rows",
    )(own, other)


def slot_rows(device, slots):
    ids = lax.broadcasted_iota(jnp.int32, (slots, 1), 0)
    return 2 * ((device // 4) ^ (ids // 2)) + ids % 2


def split_mass(mass_row):
    ids = lax.broadcasted_iota(jnp.int32, (MASS_ROWS, LANES), 0)
    upper = mass_row.astype(jnp.bfloat16).astype(jnp.float32)
    lower = mass_row - upper
    return jnp.where(ids == 0, upper, jnp.where(ids == 1, lower, 0.0)).astype(jnp.bfloat16)


def joined_mass(block):
    return jnp.sum(block.astype(jnp.float32), axis=0, keepdims=True)


def table_kernel(shift_ref, cos_ref, sin_ref):
    shifts, width = cos_ref.shape
    grid_x = shift_ref[:, 0:1]
    grid_y = shift_ref[:, 1:2]
    lane = lax.broadcasted_iota(jnp.int32, (shifts, LANES), 1)
    freq_x = (lane // BLOCK) * (2 * BLOCK) + own_half() * BLOCK + lane % BLOCK
    turn_x = (freq_x * grid_x) & (BOX - 1)
    turn_y = ((lane - KY // 2) * grid_y) & (BOX - 1)
    angle_x = turn_x.astype(jnp.float32) * (2.0 * math.pi / BOX)
    angle_y = turn_y.astype(jnp.float32) * (2.0 * math.pi / BOX)
    cos_x, sin_x = jnp.cos(angle_x), jnp.sin(angle_x)
    cos_y, sin_y = jnp.cos(angle_y), jnp.sin(angle_y)
    for j in range(width // LANES):
        where = slice(j * LANES, (j + 1) * LANES)
        cos_j, sin_j = cos_x[:, j : j + 1], sin_x[:, j : j + 1]
        cos_ref[:, where] = cos_j * cos_y - sin_j * sin_y
        sin_ref[:, where] = sin_j * cos_y + cos_j * sin_y


def phase_tables(shift_grid, width):
    shape = jax.ShapeDtypeStruct((shift_grid.shape[0], width), jnp.float32)
    return pl.pallas_call(
        table_kernel,
        in_specs=whole_vmem(1),
        out_specs=whole_vmem(2),
        out_shape=[shape, shape],
        compiler_params=pltpu.CompilerParams(vmem_limit_bytes=16 * MIB),
        cost_estimate=pl.CostEstimate(flops=2000000, bytes_accessed=2000000, transcendentals=0),
        name="phase_tables",
    )(shift_grid)


def correlate_kernel(own_images, other_images, precision_ref, assigned_ref, cos_ref, sin_ref, *refs, chunk):
    pair_refs, (out_ref, proj) = refs[:-2], refs[-2:]
    shifts = cos_ref.shape[0]
    parts = own_images.shape[0]
    slots = 2 * len(pair_refs)
    width = own_images.shape[1] // 2
    tiles = width // LANES
    per_row = 2 * tiles
    for m, ref in enumerate(pair_refs):
        proj[2 * m * per_row : 2 * (m + 1) * per_row, :] = ref[...].astype(jnp.float32)

    chunk_tiles = chunk // LANES
    contract_lanes = (((1,), (1,)), ((), ()))

    def body(step, carry):
        total, power = carry
        first = step * chunk_tiles
        real = jnp.concatenate(
            [proj[pl.ds(first + k, slots, stride=per_row), :] for k in range(chunk_tiles)], axis=1
        )
        imag = jnp.concatenate(
            [proj[pl.ds(tiles + first + k, slots, stride=per_row), :] for k in range(chunk_tiles)],
            axis=1,
        )
        where = pl.ds(pl.multiple_of(step * chunk, chunk), chunk)
        imag_where = pl.ds(pl.multiple_of(width + step * chunk, chunk), chunk)
        reals, imags = [], []
        for s in range(shifts):
            cos_s, sin_s = cos_ref[s : s + 1, where], sin_ref[s : s + 1, where]
            reals.append(real * cos_s - imag * sin_s)
            imags.append(real * sin_s + imag * cos_s)
        turned_real = jnp.concatenate(reals, axis=0).astype(jnp.bfloat16)
        turned_imag = jnp.concatenate(imags, axis=0).astype(jnp.bfloat16)
        image_real = jnp.concatenate([own_images[:, where], other_images[:, where]], axis=0)
        image_imag = jnp.concatenate([own_images[:, imag_where], other_images[:, imag_where]], axis=0)
        total = total + lax.dot_general(
            turned_real, image_real, contract_lanes, preferred_element_type=jnp.float32
        )
        total = total + lax.dot_general(
            turned_imag, image_imag, contract_lanes, preferred_element_type=jnp.float32
        )
        squares = real * real + imag * imag
        for k in range(chunk_tiles):
            power = power + squares[:, k * LANES : (k + 1) * LANES]
        return total, power

    total, power = lax.fori_loop(
        0,
        width // chunk,
        body,
        (
            jnp.zeros((shifts * slots, 2 * parts), jnp.float32),
            jnp.zeros((slots, LANES), jnp.float32),
        ),
    )
    combos = shifts * slots
    out_ref[...] = jnp.zeros_like(out_ref)
    out_ref[0:combos, 0 : 2 * parts] = total
    out_ref[combos : combos + slots, :] = jnp.broadcast_to(
        jnp.sum(power, axis=1, keepdims=True), (slots, LANES)
    )
    out_ref[combos + slots : combos + slots + 1, 0:parts] = precision_ref[...]
    out_ref[combos + slots + 1 : combos + slots + 2, 0:parts] = assigned_ref[...].astype(jnp.float32)


def correlate(own_images, other_images, precision, assigned, cos_table, sin_table, pairs):
    slots = 2 * len(pairs)
    shifts, width = cos_table.shape
    return pl.pallas_call(
        functools.partial(correlate_kernel, chunk=2048),
        in_specs=whole_vmem(6 + len(pairs)),
        out_specs=pl.BlockSpec(memory_space=pltpu.VMEM),
        out_shape=jax.ShapeDtypeStruct((shifts * slots + slots + 8, LANES), jnp.float32),
        scratch_shapes=[pltpu.VMEM((slots * 2 * width // LANES, LANES), jnp.float32)],
        compiler_params=pltpu.CompilerParams(vmem_limit_bytes=(14 + slots // 2) * MIB),
        name="correlate",
    )(own_images, other_images, precision, assigned, cos_table, sin_table, *pairs)


def rotate_back(weights, own_images, other_images, cos_ref, sin_ref, where, imag_where, slots):
    image_real = jnp.concatenate([own_images[:, where], other_images[:, where]], axis=0)
    image_imag = jnp.concatenate([own_images[:, imag_where], other_images[:, imag_where]], axis=0)
    from_real = jnp.dot(weights, image_real, preferred_element_type=jnp.float32)
    from_imag = jnp.dot(weights, image_imag, preferred_element_type=jnp.float32)
    real = imag = None
    for s in range(cos_ref.shape[0]):
        cos_s, sin_s = cos_ref[s : s + 1, where], sin_ref[s : s + 1, where]
        part_real = from_real[s * slots : (s + 1) * slots]
        part_imag = from_imag[s * slots : (s + 1) * slots]
        real_s = part_real * cos_s + part_imag * sin_s
        imag_s = part_imag * cos_s - part_real * sin_s
        real = real_s if real is None else real + real_s
        imag = imag_s if imag is None else imag + imag_s
    return real, imag


def posterior_kernel(
    mine, received, own_images, other_images, cos_ref, sin_ref,
    weight_ref, low_ref, low_send, own_mass, *, slots
):
    device = lax.axis_index("particle")
    shifts, width = cos_ref.shape
    parts = own_images.shape[0]
    combos = shifts * slots
    theirs = received[...]
    lane = lax.broadcasted_iota(jnp.int32, theirs.shape, 1)
    swapped = jnp.where(
        lane < parts, pltpu.roll(theirs, LANES - parts, 1), pltpu.roll(theirs, parts, 1)
    )
    joint = mine[...] + swapped
    power = mine[combos : combos + slots, :] + received[combos : combos + slots, :]
    precision = joint[combos + slots : combos + slots + 1]
    assigned = joint[combos + slots + 1 : combos + slots + 2].astype(jnp.int32)
    slot_class = slot_rows(device, slots) // (slots // CLASSES)
    match = (slot_class == assigned).astype(jnp.float32) * PRIOR_REWARD
    likelihood_scale = 1.0 / math.sqrt(4 * width)
    logits = [
        precision * (joint[s * slots : (s + 1) * slots] - 0.5 * power) * likelihood_scale + match
        for s in range(shifts)
    ]
    peak = functools.reduce(jnp.maximum, logits)
    peak = jnp.max(peak, axis=0, keepdims=True)
    terms = [jnp.exp(value - peak) for value in logits]
    mass = functools.reduce(jnp.add, terms)
    norm = jnp.sum(mass, axis=0, keepdims=True)
    weights = jnp.concatenate([term / norm for term in terms], axis=0)
    weights = weights[:, 0 : 2 * parts].astype(jnp.bfloat16)
    weight_ref[...] = weights
    counted = lax.broadcasted_iota(jnp.int32, (1, LANES), 1) < 2 * parts
    share = jnp.where(counted, mass / norm * precision, 0.0)
    slot_mass = jnp.sum(share, axis=1, keepdims=True)
    class_lane = lax.broadcasted_iota(jnp.int32, (slots, LANES), 1)
    mass_row = jnp.sum(
        jnp.where(class_lane == slot_class, slot_mass, 0.0), axis=0, keepdims=True
    )
    own_mass[...] = jnp.broadcast_to(mass_row, own_mass.shape)

    low = LOW_TILES * LANES
    real, imag = rotate_back(
        weights, own_images, other_images, cos_ref, sin_ref, slice(0, low), slice(width, width + low), slots
    )
    for k in range(LOW_TILES):
        piece = slice(k * LANES, (k + 1) * LANES)
        low_ref[pl.ds(k, slots, stride=2 * LOW_TILES), :] = real[:, piece]
        low_ref[pl.ds(LOW_TILES + k, slots, stride=2 * LOW_TILES), :] = imag[:, piece]
    low_body = low_ref.shape[0]
    low_send[0:low_body, :] = low_ref[...].astype(jnp.bfloat16)
    low_send[low_body:, :] = split_mass(mass_row)


def posterior(mine, received, own_images, other_images, cos_table, sin_table, slots):
    shifts = cos_table.shape[0]
    low = slots * 2 * LOW_TILES
    return pl.pallas_call(
        functools.partial(posterior_kernel, slots=slots),
        in_specs=whole_vmem(6),
        out_specs=whole_vmem(4),
        out_shape=[
            jax.ShapeDtypeStruct((shifts * slots, 2 * own_images.shape[0]), jnp.bfloat16),
            jax.ShapeDtypeStruct((low, LANES), jnp.float32),
            jax.ShapeDtypeStruct((low + MASS_ROWS, LANES), jnp.bfloat16),
            jax.ShapeDtypeStruct((8, LANES), jnp.float32),
        ],
        compiler_params=pltpu.CompilerParams(vmem_limit_bytes=(14 + slots // 2) * MIB),
        name="posterior",
    )(mine, received, own_images, other_images, cos_table, sin_table)


def backproject_kernel(weight_ref, own_images, other_images, cos_ref, sin_ref, sums, *, slots, chunk):
    width = cos_ref.shape[1]
    tiles = width // LANES
    per_row = 2 * tiles
    chunk_tiles = chunk // LANES
    weights = weight_ref[...]

    def body(step, carry):
        first = LOW_TILES + step * chunk_tiles
        start = pl.multiple_of(first * LANES, LOW_TILES * LANES)
        where = pl.ds(start, chunk)
        imag_where = pl.ds(pl.multiple_of(width + start, LOW_TILES * LANES), chunk)
        real, imag = rotate_back(
            weights, own_images, other_images, cos_ref, sin_ref, where, imag_where, slots
        )
        for k in range(chunk_tiles):
            piece = slice(k * LANES, (k + 1) * LANES)
            sums[pl.ds(first + k, slots, stride=per_row), :] = real[:, piece]
            sums[pl.ds(tiles + first + k, slots, stride=per_row), :] = imag[:, piece]
        return carry

    lax.fori_loop(0, (tiles - LOW_TILES) // chunk_tiles, body, 0)


def backproject(weights, own_images, other_images, cos_table, sin_table, slots):
    width = cos_table.shape[1]
    rows = slots * 2 * width // LANES
    return pl.pallas_call(
        functools.partial(backproject_kernel, slots=slots, chunk=LOW_TILES * LANES),
        in_specs=whole_vmem(5),
        out_specs=pl.BlockSpec(memory_space=pltpu.VMEM),
        out_shape=jax.ShapeDtypeStruct((rows, LANES), jnp.float32),
        compiler_params=pltpu.CompilerParams(vmem_limit_bytes=(14 + slots // 2) * MIB),
        cost_estimate=pl.CostEstimate(flops=20000000, bytes_accessed=20000000, transcendentals=0),
        name="backproject",
    )(weights, own_images, other_images, cos_table, sin_table)


def fold_kernel(sums, low_ref, low_received, mass, own, own_mass, *sends, slots):
    per_row = sums.shape[0] // slots
    tiles = per_row // 2
    low_body = low_ref.shape[0]
    total_mass = mass[0:1, :] + joined_mass(low_received[low_body:, :])
    block = split_mass(total_mass)
    own_mass[...] = jnp.broadcast_to(total_mass, own_mass.shape)
    for slot in range(slots):
        target = own if slot < 2 else sends[slot // 2 - 1]
        for comp in range(2):
            low = slice((2 * slot + comp) * LOW_TILES, (2 * slot + comp + 1) * LOW_TILES)
            start = slot * per_row + comp * tiles
            dest = (slot % 2) * per_row + comp * tiles
            value = (low_ref[low, :] + low_received[low, :].astype(jnp.float32)) * 0.5
            value = jnp.concatenate([value, sums[start + LOW_TILES : start + tiles, :]], axis=0)
            target[dest : dest + tiles, :] = value.astype(target.dtype)
    for send in sends:
        send[2 * per_row :, :] = block


def fold(sums, low, low_received, mass, slots):
    rows = 2 * sums.shape[0] // slots
    chips = slots // 2
    return pl.pallas_call(
        functools.partial(fold_kernel, slots=slots),
        in_specs=whole_vmem(4),
        out_specs=whole_vmem(1 + chips),
        out_shape=[
            jax.ShapeDtypeStruct((rows, LANES), jnp.float32),
            jax.ShapeDtypeStruct((8, LANES), jnp.float32),
        ]
        + [jax.ShapeDtypeStruct((rows + MASS_ROWS, LANES), jnp.bfloat16)] * (chips - 1),
        compiler_params=pltpu.CompilerParams(vmem_limit_bytes=(10 + slots // 2) * MIB),
        name="fold",
    )(sums, low, low_received, mass)


def merge_kernel(own, mass, *refs, mass_scale):
    received, (keep, send, mass_out) = refs[:-3], refs[-3:]
    rows = own.shape[0]
    half = rows // 2
    core = own_half()
    total_mass = mass[0:1, :]
    for ref in received:
        total_mass = total_mass + joined_mass(ref[rows:, :])
    for target, place in ((send, 1 - core), (keep, core)):
        where = pl.ds(pl.multiple_of(place * half, half), half)
        total = own[where, :]
        for ref in received:
            total = total + ref[where, :].astype(jnp.float32)
        target[...] = total.astype(target.dtype)
    mass_out[...] = total_mass[0, :CLASSES] * mass_scale


def merge(own, mass, received, mass_scale):
    rows = own.shape[0] // 2
    return pl.pallas_call(
        functools.partial(merge_kernel, mass_scale=mass_scale),
        in_specs=whole_vmem(2 + len(received)),
        out_specs=whole_vmem(3),
        out_shape=[
            jax.ShapeDtypeStruct((rows, LANES), jnp.float32),
            jax.ShapeDtypeStruct((rows, LANES), jnp.bfloat16),
            jax.ShapeDtypeStruct((CLASSES,), jnp.float32),
        ],
        compiler_params=pltpu.CompilerParams(vmem_limit_bytes=16 * MIB),
        name="merge",
    )(own, mass, *received)


def finish_kernel(own, received, out, *, scale):
    half = own_half()
    for step in range(own.shape[0] // BLOCK):
        rows = slice(step * BLOCK, (step + 1) * BLOCK)
        own_rows = pl.ds(pl.multiple_of((2 * step + half) * BLOCK, BLOCK), BLOCK)
        other_rows = pl.ds(pl.multiple_of((2 * step + 1 - half) * BLOCK, BLOCK), BLOCK)
        out[own_rows, :] = own[rows, :] * scale
        out[other_rows, :] = received[rows, :].astype(jnp.float32) * scale


def finish(own, received, scale):
    return pl.pallas_call(
        functools.partial(finish_kernel, scale=scale),
        in_specs=whole_vmem(2),
        out_specs=pl.BlockSpec(memory_space=pltpu.VMEM),
        out_shape=jax.ShapeDtypeStruct((2 * own.shape[0], LANES), jnp.float32),
        compiler_params=pltpu.CompilerParams(vmem_limit_bytes=16 * MIB),
        name="finish",
    )(own, received)


def local(
    images, noise_precision, assigned_class, class_refs, interp_index, interp_frac, shift_grid
):
    dev_count = lax.axis_size("particle")
    slots = dev_count // 2
    chips = slots // 2
    parts, width = images.shape
    other_half, table, index, frac = project_other(class_refs, interp_index, interp_frac)
    from_core = exchange(other_half, 1)
    own, own_images, other_images = project_own(table, index, frac, images)
    pair = pair_rows(own, from_core)
    pairs = [pair] + [exchange(pair, 4 * m) for m in range(1, chips)]
    images_received = exchange(other_images, 1)
    cos_table, sin_table = phase_tables(shift_grid, width // 4)
    mine = correlate(
        own_images,
        images_received,
        noise_precision.reshape(1, parts),
        assigned_class.reshape(1, parts),
        cos_table,
        sin_table,
        pairs,
    )
    weights, low, low_send, mass = posterior(
        mine, exchange(mine, 1), own_images, images_received, cos_table, sin_table, slots
    )
    low_received = exchange(low_send, 2)
    sums = backproject(weights, own_images, images_received, cos_table, sin_table, slots)
    folded = fold(sums, low, low_received, mass, slots)
    sends = folded[2:]
    received = [exchange(sends[m - 1], 4 * m) for m in range(chips - 1, 0, -1)]
    keep, send, class_mass = merge(
        folded[0], folded[1], received, CLASSES / (parts * dev_count)
    )
    back = finish(keep, exchange(send, 1), 1.0 / math.sqrt(parts))
    return back.reshape(1, width), class_mass


def solution(mesh):
    in_specs = (
        P(("groups", "particle"), None),
        P(("groups", "particle")),
        P(("groups", "particle")),
        P("groups", None, None, None),
        P("particle", None),
        P("particle", None),
        P(),
    )
    out_specs = (P(("groups", "particle"), None), P("groups"))
    return jax.shard_map(local, mesh=mesh, in_specs=in_specs, out_specs=out_specs, check_vma=False)
```

```python
import functools
import math

import jax
import jax.numpy as jnp
from jax import lax
from jax.experimental import pallas as pl
from jax.experimental.pallas import tpu as pltpu
from jax.sharding import PartitionSpec as P

KY = 128
BOX = 256
CLASSES = 8
LOWK = 16
LANES = 128
PRIOR_REWARD = 1.0
MASS_ROWS = 16
BLOCK = 8
LOW_TILES = LOWK * KY // LANES // 2
MIB = 1 << 20


def exchange(value, mask):
    pairs = [(source, source ^ mask) for source in range(lax.axis_size("particle"))]
    return lax.ppermute(value, "particle", pairs)


def in_hbm(value):
    return pltpu.with_memory_space_constraint(value, pltpu.HBM)


def whole_vmem(count):
    return [pl.BlockSpec(memory_space=pltpu.VMEM)] * count


def own_half():
    return lax.axis_index("particle") % 2


def tree_select(values, masks):
    for mask in masks:
        values = [
            jnp.where(mask, values[i + 1], values[i]) if i + 1 < len(values) else values[i]
            for i in range(0, len(values), 2)
        ]
    return values[0]


def project_kernel(
    table_hbm, index_hbm, frac_hbm, images_hbm, out_ref, own_images, other_images,
    table_in, index_ref, frac_ref, flat, wide, table, blended, even, odd, sems
):
    device = lax.axis_index("particle")
    row_count = lax.axis_size("particle") // 2
    half_set = device // 2 % 2
    class_id = (2 * (device // 4) + device % 2) // (row_count // CLASSES)
    core = own_half()
    highs = flat.shape[1]
    pixels = index_ref.shape[1]
    groups = table.shape[0] // 16
    stride = 8 * groups
    chunk = BLOCK * LANES
    blocks = pixels // (2 * chunk)
    copies = [
        pltpu.make_async_copy(
            table_hbm.at[pl.ds(half_set, 1), pl.ds(class_id, 1)], table_in, sems.at[0]
        ),
        pltpu.make_async_copy(index_hbm, index_ref, sems.at[1]),
        pltpu.make_async_copy(frac_hbm, frac_ref, sems.at[2]),
    ]
    for target, half in ((other_images, 1 - core), (own_images, core)):
        for comp in range(2):
            for step in range(blocks):
                source = pl.multiple_of(comp * pixels + (2 * step + half) * chunk, chunk)
                dest = (comp * blocks + step) * chunk
                copies.append(
                    pltpu.make_async_copy(
                        images_hbm.at[:, pl.ds(source, chunk)],
                        target.at[:, pl.ds(dest, chunk)],
                        sems.at[len(copies)],
                    )
                )
    for copy in copies:
        copy.start()
    copies[0].wait()

    def unfold(step, carry):
        piece = table_in[0, 0, :, pl.ds(step * 8 * LANES, 8 * LANES)].astype(jnp.float32)
        for k in range(8):
            for comp in range(2):
                flat[comp, pl.ds(step * 8 + k, 1), :] = piece[comp : comp + 1, k * LANES : (k + 1) * LANES]
        return carry

    lax.fori_loop(0, highs // 8, unfold, 0, unroll=4)
    picked = []
    for comp in range(2):
        turned = flat[comp].T
        wide[0:LANES, :] = turned
        wide[LANES : LANES + 8, :] = pltpu.roll(turned[0:8], highs - 1, 1)
        picked += [wide[7 * g : 7 * g + 8, :] for g in range(groups)]
    for pair in range(groups):
        table[16 * pair : 16 * (pair + 1), :] = jnp.concatenate(
            picked[2 * pair : 2 * pair + 2], axis=0
        ).astype(jnp.bfloat16)
    copies[1].wait()
    copies[2].wait()

    def place(step):
        block = 2 * (step % blocks) + jnp.where(step < blocks, core, 1 - core)
        return pl.ds(pl.multiple_of(block * chunk, chunk), chunk)

    def pick_lanes(step, target):
        high = index_ref[:, place(step)] >> 7
        high_ids = lax.broadcasted_iota(jnp.int32, (highs, chunk), 0)
        one_hot = jnp.where(high_ids == high, 1.0, 0.0).astype(jnp.bfloat16)
        target[...] = jnp.dot(table[...], one_hot, preferred_element_type=jnp.float32)

    def blend(step, rows):
        low = index_ref[:, place(step)] & (LANES - 1)
        frac = frac_ref[:, place(step)]
        group = (low * 147) >> 10
        first = low - 7 * group
        group = jnp.broadcast_to(group, (8, chunk))
        masks = [(group & (1 << bit)) != 0 for bit in range((groups - 1).bit_length())]
        ids = lax.broadcasted_iota(jnp.int32, (8, chunk), 0)
        weight = jnp.where(ids == first, 1.0 - frac, jnp.where(ids == first + 1, frac, 0.0))
        for comp in range(2):
            start = comp * stride
            picked = tree_select(
                [rows[start + 8 * g : start + 8 * g + 8, :] for g in range(groups)], masks
            )
            value = jnp.sum(picked * weight, axis=0, keepdims=True)
            first_row = (step // blocks * 2 + comp) * blocks * BLOCK + step % blocks * BLOCK
            for k in range(BLOCK):
                blended[pl.ds(first_row + k, 1), :] = value[:, k * LANES : (k + 1) * LANES]

    pick_lanes(0, even)

    def body(pair, carry):
        pick_lanes(2 * pair + 1, odd)
        blend(2 * pair, even)
        pick_lanes(2 * pair + 2, even)
        blend(2 * pair + 1, odd)
        return carry

    lax.fori_loop(0, blocks - 1, body, 0)
    pick_lanes(2 * blocks - 1, odd)
    blend(2 * blocks - 2, even)
    blend(2 * blocks - 1, odd)
    out_ref[...] = blended[...].astype(jnp.bfloat16)
    for copy in copies[3:]:
        copy.wait()


def project_row(class_refs, interp_index, interp_frac, images):
    vox = class_refs.shape[3]
    pixels = interp_index.shape[1]
    highs = vox // LANES
    rows = 2 * pixels // LANES
    groups = -(-LANES // 7)
    chunk = BLOCK * LANES
    half_images = jax.ShapeDtypeStruct((images.shape[0], pixels), jnp.bfloat16)
    return pl.pallas_call(
        project_kernel,
        in_specs=[pl.BlockSpec(memory_space=pltpu.HBM)] * 4,
        out_specs=whole_vmem(3),
        out_shape=[jax.ShapeDtypeStruct((rows, LANES), jnp.bfloat16), half_images, half_images],
        scratch_shapes=[
            pltpu.VMEM((1, 1, 2, vox), jnp.bfloat16),
            pltpu.VMEM((1, pixels), jnp.int32),
            pltpu.VMEM((1, pixels), jnp.float32),
            pltpu.VMEM((2, highs, LANES), jnp.float32),
            pltpu.VMEM((LANES + 8, highs), jnp.float32),
            pltpu.VMEM((16 * groups, highs), jnp.bfloat16),
            pltpu.VMEM((rows, LANES), jnp.float32),
            pltpu.VMEM((16 * groups, chunk), jnp.float32),
            pltpu.VMEM((16 * groups, chunk), jnp.float32),
            pltpu.SemaphoreType.DMA((3 + 2 * pixels // chunk,)),
        ],
        compiler_params=pltpu.CompilerParams(vmem_limit_bytes=16 * MIB),
        name="project_row",
    )(*(in_hbm(value) for value in (class_refs, interp_index, interp_frac, images)))


def slot_rows(device, slots):
    ids = lax.broadcasted_iota(jnp.int32, (slots, 1), 0)
    return 2 * ((device // 4) ^ (ids // 2)) + ids % 2


def split_mass(mass_row):
    ids = lax.broadcasted_iota(jnp.int32, (MASS_ROWS, LANES), 0)
    upper = mass_row.astype(jnp.bfloat16).astype(jnp.float32)
    lower = mass_row - upper
    return jnp.where(ids == 0, upper, jnp.where(ids == 1, lower, 0.0)).astype(jnp.bfloat16)


def joined_mass(block):
    return jnp.sum(block.astype(jnp.float32), axis=0, keepdims=True)


def table_kernel(shift_ref, cos_ref, sin_ref):
    shifts, width = cos_ref.shape
    grid_x = shift_ref[:, 0:1]
    grid_y = shift_ref[:, 1:2]
    lane = lax.broadcasted_iota(jnp.int32, (shifts, LANES), 1)
    freq_x = (lane // BLOCK) * (2 * BLOCK) + own_half() * BLOCK + lane % BLOCK
    turn_x = (freq_x * grid_x) & (BOX - 1)
    turn_y = ((lane - KY // 2) * grid_y) & (BOX - 1)
    angle_x = turn_x.astype(jnp.float32) * (2.0 * math.pi / BOX)
    angle_y = turn_y.astype(jnp.float32) * (2.0 * math.pi / BOX)
    cos_x, sin_x = jnp.cos(angle_x), jnp.sin(angle_x)
    cos_y, sin_y = jnp.cos(angle_y), jnp.sin(angle_y)
    for j in range(width // LANES):
        where = slice(j * LANES, (j + 1) * LANES)
        cos_j, sin_j = cos_x[:, j : j + 1], sin_x[:, j : j + 1]
        cos_ref[:, where] = cos_j * cos_y - sin_j * sin_y
        sin_ref[:, where] = sin_j * cos_y + cos_j * sin_y


def phase_tables(shift_grid, width):
    shape = jax.ShapeDtypeStruct((shift_grid.shape[0], width), jnp.float32)
    return pl.pallas_call(
        table_kernel,
        in_specs=whole_vmem(1),
        out_specs=whole_vmem(2),
        out_shape=[shape, shape],
        compiler_params=pltpu.CompilerParams(vmem_limit_bytes=16 * MIB),
        cost_estimate=pl.CostEstimate(flops=2000000, bytes_accessed=2000000, transcendentals=0),
        name="phase_tables",
    )(shift_grid)


def correlate_kernel(own_images, other_images, precision_ref, assigned_ref, cos_ref, sin_ref, *refs, chunk):
    row_refs, (out_ref, proj) = refs[:-2], refs[-2:]
    shifts = cos_ref.shape[0]
    parts = own_images.shape[0]
    slots = len(row_refs)
    width = own_images.shape[1] // 2
    tiles = width // LANES
    per_row = 2 * tiles
    core = own_half()
    for m in range(slots // 2):
        own_place = pl.multiple_of((2 * m + core) * per_row, per_row)
        other_place = pl.multiple_of((2 * m + 1 - core) * per_row, per_row)
        proj[pl.ds(own_place, per_row), :] = row_refs[m][0:per_row, :].astype(jnp.float32)
        proj[pl.ds(other_place, per_row), :] = row_refs[slots // 2 + m][per_row:, :].astype(
            jnp.float32
        )

    chunk_tiles = chunk // LANES
    contract_lanes = (((1,), (1,)), ((), ()))

    def body(step, carry):
        total, power = carry
        first = step * chunk_tiles
        real = jnp.concatenate(
            [proj[pl.ds(first + k, slots, stride=per_row), :] for k in range(chunk_tiles)], axis=1
        )
        imag = jnp.concatenate(
            [proj[pl.ds(tiles + first + k, slots, stride=per_row), :] for k in range(chunk_tiles)],
            axis=1,
        )
        where = pl.ds(pl.multiple_of(step * chunk, chunk), chunk)
        imag_where = pl.ds(pl.multiple_of(width + step * chunk, chunk), chunk)
        reals, imags = [], []
        for s in range(shifts):
            cos_s, sin_s = cos_ref[s : s + 1, where], sin_ref[s : s + 1, where]
            reals.append(real * cos_s - imag * sin_s)
            imags.append(real * sin_s + imag * cos_s)
        turned_real = jnp.concatenate(reals, axis=0).astype(jnp.bfloat16)
        turned_imag = jnp.concatenate(imags, axis=0).astype(jnp.bfloat16)
        image_real = jnp.concatenate([own_images[:, where], other_images[:, where]], axis=0)
        image_imag = jnp.concatenate([own_images[:, imag_where], other_images[:, imag_where]], axis=0)
        total = total + lax.dot_general(
            turned_real, image_real, contract_lanes, preferred_element_type=jnp.float32
        )
        total = total + lax.dot_general(
            turned_imag, image_imag, contract_lanes, preferred_element_type=jnp.float32
        )
        squares = real * real + imag * imag
        for k in range(chunk_tiles):
            power = power + squares[:, k * LANES : (k + 1) * LANES]
        return total, power

    total, power = lax.fori_loop(
        0,
        width // chunk,
        body,
        (
            jnp.zeros((shifts * slots, 2 * parts), jnp.float32),
            jnp.zeros((slots, LANES), jnp.float32),
        ),
    )
    combos = shifts * slots
    out_ref[...] = jnp.zeros_like(out_ref)
    out_ref[0:combos, 0 : 2 * parts] = total
    out_ref[combos : combos + slots, :] = jnp.broadcast_to(
        jnp.sum(power, axis=1, keepdims=True), (slots, LANES)
    )
    out_ref[combos + slots : combos + slots + 1, 0:parts] = precision_ref[...]
    out_ref[combos + slots + 1 : combos + slots + 2, 0:parts] = assigned_ref[...].astype(jnp.float32)


def correlate(own_images, other_images, precision, assigned, cos_table, sin_table, rows):
    slots = len(rows)
    shifts, width = cos_table.shape
    return pl.pallas_call(
        functools.partial(correlate_kernel, chunk=2048),
        in_specs=whole_vmem(6 + slots),
        out_specs=pl.BlockSpec(memory_space=pltpu.VMEM),
        out_shape=jax.ShapeDtypeStruct((shifts * slots + slots + 8, LANES), jnp.float32),
        scratch_shapes=[pltpu.VMEM((slots * 2 * width // LANES, LANES), jnp.float32)],
        compiler_params=pltpu.CompilerParams(vmem_limit_bytes=(14 + slots // 2) * MIB),
        name="correlate",
    )(own_images, other_images, precision, assigned, cos_table, sin_table, *rows)


def rotate_back(weights, own_images, other_images, cos_ref, sin_ref, where, imag_where, slots):
    image_real = jnp.concatenate([own_images[:, where], other_images[:, where]], axis=0)
    image_imag = jnp.concatenate([own_images[:, imag_where], other_images[:, imag_where]], axis=0)
    from_real = jnp.dot(weights, image_real, preferred_element_type=jnp.float32)
    from_imag = jnp.dot(weights, image_imag, preferred_element_type=jnp.float32)
    real = imag = None
    for s in range(cos_ref.shape[0]):
        cos_s, sin_s = cos_ref[s : s + 1, where], sin_ref[s : s + 1, where]
        part_real = from_real[s * slots : (s + 1) * slots]
        part_imag = from_imag[s * slots : (s + 1) * slots]
        real_s = part_real * cos_s + part_imag * sin_s
        imag_s = part_imag * cos_s - part_real * sin_s
        real = real_s if real is None else real + real_s
        imag = imag_s if imag is None else imag + imag_s
    return real, imag


def posterior_kernel(
    mine, received, own_images, other_images, cos_ref, sin_ref,
    weight_ref, low_ref, low_send, own_mass, *, slots
):
    device = lax.axis_index("particle")
    shifts, width = cos_ref.shape
    parts = own_images.shape[0]
    combos = shifts * slots
    theirs = received[...]
    lane = lax.broadcasted_iota(jnp.int32, theirs.shape, 1)
    swapped = jnp.where(
        lane < parts, pltpu.roll(theirs, LANES - parts, 1), pltpu.roll(theirs, parts, 1)
    )
    joint = mine[...] + swapped
    power = mine[combos : combos + slots, :] + received[combos : combos + slots, :]
    precision = joint[combos + slots : combos + slots + 1]
    assigned = joint[combos + slots + 1 : combos + slots + 2].astype(jnp.int32)
    slot_class = slot_rows(device, slots) // (slots // CLASSES)
    match = (slot_class == assigned).astype(jnp.float32) * PRIOR_REWARD
    likelihood_scale = 1.0 / math.sqrt(4 * width)
    logits = [
        precision * (joint[s * slots : (s + 1) * slots] - 0.5 * power) * likelihood_scale + match
        for s in range(shifts)
    ]
    peak = functools.reduce(jnp.maximum, logits)
    peak = jnp.max(peak, axis=0, keepdims=True)
    terms = [jnp.exp(value - peak) for value in logits]
    mass = functools.reduce(jnp.add, terms)
    norm = jnp.sum(mass, axis=0, keepdims=True)
    weights = jnp.concatenate([term / norm for term in terms], axis=0)
    weights = weights[:, 0 : 2 * parts].astype(jnp.bfloat16)
    weight_ref[...] = weights
    counted = lax.broadcasted_iota(jnp.int32, (1, LANES), 1) < 2 * parts
    share = jnp.where(counted, mass / norm * precision, 0.0)
    slot_mass = jnp.sum(share, axis=1, keepdims=True)
    class_lane = lax.broadcasted_iota(jnp.int32, (slots, LANES), 1)
    mass_row = jnp.sum(
        jnp.where(class_lane == slot_class, slot_mass, 0.0), axis=0, keepdims=True
    )
    own_mass[...] = jnp.broadcast_to(mass_row, own_mass.shape)

    low = LOW_TILES * LANES
    real, imag = rotate_back(
        weights, own_images, other_images, cos_ref, sin_ref, slice(0, low), slice(width, width + low), slots
    )
    for k in range(LOW_TILES):
        piece = slice(k * LANES, (k + 1) * LANES)
        low_ref[pl.ds(k, slots, stride=2 * LOW_TILES), :] = real[:, piece]
        low_ref[pl.ds(LOW_TILES + k, slots, stride=2 * LOW_TILES), :] = imag[:, piece]
    low_body = low_ref.shape[0]
    low_send[0:low_body, :] = low_ref[...].astype(jnp.bfloat16)
    low_send[low_body:, :] = split_mass(mass_row)


def posterior(mine, received, own_images, other_images, cos_table, sin_table, slots):
    shifts = cos_table.shape[0]
    low = slots * 2 * LOW_TILES
    return pl.pallas_call(
        functools.partial(posterior_kernel, slots=slots),
        in_specs=whole_vmem(6),
        out_specs=whole_vmem(4),
        out_shape=[
            jax.ShapeDtypeStruct((shifts * slots, 2 * own_images.shape[0]), jnp.bfloat16),
            jax.ShapeDtypeStruct((low, LANES), jnp.float32),
            jax.ShapeDtypeStruct((low + MASS_ROWS, LANES), jnp.bfloat16),
            jax.ShapeDtypeStruct((8, LANES), jnp.float32),
        ],
        compiler_params=pltpu.CompilerParams(vmem_limit_bytes=(14 + slots // 2) * MIB),
        name="posterior",
    )(mine, received, own_images, other_images, cos_table, sin_table)


def backproject_kernel(
    weight_ref, own_images, other_images, cos_ref, sin_ref, sums, *, slots, chunk, unroll
):
    width = cos_ref.shape[1]
    tiles = width // LANES
    per_row = 2 * tiles
    chunk_tiles = chunk // LANES
    weights = weight_ref[...]

    def body(step, carry):
        first = LOW_TILES + step * chunk_tiles
        start = pl.multiple_of(first * LANES, LOW_TILES * LANES)
        where = pl.ds(start, chunk)
        imag_where = pl.ds(pl.multiple_of(width + start, LOW_TILES * LANES), chunk)
        real, imag = rotate_back(
            weights, own_images, other_images, cos_ref, sin_ref, where, imag_where, slots
        )
        for k in range(chunk_tiles):
            piece = slice(k * LANES, (k + 1) * LANES)
            sums[pl.ds(first + k, slots, stride=per_row), :] = real[:, piece]
            sums[pl.ds(tiles + first + k, slots, stride=per_row), :] = imag[:, piece]
        return carry

    lax.fori_loop(0, (tiles - LOW_TILES) // chunk_tiles, body, 0, unroll=unroll)


def backproject(weights, own_images, other_images, cos_table, sin_table, slots):
    width = cos_table.shape[1]
    rows = slots * 2 * width // LANES
    return pl.pallas_call(
        functools.partial(
            backproject_kernel,
            slots=slots,
            chunk=LOW_TILES * LANES,
            unroll=7 if slots <= 8 else 1,
        ),
        in_specs=whole_vmem(5),
        out_specs=pl.BlockSpec(memory_space=pltpu.VMEM),
        out_shape=jax.ShapeDtypeStruct((rows, LANES), jnp.float32),
        compiler_params=pltpu.CompilerParams(vmem_limit_bytes=(14 + slots // 2) * MIB),
        cost_estimate=pl.CostEstimate(flops=20000000, bytes_accessed=20000000, transcendentals=0),
        name="backproject",
    )(weights, own_images, other_images, cos_table, sin_table)


def fold_kernel(sums, low_ref, low_received, mass, own, own_mass, *sends, slots):
    per_row = sums.shape[0] // slots
    tiles = per_row // 2
    low_body = low_ref.shape[0]
    total_mass = mass[0:1, :] + joined_mass(low_received[low_body:, :])
    block = split_mass(total_mass)
    own_mass[...] = jnp.broadcast_to(total_mass, own_mass.shape)
    for slot in range(slots):
        target = own if slot < 2 else sends[slot // 2 - 1]
        for comp in range(2):
            low = slice((2 * slot + comp) * LOW_TILES, (2 * slot + comp + 1) * LOW_TILES)
            start = slot * per_row + comp * tiles
            dest = (slot % 2) * per_row + comp * tiles
            value = (low_ref[low, :] + low_received[low, :].astype(jnp.float32)) * 0.5
            value = jnp.concatenate([value, sums[start + LOW_TILES : start + tiles, :]], axis=0)
            target[dest : dest + tiles, :] = value.astype(target.dtype)
    for send in sends:
        send[2 * per_row :, :] = block


def fold(sums, low, low_received, mass, slots):
    rows = 2 * sums.shape[0] // slots
    chips = slots // 2
    return pl.pallas_call(
        functools.partial(fold_kernel, slots=slots),
        in_specs=whole_vmem(4),
        out_specs=whole_vmem(1 + chips),
        out_shape=[
            jax.ShapeDtypeStruct((rows, LANES), jnp.float32),
            jax.ShapeDtypeStruct((8, LANES), jnp.float32),
        ]
        + [jax.ShapeDtypeStruct((rows + MASS_ROWS, LANES), jnp.bfloat16)] * (chips - 1),
        compiler_params=pltpu.CompilerParams(vmem_limit_bytes=(10 + slots // 2) * MIB),
        name="fold",
    )(sums, low, low_received, mass)


def relay_kernel(own, received, out):
    rows = out.shape[0] - MASS_ROWS
    total = own[0:rows, :].astype(jnp.float32) + received[0:rows, :].astype(jnp.float32)
    out[0:rows, :] = total.astype(out.dtype)
    out[rows:, :] = split_mass(joined_mass(own[rows:, :]) + joined_mass(received[rows:, :]))


def relay(own, received):
    return pl.pallas_call(
        relay_kernel,
        in_specs=whole_vmem(2),
        out_specs=pl.BlockSpec(memory_space=pltpu.VMEM),
        out_shape=jax.ShapeDtypeStruct(own.shape, own.dtype),
        compiler_params=pltpu.CompilerParams(vmem_limit_bytes=16 * MIB),
        name="relay",
    )(own, received)


def gather_chips(row, chips):
    rows = {0: row}
    bit = chips // 2
    while bit:
        rows.update({m ^ bit: exchange(rows[m], 4 * bit) for m in list(rows)})
        bit //= 2
    return [rows[m] for m in range(chips)]


def scatter_chips(sends, chips):
    held = dict(enumerate(sends, start=1))
    arrived = []
    bit = 1
    while bit < chips:
        away = {m: exchange(held.pop(m), 4 * bit) for m in sorted(held, reverse=True) if m & bit}
        arrived.append(away.pop(bit))
        for m, value in away.items():
            held[m ^ bit] = relay(held[m ^ bit], value)
        bit *= 2
    return arrived


def merge_kernel(own, mass, *refs):
    received, (keep, send, mass_out) = refs[:-3], refs[-3:]
    rows = own.shape[0]
    half = rows // 2
    core = own_half()
    total_mass = mass[0:1, :]
    for ref in received:
        total_mass = total_mass + joined_mass(ref[rows:, :])
    mass_out[...] = jnp.broadcast_to(total_mass, mass_out.shape)
    for target, place in ((send, 1 - core), (keep, core)):
        where = pl.ds(pl.multiple_of(place * half, half), half)
        total = own[where, :]
        for ref in received:
            total = total + ref[where, :].astype(jnp.float32)
        target[...] = total.astype(target.dtype)


def merge(own, mass, received):
    rows = own.shape[0] // 2
    return pl.pallas_call(
        merge_kernel,
        in_specs=whole_vmem(2 + len(received)),
        out_specs=whole_vmem(3),
        out_shape=[
            jax.ShapeDtypeStruct((rows, LANES), jnp.float32),
            jax.ShapeDtypeStruct((rows, LANES), jnp.bfloat16),
            jax.ShapeDtypeStruct((8, LANES), jnp.float32),
        ],
        compiler_params=pltpu.CompilerParams(vmem_limit_bytes=16 * MIB),
        name="merge",
    )(own, mass, *received)


def finish_kernel(own, received, mass, out, mass_out, *, scale, mass_scale):
    half = own_half()
    mass_out[...] = mass[0, :CLASSES] * mass_scale
    for step in range(own.shape[0] // BLOCK):
        rows = slice(step * BLOCK, (step + 1) * BLOCK)
        own_rows = pl.ds(pl.multiple_of((2 * step + half) * BLOCK, BLOCK), BLOCK)
        other_rows = pl.ds(pl.multiple_of((2 * step + 1 - half) * BLOCK, BLOCK), BLOCK)
        out[own_rows, :] = own[rows, :] * scale
        out[other_rows, :] = received[rows, :].astype(jnp.float32) * scale


def finish(own, received, mass, scale, mass_scale):
    return pl.pallas_call(
        functools.partial(finish_kernel, scale=scale, mass_scale=mass_scale),
        in_specs=whole_vmem(3),
        out_specs=whole_vmem(2),
        out_shape=[
            jax.ShapeDtypeStruct((2 * own.shape[0], LANES), jnp.float32),
            jax.ShapeDtypeStruct((CLASSES,), jnp.float32),
        ],
        compiler_params=pltpu.CompilerParams(vmem_limit_bytes=16 * MIB),
        name="finish",
    )(own, received, mass)


def local(
    images, noise_precision, assigned_class, class_refs, interp_index, interp_frac, shift_grid
):
    dev_count = lax.axis_size("particle")
    slots = dev_count // 2
    chips = slots // 2
    parts, width = images.shape
    own_row, own_images, other_images = project_row(class_refs, interp_index, interp_frac, images)
    rows = gather_chips(own_row, chips)
    rows = rows + [exchange(row, 1) for row in rows]
    images_received = exchange(other_images, 1)
    cos_table, sin_table = phase_tables(shift_grid, width // 4)
    mine = correlate(
        own_images,
        images_received,
        noise_precision.reshape(1, parts),
        assigned_class.reshape(1, parts),
        cos_table,
        sin_table,
        rows,
    )
    weights, low, low_send, mass = posterior(
        mine, exchange(mine, 1), own_images, images_received, cos_table, sin_table, slots
    )
    low_received = exchange(low_send, 2)
    sums = backproject(weights, own_images, images_received, cos_table, sin_table, slots)
    folded = fold(sums, low, low_received, mass, slots)
    received = scatter_chips(folded[2:], chips)
    keep, send, mass = merge(folded[0], folded[1], received)
    back, class_mass = finish(
        keep, exchange(send, 1), mass, 1.0 / math.sqrt(parts), CLASSES / (parts * dev_count)
    )
    return back.reshape(1, width), class_mass


def solution(mesh):
    in_specs = (
        P(("groups", "particle"), None),
        P(("groups", "particle")),
        P(("groups", "particle")),
        P("groups", None, None, None),
        P("particle", None),
        P("particle", None),
        P(),
    )
    out_specs = (P(("groups", "particle"), None), P("groups"))
    return jax.shard_map(local, mesh=mesh, in_specs=in_specs, out_specs=out_specs, check_vma=False)
```

```python
import functools
import math

import jax
import jax.numpy as jnp
from jax import lax
from jax.experimental import pallas as pl
from jax.experimental.pallas import tpu as pltpu
from jax.sharding import PartitionSpec as P

KY = 128
BOX = 256
CLASSES = 8
LOWK = 16
LANES = 128
PRIOR_REWARD = 1.0
MASS_ROWS = 16
BLOCK = 8
LOW_TILES = LOWK * KY // LANES // 2
MIB = 1 << 20


def exchange(value, mask):
    pairs = [(source, source ^ mask) for source in range(lax.axis_size("particle"))]
    return lax.ppermute(value, "particle", pairs)


def in_hbm(value):
    return pltpu.with_memory_space_constraint(value, pltpu.HBM)


def whole_vmem(count):
    return [pl.BlockSpec(memory_space=pltpu.VMEM)] * count


def own_half():
    return lax.axis_index("particle") % 2


def tree_select(values, masks):
    for mask in masks:
        values = [
            jnp.where(mask, values[i + 1], values[i]) if i + 1 < len(values) else values[i]
            for i in range(0, len(values), 2)
        ]
    return values[0]


def project_kernel(
    table_hbm, index_hbm, frac_hbm, images_hbm, out_ref, own_images, other_images,
    table_in, index_ref, frac_ref, flat, wide, table, blended, sems
):
    device = lax.axis_index("particle")
    row_count = lax.axis_size("particle") // 2
    half_set = device // 2 % 2
    class_id = (2 * (device // 4) + device % 2) // (row_count // CLASSES)
    core = own_half()
    highs = flat.shape[1]
    pixels = index_ref.shape[1]
    groups = table.shape[0] // 16
    stride = 8 * groups
    chunk = BLOCK * LANES
    blocks = pixels // (2 * chunk)
    copies = [
        pltpu.make_async_copy(
            table_hbm.at[pl.ds(half_set, 1), pl.ds(class_id, 1)], table_in, sems.at[0]
        ),
        pltpu.make_async_copy(index_hbm, index_ref, sems.at[1]),
        pltpu.make_async_copy(frac_hbm, frac_ref, sems.at[2]),
    ]
    for target, half in ((other_images, 1 - core), (own_images, core)):
        for comp in range(2):
            for step in range(blocks):
                source = pl.multiple_of(comp * pixels + (2 * step + half) * chunk, chunk)
                dest = (comp * blocks + step) * chunk
                copies.append(
                    pltpu.make_async_copy(
                        images_hbm.at[:, pl.ds(source, chunk)],
                        target.at[:, pl.ds(dest, chunk)],
                        sems.at[len(copies)],
                    )
                )
    for copy in copies:
        copy.start()
    copies[0].wait()

    def unfold(step, carry):
        piece = table_in[0, 0, :, pl.ds(step * 8 * LANES, 8 * LANES)].astype(jnp.float32)
        for k in range(8):
            for comp in range(2):
                flat[comp, pl.ds(step * 8 + k, 1), :] = piece[comp : comp + 1, k * LANES : (k + 1) * LANES]
        return carry

    lax.fori_loop(0, highs // 8, unfold, 0, unroll=4)
    picked = []
    for comp in range(2):
        turned = flat[comp].T
        wide[0:LANES, :] = turned
        wide[LANES : LANES + 8, :] = pltpu.roll(turned[0:8], highs - 1, 1)
        picked += [wide[7 * g : 7 * g + 8, :] for g in range(groups)]
    for pair in range(groups):
        table[16 * pair : 16 * (pair + 1), :] = jnp.concatenate(
            picked[2 * pair : 2 * pair + 2], axis=0
        ).astype(jnp.bfloat16)
    copies[1].wait()
    copies[2].wait()

    def place(step):
        block = 2 * (step % blocks) + jnp.where(step < blocks, core, 1 - core)
        return pl.ds(pl.multiple_of(block * chunk, chunk), chunk)

    def body(step, carry):
        index = index_ref[:, place(step)]
        frac = frac_ref[:, place(step)]
        high = jnp.broadcast_to((index >> 7).astype(jnp.float32), (16, chunk)).astype(jnp.bfloat16)
        low = index & (LANES - 1)
        group = (low * 147) >> 10
        first = low - 7 * group
        one_hot = jnp.concatenate(
            [
                jnp.where(high == (ids16 + 16 * k).astype(jnp.bfloat16), ones16, zeros16)
                for k in range(highs // 16)
            ],
            axis=0,
        )
        rows = jnp.dot(table[...], one_hot, preferred_element_type=jnp.float32)
        group = jnp.broadcast_to(group, (8, chunk))
        masks = [(group & (1 << bit)) != 0 for bit in range((groups - 1).bit_length())]
        ids = lax.broadcasted_iota(jnp.int32, (8, chunk), 0)
        weight = jnp.where(ids == first, 1.0 - frac, jnp.where(ids == first + 1, frac, 0.0))
        for comp in range(2):
            start = comp * stride
            picked = tree_select(
                [rows[start + 8 * g : start + 8 * g + 8] for g in range(groups)], masks
            )
            value = jnp.sum(picked * weight, axis=0, keepdims=True)
            first_row = (step // blocks * 2 + comp) * blocks * BLOCK + step % blocks * BLOCK
            for k in range(BLOCK):
                blended[pl.ds(first_row + k, 1), :] = value[:, k * LANES : (k + 1) * LANES]
        return carry

    ids16 = lax.broadcasted_iota(jnp.int32, (16, chunk), 0).astype(jnp.float32)
    ones16 = jnp.ones((16, chunk), jnp.bfloat16)
    zeros16 = jnp.zeros((16, chunk), jnp.bfloat16)
    lax.fori_loop(0, 2 * blocks, body, 0, unroll=2)
    out_ref[...] = blended[...].astype(jnp.bfloat16)
    for copy in copies[3:]:
        copy.wait()


def project_row(class_refs, interp_index, interp_frac, images):
    vox = class_refs.shape[3]
    pixels = interp_index.shape[1]
    highs = vox // LANES
    rows = 2 * pixels // LANES
    groups = -(-LANES // 7)
    chunk = BLOCK * LANES
    half_images = jax.ShapeDtypeStruct((images.shape[0], pixels), jnp.bfloat16)
    return pl.pallas_call(
        project_kernel,
        in_specs=[pl.BlockSpec(memory_space=pltpu.HBM)] * 4,
        out_specs=whole_vmem(3),
        out_shape=[jax.ShapeDtypeStruct((rows, LANES), jnp.bfloat16), half_images, half_images],
        scratch_shapes=[
            pltpu.VMEM((1, 1, 2, vox), jnp.bfloat16),
            pltpu.VMEM((1, pixels), jnp.int32),
            pltpu.VMEM((1, pixels), jnp.float32),
            pltpu.VMEM((2, highs, LANES), jnp.float32),
            pltpu.VMEM((LANES + 8, highs), jnp.float32),
            pltpu.VMEM((16 * groups, highs), jnp.bfloat16),
            pltpu.VMEM((rows, LANES), jnp.float32),
            pltpu.SemaphoreType.DMA((3 + 2 * pixels // chunk,)),
        ],
        compiler_params=pltpu.CompilerParams(vmem_limit_bytes=16 * MIB),
        name="project_row",
    )(*(in_hbm(value) for value in (class_refs, interp_index, interp_frac, images)))


def slot_rows(device, slots):
    ids = lax.broadcasted_iota(jnp.int32, (slots, 1), 0)
    return 2 * ((device // 4) ^ (ids // 2)) + ids % 2


def split_mass(mass_row):
    ids = lax.broadcasted_iota(jnp.int32, (MASS_ROWS, LANES), 0)
    upper = mass_row.astype(jnp.bfloat16).astype(jnp.float32)
    lower = mass_row - upper
    return jnp.where(ids == 0, upper, jnp.where(ids == 1, lower, 0.0)).astype(jnp.bfloat16)


def joined_mass(block):
    return jnp.sum(block.astype(jnp.float32), axis=0, keepdims=True)


def table_kernel(shift_ref, cos_ref, sin_ref):
    shifts, width = cos_ref.shape
    grid_x = shift_ref[:, 0:1]
    grid_y = shift_ref[:, 1:2]
    lane = lax.broadcasted_iota(jnp.int32, (shifts, LANES), 1)
    freq_x = (lane // BLOCK) * (2 * BLOCK) + own_half() * BLOCK + lane % BLOCK
    turn_x = (freq_x * grid_x) & (BOX - 1)
    turn_y = ((lane - KY // 2) * grid_y) & (BOX - 1)
    angle_x = turn_x.astype(jnp.float32) * (2.0 * math.pi / BOX)
    angle_y = turn_y.astype(jnp.float32) * (2.0 * math.pi / BOX)
    cos_x, sin_x = jnp.cos(angle_x), jnp.sin(angle_x)
    cos_y, sin_y = jnp.cos(angle_y), jnp.sin(angle_y)
    for j in range(width // LANES):
        where = slice(j * LANES, (j + 1) * LANES)
        cos_j, sin_j = cos_x[:, j : j + 1], sin_x[:, j : j + 1]
        cos_ref[:, where] = cos_j * cos_y - sin_j * sin_y
        sin_ref[:, where] = sin_j * cos_y + cos_j * sin_y


def phase_tables(shift_grid, width):
    shape = jax.ShapeDtypeStruct((shift_grid.shape[0], width), jnp.float32)
    return pl.pallas_call(
        table_kernel,
        in_specs=whole_vmem(1),
        out_specs=whole_vmem(2),
        out_shape=[shape, shape],
        compiler_params=pltpu.CompilerParams(vmem_limit_bytes=16 * MIB),
        cost_estimate=pl.CostEstimate(flops=2000000, bytes_accessed=2000000, transcendentals=0),
        name="phase_tables",
    )(shift_grid)


def correlate_kernel(own_images, other_images, precision_ref, assigned_ref, cos_ref, sin_ref, *refs, chunk):
    row_refs, (out_ref, proj) = refs[:-2], refs[-2:]
    shifts = cos_ref.shape[0]
    parts = own_images.shape[0]
    slots = len(row_refs)
    width = own_images.shape[1] // 2
    tiles = width // LANES
    per_row = 2 * tiles
    core = own_half()
    for m in range(slots // 2):
        own_place = pl.multiple_of((2 * m + core) * per_row, per_row)
        other_place = pl.multiple_of((2 * m + 1 - core) * per_row, per_row)
        proj[pl.ds(own_place, per_row), :] = row_refs[m][0:per_row, :].astype(jnp.float32)
        proj[pl.ds(other_place, per_row), :] = row_refs[slots // 2 + m][per_row:, :].astype(
            jnp.float32
        )

    chunk_tiles = chunk // LANES
    contract_lanes = (((1,), (1,)), ((), ()))

    def body(step, carry):
        total, power = carry
        first = step * chunk_tiles
        real = jnp.concatenate(
            [proj[pl.ds(first + k, slots, stride=per_row), :] for k in range(chunk_tiles)], axis=1
        )
        imag = jnp.concatenate(
            [proj[pl.ds(tiles + first + k, slots, stride=per_row), :] for k in range(chunk_tiles)],
            axis=1,
        )
        where = pl.ds(pl.multiple_of(step * chunk, chunk), chunk)
        imag_where = pl.ds(pl.multiple_of(width + step * chunk, chunk), chunk)
        reals, imags = [], []
        for s in range(shifts):
            cos_s, sin_s = cos_ref[s : s + 1, where], sin_ref[s : s + 1, where]
            reals.append(real * cos_s - imag * sin_s)
            imags.append(real * sin_s + imag * cos_s)
        turned_real = jnp.concatenate(reals, axis=0).astype(jnp.bfloat16)
        turned_imag = jnp.concatenate(imags, axis=0).astype(jnp.bfloat16)
        image_real = jnp.concatenate([own_images[:, where], other_images[:, where]], axis=0)
        image_imag = jnp.concatenate([own_images[:, imag_where], other_images[:, imag_where]], axis=0)
        total = total + lax.dot_general(
            turned_real, image_real, contract_lanes, preferred_element_type=jnp.float32
        )
        total = total + lax.dot_general(
            turned_imag, image_imag, contract_lanes, preferred_element_type=jnp.float32
        )
        squares = real * real + imag * imag
        for k in range(chunk_tiles):
            power = power + squares[:, k * LANES : (k + 1) * LANES]
        return total, power

    total, power = lax.fori_loop(
        0,
        width // chunk,
        body,
        (
            jnp.zeros((shifts * slots, 2 * parts), jnp.float32),
            jnp.zeros((slots, LANES), jnp.float32),
        ),
    )
    combos = shifts * slots
    out_ref[...] = jnp.zeros_like(out_ref)
    out_ref[0:combos, 0 : 2 * parts] = total
    out_ref[combos : combos + slots, :] = jnp.broadcast_to(
        jnp.sum(power, axis=1, keepdims=True), (slots, LANES)
    )
    out_ref[combos + slots : combos + slots + 1, 0:parts] = precision_ref[...]
    out_ref[combos + slots + 1 : combos + slots + 2, 0:parts] = assigned_ref[...].astype(jnp.float32)


def correlate(own_images, other_images, precision, assigned, cos_table, sin_table, rows):
    slots = len(rows)
    shifts, width = cos_table.shape
    return pl.pallas_call(
        functools.partial(correlate_kernel, chunk=2048),
        in_specs=whole_vmem(6 + slots),
        out_specs=pl.BlockSpec(memory_space=pltpu.VMEM),
        out_shape=jax.ShapeDtypeStruct((shifts * slots + slots + 8, LANES), jnp.float32),
        scratch_shapes=[pltpu.VMEM((slots * 2 * width // LANES, LANES), jnp.float32)],
        compiler_params=pltpu.CompilerParams(vmem_limit_bytes=(14 + slots // 2) * MIB),
        name="correlate",
    )(own_images, other_images, precision, assigned, cos_table, sin_table, *rows)


def rotate_back(weights, own_images, other_images, cos_ref, sin_ref, where, imag_where, slots):
    image_real = jnp.concatenate([own_images[:, where], other_images[:, where]], axis=0)
    image_imag = jnp.concatenate([own_images[:, imag_where], other_images[:, imag_where]], axis=0)
    from_real = jnp.dot(weights, image_real, preferred_element_type=jnp.float32)
    from_imag = jnp.dot(weights, image_imag, preferred_element_type=jnp.float32)
    real = imag = None
    for s in range(cos_ref.shape[0]):
        cos_s, sin_s = cos_ref[s : s + 1, where], sin_ref[s : s + 1, where]
        part_real = from_real[s * slots : (s + 1) * slots]
        part_imag = from_imag[s * slots : (s + 1) * slots]
        real_s = part_real * cos_s + part_imag * sin_s
        imag_s = part_imag * cos_s - part_real * sin_s
        real = real_s if real is None else real + real_s
        imag = imag_s if imag is None else imag + imag_s
    return real, imag


def posterior_kernel(
    mine, received, own_images, other_images, cos_ref, sin_ref,
    weight_ref, low_ref, low_send, own_mass, *, slots
):
    device = lax.axis_index("particle")
    shifts, width = cos_ref.shape
    parts = own_images.shape[0]
    combos = shifts * slots
    theirs = received[...]
    lane = lax.broadcasted_iota(jnp.int32, theirs.shape, 1)
    swapped = jnp.where(
        lane < parts, pltpu.roll(theirs, LANES - parts, 1), pltpu.roll(theirs, parts, 1)
    )
    joint = mine[...] + swapped
    power = mine[combos : combos + slots, :] + received[combos : combos + slots, :]
    precision = joint[combos + slots : combos + slots + 1]
    assigned = joint[combos + slots + 1 : combos + slots + 2].astype(jnp.int32)
    slot_class = slot_rows(device, slots) // (slots // CLASSES)
    match = (slot_class == assigned).astype(jnp.float32) * PRIOR_REWARD
    likelihood_scale = 1.0 / math.sqrt(4 * width)
    logits = [
        precision * (joint[s * slots : (s + 1) * slots] - 0.5 * power) * likelihood_scale + match
        for s in range(shifts)
    ]
    peak = functools.reduce(jnp.maximum, logits)
    peak = jnp.max(peak, axis=0, keepdims=True)
    terms = [jnp.exp(value - peak) for value in logits]
    mass = functools.reduce(jnp.add, terms)
    norm = jnp.sum(mass, axis=0, keepdims=True)
    weights = jnp.concatenate([term / norm for term in terms], axis=0)
    weights = weights[:, 0 : 2 * parts].astype(jnp.bfloat16)
    weight_ref[...] = weights
    counted = lax.broadcasted_iota(jnp.int32, (1, LANES), 1) < 2 * parts
    share = jnp.where(counted, mass / norm * precision, 0.0)
    slot_mass = jnp.sum(share, axis=1, keepdims=True)
    class_lane = lax.broadcasted_iota(jnp.int32, (slots, LANES), 1)
    mass_row = jnp.sum(
        jnp.where(class_lane == slot_class, slot_mass, 0.0), axis=0, keepdims=True
    )
    own_mass[...] = jnp.broadcast_to(mass_row, own_mass.shape)

    low = LOW_TILES * LANES
    real, imag = rotate_back(
        weights, own_images, other_images, cos_ref, sin_ref, slice(0, low), slice(width, width + low), slots
    )
    for k in range(LOW_TILES):
        piece = slice(k * LANES, (k + 1) * LANES)
        low_ref[pl.ds(k, slots, stride=2 * LOW_TILES), :] = real[:, piece]
        low_ref[pl.ds(LOW_TILES + k, slots, stride=2 * LOW_TILES), :] = imag[:, piece]
    low_body = low_ref.shape[0]
    low_send[0:low_body, :] = low_ref[...].astype(jnp.bfloat16)
    low_send[low_body:, :] = split_mass(mass_row)


def posterior(mine, received, own_images, other_images, cos_table, sin_table, slots):
    shifts = cos_table.shape[0]
    low = slots * 2 * LOW_TILES
    return pl.pallas_call(
        functools.partial(posterior_kernel, slots=slots),
        in_specs=whole_vmem(6),
        out_specs=whole_vmem(4),
        out_shape=[
            jax.ShapeDtypeStruct((shifts * slots, 2 * own_images.shape[0]), jnp.bfloat16),
            jax.ShapeDtypeStruct((low, LANES), jnp.float32),
            jax.ShapeDtypeStruct((low + MASS_ROWS, LANES), jnp.bfloat16),
            jax.ShapeDtypeStruct((8, LANES), jnp.float32),
        ],
        compiler_params=pltpu.CompilerParams(vmem_limit_bytes=(14 + slots // 2) * MIB),
        name="posterior",
    )(mine, received, own_images, other_images, cos_table, sin_table)


def backproject_kernel(
    weight_ref, own_images, other_images, cos_ref, sin_ref, sums, *, slots, chunk, unroll
):
    width = cos_ref.shape[1]
    tiles = width // LANES
    per_row = 2 * tiles
    chunk_tiles = chunk // LANES
    weights = weight_ref[...]

    def body(step, carry):
        first = LOW_TILES + step * chunk_tiles
        start = pl.multiple_of(first * LANES, LOW_TILES * LANES)
        where = pl.ds(start, chunk)
        imag_where = pl.ds(pl.multiple_of(width + start, LOW_TILES * LANES), chunk)
        real, imag = rotate_back(
            weights, own_images, other_images, cos_ref, sin_ref, where, imag_where, slots
        )
        for k in range(chunk_tiles):
            piece = slice(k * LANES, (k + 1) * LANES)
            sums[pl.ds(first + k, slots, stride=per_row), :] = real[:, piece]
            sums[pl.ds(tiles + first + k, slots, stride=per_row), :] = imag[:, piece]
        return carry

    lax.fori_loop(0, (tiles - LOW_TILES) // chunk_tiles, body, 0, unroll=unroll)


def backproject(weights, own_images, other_images, cos_table, sin_table, slots):
    width = cos_table.shape[1]
    rows = slots * 2 * width // LANES
    return pl.pallas_call(
        functools.partial(
            backproject_kernel,
            slots=slots,
            chunk=LOW_TILES * LANES,
            unroll=7 if slots <= 8 else 1,
        ),
        in_specs=whole_vmem(5),
        out_specs=pl.BlockSpec(memory_space=pltpu.VMEM),
        out_shape=jax.ShapeDtypeStruct((rows, LANES), jnp.float32),
        compiler_params=pltpu.CompilerParams(vmem_limit_bytes=(14 + slots // 2) * MIB),
        cost_estimate=pl.CostEstimate(flops=20000000, bytes_accessed=20000000, transcendentals=0),
        name="backproject",
    )(weights, own_images, other_images, cos_table, sin_table)


def fold_kernel(sums, low_ref, low_received, mass, own, own_mass, *sends, slots):
    per_row = sums.shape[0] // slots
    tiles = per_row // 2
    low_body = low_ref.shape[0]
    total_mass = mass[0:1, :] + joined_mass(low_received[low_body:, :])
    block = split_mass(total_mass)
    own_mass[...] = jnp.broadcast_to(total_mass, own_mass.shape)
    for slot in range(slots):
        target = own if slot < 2 else sends[slot // 2 - 1]
        for comp in range(2):
            low = slice((2 * slot + comp) * LOW_TILES, (2 * slot + comp + 1) * LOW_TILES)
            start = slot * per_row + comp * tiles
            dest = (slot % 2) * per_row + comp * tiles
            value = (low_ref[low, :] + low_received[low, :].astype(jnp.float32)) * 0.5
            value = jnp.concatenate([value, sums[start + LOW_TILES : start + tiles, :]], axis=0)
            target[dest : dest + tiles, :] = value.astype(target.dtype)
    for send in sends:
        send[2 * per_row :, :] = block


def fold(sums, low, low_received, mass, slots):
    rows = 2 * sums.shape[0] // slots
    chips = slots // 2
    return pl.pallas_call(
        functools.partial(fold_kernel, slots=slots),
        in_specs=whole_vmem(4),
        out_specs=whole_vmem(1 + chips),
        out_shape=[
            jax.ShapeDtypeStruct((rows, LANES), jnp.float32),
            jax.ShapeDtypeStruct((8, LANES), jnp.float32),
        ]
        + [jax.ShapeDtypeStruct((rows + MASS_ROWS, LANES), jnp.bfloat16)] * (chips - 1),
        compiler_params=pltpu.CompilerParams(vmem_limit_bytes=(10 + slots // 2) * MIB),
        name="fold",
    )(sums, low, low_received, mass)


def merge_kernel(own, mass, *refs):
    received, (keep, send, mass_out) = refs[:-3], refs[-3:]
    rows = own.shape[0]
    half = rows // 2
    core = own_half()
    total_mass = mass[0:1, :]
    for ref in received:
        total_mass = total_mass + joined_mass(ref[rows:, :])
    mass_out[...] = jnp.broadcast_to(total_mass, mass_out.shape)
    for target, place in ((send, 1 - core), (keep, core)):
        where = pl.ds(pl.multiple_of(place * half, half), half)
        total = own[where, :]
        for ref in received:
            total = total + ref[where, :].astype(jnp.float32)
        target[...] = total.astype(target.dtype)


def merge(own, mass, received):
    rows = own.shape[0] // 2
    return pl.pallas_call(
        merge_kernel,
        in_specs=whole_vmem(2 + len(received)),
        out_specs=whole_vmem(3),
        out_shape=[
            jax.ShapeDtypeStruct((rows, LANES), jnp.float32),
            jax.ShapeDtypeStruct((rows, LANES), jnp.bfloat16),
            jax.ShapeDtypeStruct((8, LANES), jnp.float32),
        ],
        compiler_params=pltpu.CompilerParams(vmem_limit_bytes=16 * MIB),
        name="merge",
    )(own, mass, *received)


def finish_kernel(own, received, mass, out, mass_out, *, scale, mass_scale):
    half = own_half()
    mass_out[...] = mass[0, :CLASSES] * mass_scale
    for step in range(own.shape[0] // BLOCK):
        rows = slice(step * BLOCK, (step + 1) * BLOCK)
        own_rows = pl.ds(pl.multiple_of((2 * step + half) * BLOCK, BLOCK), BLOCK)
        other_rows = pl.ds(pl.multiple_of((2 * step + 1 - half) * BLOCK, BLOCK), BLOCK)
        out[own_rows, :] = own[rows, :] * scale
        out[other_rows, :] = received[rows, :].astype(jnp.float32) * scale


def finish(own, received, mass, scale, mass_scale):
    return pl.pallas_call(
        functools.partial(finish_kernel, scale=scale, mass_scale=mass_scale),
        in_specs=whole_vmem(3),
        out_specs=whole_vmem(2),
        out_shape=[
            jax.ShapeDtypeStruct((2 * own.shape[0], LANES), jnp.float32),
            jax.ShapeDtypeStruct((CLASSES,), jnp.float32),
        ],
        compiler_params=pltpu.CompilerParams(vmem_limit_bytes=16 * MIB),
        name="finish",
    )(own, received, mass)


def local(
    images, noise_precision, assigned_class, class_refs, interp_index, interp_frac, shift_grid
):
    dev_count = lax.axis_size("particle")
    slots = dev_count // 2
    chips = slots // 2
    parts, width = images.shape
    own_row, own_images, other_images = project_row(class_refs, interp_index, interp_frac, images)
    rows = [own_row] + [exchange(own_row, 4 * m) for m in range(1, chips)]
    rows = rows + [exchange(row, 1) for row in rows]
    images_received = exchange(other_images, 1)
    cos_table, sin_table = phase_tables(shift_grid, width // 4)
    mine = correlate(
        own_images,
        images_received,
        noise_precision.reshape(1, parts),
        assigned_class.reshape(1, parts),
        cos_table,
        sin_table,
        rows,
    )
    weights, low, low_send, mass = posterior(
        mine, exchange(mine, 1), own_images, images_received, cos_table, sin_table, slots
    )
    low_received = exchange(low_send, 2)
    sums = backproject(weights, own_images, images_received, cos_table, sin_table, slots)
    folded = fold(sums, low, low_received, mass, slots)
    received = [exchange(send, 4 * m) for m, send in enumerate(folded[2:], start=1)]
    keep, send, mass = merge(folded[0], folded[1], received)
    back, class_mass = finish(
        keep, exchange(send, 1), mass, 1.0 / math.sqrt(parts), CLASSES / (parts * dev_count)
    )
    return back.reshape(1, width), class_mass


def solution(mesh):
    in_specs = (
        P(("groups", "particle"), None),
        P(("groups", "particle")),
        P(("groups", "particle")),
        P("groups", None, None, None),
        P("particle", None),
        P("particle", None),
        P(),
    )
    out_specs = (P(("groups", "particle"), None), P("groups"))
    return jax.shard_map(local, mesh=mesh, in_specs=in_specs, out_specs=out_specs, check_vma=False)
```

```python
import functools
import math

import jax
import jax.numpy as jnp
from jax import lax
from jax.experimental import pallas as pl
from jax.experimental.pallas import tpu as pltpu
from jax.sharding import PartitionSpec as P

KY = 128
BOX = 256
CLASSES = 8
LOWK = 16
LANES = 128
PRIOR_REWARD = 1.0
MASS_ROWS = 16
BLOCK = 8
LOW_TILES = LOWK * KY // LANES // 2
MIB = 1 << 20


def exchange(value, mask):
    pairs = [(source, source ^ mask) for source in range(lax.axis_size("particle"))]
    return lax.ppermute(value, "particle", pairs)


def in_hbm(value):
    return pltpu.with_memory_space_constraint(value, pltpu.HBM)


def whole_vmem(count):
    return [pl.BlockSpec(memory_space=pltpu.VMEM)] * count


def own_half():
    return lax.axis_index("particle") % 2


def tree_select(values, masks):
    for mask in masks:
        values = [
            jnp.where(mask, values[i + 1], values[i]) if i + 1 < len(values) else values[i]
            for i in range(0, len(values), 2)
        ]
    return values[0]


def project_half(table, index_ref, frac_ref, half, blended):
    pixels = index_ref.shape[1]
    highs = table.shape[1]
    groups = table.shape[0] // 16
    stride = 8 * groups
    chunk = BLOCK * LANES
    blocks = pixels // (2 * chunk)

    def body(step, carry):
        where = pl.ds(pl.multiple_of((2 * step + half) * chunk, chunk), chunk)
        index = index_ref[:, where]
        frac = frac_ref[:, where]
        high = index >> 7
        low = index & (LANES - 1)
        group = (low * 147) >> 10
        first = low - 7 * group
        high_ids = lax.broadcasted_iota(jnp.int32, (highs, chunk), 0)
        one_hot = jnp.where(high_ids == high, 1.0, 0.0).astype(jnp.bfloat16)
        rows = jnp.dot(table[...], one_hot, preferred_element_type=jnp.float32)
        group = jnp.broadcast_to(group, (8, chunk))
        masks = [(group & (1 << bit)) != 0 for bit in range((groups - 1).bit_length())]
        ids = lax.broadcasted_iota(jnp.int32, (8, chunk), 0)
        weight = jnp.where(ids == first, 1.0 - frac, jnp.where(ids == first + 1, frac, 0.0))
        for comp in range(2):
            start = comp * stride
            picked = tree_select([rows[start + 8 * g : start + 8 * g + 8] for g in range(groups)], masks)
            value = jnp.sum(picked * weight, axis=0, keepdims=True)
            for k in range(BLOCK):
                row = (comp * blocks + step) * BLOCK + k
                blended[pl.ds(row, 1), :] = value[:, k * LANES : (k + 1) * LANES]
        return carry

    lax.fori_loop(0, blocks, body, 0, unroll=2)


def project_other_kernel(
    table_hbm, index_hbm, frac_hbm, out_ref, table, index_ref, frac_ref,
    table_in, flat, wide, blended, sems
):
    device = lax.axis_index("particle")
    row_count = lax.axis_size("particle") // 2
    half_set = device // 2 % 2
    class_id = (2 * (device // 4) + device % 2) // (row_count // CLASSES)
    copies = [
        pltpu.make_async_copy(
            table_hbm.at[pl.ds(half_set, 1), pl.ds(class_id, 1)], table_in, sems.at[0]
        ),
        pltpu.make_async_copy(index_hbm, index_ref, sems.at[1]),
        pltpu.make_async_copy(frac_hbm, frac_ref, sems.at[2]),
    ]
    for copy in copies:
        copy.start()
    copies[0].wait()
    highs = flat.shape[1]
    groups = table.shape[0] // 16

    def unfold(step, carry):
        piece = table_in[0, 0, :, pl.ds(step * 8 * LANES, 8 * LANES)].astype(jnp.float32)
        for k in range(8):
            for comp in range(2):
                flat[comp, pl.ds(step * 8 + k, 1), :] = piece[comp : comp + 1, k * LANES : (k + 1) * LANES]
        return carry

    lax.fori_loop(0, highs // 8, unfold, 0, unroll=4)
    picked = []
    for comp in range(2):
        turned = flat[comp].T
        wide[0:LANES, :] = turned
        wide[LANES : LANES + 8, :] = pltpu.roll(turned[0:8], highs - 1, 1)
        picked += [wide[7 * g : 7 * g + 8, :] for g in range(groups)]
    for pair in range(groups):
        table[16 * pair : 16 * (pair + 1), :] = jnp.concatenate(
            picked[2 * pair : 2 * pair + 2], axis=0
        ).astype(jnp.bfloat16)
    copies[1].wait()
    copies[2].wait()
    project_half(table, index_ref, frac_ref, 1 - own_half(), blended)
    out_ref[...] = blended[...].astype(jnp.bfloat16)


def project_other(class_refs, interp_index, interp_frac):
    vox = class_refs.shape[3]
    pixels = interp_index.shape[1]
    highs = vox // LANES
    half_rows = pixels // LANES
    groups = -(-LANES // 7)
    return pl.pallas_call(
        project_other_kernel,
        in_specs=[pl.BlockSpec(memory_space=pltpu.HBM)] * 3,
        out_specs=whole_vmem(4),
        out_shape=[
            jax.ShapeDtypeStruct((half_rows, LANES), jnp.bfloat16),
            jax.ShapeDtypeStruct((16 * groups, highs), jnp.bfloat16),
            jax.ShapeDtypeStruct((1, pixels), jnp.int32),
            jax.ShapeDtypeStruct((1, pixels), jnp.float32),
        ],
        scratch_shapes=[
            pltpu.VMEM((1, 1, 2, vox), jnp.bfloat16),
            pltpu.VMEM((2, highs, LANES), jnp.float32),
            pltpu.VMEM((LANES + 8, highs), jnp.float32),
            pltpu.VMEM((half_rows, LANES), jnp.float32),
            pltpu.SemaphoreType.DMA((3,)),
        ],
        compiler_params=pltpu.CompilerParams(vmem_limit_bytes=16 * MIB),
        name="project_other",
    )(*(in_hbm(value) for value in (class_refs, interp_index, interp_frac)))


def project_own_kernel(
    table, index_ref, frac_ref, images_hbm, out_ref, own_images, other_images, blended, sems
):
    pixels = index_ref.shape[1]
    chunk = BLOCK * LANES
    blocks = pixels // (2 * chunk)
    copies = []
    for target, half in ((other_images, 1 - own_half()), (own_images, own_half())):
        for comp in range(2):
            for step in range(blocks):
                source = pl.multiple_of(comp * pixels + (2 * step + half) * chunk, chunk)
                dest = (comp * blocks + step) * chunk
                copies.append(
                    pltpu.make_async_copy(
                        images_hbm.at[:, pl.ds(source, chunk)],
                        target.at[:, pl.ds(dest, chunk)],
                        sems.at[len(copies)],
                    )
                )
    for copy in copies:
        copy.start()
    project_half(table, index_ref, frac_ref, own_half(), blended)
    out_ref[...] = blended[...].astype(jnp.bfloat16)
    for copy in copies:
        copy.wait()


def project_own(table, index, frac, images):
    parts, width = images.shape
    half_rows = index.shape[1] // LANES
    half_images = jax.ShapeDtypeStruct((parts, width // 2), jnp.bfloat16)
    return pl.pallas_call(
        project_own_kernel,
        in_specs=whole_vmem(3) + [pl.BlockSpec(memory_space=pltpu.HBM)],
        out_specs=whole_vmem(3),
        out_shape=[
            jax.ShapeDtypeStruct((half_rows, LANES), jnp.bfloat16),
            half_images,
            half_images,
        ],
        scratch_shapes=[
            pltpu.VMEM((half_rows, LANES), jnp.float32),
            pltpu.SemaphoreType.DMA((2 * width // (2 * BLOCK * LANES),)),
        ],
        compiler_params=pltpu.CompilerParams(vmem_limit_bytes=16 * MIB),
        cost_estimate=pl.CostEstimate(flops=2000000000, bytes_accessed=8000000, transcendentals=0),
        name="project_own",
    )(table, index, frac, in_hbm(images))


def pair_kernel(own, other, out_ref):
    count = own.shape[0]
    core = own_half()
    out_ref[pl.ds(pl.multiple_of(core * count, count), count), :] = own[...]
    out_ref[pl.ds(pl.multiple_of((1 - core) * count, count), count), :] = other[...]


def pair_rows(own, other):
    return pl.pallas_call(
        pair_kernel,
        in_specs=whole_vmem(2),
        out_specs=pl.BlockSpec(memory_space=pltpu.VMEM),
        out_shape=jax.ShapeDtypeStruct((2 * own.shape[0], LANES), own.dtype),
        compiler_params=pltpu.CompilerParams(vmem_limit_bytes=16 * MIB),
        name="pair_rows",
    )(own, other)


def slot_rows(device, slots):
    ids = lax.broadcasted_iota(jnp.int32, (slots, 1), 0)
    return 2 * ((device // 4) ^ (ids // 2)) + ids % 2


def split_mass(mass_row):
    ids = lax.broadcasted_iota(jnp.int32, (MASS_ROWS, LANES), 0)
    upper = mass_row.astype(jnp.bfloat16).astype(jnp.float32)
    lower = mass_row - upper
    return jnp.where(ids == 0, upper, jnp.where(ids == 1, lower, 0.0)).astype(jnp.bfloat16)


def joined_mass(block):
    return jnp.sum(block.astype(jnp.float32), axis=0, keepdims=True)


def table_kernel(shift_ref, cos_ref, sin_ref):
    shifts, width = cos_ref.shape
    grid_x = shift_ref[:, 0:1]
    grid_y = shift_ref[:, 1:2]
    lane = lax.broadcasted_iota(jnp.int32, (shifts, LANES), 1)
    freq_x = (lane // BLOCK) * (2 * BLOCK) + own_half() * BLOCK + lane % BLOCK
    turn_x = (freq_x * grid_x) & (BOX - 1)
    turn_y = ((lane - KY // 2) * grid_y) & (BOX - 1)
    angle_x = turn_x.astype(jnp.float32) * (2.0 * math.pi / BOX)
    angle_y = turn_y.astype(jnp.float32) * (2.0 * math.pi / BOX)
    cos_x, sin_x = jnp.cos(angle_x), jnp.sin(angle_x)
    cos_y, sin_y = jnp.cos(angle_y), jnp.sin(angle_y)
    for j in range(width // LANES):
        where = slice(j * LANES, (j + 1) * LANES)
        cos_j, sin_j = cos_x[:, j : j + 1], sin_x[:, j : j + 1]
        cos_ref[:, where] = cos_j * cos_y - sin_j * sin_y
        sin_ref[:, where] = sin_j * cos_y + cos_j * sin_y


def phase_tables(shift_grid, width):
    shape = jax.ShapeDtypeStruct((shift_grid.shape[0], width), jnp.float32)
    return pl.pallas_call(
        table_kernel,
        in_specs=whole_vmem(1),
        out_specs=whole_vmem(2),
        out_shape=[shape, shape],
        compiler_params=pltpu.CompilerParams(vmem_limit_bytes=16 * MIB),
        cost_estimate=pl.CostEstimate(flops=2000000, bytes_accessed=2000000, transcendentals=0),
        name="phase_tables",
    )(shift_grid)


def correlate_kernel(own_images, other_images, precision_ref, assigned_ref, cos_ref, sin_ref, *refs, chunk):
    pair_refs, (out_ref, proj) = refs[:-2], refs[-2:]
    shifts = cos_ref.shape[0]
    parts = own_images.shape[0]
    slots = 2 * len(pair_refs)
    width = own_images.shape[1] // 2
    tiles = width // LANES
    per_row = 2 * tiles
    for m, ref in enumerate(pair_refs):
        proj[2 * m * per_row : 2 * (m + 1) * per_row, :] = ref[...].astype(jnp.float32)

    chunk_tiles = chunk // LANES
    contract_lanes = (((1,), (1,)), ((), ()))

    def body(step, carry):
        total, power = carry
        first = step * chunk_tiles
        real = jnp.concatenate(
            [proj[pl.ds(first + k, slots, stride=per_row), :] for k in range(chunk_tiles)], axis=1
        )
        imag = jnp.concatenate(
            [proj[pl.ds(tiles + first + k, slots, stride=per_row), :] for k in range(chunk_tiles)],
            axis=1,
        )
        where = pl.ds(pl.multiple_of(step * chunk, chunk), chunk)
        imag_where = pl.ds(pl.multiple_of(width + step * chunk, chunk), chunk)
        reals, imags = [], []
        for s in range(shifts):
            cos_s, sin_s = cos_ref[s : s + 1, where], sin_ref[s : s + 1, where]
            reals.append(real * cos_s - imag * sin_s)
            imags.append(real * sin_s + imag * cos_s)
        turned_real = jnp.concatenate(reals, axis=0).astype(jnp.bfloat16)
        turned_imag = jnp.concatenate(imags, axis=0).astype(jnp.bfloat16)
        image_real = jnp.concatenate([own_images[:, where], other_images[:, where]], axis=0)
        image_imag = jnp.concatenate([own_images[:, imag_where], other_images[:, imag_where]], axis=0)
        total = total + lax.dot_general(
            turned_real, image_real, contract_lanes, preferred_element_type=jnp.float32
        )
        total = total + lax.dot_general(
            turned_imag, image_imag, contract_lanes, preferred_element_type=jnp.float32
        )
        squares = real * real + imag * imag
        for k in range(chunk_tiles):
            power = power + squares[:, k * LANES : (k + 1) * LANES]
        return total, power

    total, power = lax.fori_loop(
        0,
        width // chunk,
        body,
        (
            jnp.zeros((shifts * slots, 2 * parts), jnp.float32),
            jnp.zeros((slots, LANES), jnp.float32),
        ),
    )
    combos = shifts * slots
    out_ref[...] = jnp.zeros_like(out_ref)
    out_ref[0:combos, 0 : 2 * parts] = total
    out_ref[combos : combos + slots, :] = jnp.broadcast_to(
        jnp.sum(power, axis=1, keepdims=True), (slots, LANES)
    )
    out_ref[combos + slots : combos + slots + 1, 0:parts] = precision_ref[...]
    out_ref[combos + slots + 1 : combos + slots + 2, 0:parts] = assigned_ref[...].astype(jnp.float32)


def correlate(own_images, other_images, precision, assigned, cos_table, sin_table, pairs):
    slots = 2 * len(pairs)
    shifts, width = cos_table.shape
    return pl.pallas_call(
        functools.partial(correlate_kernel, chunk=2048),
        in_specs=whole_vmem(6 + len(pairs)),
        out_specs=pl.BlockSpec(memory_space=pltpu.VMEM),
        out_shape=jax.ShapeDtypeStruct((shifts * slots + slots + 8, LANES), jnp.float32),
        scratch_shapes=[pltpu.VMEM((slots * 2 * width // LANES, LANES), jnp.float32)],
        compiler_params=pltpu.CompilerParams(vmem_limit_bytes=(14 + slots // 2) * MIB),
        name="correlate",
    )(own_images, other_images, precision, assigned, cos_table, sin_table, *pairs)


def rotate_back(weights, own_images, other_images, cos_ref, sin_ref, where, imag_where, slots):
    image_real = jnp.concatenate([own_images[:, where], other_images[:, where]], axis=0)
    image_imag = jnp.concatenate([own_images[:, imag_where], other_images[:, imag_where]], axis=0)
    from_real = jnp.dot(weights, image_real, preferred_element_type=jnp.float32)
    from_imag = jnp.dot(weights, image_imag, preferred_element_type=jnp.float32)
    real = imag = None
    for s in range(cos_ref.shape[0]):
        cos_s, sin_s = cos_ref[s : s + 1, where], sin_ref[s : s + 1, where]
        part_real = from_real[s * slots : (s + 1) * slots]
        part_imag = from_imag[s * slots : (s + 1) * slots]
        real_s = part_real * cos_s + part_imag * sin_s
        imag_s = part_imag * cos_s - part_real * sin_s
        real = real_s if real is None else real + real_s
        imag = imag_s if imag is None else imag + imag_s
    return real, imag


def posterior_kernel(mine, received, weight_ref, own_mass, *, slots, shifts, pixels):
    device = lax.axis_index("particle")
    parts = weight_ref.shape[1] // 2
    combos = shifts * slots
    theirs = received[...]
    lane = lax.broadcasted_iota(jnp.int32, theirs.shape, 1)
    swapped = jnp.where(
        lane < parts, pltpu.roll(theirs, LANES - parts, 1), pltpu.roll(theirs, parts, 1)
    )
    joint = mine[...] + swapped
    power = mine[combos : combos + slots, :] + received[combos : combos + slots, :]
    precision = joint[combos + slots : combos + slots + 1]
    assigned = joint[combos + slots + 1 : combos + slots + 2].astype(jnp.int32)
    slot_class = slot_rows(device, slots) // (slots // CLASSES)
    match = (slot_class == assigned).astype(jnp.float32) * PRIOR_REWARD
    likelihood_scale = 1.0 / math.sqrt(2 * pixels)
    logits = [
        precision * (joint[s * slots : (s + 1) * slots] - 0.5 * power) * likelihood_scale + match
        for s in range(shifts)
    ]
    peak = functools.reduce(jnp.maximum, logits)
    peak = jnp.max(peak, axis=0, keepdims=True)
    terms = [jnp.exp(value - peak) for value in logits]
    mass = functools.reduce(jnp.add, terms)
    norm = jnp.sum(mass, axis=0, keepdims=True)
    weights = jnp.concatenate([term / norm for term in terms], axis=0)
    weights = weights[:, 0 : 2 * parts].astype(jnp.bfloat16)
    weight_ref[...] = weights
    counted = lax.broadcasted_iota(jnp.int32, (1, LANES), 1) < 2 * parts
    share = jnp.where(counted, mass / norm * precision, 0.0)
    slot_mass = jnp.sum(share, axis=1, keepdims=True)
    class_lane = lax.broadcasted_iota(jnp.int32, (slots, LANES), 1)
    mass_row = jnp.sum(
        jnp.where(class_lane == slot_class, slot_mass, 0.0), axis=0, keepdims=True
    )
    own_mass[...] = jnp.broadcast_to(mass_row, own_mass.shape)


def posterior(mine, received, slots, shifts, parts, pixels):
    return pl.pallas_call(
        functools.partial(posterior_kernel, slots=slots, shifts=shifts, pixels=pixels),
        in_specs=whole_vmem(2),
        out_specs=whole_vmem(2),
        out_shape=[
            jax.ShapeDtypeStruct((shifts * slots, 2 * parts), jnp.bfloat16),
            jax.ShapeDtypeStruct((8, LANES), jnp.float32),
        ],
        compiler_params=pltpu.CompilerParams(vmem_limit_bytes=(14 + slots // 2) * MIB),
        name="posterior",
    )(mine, received)


def backproject_kernel(
    weight_ref, mass, own_images, other_images, cos_ref, sin_ref, own, *refs, slots, chunk, unroll
):
    sends, sums = refs[:-1], refs[-1]
    width = cos_ref.shape[1]
    tiles = width // LANES
    per_row = 2 * tiles
    chunk_tiles = chunk // LANES
    weights = weight_ref[...]

    def body(step, carry):
        first = step * chunk_tiles
        where = pl.ds(pl.multiple_of(step * chunk, chunk), chunk)
        imag_where = pl.ds(pl.multiple_of(width + step * chunk, chunk), chunk)
        real, imag = rotate_back(
            weights, own_images, other_images, cos_ref, sin_ref, where, imag_where, slots
        )
        for k in range(chunk_tiles):
            piece = slice(k * LANES, (k + 1) * LANES)
            sums[pl.ds(first + k, slots, stride=per_row), :] = real[:, piece]
            sums[pl.ds(tiles + first + k, slots, stride=per_row), :] = imag[:, piece]
        return carry

    lax.fori_loop(0, width // chunk, body, 0, unroll=unroll)
    own[...] = sums[0 : 2 * per_row, :]
    block = split_mass(mass[0:1, :])
    for m, send in enumerate(sends, start=1):
        send[0 : 2 * per_row, :] = sums[2 * m * per_row : 2 * (m + 1) * per_row, :].astype(
            jnp.bfloat16
        )
        send[2 * per_row :, :] = block


def backproject(weights, mass, own_images, other_images, cos_table, sin_table, slots):
    width = cos_table.shape[1]
    rows = 2 * 2 * width // LANES
    chips = slots // 2
    return pl.pallas_call(
        functools.partial(
            backproject_kernel, slots=slots, chunk=BLOCK * LANES, unroll=8 if slots <= 8 else 1
        ),
        in_specs=whole_vmem(6),
        out_specs=whole_vmem(chips),
        out_shape=[jax.ShapeDtypeStruct((rows, LANES), jnp.float32)]
        + [jax.ShapeDtypeStruct((rows + MASS_ROWS, LANES), jnp.bfloat16)] * (chips - 1),
        scratch_shapes=[pltpu.VMEM((chips * rows, LANES), jnp.float32)],
        compiler_params=pltpu.CompilerParams(vmem_limit_bytes=(14 + slots // 2) * MIB),
        name="backproject",
    )(weights, mass, own_images, other_images, cos_table, sin_table)


def low_blocks(tiles):
    return [slice(comp * tiles, comp * tiles + LOW_TILES) for comp in range(2)]


def merge_kernel(own, mass, *refs):
    received, (keep, to_core, to_half, to_both, mass_out) = refs[:-5], refs[-5:]
    rows = own.shape[0]
    half = rows // 2
    core = own_half()
    total_mass = mass[0:1, :]
    for ref in received:
        total_mass = total_mass + joined_mass(ref[rows:, :])
    mass_out[...] = jnp.broadcast_to(total_mass, mass_out.shape)
    for target, low, place in ((to_core, to_both, 1 - core), (keep, to_half, core)):
        where = pl.ds(pl.multiple_of(place * half, half), half)
        total = own[where, :]
        for ref in received:
            total = total + ref[where, :].astype(jnp.float32)
        target[...] = total.astype(target.dtype)
        low[0 : 2 * LOW_TILES, :] = jnp.concatenate(
            [total[block] for block in low_blocks(half // 2)], axis=0
        ).astype(jnp.bfloat16)
    to_half[2 * LOW_TILES :, :] = split_mass(total_mass)


def merge(own, mass, received):
    rows = own.shape[0] // 2
    return pl.pallas_call(
        merge_kernel,
        in_specs=whole_vmem(2 + len(received)),
        out_specs=whole_vmem(5),
        out_shape=[
            jax.ShapeDtypeStruct((rows, LANES), jnp.float32),
            jax.ShapeDtypeStruct((rows, LANES), jnp.bfloat16),
            jax.ShapeDtypeStruct((2 * LOW_TILES + MASS_ROWS, LANES), jnp.bfloat16),
            jax.ShapeDtypeStruct((2 * LOW_TILES, LANES), jnp.bfloat16),
            jax.ShapeDtypeStruct((8, LANES), jnp.float32),
        ],
        compiler_params=pltpu.CompilerParams(vmem_limit_bytes=16 * MIB),
        name="merge",
    )(own, mass, *received)


def finish_kernel(keep, from_core, from_half, from_both, mass, out, mass_out, *, scale, mass_scale):
    core = own_half()
    total_mass = mass[0:1, :] + joined_mass(from_half[2 * LOW_TILES :, :])
    mass_out[...] = total_mass[0, :CLASSES] * mass_scale
    steps = keep.shape[0] // BLOCK
    low_steps = [block.start // BLOCK for block in low_blocks(keep.shape[0] // 2)]
    for own, low, place in ((keep, from_half, core), (from_core, from_both, 1 - core)):
        for step in range(steps):
            value = own[step * BLOCK : (step + 1) * BLOCK, :].astype(jnp.float32)
            if step in low_steps:
                index = low_steps.index(step)
                other = low[index * LOW_TILES : (index + 1) * LOW_TILES, :].astype(jnp.float32)
                value = (value + other) * 0.5
            out[pl.ds(pl.multiple_of((2 * step + place) * BLOCK, BLOCK), BLOCK), :] = value * scale


def finish(keep, from_core, from_half, from_both, mass, scale, mass_scale):
    return pl.pallas_call(
        functools.partial(finish_kernel, scale=scale, mass_scale=mass_scale),
        in_specs=whole_vmem(5),
        out_specs=whole_vmem(2),
        out_shape=[
            jax.ShapeDtypeStruct((2 * keep.shape[0], LANES), jnp.float32),
            jax.ShapeDtypeStruct((CLASSES,), jnp.float32),
        ],
        compiler_params=pltpu.CompilerParams(vmem_limit_bytes=16 * MIB),
        name="finish",
    )(keep, from_core, from_half, from_both, mass)


def local(
    images, noise_precision, assigned_class, class_refs, interp_index, interp_frac, shift_grid
):
    dev_count = lax.axis_size("particle")
    slots = dev_count // 2
    chips = slots // 2
    parts, width = images.shape
    shifts = shift_grid.shape[0]
    other_half, table, index, frac = project_other(class_refs, interp_index, interp_frac)
    from_core = exchange(other_half, 1)
    own, own_images, other_images = project_own(table, index, frac, images)
    pair = pair_rows(own, from_core)
    pair, other_images = lax.optimization_barrier((pair, other_images))
    pairs = [pair] + [exchange(pair, 4 * m) for m in range(1, chips)]
    images_received = exchange(other_images, 1)
    cos_table, sin_table = phase_tables(shift_grid, width // 4)
    mine = correlate(
        own_images,
        images_received,
        noise_precision.reshape(1, parts),
        assigned_class.reshape(1, parts),
        cos_table,
        sin_table,
        pairs,
    )
    weights, mass = posterior(mine, exchange(mine, 1), slots, shifts, parts, width // 2)
    sums = backproject(
        weights, mass, own_images, images_received, cos_table, sin_table, slots
    )
    received = [exchange(send, 4 * m) for m, send in enumerate(sums[1:], start=1)]
    keep, to_core, to_half, to_both, mass = merge(sums[0], mass, received)
    back, class_mass = finish(
        keep,
        exchange(to_core, 1),
        exchange(to_half, 2),
        exchange(to_both, 3),
        mass,
        1.0 / math.sqrt(parts),
        CLASSES / (parts * dev_count),
    )
    return back.reshape(1, width), class_mass


def solution(mesh):
    in_specs = (
        P(("groups", "particle"), None),
        P(("groups", "particle")),
        P(("groups", "particle")),
        P("groups", None, None, None),
        P("particle", None),
        P("particle", None),
        P(),
    )
    out_specs = (P(("groups", "particle"), None), P("groups"))
    return jax.shard_map(local, mesh=mesh, in_specs=in_specs, out_specs=out_specs, check_vma=False)
```

```python
import functools
import math

import jax
import jax.numpy as jnp
from jax import lax
from jax.experimental import pallas as pl
from jax.experimental.pallas import tpu as pltpu
from jax.sharding import PartitionSpec as P

KY = 128
BOX = 256
CLASSES = 8
LOWK = 16
LANES = 128
PRIOR_REWARD = 1.0
MASS_ROWS = 16
BLOCK = 8
PROJECT_CHUNK = 256
LOW_TILES = LOWK * KY // LANES // 2
MIB = 1 << 20


def exchange(value, mask):
    pairs = [(source, source ^ mask) for source in range(lax.axis_size("particle"))]
    return lax.ppermute(value, "particle", pairs)


def in_hbm(value):
    return pltpu.with_memory_space_constraint(value, pltpu.HBM)


def whole_vmem(count):
    return [pl.BlockSpec(memory_space=pltpu.VMEM)] * count


def own_half():
    return lax.axis_index("particle") % 2


def tree_select(values, masks):
    for mask in masks:
        values = [
            jnp.where(mask, values[i + 1], values[i]) if i + 1 < len(values) else values[i]
            for i in range(0, len(values), 2)
        ]
    return values[0]


def project_half(table, index_ref, frac_ref, half, blended):
    pixels = index_ref.shape[1]
    highs = table.shape[1]
    groups = table.shape[0] // 16
    stride = 8 * groups
    chunk = PROJECT_CHUNK
    tiles = chunk // LANES
    per_block = BLOCK // tiles
    half_tiles = pixels // (2 * LANES)

    def body(step, carry):
        block = 2 * (step // per_block) + half
        where = pl.ds(pl.multiple_of((block * per_block + step % per_block) * chunk, chunk), chunk)
        index = index_ref[:, where]
        frac = frac_ref[:, where]
        high = index >> 7
        low = index & (LANES - 1)
        group = (low * 147) >> 10
        first = low - 7 * group
        high_ids = lax.broadcasted_iota(jnp.int32, (highs, chunk), 0)
        one_hot = jnp.where(high_ids == high, 1.0, 0.0).astype(jnp.bfloat16)
        rows = jnp.dot(table[...], one_hot, preferred_element_type=jnp.float32)
        group = jnp.broadcast_to(group, (8, chunk))
        masks = [(group & (1 << bit)) != 0 for bit in range((groups - 1).bit_length())]
        ids = lax.broadcasted_iota(jnp.int32, (8, chunk), 0)
        weight = jnp.where(ids == first, 1.0 - frac, jnp.where(ids == first + 1, frac, 0.0))
        for comp in range(2):
            start = comp * stride
            picked = tree_select([rows[start + 8 * g : start + 8 * g + 8] for g in range(groups)], masks)
            value = jnp.sum(picked * weight, axis=0, keepdims=True)
            for k in range(tiles):
                row = comp * half_tiles + step * tiles + k
                blended[pl.ds(row, 1), :] = value[:, k * LANES : (k + 1) * LANES]
        return carry

    lax.fori_loop(0, half_tiles // tiles, body, 0, unroll=8)


def project_other_kernel(
    table_hbm, index_hbm, frac_hbm, out_ref, table, index_ref, frac_ref,
    table_in, flat, wide, blended, sems
):
    device = lax.axis_index("particle")
    row_count = lax.axis_size("particle") // 2
    half_set = device // 2 % 2
    class_id = (2 * (device // 4) + device % 2) // (row_count // CLASSES)
    copies = [
        pltpu.make_async_copy(
            table_hbm.at[pl.ds(half_set, 1), pl.ds(class_id, 1)], table_in, sems.at[0]
        ),
        pltpu.make_async_copy(index_hbm, index_ref, sems.at[1]),
        pltpu.make_async_copy(frac_hbm, frac_ref, sems.at[2]),
    ]
    for copy in copies:
        copy.start()
    copies[0].wait()
    highs = flat.shape[1]
    groups = table.shape[0] // 16

    def unfold(step, carry):
        piece = table_in[0, 0, :, pl.ds(step * 8 * LANES, 8 * LANES)].astype(jnp.float32)
        for k in range(8):
            for comp in range(2):
                flat[comp, pl.ds(step * 8 + k, 1), :] = piece[comp : comp + 1, k * LANES : (k + 1) * LANES]
        return carry

    lax.fori_loop(0, highs // 8, unfold, 0, unroll=4)
    picked = []
    for comp in range(2):
        turned = flat[comp].T
        wide[0:LANES, :] = turned
        wide[LANES : LANES + 8, :] = pltpu.roll(turned[0:8], highs - 1, 1)
        picked += [wide[7 * g : 7 * g + 8, :] for g in range(groups)]
    for pair in range(groups):
        table[16 * pair : 16 * (pair + 1), :] = jnp.concatenate(
            picked[2 * pair : 2 * pair + 2], axis=0
        ).astype(jnp.bfloat16)
    copies[1].wait()
    copies[2].wait()
    project_half(table, index_ref, frac_ref, 1 - own_half(), blended)
    out_ref[...] = blended[...].astype(jnp.bfloat16)


def project_other(class_refs, interp_index, interp_frac):
    vox = class_refs.shape[3]
    pixels = interp_index.shape[1]
    highs = vox // LANES
    half_rows = pixels // LANES
    groups = -(-LANES // 7)
    return pl.pallas_call(
        project_other_kernel,
        in_specs=[pl.BlockSpec(memory_space=pltpu.HBM)] * 3,
        out_specs=whole_vmem(4),
        out_shape=[
            jax.ShapeDtypeStruct((half_rows, LANES), jnp.bfloat16),
            jax.ShapeDtypeStruct((16 * groups, highs), jnp.bfloat16),
            jax.ShapeDtypeStruct((1, pixels), jnp.int32),
            jax.ShapeDtypeStruct((1, pixels), jnp.float32),
        ],
        scratch_shapes=[
            pltpu.VMEM((1, 1, 2, vox), jnp.bfloat16),
            pltpu.VMEM((2, highs, LANES), jnp.float32),
            pltpu.VMEM((LANES + 8, highs), jnp.float32),
            pltpu.VMEM((half_rows, LANES), jnp.float32),
            pltpu.SemaphoreType.DMA((3,)),
        ],
        compiler_params=pltpu.CompilerParams(vmem_limit_bytes=16 * MIB),
        name="project_other",
    )(*(in_hbm(value) for value in (class_refs, interp_index, interp_frac)))


def project_own_kernel(
    table, index_ref, frac_ref, images_hbm, out_ref, own_images, other_images, blended, sems
):
    pixels = index_ref.shape[1]
    chunk = BLOCK * LANES
    blocks = pixels // (2 * chunk)
    copies = []
    for target, half in ((other_images, 1 - own_half()), (own_images, own_half())):
        for comp in range(2):
            for step in range(blocks):
                source = pl.multiple_of(comp * pixels + (2 * step + half) * chunk, chunk)
                dest = (comp * blocks + step) * chunk
                copies.append(
                    pltpu.make_async_copy(
                        images_hbm.at[:, pl.ds(source, chunk)],
                        target.at[:, pl.ds(dest, chunk)],
                        sems.at[len(copies)],
                    )
                )
    for copy in copies:
        copy.start()
    project_half(table, index_ref, frac_ref, own_half(), blended)
    out_ref[...] = blended[...].astype(jnp.bfloat16)
    for copy in copies:
        copy.wait()


def project_own(table, index, frac, images):
    parts, width = images.shape
    half_rows = index.shape[1] // LANES
    half_images = jax.ShapeDtypeStruct((parts, width // 2), jnp.bfloat16)
    return pl.pallas_call(
        project_own_kernel,
        in_specs=whole_vmem(3) + [pl.BlockSpec(memory_space=pltpu.HBM)],
        out_specs=whole_vmem(3),
        out_shape=[
            jax.ShapeDtypeStruct((half_rows, LANES), jnp.bfloat16),
            half_images,
            half_images,
        ],
        scratch_shapes=[
            pltpu.VMEM((half_rows, LANES), jnp.float32),
            pltpu.SemaphoreType.DMA((2 * width // (2 * BLOCK * LANES),)),
        ],
        compiler_params=pltpu.CompilerParams(vmem_limit_bytes=16 * MIB),
        cost_estimate=pl.CostEstimate(flops=2000000000, bytes_accessed=8000000, transcendentals=0),
        name="project_own",
    )(table, index, frac, in_hbm(images))


def pair_kernel(own, other, out_ref):
    count = own.shape[0]
    core = own_half()
    out_ref[pl.ds(pl.multiple_of(core * count, count), count), :] = own[...]
    out_ref[pl.ds(pl.multiple_of((1 - core) * count, count), count), :] = other[...]


def pair_rows(own, other):
    return pl.pallas_call(
        pair_kernel,
        in_specs=whole_vmem(2),
        out_specs=pl.BlockSpec(memory_space=pltpu.VMEM),
        out_shape=jax.ShapeDtypeStruct((2 * own.shape[0], LANES), own.dtype),
        compiler_params=pltpu.CompilerParams(vmem_limit_bytes=16 * MIB),
        name="pair_rows",
    )(own, other)


def slot_rows(device, slots):
    ids = lax.broadcasted_iota(jnp.int32, (slots, 1), 0)
    return 2 * ((device // 4) ^ (ids // 2)) + ids % 2


def split_mass(mass_row):
    ids = lax.broadcasted_iota(jnp.int32, (MASS_ROWS, LANES), 0)
    upper = mass_row.astype(jnp.bfloat16).astype(jnp.float32)
    lower = mass_row - upper
    return jnp.where(ids == 0, upper, jnp.where(ids == 1, lower, 0.0)).astype(jnp.bfloat16)


def joined_mass(block):
    return jnp.sum(block.astype(jnp.float32), axis=0, keepdims=True)


def table_kernel(shift_ref, cos_ref, sin_ref):
    shifts, width = cos_ref.shape
    grid_x = shift_ref[:, 0:1]
    grid_y = shift_ref[:, 1:2]
    lane = lax.broadcasted_iota(jnp.int32, (shifts, LANES), 1)
    freq_x = (lane // BLOCK) * (2 * BLOCK) + own_half() * BLOCK + lane % BLOCK
    turn_x = (freq_x * grid_x) & (BOX - 1)
    turn_y = ((lane - KY // 2) * grid_y) & (BOX - 1)
    angle_x = turn_x.astype(jnp.float32) * (2.0 * math.pi / BOX)
    angle_y = turn_y.astype(jnp.float32) * (2.0 * math.pi / BOX)
    cos_x, sin_x = jnp.cos(angle_x), jnp.sin(angle_x)
    cos_y, sin_y = jnp.cos(angle_y), jnp.sin(angle_y)
    for j in range(width // LANES):
        where = slice(j * LANES, (j + 1) * LANES)
        cos_j, sin_j = cos_x[:, j : j + 1], sin_x[:, j : j + 1]
        cos_ref[:, where] = cos_j * cos_y - sin_j * sin_y
        sin_ref[:, where] = sin_j * cos_y + cos_j * sin_y


def phase_tables(shift_grid, width):
    shape = jax.ShapeDtypeStruct((shift_grid.shape[0], width), jnp.float32)
    return pl.pallas_call(
        table_kernel,
        in_specs=whole_vmem(1),
        out_specs=whole_vmem(2),
        out_shape=[shape, shape],
        compiler_params=pltpu.CompilerParams(vmem_limit_bytes=16 * MIB),
        cost_estimate=pl.CostEstimate(flops=2000000, bytes_accessed=2000000, transcendentals=0),
        name="phase_tables",
    )(shift_grid)


def correlate_kernel(own_images, other_images, precision_ref, assigned_ref, cos_ref, sin_ref, *refs, chunk):
    pair_refs, (out_ref, proj) = refs[:-2], refs[-2:]
    shifts = cos_ref.shape[0]
    parts = own_images.shape[0]
    slots = 2 * len(pair_refs)
    width = own_images.shape[1] // 2
    tiles = width // LANES
    per_row = 2 * tiles
    for m, ref in enumerate(pair_refs):
        proj[2 * m * per_row : 2 * (m + 1) * per_row, :] = ref[...].astype(jnp.float32)

    chunk_tiles = chunk // LANES
    contract_lanes = (((1,), (1,)), ((), ()))

    def body(step, carry):
        total, power = carry
        first = step * chunk_tiles
        real = jnp.concatenate(
            [proj[pl.ds(first + k, slots, stride=per_row), :] for k in range(chunk_tiles)], axis=1
        )
        imag = jnp.concatenate(
            [proj[pl.ds(tiles + first + k, slots, stride=per_row), :] for k in range(chunk_tiles)],
            axis=1,
        )
        where = pl.ds(pl.multiple_of(step * chunk, chunk), chunk)
        imag_where = pl.ds(pl.multiple_of(width + step * chunk, chunk), chunk)
        reals, imags = [], []
        for s in range(shifts):
            cos_s, sin_s = cos_ref[s : s + 1, where], sin_ref[s : s + 1, where]
            reals.append(real * cos_s - imag * sin_s)
            imags.append(real * sin_s + imag * cos_s)
        turned_real = jnp.concatenate(reals, axis=0).astype(jnp.bfloat16)
        turned_imag = jnp.concatenate(imags, axis=0).astype(jnp.bfloat16)
        image_real = jnp.concatenate([own_images[:, where], other_images[:, where]], axis=0)
        image_imag = jnp.concatenate([own_images[:, imag_where], other_images[:, imag_where]], axis=0)
        total = total + lax.dot_general(
            turned_real, image_real, contract_lanes, preferred_element_type=jnp.float32
        )
        total = total + lax.dot_general(
            turned_imag, image_imag, contract_lanes, preferred_element_type=jnp.float32
        )
        squares = real * real + imag * imag
        for k in range(chunk_tiles):
            power = power + squares[:, k * LANES : (k + 1) * LANES]
        return total, power

    total, power = lax.fori_loop(
        0,
        width // chunk,
        body,
        (
            jnp.zeros((shifts * slots, 2 * parts), jnp.float32),
            jnp.zeros((slots, LANES), jnp.float32),
        ),
    )
    combos = shifts * slots
    out_ref[...] = jnp.zeros_like(out_ref)
    out_ref[0:combos, 0 : 2 * parts] = total
    out_ref[combos : combos + slots, :] = jnp.broadcast_to(
        jnp.sum(power, axis=1, keepdims=True), (slots, LANES)
    )
    out_ref[combos + slots : combos + slots + 1, 0:parts] = precision_ref[...]
    out_ref[combos + slots + 1 : combos + slots + 2, 0:parts] = assigned_ref[...].astype(jnp.float32)


def correlate(own_images, other_images, precision, assigned, cos_table, sin_table, pairs):
    slots = 2 * len(pairs)
    shifts, width = cos_table.shape
    return pl.pallas_call(
        functools.partial(correlate_kernel, chunk=2048),
        in_specs=whole_vmem(6 + len(pairs)),
        out_specs=pl.BlockSpec(memory_space=pltpu.VMEM),
        out_shape=jax.ShapeDtypeStruct((shifts * slots + slots + 8, LANES), jnp.float32),
        scratch_shapes=[pltpu.VMEM((slots * 2 * width // LANES, LANES), jnp.float32)],
        compiler_params=pltpu.CompilerParams(vmem_limit_bytes=(14 + slots // 2) * MIB),
        name="correlate",
    )(own_images, other_images, precision, assigned, cos_table, sin_table, *pairs)


def rotate_back(weights, own_images, other_images, cos_ref, sin_ref, where, imag_where, slots):
    image_real = jnp.concatenate([own_images[:, where], other_images[:, where]], axis=0)
    image_imag = jnp.concatenate([own_images[:, imag_where], other_images[:, imag_where]], axis=0)
    from_real = jnp.dot(weights, image_real, preferred_element_type=jnp.float32)
    from_imag = jnp.dot(weights, image_imag, preferred_element_type=jnp.float32)
    real = imag = None
    for s in range(cos_ref.shape[0]):
        cos_s, sin_s = cos_ref[s : s + 1, where], sin_ref[s : s + 1, where]
        part_real = from_real[s * slots : (s + 1) * slots]
        part_imag = from_imag[s * slots : (s + 1) * slots]
        real_s = part_real * cos_s + part_imag * sin_s
        imag_s = part_imag * cos_s - part_real * sin_s
        real = real_s if real is None else real + real_s
        imag = imag_s if imag is None else imag + imag_s
    return real, imag


def posterior_kernel(
    mine, received, own_images, other_images, cos_ref, sin_ref,
    weight_ref, low_ref, low_send, own_mass, *, slots
):
    device = lax.axis_index("particle")
    shifts, width = cos_ref.shape
    parts = own_images.shape[0]
    combos = shifts * slots
    theirs = received[...]
    lane = lax.broadcasted_iota(jnp.int32, theirs.shape, 1)
    swapped = jnp.where(
        lane < parts, pltpu.roll(theirs, LANES - parts, 1), pltpu.roll(theirs, parts, 1)
    )
    joint = mine[...] + swapped
    power = mine[combos : combos + slots, :] + received[combos : combos + slots, :]
    precision = joint[combos + slots : combos + slots + 1]
    assigned = joint[combos + slots + 1 : combos + slots + 2].astype(jnp.int32)
    slot_class = slot_rows(device, slots) // (slots // CLASSES)
    match = (slot_class == assigned).astype(jnp.float32) * PRIOR_REWARD
    likelihood_scale = 1.0 / math.sqrt(4 * width)
    logits = [
        precision * (joint[s * slots : (s + 1) * slots] - 0.5 * power) * likelihood_scale + match
        for s in range(shifts)
    ]
    peak = functools.reduce(jnp.maximum, logits)
    peak = jnp.max(peak, axis=0, keepdims=True)
    terms = [jnp.exp(value - peak) for value in logits]
    mass = functools.reduce(jnp.add, terms)
    norm = jnp.sum(mass, axis=0, keepdims=True)
    weights = jnp.concatenate([term / norm for term in terms], axis=0)
    weights = weights[:, 0 : 2 * parts].astype(jnp.bfloat16)
    weight_ref[...] = weights
    counted = lax.broadcasted_iota(jnp.int32, (1, LANES), 1) < 2 * parts
    share = jnp.where(counted, mass / norm * precision, 0.0)
    slot_mass = jnp.sum(share, axis=1, keepdims=True)
    class_lane = lax.broadcasted_iota(jnp.int32, (slots, LANES), 1)
    mass_row = jnp.sum(
        jnp.where(class_lane == slot_class, slot_mass, 0.0), axis=0, keepdims=True
    )
    own_mass[...] = jnp.broadcast_to(mass_row, own_mass.shape)

    low = LOW_TILES * LANES
    real, imag = rotate_back(
        weights, own_images, other_images, cos_ref, sin_ref, slice(0, low), slice(width, width + low), slots
    )
    for k in range(LOW_TILES):
        piece = slice(k * LANES, (k + 1) * LANES)
        low_ref[pl.ds(k, slots, stride=2 * LOW_TILES), :] = real[:, piece]
        low_ref[pl.ds(LOW_TILES + k, slots, stride=2 * LOW_TILES), :] = imag[:, piece]
    low_body = low_ref.shape[0]
    low_send[0:low_body, :] = low_ref[...].astype(jnp.bfloat16)
    low_send[low_body:, :] = split_mass(mass_row)


def posterior(mine, received, own_images, other_images, cos_table, sin_table, slots):
    shifts = cos_table.shape[0]
    low = slots * 2 * LOW_TILES
    return pl.pallas_call(
        functools.partial(posterior_kernel, slots=slots),
        in_specs=whole_vmem(6),
        out_specs=whole_vmem(4),
        out_shape=[
            jax.ShapeDtypeStruct((shifts * slots, 2 * own_images.shape[0]), jnp.bfloat16),
            jax.ShapeDtypeStruct((low, LANES), jnp.float32),
            jax.ShapeDtypeStruct((low + MASS_ROWS, LANES), jnp.bfloat16),
            jax.ShapeDtypeStruct((8, LANES), jnp.float32),
        ],
        compiler_params=pltpu.CompilerParams(vmem_limit_bytes=(14 + slots // 2) * MIB),
        name="posterior",
    )(mine, received, own_images, other_images, cos_table, sin_table)


def backproject_kernel(
    weight_ref, own_images, other_images, cos_ref, sin_ref, own, *refs, slots, chunk, unroll
):
    sends, sums = refs[:-1], refs[-1]
    width = cos_ref.shape[1]
    tiles = width // LANES - LOW_TILES
    per_row = 2 * tiles
    chunk_tiles = chunk // LANES
    weights = weight_ref[...]

    def body(step, carry):
        first = step * chunk_tiles
        start = pl.multiple_of((LOW_TILES + first) * LANES, LOW_TILES * LANES)
        where = pl.ds(start, chunk)
        imag_where = pl.ds(pl.multiple_of(width + start, LOW_TILES * LANES), chunk)
        real, imag = rotate_back(
            weights, own_images, other_images, cos_ref, sin_ref, where, imag_where, slots
        )
        for k in range(chunk_tiles):
            piece = slice(k * LANES, (k + 1) * LANES)
            sums[pl.ds(first + k, slots, stride=per_row), :] = real[:, piece]
            sums[pl.ds(tiles + first + k, slots, stride=per_row), :] = imag[:, piece]
        return carry

    lax.fori_loop(0, tiles // chunk_tiles, body, 0, unroll=unroll)
    own[...] = sums[0 : 2 * per_row, :]
    for m, send in enumerate(sends, start=1):
        send[...] = sums[2 * m * per_row : 2 * (m + 1) * per_row, :].astype(jnp.bfloat16)


def backproject(weights, own_images, other_images, cos_table, sin_table, slots):
    width = cos_table.shape[1]
    rows = 2 * 2 * (width // LANES - LOW_TILES)
    chips = slots // 2
    return pl.pallas_call(
        functools.partial(
            backproject_kernel, slots=slots, chunk=LOW_TILES * LANES, unroll=7 if slots <= 8 else 1
        ),
        in_specs=whole_vmem(5),
        out_specs=whole_vmem(chips),
        out_shape=[jax.ShapeDtypeStruct((rows, LANES), jnp.float32)]
        + [jax.ShapeDtypeStruct((rows, LANES), jnp.bfloat16)] * (chips - 1),
        scratch_shapes=[pltpu.VMEM((chips * rows, LANES), jnp.float32)],
        compiler_params=pltpu.CompilerParams(vmem_limit_bytes=(14 + slots // 2) * MIB),
        cost_estimate=pl.CostEstimate(flops=2000000000, bytes_accessed=8000000, transcendentals=0),
        name="backproject",
    )(weights, own_images, other_images, cos_table, sin_table)


def fold_kernel(low_ref, low_received, mass, own, own_mass, *sends):
    rows = own.shape[0]
    low_body = low_ref.shape[0]
    total_mass = mass[0:1, :] + joined_mass(low_received[low_body:, :])
    block = split_mass(total_mass)
    own_mass[...] = jnp.broadcast_to(total_mass, own_mass.shape)
    for m, target in enumerate((own,) + sends):
        part = slice(m * rows, (m + 1) * rows)
        value = (low_ref[part, :] + low_received[part, :].astype(jnp.float32)) * 0.5
        target[0:rows, :] = value.astype(target.dtype)
        if m > 0:
            target[rows:, :] = block


def fold(low, low_received, mass, chips):
    rows = low.shape[0] // chips
    return pl.pallas_call(
        fold_kernel,
        in_specs=whole_vmem(3),
        out_specs=whole_vmem(1 + chips),
        out_shape=[
            jax.ShapeDtypeStruct((rows, LANES), jnp.float32),
            jax.ShapeDtypeStruct((8, LANES), jnp.float32),
        ]
        + [jax.ShapeDtypeStruct((rows + MASS_ROWS, LANES), jnp.bfloat16)] * (chips - 1),
        compiler_params=pltpu.CompilerParams(vmem_limit_bytes=16 * MIB),
        name="fold",
    )(low, low_received, mass)


def merge_kernel(own, own_low, mass, *refs, others):
    received, low_received = refs[:others], refs[others : 2 * others]
    keep, to_core, mass_out = refs[2 * others :]
    core = own_half()
    low_half = own_low.shape[0] // 2
    half = own.shape[0] // 2
    total_mass = mass[0:1, :]
    for ref in low_received:
        total_mass = total_mass + joined_mass(ref[2 * low_half :, :])
    mass_out[...] = jnp.broadcast_to(total_mass, mass_out.shape)
    for target, place in ((to_core, 1 - core), (keep, core)):
        where = pl.ds(pl.multiple_of(place * half, half), half)
        total = own[where, :]
        for ref in received:
            total = total + ref[where, :].astype(jnp.float32)
        where = pl.ds(pl.multiple_of(place * low_half, low_half), low_half)
        low = own_low[where, :]
        for ref in low_received:
            low = low + ref[where, :].astype(jnp.float32)
        target[...] = jnp.concatenate(
            [low[0:LOW_TILES], total[0 : half // 2], low[LOW_TILES:], total[half // 2 :]], axis=0
        ).astype(target.dtype)


def merge(own, own_low, mass, received, low_received):
    rows = (own.shape[0] + own_low.shape[0]) // 2
    return pl.pallas_call(
        functools.partial(merge_kernel, others=len(received)),
        in_specs=whole_vmem(3 + 2 * len(received)),
        out_specs=whole_vmem(3),
        out_shape=[
            jax.ShapeDtypeStruct((rows, LANES), jnp.float32),
            jax.ShapeDtypeStruct((rows, LANES), jnp.bfloat16),
            jax.ShapeDtypeStruct((8, LANES), jnp.float32),
        ],
        compiler_params=pltpu.CompilerParams(vmem_limit_bytes=16 * MIB),
        name="merge",
    )(own, own_low, mass, *received, *low_received)


def finish_kernel(own, received, mass, out, mass_out, *, scale, mass_scale):
    core = own_half()
    mass_out[...] = mass[0, :CLASSES] * mass_scale
    for step in range(own.shape[0] // BLOCK):
        rows = slice(step * BLOCK, (step + 1) * BLOCK)
        own_rows = pl.ds(pl.multiple_of((2 * step + core) * BLOCK, BLOCK), BLOCK)
        other_rows = pl.ds(pl.multiple_of((2 * step + 1 - core) * BLOCK, BLOCK), BLOCK)
        out[own_rows, :] = own[rows, :] * scale
        out[other_rows, :] = received[rows, :].astype(jnp.float32) * scale


def finish(own, received, mass, scale, mass_scale):
    return pl.pallas_call(
        functools.partial(finish_kernel, scale=scale, mass_scale=mass_scale),
        in_specs=whole_vmem(3),
        out_specs=whole_vmem(2),
        out_shape=[
            jax.ShapeDtypeStruct((2 * own.shape[0], LANES), jnp.float32),
            jax.ShapeDtypeStruct((CLASSES,), jnp.float32),
        ],
        compiler_params=pltpu.CompilerParams(vmem_limit_bytes=16 * MIB),
        name="finish",
    )(own, received, mass)


def local(
    images, noise_precision, assigned_class, class_refs, interp_index, interp_frac, shift_grid
):
    dev_count = lax.axis_size("particle")
    slots = dev_count // 2
    chips = slots // 2
    parts, width = images.shape
    other_half, table, index, frac = project_other(class_refs, interp_index, interp_frac)
    from_core = exchange(other_half, 1)
    own, own_images, other_images = project_own(table, index, frac, images)
    pair = pair_rows(own, from_core)
    pair, other_images = lax.optimization_barrier((pair, other_images))
    pairs = [pair] + [exchange(pair, 4 * m) for m in range(1, chips)]
    images_received = exchange(other_images, 1)
    cos_table, sin_table = phase_tables(shift_grid, width // 4)
    mine = correlate(
        own_images,
        images_received,
        noise_precision.reshape(1, parts),
        assigned_class.reshape(1, parts),
        cos_table,
        sin_table,
        pairs,
    )
    weights, low, low_send, mass = posterior(
        mine, exchange(mine, 1), own_images, images_received, cos_table, sin_table, slots
    )
    low_from_half = exchange(low_send, 2)
    sums = backproject(weights, own_images, images_received, cos_table, sin_table, slots)
    received = [exchange(send, 4 * m) for m, send in enumerate(sums[1:], start=1)]
    folded = fold(low, low_from_half, mass, chips)
    low_received = [exchange(send, 4 * m) for m, send in enumerate(folded[2:], start=1)]
    keep, send, mass = merge(sums[0], folded[0], folded[1], received, low_received)
    back, class_mass = finish(
        keep, exchange(send, 1), mass, 1.0 / math.sqrt(parts), CLASSES / (parts * dev_count)
    )
    return back.reshape(1, width), class_mass


def solution(mesh):
    in_specs = (
        P(("groups", "particle"), None),
        P(("groups", "particle")),
        P(("groups", "particle")),
        P("groups", None, None, None),
        P("particle", None),
        P("particle", None),
        P(),
    )
    out_specs = (P(("groups", "particle"), None), P("groups"))
    return jax.shard_map(local, mesh=mesh, in_specs=in_specs, out_specs=out_specs, check_vma=False)
```

```python
import functools
import math

import jax
import jax.numpy as jnp
from jax import lax
from jax.experimental import pallas as pl
from jax.experimental.pallas import tpu as pltpu
from jax.sharding import PartitionSpec as P

KY = 128
BOX = 256
CLASSES = 8
LOWK = 16
LANES = 128
PRIOR_REWARD = 1.0
MASS_ROWS = 16
BLOCK = 8
PROJECT_CHUNK = 256
LOW_TILES = LOWK * KY // LANES // 2
MIB = 1 << 20


def exchange(value, mask):
    pairs = [(source, source ^ mask) for source in range(lax.axis_size("particle"))]
    return lax.ppermute(value, "particle", pairs)


def in_hbm(value):
    return pltpu.with_memory_space_constraint(value, pltpu.HBM)


def whole_vmem(count):
    return [pl.BlockSpec(memory_space=pltpu.VMEM)] * count


def own_half():
    return lax.axis_index("particle") % 2


def tree_select(values, masks):
    for mask in masks:
        values = [
            jnp.where(mask, values[i + 1], values[i]) if i + 1 < len(values) else values[i]
            for i in range(0, len(values), 2)
        ]
    return values[0]


def project_half(table, index_ref, frac_ref, half, blended):
    pixels = index_ref.shape[1]
    highs = table.shape[1]
    groups = table.shape[0] // 16
    stride = 8 * groups
    chunk = PROJECT_CHUNK
    tiles = chunk // LANES
    per_block = BLOCK // tiles
    half_tiles = pixels // (2 * LANES)

    def body(step, carry):
        block = 2 * (step // per_block) + half
        where = pl.ds(pl.multiple_of((block * per_block + step % per_block) * chunk, chunk), chunk)
        index = index_ref[:, where]
        frac = frac_ref[:, where]
        high = index >> 7
        low = index & (LANES - 1)
        group = (low * 147) >> 10
        first = low - 7 * group
        high_ids = lax.broadcasted_iota(jnp.int32, (highs, chunk), 0)
        one_hot = jnp.where(high_ids == high, 1.0, 0.0).astype(jnp.bfloat16)
        rows = jnp.dot(table[...], one_hot, preferred_element_type=jnp.float32)
        group = jnp.broadcast_to(group, (8, chunk))
        masks = [(group & (1 << bit)) != 0 for bit in range((groups - 1).bit_length())]
        ids = lax.broadcasted_iota(jnp.int32, (8, chunk), 0)
        weight = jnp.where(ids == first, 1.0 - frac, jnp.where(ids == first + 1, frac, 0.0))
        for comp in range(2):
            start = comp * stride
            picked = tree_select([rows[start + 8 * g : start + 8 * g + 8] for g in range(groups)], masks)
            value = jnp.sum(picked * weight, axis=0, keepdims=True)
            for k in range(tiles):
                row = comp * half_tiles + step * tiles + k
                blended[pl.ds(row, 1), :] = value[:, k * LANES : (k + 1) * LANES]
        return carry

    lax.fori_loop(0, half_tiles // tiles, body, 0, unroll=8)


def project_other_kernel(
    table_hbm, index_hbm, frac_hbm, out_ref, table, index_ref, frac_ref,
    table_in, flat, wide, blended, sems
):
    device = lax.axis_index("particle")
    row_count = lax.axis_size("particle") // 2
    half_set = device // 2 % 2
    class_id = (2 * (device // 4) + device % 2) // (row_count // CLASSES)
    copies = [
        pltpu.make_async_copy(
            table_hbm.at[pl.ds(half_set, 1), pl.ds(class_id, 1)], table_in, sems.at[0]
        ),
        pltpu.make_async_copy(index_hbm, index_ref, sems.at[1]),
        pltpu.make_async_copy(frac_hbm, frac_ref, sems.at[2]),
    ]
    for copy in copies:
        copy.start()
    copies[0].wait()
    highs = flat.shape[1]
    groups = table.shape[0] // 16

    def unfold(step, carry):
        piece = table_in[0, 0, :, pl.ds(step * 8 * LANES, 8 * LANES)].astype(jnp.float32)
        for k in range(8):
            for comp in range(2):
                flat[comp, pl.ds(step * 8 + k, 1), :] = piece[comp : comp + 1, k * LANES : (k + 1) * LANES]
        return carry

    lax.fori_loop(0, highs // 8, unfold, 0, unroll=4)
    picked = []
    for comp in range(2):
        turned = flat[comp].T
        wide[0:LANES, :] = turned
        wide[LANES : LANES + 8, :] = pltpu.roll(turned[0:8], highs - 1, 1)
        picked += [wide[7 * g : 7 * g + 8, :] for g in range(groups)]
    for pair in range(groups):
        table[16 * pair : 16 * (pair + 1), :] = jnp.concatenate(
            picked[2 * pair : 2 * pair + 2], axis=0
        ).astype(jnp.bfloat16)
    copies[1].wait()
    copies[2].wait()
    project_half(table, index_ref, frac_ref, 1 - own_half(), blended)
    out_ref[...] = blended[...].astype(jnp.bfloat16)


def project_other(class_refs, interp_index, interp_frac):
    vox = class_refs.shape[3]
    pixels = interp_index.shape[1]
    highs = vox // LANES
    half_rows = pixels // LANES
    groups = -(-LANES // 7)
    return pl.pallas_call(
        project_other_kernel,
        in_specs=[pl.BlockSpec(memory_space=pltpu.HBM)] * 3,
        out_specs=whole_vmem(4),
        out_shape=[
            jax.ShapeDtypeStruct((half_rows, LANES), jnp.bfloat16),
            jax.ShapeDtypeStruct((16 * groups, highs), jnp.bfloat16),
            jax.ShapeDtypeStruct((1, pixels), jnp.int32),
            jax.ShapeDtypeStruct((1, pixels), jnp.float32),
        ],
        scratch_shapes=[
            pltpu.VMEM((1, 1, 2, vox), jnp.bfloat16),
            pltpu.VMEM((2, highs, LANES), jnp.float32),
            pltpu.VMEM((LANES + 8, highs), jnp.float32),
            pltpu.VMEM((half_rows, LANES), jnp.float32),
            pltpu.SemaphoreType.DMA((3,)),
        ],
        compiler_params=pltpu.CompilerParams(vmem_limit_bytes=16 * MIB),
        name="project_other",
    )(*(in_hbm(value) for value in (class_refs, interp_index, interp_frac)))


def project_own_kernel(
    table, index_ref, frac_ref, images_hbm, out_ref, own_images, other_images, blended, sems
):
    pixels = index_ref.shape[1]
    chunk = BLOCK * LANES
    blocks = pixels // (2 * chunk)
    copies = []
    for target, half in ((other_images, 1 - own_half()), (own_images, own_half())):
        for comp in range(2):
            for step in range(blocks):
                source = pl.multiple_of(comp * pixels + (2 * step + half) * chunk, chunk)
                dest = (comp * blocks + step) * chunk
                copies.append(
                    pltpu.make_async_copy(
                        images_hbm.at[:, pl.ds(source, chunk)],
                        target.at[:, pl.ds(dest, chunk)],
                        sems.at[len(copies)],
                    )
                )
    for copy in copies:
        copy.start()
    project_half(table, index_ref, frac_ref, own_half(), blended)
    out_ref[...] = blended[...].astype(jnp.bfloat16)
    for copy in copies:
        copy.wait()


def project_own(table, index, frac, images):
    parts, width = images.shape
    half_rows = index.shape[1] // LANES
    half_images = jax.ShapeDtypeStruct((parts, width // 2), jnp.bfloat16)
    return pl.pallas_call(
        project_own_kernel,
        in_specs=whole_vmem(3) + [pl.BlockSpec(memory_space=pltpu.HBM)],
        out_specs=whole_vmem(3),
        out_shape=[
            jax.ShapeDtypeStruct((half_rows, LANES), jnp.bfloat16),
            half_images,
            half_images,
        ],
        scratch_shapes=[
            pltpu.VMEM((half_rows, LANES), jnp.float32),
            pltpu.SemaphoreType.DMA((2 * width // (2 * BLOCK * LANES),)),
        ],
        compiler_params=pltpu.CompilerParams(vmem_limit_bytes=16 * MIB),
        cost_estimate=pl.CostEstimate(flops=2000000000, bytes_accessed=8000000, transcendentals=0),
        name="project_own",
    )(table, index, frac, in_hbm(images))


def pair_kernel(own, other, out_ref):
    count = own.shape[0]
    core = own_half()
    out_ref[pl.ds(pl.multiple_of(core * count, count), count), :] = own[...]
    out_ref[pl.ds(pl.multiple_of((1 - core) * count, count), count), :] = other[...]


def pair_rows(own, other):
    return pl.pallas_call(
        pair_kernel,
        in_specs=whole_vmem(2),
        out_specs=pl.BlockSpec(memory_space=pltpu.VMEM),
        out_shape=jax.ShapeDtypeStruct((2 * own.shape[0], LANES), own.dtype),
        compiler_params=pltpu.CompilerParams(vmem_limit_bytes=16 * MIB),
        name="pair_rows",
    )(own, other)


def chip_order(chips):
    return [0, chips - 1] + list(range(1, chips - 1))


def slot_orientation(device, slot, slots):
    return 2 * ((device // 4) ^ chip_order(slots // 2)[slot // 2]) + slot % 2


def split_mass(mass_row):
    ids = lax.broadcasted_iota(jnp.int32, (MASS_ROWS, LANES), 0)
    upper = mass_row.astype(jnp.bfloat16).astype(jnp.float32)
    lower = mass_row - upper
    return jnp.where(ids == 0, upper, jnp.where(ids == 1, lower, 0.0)).astype(jnp.bfloat16)


def joined_mass(block):
    return jnp.sum(block.astype(jnp.float32), axis=0, keepdims=True)


def table_kernel(shift_ref, cos_ref, sin_ref):
    shifts, width = cos_ref.shape
    grid_x = shift_ref[:, 0:1]
    grid_y = shift_ref[:, 1:2]
    lane = lax.broadcasted_iota(jnp.int32, (shifts, LANES), 1)
    freq_x = (lane // BLOCK) * (2 * BLOCK) + own_half() * BLOCK + lane % BLOCK
    turn_x = (freq_x * grid_x) & (BOX - 1)
    turn_y = ((lane - KY // 2) * grid_y) & (BOX - 1)
    angle_x = turn_x.astype(jnp.float32) * (2.0 * math.pi / BOX)
    angle_y = turn_y.astype(jnp.float32) * (2.0 * math.pi / BOX)
    cos_x, sin_x = jnp.cos(angle_x), jnp.sin(angle_x)
    cos_y, sin_y = jnp.cos(angle_y), jnp.sin(angle_y)
    for j in range(width // LANES):
        where = slice(j * LANES, (j + 1) * LANES)
        cos_j, sin_j = cos_x[:, j : j + 1], sin_x[:, j : j + 1]
        cos_ref[:, where] = cos_j * cos_y - sin_j * sin_y
        sin_ref[:, where] = sin_j * cos_y + cos_j * sin_y


def phase_tables(shift_grid, width):
    shape = jax.ShapeDtypeStruct((shift_grid.shape[0], width), jnp.float32)
    return pl.pallas_call(
        table_kernel,
        in_specs=whole_vmem(1),
        out_specs=whole_vmem(2),
        out_shape=[shape, shape],
        compiler_params=pltpu.CompilerParams(vmem_limit_bytes=16 * MIB),
        cost_estimate=pl.CostEstimate(flops=2000000, bytes_accessed=2000000, transcendentals=0),
        name="phase_tables",
    )(shift_grid)


def correlate_kernel(own_images, other_images, cos_ref, sin_ref, *refs, chunk):
    pair_refs, (out_ref, proj) = refs[:-2], refs[-2:]
    shifts = cos_ref.shape[0]
    parts = own_images.shape[0]
    slots = 2 * len(pair_refs)
    width = own_images.shape[1] // 2
    tiles = width // LANES
    per_row = 2 * tiles
    combos = shifts * slots
    for slot in range(slots):
        place = slice(slot % 2 * per_row, (slot % 2 + 1) * per_row)
        row = pair_refs[slot // 2][place, :].astype(jnp.float32)
        proj[slot * per_row : (slot + 1) * per_row, :] = row
        out_ref[combos + slot : combos + slot + 1, :] = jnp.sum(row * row, axis=0, keepdims=True)

    chunk_tiles = chunk // LANES
    contract_lanes = (((1,), (1,)), ((), ()))

    def body(step, total):
        first = step * chunk_tiles
        where = pl.ds(pl.multiple_of(step * chunk, chunk), chunk)
        imag_where = pl.ds(pl.multiple_of(width + step * chunk, chunk), chunk)
        cos_part, sin_part = cos_ref[:, where], sin_ref[:, where]
        reals, imags = [], []
        for slot in range(slots):
            start = slot * per_row + first
            real = jnp.concatenate(
                [proj[pl.ds(start + k, 1), :] for k in range(chunk_tiles)], axis=1
            )
            imag = jnp.concatenate(
                [proj[pl.ds(start + tiles + k, 1), :] for k in range(chunk_tiles)], axis=1
            )
            reals.append(real * cos_part - imag * sin_part)
            imags.append(real * sin_part + imag * cos_part)
        turned_real = jnp.concatenate(reals, axis=0).astype(jnp.bfloat16)
        turned_imag = jnp.concatenate(imags, axis=0).astype(jnp.bfloat16)
        image_real = jnp.concatenate([own_images[:, where], other_images[:, where]], axis=0)
        image_imag = jnp.concatenate([own_images[:, imag_where], other_images[:, imag_where]], axis=0)
        total = total + lax.dot_general(
            turned_real, image_real, contract_lanes, preferred_element_type=jnp.float32
        )
        return total + lax.dot_general(
            turned_imag, image_imag, contract_lanes, preferred_element_type=jnp.float32
        )

    total = lax.fori_loop(
        0, width // chunk, body, jnp.zeros((combos, 2 * parts), jnp.float32), unroll=2
    )
    out_ref[0:combos, :] = jnp.zeros((combos, LANES), jnp.float32)
    out_ref[0:combos, 0 : 2 * parts] = total


def correlate(own_images, other_images, cos_table, sin_table, pairs):
    slots = 2 * len(pairs)
    shifts, width = cos_table.shape
    return pl.pallas_call(
        functools.partial(correlate_kernel, chunk=2048),
        in_specs=whole_vmem(4 + len(pairs)),
        out_specs=pl.BlockSpec(memory_space=pltpu.VMEM),
        out_shape=jax.ShapeDtypeStruct((shifts * slots + slots, LANES), jnp.float32),
        scratch_shapes=[pltpu.VMEM((slots * 2 * width // LANES, LANES), jnp.float32)],
        compiler_params=pltpu.CompilerParams(vmem_limit_bytes=(14 + slots) * MIB),
        cost_estimate=pl.CostEstimate(flops=1500000000, bytes_accessed=6000000, transcendentals=0),
        name="correlate",
    )(own_images, other_images, cos_table, sin_table, *pairs)


def collect_kernel(near, far, precision_ref, assigned_ref, out_ref, *, combos):
    slots = near.shape[0] - combos
    parts = precision_ref.shape[1]
    for index, ref in enumerate((near, far)):
        out_ref[index * combos : (index + 1) * combos, :] = ref[0:combos, :]
        power = 2 * combos + index * slots
        out_ref[power : power + slots, :] = ref[combos:, :]
    rest = 2 * combos + 2 * slots
    out_ref[rest:, :] = jnp.zeros((8, LANES), jnp.float32)
    out_ref[rest : rest + 1, 0:parts] = precision_ref[...]
    out_ref[rest + 1 : rest + 2, 0:parts] = assigned_ref[...].astype(jnp.float32)


def collect(near, far, precision, assigned, combos):
    rows = 2 * near.shape[0] + 8
    return pl.pallas_call(
        functools.partial(collect_kernel, combos=combos),
        in_specs=whole_vmem(4),
        out_specs=pl.BlockSpec(memory_space=pltpu.VMEM),
        out_shape=jax.ShapeDtypeStruct((rows, LANES), jnp.float32),
        compiler_params=pltpu.CompilerParams(vmem_limit_bytes=16 * MIB),
        name="collect",
    )(near, far, precision, assigned)


def rotate_back(weights, own_images, other_images, cos_ref, sin_ref, where, imag_where, slots):
    image_real = jnp.concatenate([own_images[:, where], other_images[:, where]], axis=0)
    image_imag = jnp.concatenate([own_images[:, imag_where], other_images[:, imag_where]], axis=0)
    from_real = jnp.dot(weights, image_real, preferred_element_type=jnp.float32)
    from_imag = jnp.dot(weights, image_imag, preferred_element_type=jnp.float32)
    real = imag = None
    for s in range(cos_ref.shape[0]):
        cos_s, sin_s = cos_ref[s : s + 1, where], sin_ref[s : s + 1, where]
        part_real = from_real[s * slots : (s + 1) * slots]
        part_imag = from_imag[s * slots : (s + 1) * slots]
        real_s = part_real * cos_s + part_imag * sin_s
        imag_s = part_imag * cos_s - part_real * sin_s
        real = real_s if real is None else real + real_s
        imag = imag_s if imag is None else imag + imag_s
    return real, imag


def posterior_kernel(
    mine, received, own_images, other_images, cos_ref, sin_ref,
    weight_ref, low_ref, low_send, own_mass, ordered, *, slots
):
    device = lax.axis_index("particle")
    shifts, width = cos_ref.shape
    parts = own_images.shape[0]
    combos = shifts * slots
    theirs = received[...]
    lane = lax.broadcasted_iota(jnp.int32, theirs.shape, 1)
    swapped = jnp.where(
        lane < parts, pltpu.roll(theirs, LANES - parts, 1), pltpu.roll(theirs, parts, 1)
    )
    joint = mine[...] + swapped
    power = jnp.sum(
        mine[combos : combos + slots, :] + received[combos : combos + slots, :], axis=1, keepdims=True
    )
    precision = joint[combos + slots : combos + slots + 1]
    assigned = joint[combos + slots + 1 : combos + slots + 2].astype(jnp.int32)
    likelihood_scale = 1.0 / math.sqrt(4 * width)
    classes = [slot_orientation(device, slot, slots) // (slots // CLASSES) for slot in range(slots)]
    logits = []
    for slot in range(slots):
        match = (assigned == classes[slot]).astype(jnp.float32) * PRIOR_REWARD
        part = joint[slot * shifts : (slot + 1) * shifts]
        logits.append(precision * (part - 0.5 * power[slot : slot + 1]) * likelihood_scale + match)
    peak = jnp.max(functools.reduce(jnp.maximum, logits), axis=0, keepdims=True)
    terms = [jnp.exp(value - peak) for value in logits]
    norm = jnp.sum(functools.reduce(jnp.add, terms), axis=0, keepdims=True)
    counted = lax.broadcasted_iota(jnp.int32, (1, LANES), 1) < 2 * parts
    class_lane = lax.broadcasted_iota(jnp.int32, (1, LANES), 1)
    mass_row = jnp.zeros((1, LANES), jnp.float32)
    for slot in range(slots):
        value = terms[slot] / norm
        ordered[slot * shifts : (slot + 1) * shifts, :] = value
        share = jnp.where(counted, jnp.sum(value, axis=0, keepdims=True) * precision, 0.0)
        share = jnp.sum(share, axis=1, keepdims=True)
        mass_row = mass_row + jnp.where(class_lane == classes[slot], share, 0.0)
    weights = jnp.concatenate(
        [ordered[pl.ds(s, slots, stride=shifts), :] for s in range(shifts)], axis=0
    )
    weights = weights[:, 0 : 2 * parts].astype(jnp.bfloat16)
    weight_ref[...] = weights
    own_mass[...] = jnp.broadcast_to(mass_row, own_mass.shape)

    low = LOW_TILES * LANES
    real, imag = rotate_back(
        weights, own_images, other_images, cos_ref, sin_ref, slice(0, low), slice(width, width + low), slots
    )
    for k in range(LOW_TILES):
        piece = slice(k * LANES, (k + 1) * LANES)
        low_ref[pl.ds(k, slots, stride=2 * LOW_TILES), :] = real[:, piece]
        low_ref[pl.ds(LOW_TILES + k, slots, stride=2 * LOW_TILES), :] = imag[:, piece]
    low_body = low_ref.shape[0]
    low_send[0:low_body, :] = low_ref[...].astype(jnp.bfloat16)
    low_send[low_body:, :] = split_mass(mass_row)


def posterior(mine, received, own_images, other_images, cos_table, sin_table, slots):
    shifts = cos_table.shape[0]
    low = slots * 2 * LOW_TILES
    return pl.pallas_call(
        functools.partial(posterior_kernel, slots=slots),
        in_specs=whole_vmem(6),
        out_specs=whole_vmem(4),
        out_shape=[
            jax.ShapeDtypeStruct((shifts * slots, 2 * own_images.shape[0]), jnp.bfloat16),
            jax.ShapeDtypeStruct((low, LANES), jnp.float32),
            jax.ShapeDtypeStruct((low + MASS_ROWS, LANES), jnp.bfloat16),
            jax.ShapeDtypeStruct((8, LANES), jnp.float32),
        ],
        scratch_shapes=[pltpu.VMEM((shifts * slots, LANES), jnp.float32)],
        compiler_params=pltpu.CompilerParams(vmem_limit_bytes=(14 + slots // 2) * MIB),
        name="posterior",
    )(mine, received, own_images, other_images, cos_table, sin_table)


def backproject_kernel(
    weight_ref, own_images, other_images, cos_ref, sin_ref, own, *refs, slots, chunk, unroll
):
    sends, sums = refs[:-1], refs[-1]
    width = cos_ref.shape[1]
    tiles = width // LANES - LOW_TILES
    per_row = 2 * tiles
    chunk_tiles = chunk // LANES
    weights = weight_ref[...]

    def body(step, carry):
        first = step * chunk_tiles
        start = pl.multiple_of((LOW_TILES + first) * LANES, LOW_TILES * LANES)
        where = pl.ds(start, chunk)
        imag_where = pl.ds(pl.multiple_of(width + start, LOW_TILES * LANES), chunk)
        real, imag = rotate_back(
            weights, own_images, other_images, cos_ref, sin_ref, where, imag_where, slots
        )
        for k in range(chunk_tiles):
            piece = slice(k * LANES, (k + 1) * LANES)
            sums[pl.ds(first + k, slots, stride=per_row), :] = real[:, piece]
            sums[pl.ds(tiles + first + k, slots, stride=per_row), :] = imag[:, piece]
        return carry

    lax.fori_loop(0, tiles // chunk_tiles, body, 0, unroll=unroll)
    own[...] = sums[0 : 2 * per_row, :]
    for m, send in enumerate(sends, start=1):
        send[...] = sums[2 * m * per_row : 2 * (m + 1) * per_row, :].astype(jnp.bfloat16)


def backproject(weights, own_images, other_images, cos_table, sin_table, slots):
    width = cos_table.shape[1]
    rows = 2 * 2 * (width // LANES - LOW_TILES)
    chips = slots // 2
    return pl.pallas_call(
        functools.partial(
            backproject_kernel, slots=slots, chunk=LOW_TILES * LANES, unroll=7 if slots <= 8 else 1
        ),
        in_specs=whole_vmem(5),
        out_specs=whole_vmem(chips),
        out_shape=[jax.ShapeDtypeStruct((rows, LANES), jnp.float32)]
        + [jax.ShapeDtypeStruct((rows, LANES), jnp.bfloat16)] * (chips - 1),
        scratch_shapes=[pltpu.VMEM((chips * rows, LANES), jnp.float32)],
        compiler_params=pltpu.CompilerParams(vmem_limit_bytes=(14 + slots // 2) * MIB),
        cost_estimate=pl.CostEstimate(flops=2000000000, bytes_accessed=8000000, transcendentals=0),
        name="backproject",
    )(weights, own_images, other_images, cos_table, sin_table)


def fold_kernel(low_ref, low_received, mass, *refs, chips):
    mains, (own, own_mass), sends = refs[: chips - 1], refs[chips - 1 : chips + 1], refs[chips + 1 :]
    rows = own.shape[0]
    low_body = low_ref.shape[0]
    total_mass = mass[0:1, :] + joined_mass(low_received[low_body:, :])
    block = split_mass(total_mass)
    own_mass[...] = jnp.broadcast_to(total_mass, own_mass.shape)
    for m, target in enumerate((own,) + tuple(sends)):
        part = slice(m * rows, (m + 1) * rows)
        value = (low_ref[part, :] + low_received[part, :].astype(jnp.float32)) * 0.5
        target[0:rows, :] = value.astype(target.dtype)
        if m > 0:
            target[rows : rows + MASS_ROWS, :] = block
            target[rows + MASS_ROWS :, :] = mains[m - 1][...]


def fold(low, low_received, mass, mains):
    chips = len(mains) + 1
    rows = low.shape[0] // chips
    return pl.pallas_call(
        functools.partial(fold_kernel, chips=chips),
        in_specs=whole_vmem(2 + chips),
        out_specs=whole_vmem(1 + chips),
        out_shape=[
            jax.ShapeDtypeStruct((rows, LANES), jnp.float32),
            jax.ShapeDtypeStruct((8, LANES), jnp.float32),
        ]
        + [
            jax.ShapeDtypeStruct((rows + MASS_ROWS + main.shape[0], LANES), jnp.bfloat16)
            for main in mains
        ],
        compiler_params=pltpu.CompilerParams(vmem_limit_bytes=16 * MIB),
        name="fold",
    )(low, low_received, mass, *mains)


def merge_kernel(own, own_low, mass, *refs):
    received, (keep, to_core, mass_out) = refs[:-3], refs[-3:]
    core = own_half()
    low_rows = own_low.shape[0]
    low_half = low_rows // 2
    head = low_rows + MASS_ROWS
    half = own.shape[0] // 2
    total_mass = mass[0:1, :]
    for ref in received:
        total_mass = total_mass + joined_mass(ref[low_rows:head, :])
    mass_out[...] = jnp.broadcast_to(total_mass, mass_out.shape)
    for target, place in ((to_core, 1 - core), (keep, core)):
        start = pl.multiple_of(place * half, half)
        total = own[pl.ds(start, half), :]
        for ref in received:
            total = total + ref[pl.ds(head + start, half), :].astype(jnp.float32)
        where = pl.ds(pl.multiple_of(place * low_half, low_half), low_half)
        low = own_low[where, :]
        for ref in received:
            low = low + ref[where, :].astype(jnp.float32)
        target[...] = jnp.concatenate(
            [low[0:LOW_TILES], total[0 : half // 2], low[LOW_TILES:], total[half // 2 :]], axis=0
        ).astype(target.dtype)


def merge(own, own_low, mass, received):
    rows = (own.shape[0] + own_low.shape[0]) // 2
    return pl.pallas_call(
        merge_kernel,
        in_specs=whole_vmem(3 + len(received)),
        out_specs=whole_vmem(3),
        out_shape=[
            jax.ShapeDtypeStruct((rows, LANES), jnp.float32),
            jax.ShapeDtypeStruct((rows, LANES), jnp.bfloat16),
            jax.ShapeDtypeStruct((8, LANES), jnp.float32),
        ],
        compiler_params=pltpu.CompilerParams(vmem_limit_bytes=16 * MIB),
        name="merge",
    )(own, own_low, mass, *received)


def finish_kernel(own, received, mass, out, mass_out, *, scale, mass_scale):
    core = own_half()
    mass_out[...] = mass[0, :CLASSES] * mass_scale
    for step in range(own.shape[0] // BLOCK):
        rows = slice(step * BLOCK, (step + 1) * BLOCK)
        own_rows = pl.ds(pl.multiple_of((2 * step + core) * BLOCK, BLOCK), BLOCK)
        other_rows = pl.ds(pl.multiple_of((2 * step + 1 - core) * BLOCK, BLOCK), BLOCK)
        out[own_rows, :] = own[rows, :] * scale
        out[other_rows, :] = received[rows, :].astype(jnp.float32) * scale


def finish(own, received, mass, scale, mass_scale):
    return pl.pallas_call(
        functools.partial(finish_kernel, scale=scale, mass_scale=mass_scale),
        in_specs=whole_vmem(3),
        out_specs=whole_vmem(2),
        out_shape=[
            jax.ShapeDtypeStruct((2 * own.shape[0], LANES), jnp.float32),
            jax.ShapeDtypeStruct((CLASSES,), jnp.float32),
        ],
        compiler_params=pltpu.CompilerParams(vmem_limit_bytes=16 * MIB),
        name="finish",
    )(own, received, mass)


def local(
    images, noise_precision, assigned_class, class_refs, interp_index, interp_frac, shift_grid
):
    dev_count = lax.axis_size("particle")
    slots = dev_count // 2
    chips = slots // 2
    parts, width = images.shape
    other_half, table, index, frac = project_other(class_refs, interp_index, interp_frac)
    from_core = exchange(other_half, 1)
    own, own_images, other_images = project_own(table, index, frac, images)
    pair = pair_rows(own, from_core)
    pair, other_images = lax.optimization_barrier((pair, other_images))
    others = chip_order(chips)[1:]
    pairs = [pair] + [exchange(pair, 4 * m) for m in others]
    images_received = exchange(other_images, 1)
    cos_table, sin_table = phase_tables(shift_grid, width // 4)
    near, far = (
        correlate(own_images, images_received, cos_table, sin_table, part)
        for part in (pairs[: chips // 2], pairs[chips // 2 :])
    )
    mine = collect(
        near,
        far,
        noise_precision.reshape(1, parts),
        assigned_class.reshape(1, parts),
        shift_grid.shape[0] * slots // 2,
    )
    weights, low, low_send, mass = posterior(
        mine, exchange(mine, 1), own_images, images_received, cos_table, sin_table, slots
    )
    low_from_half = exchange(low_send, 2)
    sums = backproject(weights, own_images, images_received, cos_table, sin_table, slots)
    folded = fold(low, low_from_half, mass, sums[1:])
    chip_sums = [exchange(send, 4 * m) for m, send in zip(others, folded[2:])]
    keep, send, mass = merge(sums[0], folded[0], folded[1], chip_sums)
    back, class_mass = finish(
        keep, exchange(send, 1), mass, 1.0 / math.sqrt(parts), CLASSES / (parts * dev_count)
    )
    return back.reshape(1, width), class_mass


def solution(mesh):
    in_specs = (
        P(("groups", "particle"), None),
        P(("groups", "particle")),
        P(("groups", "particle")),
        P("groups", None, None, None),
        P("particle", None),
        P("particle", None),
        P(),
    )
    out_specs = (P(("groups", "particle"), None), P("groups"))
    return jax.shard_map(local, mesh=mesh, in_specs=in_specs, out_specs=out_specs, check_vma=False)
```

```python
import functools
import math

import jax
import jax.numpy as jnp
from jax import lax
from jax.experimental import pallas as pl
from jax.experimental.pallas import tpu as pltpu
from jax.sharding import PartitionSpec as P

KY = 128
BOX = 256
CLASSES = 8
LOWK = 16
LANES = 128
PRIOR_REWARD = 1.0
MASS_ROWS = 16
BLOCK = 8
PROJECT_CHUNK = 256
LOW_TILES = LOWK * KY // LANES // 2
MIB = 1 << 20


def exchange(value, mask):
    pairs = [(source, source ^ mask) for source in range(lax.axis_size("particle"))]
    return lax.ppermute(value, "particle", pairs)


def in_hbm(value):
    return pltpu.with_memory_space_constraint(value, pltpu.HBM)


def whole_vmem(count):
    return [pl.BlockSpec(memory_space=pltpu.VMEM)] * count


def own_half():
    return lax.axis_index("particle") % 2


def tree_select(values, masks):
    for mask in masks:
        values = [
            jnp.where(mask, values[i + 1], values[i]) if i + 1 < len(values) else values[i]
            for i in range(0, len(values), 2)
        ]
    return values[0]


def project_half(table, index_ref, frac_ref, half, blended):
    pixels = index_ref.shape[1]
    highs = table.shape[1]
    groups = table.shape[0] // 16
    stride = 8 * groups
    chunk = PROJECT_CHUNK
    tiles = chunk // LANES
    per_block = BLOCK // tiles
    half_tiles = pixels // (2 * LANES)

    def body(step, carry):
        block = 2 * (step // per_block) + half
        where = pl.ds(pl.multiple_of((block * per_block + step % per_block) * chunk, chunk), chunk)
        index = index_ref[:, where]
        frac = frac_ref[:, where]
        high = index >> 7
        low = index & (LANES - 1)
        group = (low * 147) >> 10
        first = low - 7 * group
        high_ids = lax.broadcasted_iota(jnp.int32, (highs, chunk), 0)
        one_hot = jnp.where(high_ids == high, 1.0, 0.0).astype(jnp.bfloat16)
        rows = jnp.dot(table[...], one_hot, preferred_element_type=jnp.float32)
        group = jnp.broadcast_to(group, (8, chunk))
        masks = [(group & (1 << bit)) != 0 for bit in range((groups - 1).bit_length())]
        ids = lax.broadcasted_iota(jnp.int32, (8, chunk), 0)
        weight = jnp.where(ids == first, 1.0 - frac, jnp.where(ids == first + 1, frac, 0.0))
        for comp in range(2):
            start = comp * stride
            picked = tree_select([rows[start + 8 * g : start + 8 * g + 8] for g in range(groups)], masks)
            value = jnp.sum(picked * weight, axis=0, keepdims=True)
            for k in range(tiles):
                row = comp * half_tiles + step * tiles + k
                blended[pl.ds(row, 1), :] = value[:, k * LANES : (k + 1) * LANES]
        return carry

    lax.fori_loop(0, half_tiles // tiles, body, 0, unroll=8)


def project_other_kernel(
    table_hbm, index_hbm, frac_hbm, images_hbm,
    out_ref, table, index_ref, frac_ref, own_images, other_images,
    table_in, flat, wide, blended, sems
):
    device = lax.axis_index("particle")
    row_count = lax.axis_size("particle") // 2
    half_set = device // 2 % 2
    class_id = (2 * (device // 4) + device % 2) // (row_count // CLASSES)
    copies = [
        pltpu.make_async_copy(
            table_hbm.at[pl.ds(half_set, 1), pl.ds(class_id, 1)], table_in, sems.at[0]
        ),
        pltpu.make_async_copy(index_hbm, index_ref, sems.at[1]),
        pltpu.make_async_copy(frac_hbm, frac_ref, sems.at[2]),
    ]
    pixels = index_ref.shape[1]
    chunk = BLOCK * LANES
    blocks = pixels // (2 * chunk)
    for target, half in ((other_images, 1 - own_half()), (own_images, own_half())):
        for comp in range(2):
            for step in range(blocks):
                source = pl.multiple_of(comp * pixels + (2 * step + half) * chunk, chunk)
                dest = (comp * blocks + step) * chunk
                copies.append(
                    pltpu.make_async_copy(
                        images_hbm.at[:, pl.ds(source, chunk)],
                        target.at[:, pl.ds(dest, chunk)],
                        sems.at[len(copies)],
                    )
                )
    for copy in copies[:3]:
        copy.start()
    copies[0].wait()
    for copy in copies[3:]:
        copy.start()
    highs = flat.shape[1]
    groups = table.shape[0] // 16

    def unfold(step, carry):
        piece = table_in[0, 0, :, pl.ds(step * 8 * LANES, 8 * LANES)].astype(jnp.float32)
        for k in range(8):
            for comp in range(2):
                flat[comp, pl.ds(step * 8 + k, 1), :] = piece[comp : comp + 1, k * LANES : (k + 1) * LANES]
        return carry

    lax.fori_loop(0, highs // 8, unfold, 0, unroll=4)
    picked = []
    for comp in range(2):
        turned = flat[comp].T
        wide[0:LANES, :] = turned
        wide[LANES : LANES + 8, :] = pltpu.roll(turned[0:8], highs - 1, 1)
        picked += [wide[7 * g : 7 * g + 8, :] for g in range(groups)]
    for pair in range(groups):
        table[16 * pair : 16 * (pair + 1), :] = jnp.concatenate(
            picked[2 * pair : 2 * pair + 2], axis=0
        ).astype(jnp.bfloat16)
    copies[1].wait()
    copies[2].wait()
    project_half(table, index_ref, frac_ref, 1 - own_half(), blended)
    out_ref[...] = blended[...].astype(jnp.bfloat16)
    for copy in copies[3:]:
        copy.wait()


def project_other(class_refs, interp_index, interp_frac, images):
    vox = class_refs.shape[3]
    pixels = interp_index.shape[1]
    highs = vox // LANES
    half_rows = pixels // LANES
    groups = -(-LANES // 7)
    half_images = jax.ShapeDtypeStruct((images.shape[0], pixels), jnp.bfloat16)
    copies = 3 + 2 * pixels // (BLOCK * LANES)
    return pl.pallas_call(
        project_other_kernel,
        in_specs=[pl.BlockSpec(memory_space=pltpu.HBM)] * 4,
        out_specs=whole_vmem(6),
        out_shape=[
            jax.ShapeDtypeStruct((half_rows, LANES), jnp.bfloat16),
            jax.ShapeDtypeStruct((16 * groups, highs), jnp.bfloat16),
            jax.ShapeDtypeStruct((1, pixels), jnp.int32),
            jax.ShapeDtypeStruct((1, pixels), jnp.float32),
            half_images,
            half_images,
        ],
        scratch_shapes=[
            pltpu.VMEM((1, 1, 2, vox), jnp.bfloat16),
            pltpu.VMEM((2, highs, LANES), jnp.float32),
            pltpu.VMEM((LANES + 8, highs), jnp.float32),
            pltpu.VMEM((half_rows, LANES), jnp.float32),
            pltpu.SemaphoreType.DMA((copies,)),
        ],
        compiler_params=pltpu.CompilerParams(vmem_limit_bytes=16 * MIB),
        name="project_other",
    )(*(in_hbm(value) for value in (class_refs, interp_index, interp_frac, images)))


def project_own_kernel(table, index_ref, frac_ref, out_ref, blended):
    project_half(table, index_ref, frac_ref, own_half(), blended)
    out_ref[...] = blended[...].astype(jnp.bfloat16)


def project_own(table, index, frac):
    half_rows = index.shape[1] // LANES
    return pl.pallas_call(
        project_own_kernel,
        in_specs=whole_vmem(3),
        out_specs=pl.BlockSpec(memory_space=pltpu.VMEM),
        out_shape=jax.ShapeDtypeStruct((half_rows, LANES), jnp.bfloat16),
        scratch_shapes=[pltpu.VMEM((half_rows, LANES), jnp.float32)],
        compiler_params=pltpu.CompilerParams(vmem_limit_bytes=16 * MIB),
        cost_estimate=pl.CostEstimate(flops=2000000000, bytes_accessed=8000000, transcendentals=0),
        name="project_own",
    )(table, index, frac)


def pair_kernel(own, other, out_ref):
    count = own.shape[0]
    core = own_half()
    out_ref[pl.ds(pl.multiple_of(core * count, count), count), :] = own[...]
    out_ref[pl.ds(pl.multiple_of((1 - core) * count, count), count), :] = other[...]


def pair_rows(own, other):
    return pl.pallas_call(
        pair_kernel,
        in_specs=whole_vmem(2),
        out_specs=pl.BlockSpec(memory_space=pltpu.VMEM),
        out_shape=jax.ShapeDtypeStruct((2 * own.shape[0], LANES), own.dtype),
        compiler_params=pltpu.CompilerParams(vmem_limit_bytes=16 * MIB),
        name="pair_rows",
    )(own, other)


def chip_order(chips):
    return [0] + list(range(chips - 1, 0, -1))


def slot_orientation(device, slot, slots):
    return 2 * ((device // 4) ^ chip_order(slots // 2)[slot // 2]) + slot % 2


def split_mass(mass_row):
    ids = lax.broadcasted_iota(jnp.int32, (MASS_ROWS, LANES), 0)
    upper = mass_row.astype(jnp.bfloat16).astype(jnp.float32)
    lower = mass_row - upper
    return jnp.where(ids == 0, upper, jnp.where(ids == 1, lower, 0.0)).astype(jnp.bfloat16)


def joined_mass(block):
    return jnp.sum(block.astype(jnp.float32), axis=0, keepdims=True)


def fill_tables(shift_ref, cos_ref, sin_ref):
    shifts, width = cos_ref.shape
    grid_x = shift_ref[:, 0:1]
    grid_y = shift_ref[:, 1:2]
    lane = lax.broadcasted_iota(jnp.int32, (shifts, LANES), 1)
    freq_x = (lane // BLOCK) * (2 * BLOCK) + own_half() * BLOCK + lane % BLOCK
    turn_x = (freq_x * grid_x) & (BOX - 1)
    turn_y = ((lane - KY // 2) * grid_y) & (BOX - 1)
    angle_x = turn_x.astype(jnp.float32) * (2.0 * math.pi / BOX)
    angle_y = turn_y.astype(jnp.float32) * (2.0 * math.pi / BOX)
    cos_x, sin_x = jnp.cos(angle_x), jnp.sin(angle_x)
    cos_y, sin_y = jnp.cos(angle_y), jnp.sin(angle_y)
    for j in range(width // LANES):
        where = slice(j * LANES, (j + 1) * LANES)
        cos_j, sin_j = cos_x[:, j : j + 1], sin_x[:, j : j + 1]
        cos_ref[:, where] = cos_j * cos_y - sin_j * sin_y
        sin_ref[:, where] = sin_j * cos_y + cos_j * sin_y


def correlate_first_kernel(shift_ref, own_images, other_images, *refs, chunk):
    pair_refs, (out_ref, cos_ref, sin_ref, proj) = refs[:-4], refs[-4:]
    fill_tables(shift_ref, cos_ref, sin_ref)
    correlate_kernel(
        cos_ref, sin_ref, own_images, other_images, *pair_refs, out_ref, proj, chunk=chunk
    )


def correlate_kernel(cos_ref, sin_ref, own_images, other_images, *refs, chunk):
    pair_refs, (out_ref, proj) = refs[:-2], refs[-2:]
    shifts = cos_ref.shape[0]
    parts = own_images.shape[0]
    slots = 2 * len(pair_refs)
    width = own_images.shape[1] // 2
    tiles = width // LANES
    per_row = 2 * tiles
    combos = shifts * slots
    for slot in range(slots):
        place = slice(slot % 2 * per_row, (slot % 2 + 1) * per_row)
        row = pair_refs[slot // 2][place, :].astype(jnp.float32)
        proj[slot * per_row : (slot + 1) * per_row, :] = row
        out_ref[combos + slot : combos + slot + 1, :] = jnp.sum(row * row, axis=0, keepdims=True)

    chunk_tiles = chunk // LANES
    contract_lanes = (((1,), (1,)), ((), ()))

    def body(step, total):
        first = step * chunk_tiles
        where = pl.ds(pl.multiple_of(step * chunk, chunk), chunk)
        imag_where = pl.ds(pl.multiple_of(width + step * chunk, chunk), chunk)
        cos_part, sin_part = cos_ref[:, where], sin_ref[:, where]
        reals, imags = [], []
        for slot in range(slots):
            start = slot * per_row + first
            real = jnp.concatenate(
                [proj[pl.ds(start + k, 1), :] for k in range(chunk_tiles)], axis=1
            )
            imag = jnp.concatenate(
                [proj[pl.ds(start + tiles + k, 1), :] for k in range(chunk_tiles)], axis=1
            )
            reals.append(real * cos_part - imag * sin_part)
            imags.append(real * sin_part + imag * cos_part)
        turned_real = jnp.concatenate(reals, axis=0).astype(jnp.bfloat16)
        turned_imag = jnp.concatenate(imags, axis=0).astype(jnp.bfloat16)
        image_real = jnp.concatenate([own_images[:, where], other_images[:, where]], axis=0)
        image_imag = jnp.concatenate([own_images[:, imag_where], other_images[:, imag_where]], axis=0)
        total = total + lax.dot_general(
            turned_real, image_real, contract_lanes, preferred_element_type=jnp.float32
        )
        return total + lax.dot_general(
            turned_imag, image_imag, contract_lanes, preferred_element_type=jnp.float32
        )

    total = lax.fori_loop(
        0, width // chunk, body, jnp.zeros((combos, 2 * parts), jnp.float32), unroll=2
    )
    out_ref[0:combos, :] = jnp.zeros((combos, LANES), jnp.float32)
    out_ref[0:combos, 0 : 2 * parts] = total


def correlate(own_images, other_images, pairs, shift_grid=None, tables=None):
    slots = 2 * len(pairs)
    width = own_images.shape[1] // 2
    shifts = shift_grid.shape[0] if tables is None else tables[0].shape[0]
    first = (shift_grid,) if tables is None else tuple(tables)
    table = jax.ShapeDtypeStruct((shifts, width), jnp.float32)
    outs = [jax.ShapeDtypeStruct((shifts * slots + slots, LANES), jnp.float32)]
    outs += [table, table] if tables is None else []
    kernel = correlate_first_kernel if tables is None else correlate_kernel
    return pl.pallas_call(
        functools.partial(kernel, chunk=2048),
        in_specs=whole_vmem(len(first) + 2 + len(pairs)),
        out_specs=whole_vmem(len(outs)),
        out_shape=outs,
        scratch_shapes=[pltpu.VMEM((slots * 2 * width // LANES, LANES), jnp.float32)],
        compiler_params=pltpu.CompilerParams(vmem_limit_bytes=(14 + slots) * MIB),
        cost_estimate=pl.CostEstimate(flops=1000000000, bytes_accessed=4000000, transcendentals=0),
        name="correlate",
    )(*first, own_images, other_images, *pairs)


def collect_kernel(*refs, combos):
    parts_refs, (precision_ref, assigned_ref, out_ref) = refs[:-3], refs[-3:]
    count = len(parts_refs)
    slots = parts_refs[0].shape[0] - combos
    parts = precision_ref.shape[1]
    for index, ref in enumerate(parts_refs[::-1]):
        out_ref[index * combos : (index + 1) * combos, :] = ref[0:combos, :]
        power = count * combos + index * slots
        out_ref[power : power + slots, :] = ref[combos:, :]
    rest = count * (combos + slots)
    out_ref[rest:, :] = jnp.zeros((8, LANES), jnp.float32)
    out_ref[rest : rest + 1, 0:parts] = precision_ref[...]
    out_ref[rest + 1 : rest + 2, 0:parts] = assigned_ref[...].astype(jnp.float32)


def collect(passes, precision, assigned, combos):
    rows = len(passes) * passes[0].shape[0] + 8
    return pl.pallas_call(
        functools.partial(collect_kernel, combos=combos),
        in_specs=whole_vmem(2 + len(passes)),
        out_specs=pl.BlockSpec(memory_space=pltpu.VMEM),
        out_shape=jax.ShapeDtypeStruct((rows, LANES), jnp.float32),
        compiler_params=pltpu.CompilerParams(vmem_limit_bytes=16 * MIB),
        name="collect",
    )(*passes[::-1], precision, assigned)


def rotate_back(weights, own_images, other_images, cos_ref, sin_ref, where, imag_where, slots):
    image_real = jnp.concatenate([own_images[:, where], other_images[:, where]], axis=0)
    image_imag = jnp.concatenate([own_images[:, imag_where], other_images[:, imag_where]], axis=0)
    from_real = jnp.dot(weights, image_real, preferred_element_type=jnp.float32)
    from_imag = jnp.dot(weights, image_imag, preferred_element_type=jnp.float32)
    real = imag = None
    for s in range(cos_ref.shape[0]):
        cos_s, sin_s = cos_ref[s : s + 1, where], sin_ref[s : s + 1, where]
        part_real = from_real[s * slots : (s + 1) * slots]
        part_imag = from_imag[s * slots : (s + 1) * slots]
        real_s = part_real * cos_s + part_imag * sin_s
        imag_s = part_imag * cos_s - part_real * sin_s
        real = real_s if real is None else real + real_s
        imag = imag_s if imag is None else imag + imag_s
    return real, imag


def posterior_kernel(
    mine, received, own_images, other_images, cos_ref, sin_ref,
    weight_ref, low_ref, low_send, own_mass, ordered, *, slots
):
    device = lax.axis_index("particle")
    shifts, width = cos_ref.shape
    parts = own_images.shape[0]
    combos = shifts * slots
    theirs = received[...]
    lane = lax.broadcasted_iota(jnp.int32, theirs.shape, 1)
    swapped = jnp.where(
        lane < parts, pltpu.roll(theirs, LANES - parts, 1), pltpu.roll(theirs, parts, 1)
    )
    joint = mine[...] + swapped
    power = jnp.sum(
        mine[combos : combos + slots, :] + received[combos : combos + slots, :], axis=1, keepdims=True
    )
    precision = joint[combos + slots : combos + slots + 1]
    assigned = joint[combos + slots + 1 : combos + slots + 2].astype(jnp.int32)
    likelihood_scale = 1.0 / math.sqrt(4 * width)
    classes = [slot_orientation(device, slot, slots) // (slots // CLASSES) for slot in range(slots)]
    logits = []
    for slot in range(slots):
        match = (assigned == classes[slot]).astype(jnp.float32) * PRIOR_REWARD
        part = joint[slot * shifts : (slot + 1) * shifts]
        logits.append(precision * (part - 0.5 * power[slot : slot + 1]) * likelihood_scale + match)
    peak = jnp.max(functools.reduce(jnp.maximum, logits), axis=0, keepdims=True)
    terms = [jnp.exp(value - peak) for value in logits]
    norm = jnp.sum(functools.reduce(jnp.add, terms), axis=0, keepdims=True)
    counted = lax.broadcasted_iota(jnp.int32, (1, LANES), 1) < 2 * parts
    class_lane = lax.broadcasted_iota(jnp.int32, (1, LANES), 1)
    mass_row = jnp.zeros((1, LANES), jnp.float32)
    for slot in range(slots):
        value = terms[slot] / norm
        ordered[slot * shifts : (slot + 1) * shifts, :] = value
        share = jnp.where(counted, jnp.sum(value, axis=0, keepdims=True) * precision, 0.0)
        share = jnp.sum(share, axis=1, keepdims=True)
        mass_row = mass_row + jnp.where(class_lane == classes[slot], share, 0.0)
    weights = jnp.concatenate(
        [ordered[pl.ds(s, slots, stride=shifts), :] for s in range(shifts)], axis=0
    )
    weights = weights[:, 0 : 2 * parts].astype(jnp.bfloat16)
    weight_ref[...] = weights
    own_mass[...] = jnp.broadcast_to(mass_row, own_mass.shape)

    low = LOW_TILES * LANES
    real, imag = rotate_back(
        weights, own_images, other_images, cos_ref, sin_ref, slice(0, low), slice(width, width + low), slots
    )
    for k in range(LOW_TILES):
        piece = slice(k * LANES, (k + 1) * LANES)
        low_ref[pl.ds(k, slots, stride=2 * LOW_TILES), :] = real[:, piece]
        low_ref[pl.ds(LOW_TILES + k, slots, stride=2 * LOW_TILES), :] = imag[:, piece]
    low_body = low_ref.shape[0]
    low_send[0:low_body, :] = low_ref[...].astype(jnp.bfloat16)
    low_send[low_body:, :] = split_mass(mass_row)


def posterior(mine, received, own_images, other_images, cos_table, sin_table, slots):
    shifts = cos_table.shape[0]
    low = slots * 2 * LOW_TILES
    return pl.pallas_call(
        functools.partial(posterior_kernel, slots=slots),
        in_specs=whole_vmem(6),
        out_specs=whole_vmem(4),
        out_shape=[
            jax.ShapeDtypeStruct((shifts * slots, 2 * own_images.shape[0]), jnp.bfloat16),
            jax.ShapeDtypeStruct((low, LANES), jnp.float32),
            jax.ShapeDtypeStruct((low + MASS_ROWS, LANES), jnp.bfloat16),
            jax.ShapeDtypeStruct((8, LANES), jnp.float32),
        ],
        scratch_shapes=[pltpu.VMEM((shifts * slots, LANES), jnp.float32)],
        compiler_params=pltpu.CompilerParams(vmem_limit_bytes=(14 + slots // 2) * MIB),
        name="posterior",
    )(mine, received, own_images, other_images, cos_table, sin_table)


def backproject_kernel(
    weight_ref, own_images, other_images, cos_ref, sin_ref, own, *refs, slots, chunk, unroll
):
    sends, sums = refs[:-1], refs[-1]
    width = cos_ref.shape[1]
    tiles = width // LANES - LOW_TILES
    per_row = 2 * tiles
    chunk_tiles = chunk // LANES
    weights = weight_ref[...]

    def body(step, carry):
        first = step * chunk_tiles
        start = pl.multiple_of((LOW_TILES + first) * LANES, LOW_TILES * LANES)
        where = pl.ds(start, chunk)
        imag_where = pl.ds(pl.multiple_of(width + start, LOW_TILES * LANES), chunk)
        real, imag = rotate_back(
            weights, own_images, other_images, cos_ref, sin_ref, where, imag_where, slots
        )
        for k in range(chunk_tiles):
            piece = slice(k * LANES, (k + 1) * LANES)
            sums[pl.ds(first + k, slots, stride=per_row), :] = real[:, piece]
            sums[pl.ds(tiles + first + k, slots, stride=per_row), :] = imag[:, piece]
        return carry

    lax.fori_loop(0, tiles // chunk_tiles, body, 0, unroll=unroll)
    own[...] = sums[0 : 2 * per_row, :]
    for m, send in enumerate(sends, start=1):
        send[...] = sums[2 * m * per_row : 2 * (m + 1) * per_row, :].astype(jnp.bfloat16)


def backproject(weights, own_images, other_images, cos_table, sin_table, slots):
    width = cos_table.shape[1]
    rows = 2 * 2 * (width // LANES - LOW_TILES)
    chips = slots // 2
    return pl.pallas_call(
        functools.partial(
            backproject_kernel, slots=slots, chunk=LOW_TILES * LANES, unroll=7 if slots <= 8 else 1
        ),
        in_specs=whole_vmem(5),
        out_specs=whole_vmem(chips),
        out_shape=[jax.ShapeDtypeStruct((rows, LANES), jnp.float32)]
        + [jax.ShapeDtypeStruct((rows, LANES), jnp.bfloat16)] * (chips - 1),
        scratch_shapes=[pltpu.VMEM((chips * rows, LANES), jnp.float32)],
        compiler_params=pltpu.CompilerParams(vmem_limit_bytes=(14 + slots // 2) * MIB),
        cost_estimate=pl.CostEstimate(flops=2000000000, bytes_accessed=8000000, transcendentals=0),
        name="backproject",
    )(weights, own_images, other_images, cos_table, sin_table)


def fold_kernel(low_ref, low_received, mass, *refs, chips):
    mains, (own, own_mass), sends = refs[: chips - 1], refs[chips - 1 : chips + 1], refs[chips + 1 :]
    rows = own.shape[0]
    low_body = low_ref.shape[0]
    total_mass = mass[0:1, :] + joined_mass(low_received[low_body:, :])
    block = split_mass(total_mass)
    own_mass[...] = jnp.broadcast_to(total_mass, own_mass.shape)
    for m, target in enumerate((own,) + tuple(sends)):
        part = slice(m * rows, (m + 1) * rows)
        value = (low_ref[part, :] + low_received[part, :].astype(jnp.float32)) * 0.5
        target[0:rows, :] = value.astype(target.dtype)
        if m > 0:
            target[rows : rows + MASS_ROWS, :] = block
            target[rows + MASS_ROWS :, :] = mains[m - 1][...]


def fold(low, low_received, mass, mains):
    chips = len(mains) + 1
    rows = low.shape[0] // chips
    return pl.pallas_call(
        functools.partial(fold_kernel, chips=chips),
        in_specs=whole_vmem(2 + chips),
        out_specs=whole_vmem(1 + chips),
        out_shape=[
            jax.ShapeDtypeStruct((rows, LANES), jnp.float32),
            jax.ShapeDtypeStruct((8, LANES), jnp.float32),
        ]
        + [
            jax.ShapeDtypeStruct((rows + MASS_ROWS + main.shape[0], LANES), jnp.bfloat16)
            for main in mains
        ],
        compiler_params=pltpu.CompilerParams(vmem_limit_bytes=16 * MIB),
        name="fold",
    )(low, low_received, mass, *mains)


def merge_kernel(own, own_low, mass, *refs):
    received, (keep, to_core, mass_out) = refs[:-3], refs[-3:]
    core = own_half()
    low_rows = own_low.shape[0]
    low_half = low_rows // 2
    head = low_rows + MASS_ROWS
    half = own.shape[0] // 2
    total_mass = mass[0:1, :]
    for ref in received:
        total_mass = total_mass + joined_mass(ref[low_rows:head, :])
    mass_out[...] = jnp.broadcast_to(total_mass, mass_out.shape)
    for target, place in ((to_core, 1 - core), (keep, core)):
        start = pl.multiple_of(place * half, half)
        total = own[pl.ds(start, half), :]
        for ref in received:
            total = total + ref[pl.ds(head + start, half), :].astype(jnp.float32)
        where = pl.ds(pl.multiple_of(place * low_half, low_half), low_half)
        low = own_low[where, :]
        for ref in received:
            low = low + ref[where, :].astype(jnp.float32)
        target[...] = jnp.concatenate(
            [low[0:LOW_TILES], total[0 : half // 2], low[LOW_TILES:], total[half // 2 :]], axis=0
        ).astype(target.dtype)


def merge(own, own_low, mass, received):
    rows = (own.shape[0] + own_low.shape[0]) // 2
    return pl.pallas_call(
        merge_kernel,
        in_specs=whole_vmem(3 + len(received)),
        out_specs=whole_vmem(3),
        out_shape=[
            jax.ShapeDtypeStruct((rows, LANES), jnp.float32),
            jax.ShapeDtypeStruct((rows, LANES), jnp.bfloat16),
            jax.ShapeDtypeStruct((8, LANES), jnp.float32),
        ],
        compiler_params=pltpu.CompilerParams(vmem_limit_bytes=16 * MIB),
        name="merge",
    )(own, own_low, mass, *received)


def finish_kernel(own, received, mass, out, mass_out, *, scale, mass_scale):
    core = own_half()
    mass_out[...] = mass[0, :CLASSES] * mass_scale
    for step in range(own.shape[0] // BLOCK):
        rows = slice(step * BLOCK, (step + 1) * BLOCK)
        own_rows = pl.ds(pl.multiple_of((2 * step + core) * BLOCK, BLOCK), BLOCK)
        other_rows = pl.ds(pl.multiple_of((2 * step + 1 - core) * BLOCK, BLOCK), BLOCK)
        out[own_rows, :] = own[rows, :] * scale
        out[other_rows, :] = received[rows, :].astype(jnp.float32) * scale


def finish(own, received, mass, scale, mass_scale):
    return pl.pallas_call(
        functools.partial(finish_kernel, scale=scale, mass_scale=mass_scale),
        in_specs=whole_vmem(3),
        out_specs=whole_vmem(2),
        out_shape=[
            jax.ShapeDtypeStruct((2 * own.shape[0], LANES), jnp.float32),
            jax.ShapeDtypeStruct((CLASSES,), jnp.float32),
        ],
        compiler_params=pltpu.CompilerParams(vmem_limit_bytes=16 * MIB),
        name="finish",
    )(own, received, mass)


def local(
    images, noise_precision, assigned_class, class_refs, interp_index, interp_frac, shift_grid
):
    dev_count = lax.axis_size("particle")
    slots = dev_count // 2
    chips = slots // 2
    parts, width = images.shape
    other_half, table, index, frac, own_images, other_images = project_other(
        class_refs, interp_index, interp_frac, images
    )
    from_core = exchange(other_half, 1)
    images_received = exchange(other_images, 1)
    pair = pair_rows(project_own(table, index, frac), from_core)
    others = chip_order(chips)[1:]
    pairs = [pair] + [exchange(pair, 4 * m) for m in others]
    group = chips // 4
    first, cos_table, sin_table = correlate(
        own_images, images_received, pairs[:group], shift_grid=shift_grid
    )
    passes = [first]
    for start in range(group, chips, group):
        passes += correlate(
            own_images,
            images_received,
            pairs[start : start + group],
            tables=(cos_table, sin_table),
        )
    mine = collect(
        passes,
        noise_precision.reshape(1, parts),
        assigned_class.reshape(1, parts),
        shift_grid.shape[0] * 2 * group,
    )
    weights, low, low_send, mass = posterior(
        mine, exchange(mine, 1), own_images, images_received, cos_table, sin_table, slots
    )
    low_from_half = exchange(low_send, 2)
    sums = backproject(weights, own_images, images_received, cos_table, sin_table, slots)
    folded = fold(low, low_from_half, mass, sums[1:])
    chip_sums = [exchange(send, 4 * m) for m, send in zip(others, folded[2:])]
    keep, send, mass = merge(sums[0], folded[0], folded[1], chip_sums)
    back, class_mass = finish(
        keep, exchange(send, 1), mass, 1.0 / math.sqrt(parts), CLASSES / (parts * dev_count)
    )
    return back.reshape(1, width), class_mass


def solution(mesh):
    in_specs = (
        P(("groups", "particle"), None),
        P(("groups", "particle")),
        P(("groups", "particle")),
        P("groups", None, None, None),
        P("particle", None),
        P("particle", None),
        P(),
    )
    out_specs = (P(("groups", "particle"), None), P("groups"))
    return jax.shard_map(local, mesh=mesh, in_specs=in_specs, out_specs=out_specs, check_vma=False)
```

```python
import functools
import math

import jax
import jax.numpy as jnp
from jax import lax
from jax.experimental import pallas as pl
from jax.experimental.pallas import tpu as pltpu
from jax.sharding import PartitionSpec as P

KY = 128
BOX = 256
CLASSES = 8
LOWK = 16
LANES = 128
PRIOR_REWARD = 1.0
MASS_ROWS = 16
BLOCK = 8
PROJECT_CHUNK = 256
LOW_TILES = LOWK * KY // LANES // 2
MIB = 1 << 20


def exchange(value, mask):
    pairs = [(source, source ^ mask) for source in range(lax.axis_size("particle"))]
    return lax.ppermute(value, "particle", pairs)


def in_hbm(value):
    return pltpu.with_memory_space_constraint(value, pltpu.HBM)


def whole_vmem(count):
    return [pl.BlockSpec(memory_space=pltpu.VMEM)] * count


def own_half():
    return lax.axis_index("particle") % 2


def tree_select(values, masks):
    for mask in masks:
        values = [
            jnp.where(mask, values[i + 1], values[i]) if i + 1 < len(values) else values[i]
            for i in range(0, len(values), 2)
        ]
    return values[0]


def project_half(table, index_ref, frac_ref, half, blended):
    pixels = index_ref.shape[1]
    highs = table.shape[1]
    groups = table.shape[0] // 16
    stride = 8 * groups
    chunk = PROJECT_CHUNK
    tiles = chunk // LANES
    per_block = BLOCK // tiles
    half_tiles = pixels // (2 * LANES)

    def body(step, carry):
        block = 2 * (step // per_block) + half
        where = pl.ds(pl.multiple_of((block * per_block + step % per_block) * chunk, chunk), chunk)
        index = index_ref[:, where]
        frac = frac_ref[:, where]
        high = index >> 7
        low = index & (LANES - 1)
        group = (low * 147) >> 10
        first = low - 7 * group
        high_ids = lax.broadcasted_iota(jnp.int32, (highs, chunk), 0)
        one_hot = jnp.where(high_ids == high, 1.0, 0.0).astype(jnp.bfloat16)
        rows = jnp.dot(table[...], one_hot, preferred_element_type=jnp.float32)
        group = jnp.broadcast_to(group, (8, chunk))
        masks = [(group & (1 << bit)) != 0 for bit in range((groups - 1).bit_length())]
        ids = lax.broadcasted_iota(jnp.int32, (8, chunk), 0)
        weight = jnp.where(ids == first, 1.0 - frac, jnp.where(ids == first + 1, frac, 0.0))
        for comp in range(2):
            start = comp * stride
            picked = tree_select([rows[start + 8 * g : start + 8 * g + 8] for g in range(groups)], masks)
            value = jnp.sum(picked * weight, axis=0, keepdims=True)
            for k in range(tiles):
                row = comp * half_tiles + step * tiles + k
                blended[pl.ds(row, 1), :] = value[:, k * LANES : (k + 1) * LANES]
        return carry

    lax.fori_loop(0, half_tiles // tiles, body, 0, unroll=8)


def project_other_kernel(
    table_hbm, index_hbm, frac_hbm, images_hbm,
    out_ref, table, index_ref, frac_ref, own_images, other_images,
    table_in, flat, wide, blended, sems
):
    device = lax.axis_index("particle")
    row_count = lax.axis_size("particle") // 2
    half_set = device // 2 % 2
    class_id = (2 * (device // 4) + device % 2) // (row_count // CLASSES)
    copies = [
        pltpu.make_async_copy(
            table_hbm.at[pl.ds(half_set, 1), pl.ds(class_id, 1)], table_in, sems.at[0]
        ),
        pltpu.make_async_copy(index_hbm, index_ref, sems.at[1]),
        pltpu.make_async_copy(frac_hbm, frac_ref, sems.at[2]),
    ]
    pixels = index_ref.shape[1]
    chunk = BLOCK * LANES
    blocks = pixels // (2 * chunk)
    for target, half in ((other_images, 1 - own_half()), (own_images, own_half())):
        for comp in range(2):
            for step in range(blocks + 1):
                block = 2 * step + half if step < blocks else 1 - half
                source = pl.multiple_of(comp * pixels + block * chunk, chunk)
                dest = (comp * (blocks + 1) + step) * chunk
                copies.append(
                    pltpu.make_async_copy(
                        images_hbm.at[:, pl.ds(source, chunk)],
                        target.at[:, pl.ds(dest, chunk)],
                        sems.at[len(copies)],
                    )
                )
    for copy in copies[:3]:
        copy.start()
    copies[0].wait()
    for copy in copies[3:]:
        copy.start()
    highs = flat.shape[1]
    groups = table.shape[0] // 16

    def unfold(step, carry):
        piece = table_in[0, 0, :, pl.ds(step * 8 * LANES, 8 * LANES)].astype(jnp.float32)
        for k in range(8):
            for comp in range(2):
                flat[comp, pl.ds(step * 8 + k, 1), :] = piece[comp : comp + 1, k * LANES : (k + 1) * LANES]
        return carry

    lax.fori_loop(0, highs // 8, unfold, 0, unroll=4)
    picked = []
    for comp in range(2):
        turned = flat[comp].T
        wide[0:LANES, :] = turned
        wide[LANES : LANES + 8, :] = pltpu.roll(turned[0:8], highs - 1, 1)
        picked += [wide[7 * g : 7 * g + 8, :] for g in range(groups)]
    for pair in range(groups):
        table[16 * pair : 16 * (pair + 1), :] = jnp.concatenate(
            picked[2 * pair : 2 * pair + 2], axis=0
        ).astype(jnp.bfloat16)
    copies[1].wait()
    copies[2].wait()
    project_half(table, index_ref, frac_ref, 1 - own_half(), blended)
    out_ref[...] = blended[...].astype(jnp.bfloat16)
    for copy in copies[3:]:
        copy.wait()


def project_other(class_refs, interp_index, interp_frac, images):
    vox = class_refs.shape[3]
    pixels = interp_index.shape[1]
    highs = vox // LANES
    half_rows = pixels // LANES
    groups = -(-LANES // 7)
    half_images = jax.ShapeDtypeStruct(
        (images.shape[0], pixels + 2 * LOW_TILES * LANES), jnp.bfloat16
    )
    copies = 3 + 2 * half_images.shape[1] // (BLOCK * LANES)
    return pl.pallas_call(
        project_other_kernel,
        in_specs=[pl.BlockSpec(memory_space=pltpu.HBM)] * 4,
        out_specs=whole_vmem(6),
        out_shape=[
            jax.ShapeDtypeStruct((half_rows, LANES), jnp.bfloat16),
            jax.ShapeDtypeStruct((16 * groups, highs), jnp.bfloat16),
            jax.ShapeDtypeStruct((1, pixels), jnp.int32),
            jax.ShapeDtypeStruct((1, pixels), jnp.float32),
            half_images,
            half_images,
        ],
        scratch_shapes=[
            pltpu.VMEM((1, 1, 2, vox), jnp.bfloat16),
            pltpu.VMEM((2, highs, LANES), jnp.float32),
            pltpu.VMEM((LANES + 8, highs), jnp.float32),
            pltpu.VMEM((half_rows, LANES), jnp.float32),
            pltpu.SemaphoreType.DMA((copies,)),
        ],
        compiler_params=pltpu.CompilerParams(vmem_limit_bytes=16 * MIB),
        name="project_other",
    )(*(in_hbm(value) for value in (class_refs, interp_index, interp_frac, images)))


def project_own_kernel(table, index_ref, frac_ref, out_ref, blended):
    project_half(table, index_ref, frac_ref, own_half(), blended)
    out_ref[...] = blended[...].astype(jnp.bfloat16)


def project_own(table, index, frac):
    half_rows = index.shape[1] // LANES
    return pl.pallas_call(
        project_own_kernel,
        in_specs=whole_vmem(3),
        out_specs=pl.BlockSpec(memory_space=pltpu.VMEM),
        out_shape=jax.ShapeDtypeStruct((half_rows, LANES), jnp.bfloat16),
        scratch_shapes=[pltpu.VMEM((half_rows, LANES), jnp.float32)],
        compiler_params=pltpu.CompilerParams(vmem_limit_bytes=16 * MIB),
        cost_estimate=pl.CostEstimate(flops=2000000000, bytes_accessed=8000000, transcendentals=0),
        name="project_own",
    )(table, index, frac)


def pair_kernel(own, other, out_ref):
    count = own.shape[0]
    core = own_half()
    out_ref[pl.ds(pl.multiple_of(core * count, count), count), :] = own[...]
    out_ref[pl.ds(pl.multiple_of((1 - core) * count, count), count), :] = other[...]


def pair_rows(own, other):
    return pl.pallas_call(
        pair_kernel,
        in_specs=whole_vmem(2),
        out_specs=pl.BlockSpec(memory_space=pltpu.VMEM),
        out_shape=jax.ShapeDtypeStruct((2 * own.shape[0], LANES), own.dtype),
        compiler_params=pltpu.CompilerParams(vmem_limit_bytes=16 * MIB),
        name="pair_rows",
    )(own, other)


def chip_order(chips):
    return [0] + list(range(chips - 1, 0, -1))


def slot_orientation(device, slot, slots):
    return 2 * ((device // 4) ^ chip_order(slots // 2)[slot // 2]) + slot % 2


def split_mass(mass_row):
    ids = lax.broadcasted_iota(jnp.int32, (MASS_ROWS, LANES), 0)
    upper = mass_row.astype(jnp.bfloat16).astype(jnp.float32)
    lower = mass_row - upper
    return jnp.where(ids == 0, upper, jnp.where(ids == 1, lower, 0.0)).astype(jnp.bfloat16)


def joined_mass(block):
    return jnp.sum(block.astype(jnp.float32), axis=0, keepdims=True)


def fill_tables(shift_ref, cos_ref, sin_ref):
    shifts, width = cos_ref.shape
    grid_x = shift_ref[:, 0:1]
    grid_y = shift_ref[:, 1:2]
    lane = lax.broadcasted_iota(jnp.int32, (shifts, LANES), 1)
    main = width // LANES - LOW_TILES
    freq_x = (lane // BLOCK) * (2 * BLOCK) + own_half() * BLOCK + lane % BLOCK
    freq_x = jnp.where(lane < main, freq_x, (1 - own_half()) * BLOCK + lane - main)
    turn_x = (freq_x * grid_x) & (BOX - 1)
    turn_y = ((lane - KY // 2) * grid_y) & (BOX - 1)
    angle_x = turn_x.astype(jnp.float32) * (2.0 * math.pi / BOX)
    angle_y = turn_y.astype(jnp.float32) * (2.0 * math.pi / BOX)
    cos_x, sin_x = jnp.cos(angle_x), jnp.sin(angle_x)
    cos_y, sin_y = jnp.cos(angle_y), jnp.sin(angle_y)
    for j in range(width // LANES):
        where = slice(j * LANES, (j + 1) * LANES)
        cos_j, sin_j = cos_x[:, j : j + 1], sin_x[:, j : j + 1]
        cos_ref[:, where] = cos_j * cos_y - sin_j * sin_y
        sin_ref[:, where] = sin_j * cos_y + cos_j * sin_y


def correlate_first_kernel(shift_ref, own_images, other_images, *refs, chunk):
    pair_refs, (out_ref, cos_ref, sin_ref, proj) = refs[:-4], refs[-4:]
    fill_tables(shift_ref, cos_ref, sin_ref)
    correlate_kernel(
        cos_ref, sin_ref, own_images, other_images, *pair_refs, out_ref, proj, chunk=chunk
    )


def correlate_kernel(cos_ref, sin_ref, own_images, other_images, *refs, chunk):
    pair_refs, (out_ref, proj) = refs[:-2], refs[-2:]
    shifts = cos_ref.shape[0]
    parts = own_images.shape[0]
    slots = 2 * len(pair_refs)
    full = own_images.shape[1] // 2
    width = full - LOW_TILES * LANES
    tiles = width // LANES
    per_row = 2 * tiles
    combos = shifts * slots
    for slot in range(slots):
        place = slice(slot % 2 * per_row, (slot % 2 + 1) * per_row)
        row = pair_refs[slot // 2][place, :].astype(jnp.float32)
        proj[slot * per_row : (slot + 1) * per_row, :] = row
        out_ref[combos + slot : combos + slot + 1, :] = jnp.sum(row * row, axis=0, keepdims=True)

    chunk_tiles = chunk // LANES
    contract_lanes = (((1,), (1,)), ((), ()))

    def body(step, total):
        first = step * chunk_tiles
        where = pl.ds(pl.multiple_of(step * chunk, chunk), chunk)
        imag_where = pl.ds(pl.multiple_of(full + step * chunk, LOW_TILES * LANES), chunk)
        cos_part, sin_part = cos_ref[:, where], sin_ref[:, where]
        reals, imags = [], []
        for slot in range(slots):
            start = slot * per_row + first
            real = jnp.concatenate(
                [proj[pl.ds(start + k, 1), :] for k in range(chunk_tiles)], axis=1
            )
            imag = jnp.concatenate(
                [proj[pl.ds(start + tiles + k, 1), :] for k in range(chunk_tiles)], axis=1
            )
            reals.append(real * cos_part - imag * sin_part)
            imags.append(real * sin_part + imag * cos_part)
        turned_real = jnp.concatenate(reals, axis=0).astype(jnp.bfloat16)
        turned_imag = jnp.concatenate(imags, axis=0).astype(jnp.bfloat16)
        image_real = jnp.concatenate([own_images[:, where], other_images[:, where]], axis=0)
        image_imag = jnp.concatenate([own_images[:, imag_where], other_images[:, imag_where]], axis=0)
        total = total + lax.dot_general(
            turned_real, image_real, contract_lanes, preferred_element_type=jnp.float32
        )
        return total + lax.dot_general(
            turned_imag, image_imag, contract_lanes, preferred_element_type=jnp.float32
        )

    total = lax.fori_loop(
        0, width // chunk, body, jnp.zeros((combos, 2 * parts), jnp.float32), unroll=2
    )
    out_ref[0:combos, :] = jnp.zeros((combos, LANES), jnp.float32)
    out_ref[0:combos, 0 : 2 * parts] = total


def correlate(own_images, other_images, pairs, shift_grid=None, tables=None):
    slots = 2 * len(pairs)
    width = own_images.shape[1] // 2 - LOW_TILES * LANES
    shifts = shift_grid.shape[0] if tables is None else tables[0].shape[0]
    first = (shift_grid,) if tables is None else tuple(tables)
    table = jax.ShapeDtypeStruct((shifts, width + LOW_TILES * LANES), jnp.float32)
    outs = [jax.ShapeDtypeStruct((shifts * slots + slots, LANES), jnp.float32)]
    outs += [table, table] if tables is None else []
    kernel = correlate_first_kernel if tables is None else correlate_kernel
    return pl.pallas_call(
        functools.partial(kernel, chunk=2048),
        in_specs=whole_vmem(len(first) + 2 + len(pairs)),
        out_specs=whole_vmem(len(outs)),
        out_shape=outs,
        scratch_shapes=[pltpu.VMEM((slots * 2 * width // LANES, LANES), jnp.float32)],
        compiler_params=pltpu.CompilerParams(vmem_limit_bytes=(14 + slots) * MIB),
        cost_estimate=pl.CostEstimate(flops=1000000000, bytes_accessed=4000000, transcendentals=0),
        name="correlate",
    )(*first, own_images, other_images, *pairs)


def collect_kernel(*refs, combos):
    parts_refs, (precision_ref, assigned_ref, out_ref) = refs[:-3], refs[-3:]
    count = len(parts_refs)
    slots = parts_refs[0].shape[0] - combos
    parts = precision_ref.shape[1]
    for index, ref in enumerate(parts_refs):
        out_ref[index * combos : (index + 1) * combos, :] = ref[0:combos, :]
        power = count * combos + index * slots
        out_ref[power : power + slots, :] = ref[combos:, :]
    rest = count * (combos + slots)
    out_ref[rest:, :] = jnp.zeros((8, LANES), jnp.float32)
    out_ref[rest : rest + 1, 0:parts] = precision_ref[...]
    out_ref[rest + 1 : rest + 2, 0:parts] = assigned_ref[...].astype(jnp.float32)


def collect(passes, precision, assigned, combos):
    rows = len(passes) * passes[0].shape[0] + 8
    return pl.pallas_call(
        functools.partial(collect_kernel, combos=combos),
        in_specs=whole_vmem(2 + len(passes)),
        out_specs=pl.BlockSpec(memory_space=pltpu.VMEM),
        out_shape=jax.ShapeDtypeStruct((rows, LANES), jnp.float32),
        compiler_params=pltpu.CompilerParams(vmem_limit_bytes=16 * MIB),
        name="collect",
    )(*passes, precision, assigned)


def rotate_back(weights, own_images, other_images, cos_ref, sin_ref, where, imag_where, slots):
    image_real = jnp.concatenate([own_images[:, where], other_images[:, where]], axis=0)
    image_imag = jnp.concatenate([own_images[:, imag_where], other_images[:, imag_where]], axis=0)
    from_real = jnp.dot(weights, image_real, preferred_element_type=jnp.float32)
    from_imag = jnp.dot(weights, image_imag, preferred_element_type=jnp.float32)
    real = imag = None
    for s in range(cos_ref.shape[0]):
        cos_s, sin_s = cos_ref[s : s + 1, where], sin_ref[s : s + 1, where]
        part_real = from_real[s * slots : (s + 1) * slots]
        part_imag = from_imag[s * slots : (s + 1) * slots]
        real_s = part_real * cos_s + part_imag * sin_s
        imag_s = part_imag * cos_s - part_real * sin_s
        real = real_s if real is None else real + real_s
        imag = imag_s if imag is None else imag + imag_s
    return real, imag


def posterior_kernel(mine, received, weight_ref, own_mass, ordered, *, slots, shifts, pixels):
    device = lax.axis_index("particle")
    parts = weight_ref.shape[1] // 2
    combos = shifts * slots
    theirs = received[...]
    lane = lax.broadcasted_iota(jnp.int32, theirs.shape, 1)
    swapped = jnp.where(
        lane < parts, pltpu.roll(theirs, LANES - parts, 1), pltpu.roll(theirs, parts, 1)
    )
    joint = mine[...] + swapped
    power = jnp.sum(
        mine[combos : combos + slots, :] + received[combos : combos + slots, :], axis=1, keepdims=True
    )
    precision = joint[combos + slots : combos + slots + 1]
    assigned = joint[combos + slots + 1 : combos + slots + 2].astype(jnp.int32)
    likelihood_scale = 1.0 / math.sqrt(2 * pixels)
    classes = [slot_orientation(device, slot, slots) // (slots // CLASSES) for slot in range(slots)]
    logits = []
    for slot in range(slots):
        match = (assigned == classes[slot]).astype(jnp.float32) * PRIOR_REWARD
        part = joint[slot * shifts : (slot + 1) * shifts]
        logits.append(precision * (part - 0.5 * power[slot : slot + 1]) * likelihood_scale + match)
    peak = jnp.max(functools.reduce(jnp.maximum, logits), axis=0, keepdims=True)
    terms = [jnp.exp(value - peak) for value in logits]
    norm = jnp.sum(functools.reduce(jnp.add, terms), axis=0, keepdims=True)
    counted = lax.broadcasted_iota(jnp.int32, (1, LANES), 1) < 2 * parts
    class_lane = lax.broadcasted_iota(jnp.int32, (1, LANES), 1)
    mass_row = jnp.zeros((1, LANES), jnp.float32)
    for slot in range(slots):
        value = terms[slot] / norm
        ordered[slot * shifts : (slot + 1) * shifts, :] = value
        share = jnp.where(counted, jnp.sum(value, axis=0, keepdims=True) * precision, 0.0)
        share = jnp.sum(share, axis=1, keepdims=True)
        mass_row = mass_row + jnp.where(class_lane == classes[slot], share, 0.0)
    weights = jnp.concatenate(
        [ordered[pl.ds(s, slots, stride=shifts), :] for s in range(shifts)], axis=0
    )
    weights = weights[:, 0 : 2 * parts].astype(jnp.bfloat16)
    weight_ref[...] = weights
    own_mass[...] = jnp.broadcast_to(mass_row, own_mass.shape)


def posterior(mine, received, slots, shifts, parts, pixels):
    return pl.pallas_call(
        functools.partial(posterior_kernel, slots=slots, shifts=shifts, pixels=pixels),
        in_specs=whole_vmem(2),
        out_specs=whole_vmem(2),
        out_shape=[
            jax.ShapeDtypeStruct((shifts * slots, 2 * parts), jnp.bfloat16),
            jax.ShapeDtypeStruct((8, LANES), jnp.float32),
        ],
        scratch_shapes=[pltpu.VMEM((shifts * slots, LANES), jnp.float32)],
        compiler_params=pltpu.CompilerParams(vmem_limit_bytes=(14 + slots // 2) * MIB),
        name="posterior",
    )(mine, received)


def backproject_kernel(
    weight_ref, mass, own_images, other_images, cos_ref, sin_ref, own, *refs, slots, chunk, unroll
):
    sends, sums = refs[:-1], refs[-1]
    core = own_half()
    width = cos_ref.shape[1]
    tiles = width // LANES
    main = tiles - 2 * LOW_TILES
    per_row = 2 * tiles
    chunk_tiles = chunk // LANES
    weights = weight_ref[...]

    def body(step, carry):
        first = step * chunk_tiles
        where = pl.ds(pl.multiple_of(step * chunk, chunk), chunk)
        imag_where = pl.ds(pl.multiple_of(width + step * chunk, chunk), chunk)
        real, imag = rotate_back(
            weights, own_images, other_images, cos_ref, sin_ref, where, imag_where, slots
        )
        for k in range(chunk_tiles):
            piece = slice(k * LANES, (k + 1) * LANES)
            sums[pl.ds(first + k, slots, stride=per_row), :] = real[:, piece]
            sums[pl.ds(tiles + first + k, slots, stride=per_row), :] = imag[:, piece]
        return carry

    lax.fori_loop(0, width // chunk, body, 0, unroll=unroll)
    block = split_mass(mass[0:1, :])
    for index, target in enumerate((own,) + sends):
        for row in range(2):
            for comp in range(2):
                start = (2 * index + row) * per_row + comp * tiles + LOW_TILES
                dest = (2 * row + comp) * main
                target[dest : dest + main, :] = sums[start : start + main, :].astype(target.dtype)
        low = []
        for offset in (0, tiles, tiles - LOW_TILES, 2 * tiles - LOW_TILES):
            start = pl.multiple_of((2 * index + core) * per_row + offset, LOW_TILES)
            low.append(sums[pl.ds(start, LOW_TILES), :])
        head = 4 * main
        target[head : head + 4 * LOW_TILES, :] = jnp.concatenate(low, axis=0).astype(target.dtype)
        if index > 0:
            target[head + 4 * LOW_TILES :, :] = block


def backproject(weights, mass, own_images, other_images, cos_table, sin_table, slots):
    tiles = cos_table.shape[1] // LANES
    chips = slots // 2
    rows = 4 * (tiles - LOW_TILES)
    return pl.pallas_call(
        functools.partial(
            backproject_kernel, slots=slots, chunk=BLOCK * LANES, unroll=9 if slots <= 8 else 1
        ),
        in_specs=whole_vmem(6),
        out_specs=whole_vmem(chips),
        out_shape=[jax.ShapeDtypeStruct((rows, LANES), jnp.float32)]
        + [jax.ShapeDtypeStruct((rows + MASS_ROWS, LANES), jnp.bfloat16)] * (chips - 1),
        scratch_shapes=[pltpu.VMEM((slots * 2 * tiles, LANES), jnp.float32)],
        compiler_params=pltpu.CompilerParams(vmem_limit_bytes=(14 + slots // 2) * MIB),
        name="backproject",
    )(weights, mass, own_images, other_images, cos_table, sin_table)


def merge_kernel(own, mass, *refs):
    received, (keep, to_core, low, to_half, mass_out) = refs[:-5], refs[-5:]
    core = own_half()
    half = keep.shape[0]
    rows = own.shape[0]
    total_mass = mass[0:1, :]
    total_low = own[2 * half :, :]
    for ref in received:
        total_mass = total_mass + joined_mass(ref[rows:, :])
        total_low = total_low + ref[2 * half : rows, :].astype(jnp.float32)
    mass_out[...] = jnp.broadcast_to(total_mass, mass_out.shape)
    low[...] = total_low
    to_half[0 : rows - 2 * half, :] = total_low.astype(jnp.bfloat16)
    to_half[rows - 2 * half :, :] = split_mass(total_mass)
    for target, place in ((to_core, 1 - core), (keep, core)):
        where = pl.ds(pl.multiple_of(place * half, half), half)
        total = own[where, :]
        for ref in received:
            total = total + ref[where, :].astype(jnp.float32)
        target[...] = total.astype(target.dtype)


def merge(own, mass, received):
    low = 4 * LOW_TILES
    half = (own.shape[0] - low) // 2
    return pl.pallas_call(
        merge_kernel,
        in_specs=whole_vmem(2 + len(received)),
        out_specs=whole_vmem(5),
        out_shape=[
            jax.ShapeDtypeStruct((half, LANES), jnp.float32),
            jax.ShapeDtypeStruct((half, LANES), jnp.bfloat16),
            jax.ShapeDtypeStruct((low, LANES), jnp.float32),
            jax.ShapeDtypeStruct((low + MASS_ROWS, LANES), jnp.bfloat16),
            jax.ShapeDtypeStruct((8, LANES), jnp.float32),
        ],
        compiler_params=pltpu.CompilerParams(vmem_limit_bytes=16 * MIB),
        name="merge",
    )(own, mass, *received)


def finish_kernel(keep, from_core, low, from_half, mass, out, mass_out, *, scale, mass_scale):
    core = own_half()
    low_rows = low.shape[0]
    total_mass = mass[0:1, :] + joined_mass(from_half[low_rows:, :])
    mass_out[...] = total_mass[0, :CLASSES] * mass_scale
    mean = (low[...] + from_half[0:low_rows, :].astype(jnp.float32)) * (0.5 * scale)
    main = keep.shape[0] // 2
    blocks = main // BLOCK + 1
    for index, (source, place) in enumerate(((keep, core), (from_core, 1 - core))):
        for comp in range(2):
            for block in range(blocks):
                if block == 0:
                    start = (2 * index + comp) * LOW_TILES
                    value = mean[start : start + LOW_TILES]
                else:
                    start = comp * main + (block - 1) * BLOCK
                    value = source[start : start + BLOCK, :].astype(jnp.float32) * scale
                dest = pl.multiple_of((2 * (comp * blocks + block) + place) * BLOCK, BLOCK)
                out[pl.ds(dest, BLOCK), :] = value


def finish(keep, from_core, low, from_half, mass, scale, mass_scale):
    return pl.pallas_call(
        functools.partial(finish_kernel, scale=scale, mass_scale=mass_scale),
        in_specs=whole_vmem(5),
        out_specs=whole_vmem(2),
        out_shape=[
            jax.ShapeDtypeStruct((2 * keep.shape[0] + low.shape[0], LANES), jnp.float32),
            jax.ShapeDtypeStruct((CLASSES,), jnp.float32),
        ],
        compiler_params=pltpu.CompilerParams(vmem_limit_bytes=16 * MIB),
        name="finish",
    )(keep, from_core, low, from_half, mass)


def local(
    images, noise_precision, assigned_class, class_refs, interp_index, interp_frac, shift_grid
):
    dev_count = lax.axis_size("particle")
    slots = dev_count // 2
    chips = slots // 2
    parts, width = images.shape
    other_half, table, index, frac, own_images, other_images = project_other(
        class_refs, interp_index, interp_frac, images
    )
    from_core = exchange(other_half, 1)
    images_received = exchange(other_images, 1)
    pair = pair_rows(project_own(table, index, frac), from_core)
    others = chip_order(chips)[1:]
    pairs = [pair] + [exchange(pair, 4 * m) for m in others]
    group = chips // 2
    first, cos_table, sin_table = correlate(
        own_images, images_received, pairs[:group], shift_grid=shift_grid
    )
    passes = [first]
    for start in range(group, chips, group):
        passes += correlate(
            own_images,
            images_received,
            pairs[start : start + group],
            tables=(cos_table, sin_table),
        )
    mine = collect(
        passes,
        noise_precision.reshape(1, parts),
        assigned_class.reshape(1, parts),
        shift_grid.shape[0] * 2 * group,
    )
    weights, mass = posterior(
        mine, exchange(mine, 1), slots, shift_grid.shape[0], parts, width // 2
    )
    sums = backproject(
        weights, mass, own_images, images_received, cos_table, sin_table, slots
    )
    received = [exchange(send, 4 * m) for m, send in zip(others, sums[1:])]
    keep, to_core, low, to_half, mass = merge(sums[0], mass, received)
    back, class_mass = finish(
        keep,
        exchange(to_core, 1),
        low,
        exchange(to_half, 2),
        mass,
        1.0 / math.sqrt(parts),
        CLASSES / (parts * dev_count),
    )
    return back.reshape(1, width), class_mass


def solution(mesh):
    in_specs = (
        P(("groups", "particle"), None),
        P(("groups", "particle")),
        P(("groups", "particle")),
        P("groups", None, None, None),
        P("particle", None),
        P("particle", None),
        P(),
    )
    out_specs = (P(("groups", "particle"), None), P("groups"))
    return jax.shard_map(local, mesh=mesh, in_specs=in_specs, out_specs=out_specs, check_vma=False)
```

```python
import functools
import math

import jax
import jax.numpy as jnp
from jax import lax
from jax.experimental import pallas as pl
from jax.experimental.pallas import tpu as pltpu
from jax.sharding import PartitionSpec as P

KY = 128
BOX = 256
CLASSES = 8
LOWK = 16
LANES = 128
PRIOR_REWARD = 1.0
MASS_ROWS = 16
BLOCK = 8
PROJECT_CHUNK = 256
LOW_TILES = LOWK * KY // LANES // 2
MIB = 1 << 20


def exchange(value, mask):
    pairs = [(source, source ^ mask) for source in range(lax.axis_size("particle"))]
    return lax.ppermute(value, "particle", pairs)


def in_hbm(value):
    return pltpu.with_memory_space_constraint(value, pltpu.HBM)


def whole_vmem(count):
    return [pl.BlockSpec(memory_space=pltpu.VMEM)] * count


def own_half():
    return lax.axis_index("particle") % 2


def tree_select(values, masks):
    for mask in masks:
        values = [
            jnp.where(mask, values[i + 1], values[i]) if i + 1 < len(values) else values[i]
            for i in range(0, len(values), 2)
        ]
    return values[0]


def project_half(table, index_ref, frac_ref, half, blended):
    pixels = index_ref.shape[1]
    highs = table.shape[1]
    groups = table.shape[0] // 16
    stride = 8 * groups
    chunk = PROJECT_CHUNK
    tiles = chunk // LANES
    per_block = BLOCK // tiles
    half_tiles = pixels // (2 * LANES)

    def body(step, carry):
        block = 2 * (step // per_block) + half
        where = pl.ds(pl.multiple_of((block * per_block + step % per_block) * chunk, chunk), chunk)
        index = index_ref[:, where]
        frac = frac_ref[:, where]
        high = index >> 7
        low = index & (LANES - 1)
        group = (low * 147) >> 10
        first = low - 7 * group
        high_ids = lax.broadcasted_iota(jnp.int32, (highs, chunk), 0)
        one_hot = jnp.where(high_ids == high, 1.0, 0.0).astype(jnp.bfloat16)
        rows = jnp.dot(table[...], one_hot, preferred_element_type=jnp.float32)
        group = jnp.broadcast_to(group, (8, chunk))
        masks = [(group & (1 << bit)) != 0 for bit in range((groups - 1).bit_length())]
        ids = lax.broadcasted_iota(jnp.int32, (8, chunk), 0)
        weight = jnp.where(ids == first, 1.0 - frac, jnp.where(ids == first + 1, frac, 0.0))
        for comp in range(2):
            start = comp * stride
            picked = tree_select([rows[start + 8 * g : start + 8 * g + 8] for g in range(groups)], masks)
            value = jnp.sum(picked * weight, axis=0, keepdims=True)
            for k in range(tiles):
                row = comp * half_tiles + step * tiles + k
                blended[pl.ds(row, 1), :] = value[:, k * LANES : (k + 1) * LANES]
        return carry

    lax.fori_loop(0, half_tiles // tiles, body, 0, unroll=8)


def image_copies(images_hbm, target, sems, first, half, pixels):
    chunk = BLOCK * LANES
    blocks = pixels // (2 * chunk)
    copies = []
    for comp in range(2):
        for step in range(blocks):
            source = pl.multiple_of(comp * pixels + (2 * step + half) * chunk, chunk)
            dest = (comp * blocks + step) * chunk
            copies.append(
                pltpu.make_async_copy(
                    images_hbm.at[:, pl.ds(source, chunk)],
                    target.at[:, pl.ds(dest, chunk)],
                    sems.at[first + len(copies)],
                )
            )
    return copies


def project_other_kernel(
    table_hbm, index_hbm, frac_hbm, images_hbm,
    out_ref, table, index_ref, frac_ref, table_in, flat, wide, blended, sems
):
    device = lax.axis_index("particle")
    row_count = lax.axis_size("particle") // 2
    half_set = device // 2 % 2
    class_id = (2 * (device // 4) + device % 2) // (row_count // CLASSES)
    copies = [
        pltpu.make_async_copy(
            table_hbm.at[pl.ds(half_set, 1), pl.ds(class_id, 1)], table_in, sems.at[0]
        ),
        pltpu.make_async_copy(index_hbm, index_ref, sems.at[1]),
        pltpu.make_async_copy(frac_hbm, frac_ref, sems.at[2]),
    ]
    pixels = index_ref.shape[1]
    copies += image_copies(images_hbm, out_ref, sems, 3, 1 - own_half(), pixels)
    for copy in copies[:3]:
        copy.start()
    copies[0].wait()
    for copy in copies[3:]:
        copy.start()
    highs = flat.shape[1]
    groups = table.shape[0] // 16

    def unfold(step, carry):
        piece = table_in[0, 0, :, pl.ds(step * 8 * LANES, 8 * LANES)].astype(jnp.float32)
        for k in range(8):
            for comp in range(2):
                flat[comp, pl.ds(step * 8 + k, 1), :] = piece[comp : comp + 1, k * LANES : (k + 1) * LANES]
        return carry

    lax.fori_loop(0, highs // 8, unfold, 0, unroll=4)
    picked = []
    for comp in range(2):
        turned = flat[comp].T
        wide[0:LANES, :] = turned
        wide[LANES : LANES + 8, :] = pltpu.roll(turned[0:8], highs - 1, 1)
        picked += [wide[7 * g : 7 * g + 8, :] for g in range(groups)]
    for pair in range(groups):
        table[16 * pair : 16 * (pair + 1), :] = jnp.concatenate(
            picked[2 * pair : 2 * pair + 2], axis=0
        ).astype(jnp.bfloat16)
    copies[1].wait()
    copies[2].wait()
    project_half(table, index_ref, frac_ref, 1 - own_half(), blended)
    parts = out_ref.shape[0]
    for k in range(blended.shape[0] // parts):
        out_ref[:, pixels + k * LANES : pixels + (k + 1) * LANES] = blended[
            k * parts : (k + 1) * parts, :
        ].astype(jnp.bfloat16)
    for copy in copies[3:]:
        copy.wait()


def project_other(class_refs, interp_index, interp_frac, images):
    vox = class_refs.shape[3]
    pixels = interp_index.shape[1]
    highs = vox // LANES
    half_rows = pixels // LANES
    groups = -(-LANES // 7)
    parts = images.shape[0]
    copies = 3 + pixels // (BLOCK * LANES)
    return pl.pallas_call(
        project_other_kernel,
        in_specs=[pl.BlockSpec(memory_space=pltpu.HBM)] * 4,
        out_specs=whole_vmem(4),
        out_shape=[
            jax.ShapeDtypeStruct((parts, pixels + half_rows * LANES // parts), jnp.bfloat16),
            jax.ShapeDtypeStruct((16 * groups, highs), jnp.bfloat16),
            jax.ShapeDtypeStruct((1, pixels), jnp.int32),
            jax.ShapeDtypeStruct((1, pixels), jnp.float32),
        ],
        scratch_shapes=[
            pltpu.VMEM((1, 1, 2, vox), jnp.bfloat16),
            pltpu.VMEM((2, highs, LANES), jnp.float32),
            pltpu.VMEM((LANES + 8, highs), jnp.float32),
            pltpu.VMEM((half_rows, LANES), jnp.float32),
            pltpu.SemaphoreType.DMA((copies,)),
        ],
        compiler_params=pltpu.CompilerParams(vmem_limit_bytes=16 * MIB),
        name="project_other",
    )(*(in_hbm(value) for value in (class_refs, interp_index, interp_frac, images)))


def project_own_kernel(table, index_ref, frac_ref, images_hbm, out_ref, own_images, blended, sems):
    copies = image_copies(images_hbm, own_images, sems, 0, own_half(), index_ref.shape[1])
    for copy in copies:
        copy.start()
    project_half(table, index_ref, frac_ref, own_half(), blended)
    out_ref[...] = blended[...].astype(jnp.bfloat16)
    for copy in copies:
        copy.wait()


def project_own(table, index, frac, images):
    pixels = index.shape[1]
    half_rows = pixels // LANES
    return pl.pallas_call(
        project_own_kernel,
        in_specs=whole_vmem(3) + [pl.BlockSpec(memory_space=pltpu.HBM)],
        out_specs=whole_vmem(2),
        out_shape=[
            jax.ShapeDtypeStruct((half_rows, LANES), jnp.bfloat16),
            jax.ShapeDtypeStruct((images.shape[0], pixels), jnp.bfloat16),
        ],
        scratch_shapes=[
            pltpu.VMEM((half_rows, LANES), jnp.float32),
            pltpu.SemaphoreType.DMA((pixels // (BLOCK * LANES),)),
        ],
        compiler_params=pltpu.CompilerParams(vmem_limit_bytes=16 * MIB),
        cost_estimate=pl.CostEstimate(flops=2000000000, bytes_accessed=8000000, transcendentals=0),
        name="project_own",
    )(table, index, frac, in_hbm(images))


def pair_kernel(own, other, out_ref):
    count = own.shape[0]
    parts, width = other.shape
    tiles = count // parts
    core = own_half()
    out_ref[pl.ds(pl.multiple_of(core * count, count), count), :] = own[...]
    for k in range(tiles):
        lanes = slice(width - (tiles - k) * LANES, width - (tiles - k - 1) * LANES)
        rows = pl.ds(pl.multiple_of((1 - core) * count + k * parts, parts), parts)
        out_ref[rows, :] = other[:, lanes]


def pair_rows(own, other):
    return pl.pallas_call(
        pair_kernel,
        in_specs=whole_vmem(2),
        out_specs=pl.BlockSpec(memory_space=pltpu.VMEM),
        out_shape=jax.ShapeDtypeStruct((2 * own.shape[0], LANES), own.dtype),
        compiler_params=pltpu.CompilerParams(vmem_limit_bytes=16 * MIB),
        name="pair_rows",
    )(own, other)


def chip_order(chips):
    return [0] + list(range(chips - 1, 0, -1))


def slot_orientation(device, slot, slots):
    return 2 * ((device // 4) ^ chip_order(slots // 2)[slot // 2]) + slot % 2


def split_mass(mass_row):
    ids = lax.broadcasted_iota(jnp.int32, (MASS_ROWS, LANES), 0)
    upper = mass_row.astype(jnp.bfloat16).astype(jnp.float32)
    lower = mass_row - upper
    return jnp.where(ids == 0, upper, jnp.where(ids == 1, lower, 0.0)).astype(jnp.bfloat16)


def joined_mass(block):
    return jnp.sum(block.astype(jnp.float32), axis=0, keepdims=True)


def fill_tables(shift_ref, cos_ref, sin_ref):
    shifts, width = cos_ref.shape
    grid_x = shift_ref[:, 0:1]
    grid_y = shift_ref[:, 1:2]
    lane = lax.broadcasted_iota(jnp.int32, (shifts, LANES), 1)
    freq_x = (lane // BLOCK) * (2 * BLOCK) + own_half() * BLOCK + lane % BLOCK
    turn_x = (freq_x * grid_x) & (BOX - 1)
    turn_y = ((lane - KY // 2) * grid_y) & (BOX - 1)
    angle_x = turn_x.astype(jnp.float32) * (2.0 * math.pi / BOX)
    angle_y = turn_y.astype(jnp.float32) * (2.0 * math.pi / BOX)
    cos_x, sin_x = jnp.cos(angle_x), jnp.sin(angle_x)
    cos_y, sin_y = jnp.cos(angle_y), jnp.sin(angle_y)
    for j in range(width // LANES):
        where = slice(j * LANES, (j + 1) * LANES)
        cos_j, sin_j = cos_x[:, j : j + 1], sin_x[:, j : j + 1]
        cos_ref[:, where] = cos_j * cos_y - sin_j * sin_y
        sin_ref[:, where] = sin_j * cos_y + cos_j * sin_y


def correlate_first_kernel(shift_ref, own_images, other_images, *refs, chunk):
    pair_refs, (out_ref, cos_ref, sin_ref, proj) = refs[:-4], refs[-4:]
    fill_tables(shift_ref, cos_ref, sin_ref)
    correlate_kernel(
        cos_ref, sin_ref, own_images, other_images, *pair_refs, out_ref, proj, chunk=chunk
    )


def correlate_kernel(cos_ref, sin_ref, own_images, other_images, *refs, chunk):
    pair_refs, (out_ref, proj) = refs[:-2], refs[-2:]
    shifts = cos_ref.shape[0]
    parts = own_images.shape[0]
    slots = 2 * len(pair_refs)
    width = own_images.shape[1] // 2
    tiles = width // LANES
    per_row = 2 * tiles
    combos = shifts * slots
    for slot in range(slots):
        place = slice(slot % 2 * per_row, (slot % 2 + 1) * per_row)
        row = pair_refs[slot // 2][place, :].astype(jnp.float32)
        proj[slot * per_row : (slot + 1) * per_row, :] = row
        out_ref[combos + slot : combos + slot + 1, :] = jnp.sum(row * row, axis=0, keepdims=True)

    chunk_tiles = chunk // LANES
    contract_lanes = (((1,), (1,)), ((), ()))

    def body(step, total):
        first = step * chunk_tiles
        where = pl.ds(pl.multiple_of(step * chunk, chunk), chunk)
        imag_where = pl.ds(pl.multiple_of(width + step * chunk, chunk), chunk)
        cos_part, sin_part = cos_ref[:, where], sin_ref[:, where]
        reals, imags = [], []
        for slot in range(slots):
            start = slot * per_row + first
            real = jnp.concatenate(
                [proj[pl.ds(start + k, 1), :] for k in range(chunk_tiles)], axis=1
            )
            imag = jnp.concatenate(
                [proj[pl.ds(start + tiles + k, 1), :] for k in range(chunk_tiles)], axis=1
            )
            reals.append(real * cos_part - imag * sin_part)
            imags.append(real * sin_part + imag * cos_part)
        turned_real = jnp.concatenate(reals, axis=0).astype(jnp.bfloat16)
        turned_imag = jnp.concatenate(imags, axis=0).astype(jnp.bfloat16)
        image_real = jnp.concatenate([own_images[:, where], other_images[:, where]], axis=0)
        image_imag = jnp.concatenate([own_images[:, imag_where], other_images[:, imag_where]], axis=0)
        total = total + lax.dot_general(
            turned_real, image_real, contract_lanes, preferred_element_type=jnp.float32
        )
        return total + lax.dot_general(
            turned_imag, image_imag, contract_lanes, preferred_element_type=jnp.float32
        )

    total = lax.fori_loop(
        0, width // chunk, body, jnp.zeros((combos, 2 * parts), jnp.float32), unroll=2
    )
    out_ref[0:combos, :] = jnp.zeros((combos, LANES), jnp.float32)
    out_ref[0:combos, 0 : 2 * parts] = total


def correlate(own_images, other_images, pairs, shift_grid=None, tables=None):
    slots = 2 * len(pairs)
    width = own_images.shape[1] // 2
    shifts = shift_grid.shape[0] if tables is None else tables[0].shape[0]
    first = (shift_grid,) if tables is None else tuple(tables)
    table = jax.ShapeDtypeStruct((shifts, width), jnp.float32)
    outs = [jax.ShapeDtypeStruct((shifts * slots + slots, LANES), jnp.float32)]
    outs += [table, table] if tables is None else []
    kernel = correlate_first_kernel if tables is None else correlate_kernel
    return pl.pallas_call(
        functools.partial(kernel, chunk=2048),
        in_specs=whole_vmem(len(first) + 2 + len(pairs)),
        out_specs=whole_vmem(len(outs)),
        out_shape=outs,
        scratch_shapes=[pltpu.VMEM((slots * 2 * width // LANES, LANES), jnp.float32)],
        compiler_params=pltpu.CompilerParams(vmem_limit_bytes=(14 + slots) * MIB),
        cost_estimate=pl.CostEstimate(flops=1000000000, bytes_accessed=4000000, transcendentals=0),
        name="correlate",
    )(*first, own_images, other_images, *pairs)


def collect_kernel(*refs, combos):
    parts_refs, (precision_ref, assigned_ref, out_ref) = refs[:-3], refs[-3:]
    count = len(parts_refs)
    slots = parts_refs[0].shape[0] - combos
    parts = precision_ref.shape[1]
    for index, ref in enumerate(parts_refs):
        out_ref[index * combos : (index + 1) * combos, :] = ref[0:combos, :]
        power = count * combos + index * slots
        out_ref[power : power + slots, :] = ref[combos:, :]
    rest = count * (combos + slots)
    out_ref[rest:, :] = jnp.zeros((8, LANES), jnp.float32)
    out_ref[rest : rest + 1, 0:parts] = precision_ref[...]
    out_ref[rest + 1 : rest + 2, 0:parts] = assigned_ref[...].astype(jnp.float32)


def collect(passes, precision, assigned, combos):
    rows = len(passes) * passes[0].shape[0] + 8
    return pl.pallas_call(
        functools.partial(collect_kernel, combos=combos),
        in_specs=whole_vmem(2 + len(passes)),
        out_specs=pl.BlockSpec(memory_space=pltpu.VMEM),
        out_shape=jax.ShapeDtypeStruct((rows, LANES), jnp.float32),
        compiler_params=pltpu.CompilerParams(vmem_limit_bytes=16 * MIB),
        name="collect",
    )(*passes, precision, assigned)


def rotate_back(weights, own_images, other_images, cos_ref, sin_ref, where, imag_where, slots):
    image_real = jnp.concatenate([own_images[:, where], other_images[:, where]], axis=0)
    image_imag = jnp.concatenate([own_images[:, imag_where], other_images[:, imag_where]], axis=0)
    from_real = jnp.dot(weights, image_real, preferred_element_type=jnp.float32)
    from_imag = jnp.dot(weights, image_imag, preferred_element_type=jnp.float32)
    real = imag = None
    for s in range(cos_ref.shape[0]):
        cos_s, sin_s = cos_ref[s : s + 1, where], sin_ref[s : s + 1, where]
        part_real = from_real[s * slots : (s + 1) * slots]
        part_imag = from_imag[s * slots : (s + 1) * slots]
        real_s = part_real * cos_s + part_imag * sin_s
        imag_s = part_imag * cos_s - part_real * sin_s
        real = real_s if real is None else real + real_s
        imag = imag_s if imag is None else imag + imag_s
    return real, imag


def posterior_kernel(
    mine, received, own_images, other_images, cos_ref, sin_ref,
    weight_ref, low_ref, low_send, own_mass, ordered, *, slots
):
    device = lax.axis_index("particle")
    shifts, width = cos_ref.shape
    parts = own_images.shape[0]
    combos = shifts * slots
    theirs = received[...]
    lane = lax.broadcasted_iota(jnp.int32, theirs.shape, 1)
    swapped = jnp.where(
        lane < parts, pltpu.roll(theirs, LANES - parts, 1), pltpu.roll(theirs, parts, 1)
    )
    joint = mine[...] + swapped
    power = jnp.sum(
        mine[combos : combos + slots, :] + received[combos : combos + slots, :], axis=1, keepdims=True
    )
    precision = joint[combos + slots : combos + slots + 1]
    assigned = joint[combos + slots + 1 : combos + slots + 2].astype(jnp.int32)
    likelihood_scale = 1.0 / math.sqrt(4 * width)
    classes = [slot_orientation(device, slot, slots) // (slots // CLASSES) for slot in range(slots)]
    logits = []
    for slot in range(slots):
        match = (assigned == classes[slot]).astype(jnp.float32) * PRIOR_REWARD
        part = joint[slot * shifts : (slot + 1) * shifts]
        logits.append(precision * (part - 0.5 * power[slot : slot + 1]) * likelihood_scale + match)
    peak = jnp.max(functools.reduce(jnp.maximum, logits), axis=0, keepdims=True)
    terms = [jnp.exp(value - peak) for value in logits]
    norm = jnp.sum(functools.reduce(jnp.add, terms), axis=0, keepdims=True)
    counted = lax.broadcasted_iota(jnp.int32, (1, LANES), 1) < 2 * parts
    class_lane = lax.broadcasted_iota(jnp.int32, (1, LANES), 1)
    mass_row = jnp.zeros((1, LANES), jnp.float32)
    for slot in range(slots):
        value = terms[slot] / norm
        ordered[slot * shifts : (slot + 1) * shifts, :] = value
        share = jnp.where(counted, jnp.sum(value, axis=0, keepdims=True) * precision, 0.0)
        share = jnp.sum(share, axis=1, keepdims=True)
        mass_row = mass_row + jnp.where(class_lane == classes[slot], share, 0.0)
    weights = jnp.concatenate(
        [ordered[pl.ds(s, slots, stride=shifts), :] for s in range(shifts)], axis=0
    )
    weights = weights[:, 0 : 2 * parts].astype(jnp.bfloat16)
    weight_ref[...] = weights
    own_mass[...] = jnp.broadcast_to(mass_row, own_mass.shape)

    low = LOW_TILES * LANES
    real, imag = rotate_back(
        weights, own_images, other_images, cos_ref, sin_ref, slice(0, low), slice(width, width + low), slots
    )
    for k in range(LOW_TILES):
        piece = slice(k * LANES, (k + 1) * LANES)
        low_ref[pl.ds(k, slots, stride=2 * LOW_TILES), :] = real[:, piece]
        low_ref[pl.ds(LOW_TILES + k, slots, stride=2 * LOW_TILES), :] = imag[:, piece]
    low_body = low_ref.shape[0]
    low_send[0:low_body, :] = low_ref[...].astype(jnp.bfloat16)
    low_send[low_body:, :] = split_mass(mass_row)


def posterior(mine, received, own_images, other_images, cos_table, sin_table, slots):
    shifts = cos_table.shape[0]
    low = slots * 2 * LOW_TILES
    return pl.pallas_call(
        functools.partial(posterior_kernel, slots=slots),
        in_specs=whole_vmem(6),
        out_specs=whole_vmem(4),
        out_shape=[
            jax.ShapeDtypeStruct((shifts * slots, 2 * own_images.shape[0]), jnp.bfloat16),
            jax.ShapeDtypeStruct((low, LANES), jnp.float32),
            jax.ShapeDtypeStruct((low + MASS_ROWS, LANES), jnp.bfloat16),
            jax.ShapeDtypeStruct((8, LANES), jnp.float32),
        ],
        scratch_shapes=[pltpu.VMEM((shifts * slots, LANES), jnp.float32)],
        compiler_params=pltpu.CompilerParams(vmem_limit_bytes=(14 + slots // 2) * MIB),
        name="posterior",
    )(mine, received, own_images, other_images, cos_table, sin_table)


def backproject_kernel(
    weight_ref, own_images, other_images, cos_ref, sin_ref, own, *refs, slots, chunk, unroll
):
    sends, sums = refs[:-1], refs[-1]
    width = cos_ref.shape[1]
    tiles = width // LANES - LOW_TILES
    per_row = 2 * tiles
    chunk_tiles = chunk // LANES
    weights = weight_ref[...]

    def body(step, carry):
        first = step * chunk_tiles
        start = pl.multiple_of((LOW_TILES + first) * LANES, LOW_TILES * LANES)
        where = pl.ds(start, chunk)
        imag_where = pl.ds(pl.multiple_of(width + start, LOW_TILES * LANES), chunk)
        real, imag = rotate_back(
            weights, own_images, other_images, cos_ref, sin_ref, where, imag_where, slots
        )
        for k in range(chunk_tiles):
            piece = slice(k * LANES, (k + 1) * LANES)
            sums[pl.ds(first + k, slots, stride=per_row), :] = real[:, piece]
            sums[pl.ds(tiles + first + k, slots, stride=per_row), :] = imag[:, piece]
        return carry

    lax.fori_loop(0, tiles // chunk_tiles, body, 0, unroll=unroll)
    own[...] = sums[0 : 2 * per_row, :]
    for m, send in enumerate(sends, start=1):
        send[...] = sums[2 * m * per_row : 2 * (m + 1) * per_row, :].astype(jnp.bfloat16)


def backproject(weights, own_images, other_images, cos_table, sin_table, slots):
    width = cos_table.shape[1]
    rows = 2 * 2 * (width // LANES - LOW_TILES)
    chips = slots // 2
    return pl.pallas_call(
        functools.partial(
            backproject_kernel, slots=slots, chunk=LOW_TILES * LANES, unroll=7 if slots <= 8 else 1
        ),
        in_specs=whole_vmem(5),
        out_specs=whole_vmem(chips),
        out_shape=[jax.ShapeDtypeStruct((rows, LANES), jnp.float32)]
        + [jax.ShapeDtypeStruct((rows, LANES), jnp.bfloat16)] * (chips - 1),
        scratch_shapes=[pltpu.VMEM((chips * rows, LANES), jnp.float32)],
        compiler_params=pltpu.CompilerParams(vmem_limit_bytes=(14 + slots // 2) * MIB),
        cost_estimate=pl.CostEstimate(flops=2000000000, bytes_accessed=8000000, transcendentals=0),
        name="backproject",
    )(weights, own_images, other_images, cos_table, sin_table)


def fold_kernel(low_ref, low_received, mass, *refs, chips):
    mains, (own, own_mass), sends = refs[: chips - 1], refs[chips - 1 : chips + 1], refs[chips + 1 :]
    rows = own.shape[0]
    low_body = low_ref.shape[0]
    total_mass = mass[0:1, :] + joined_mass(low_received[low_body:, :])
    block = split_mass(total_mass)
    own_mass[...] = jnp.broadcast_to(total_mass, own_mass.shape)
    for m, target in enumerate((own,) + tuple(sends)):
        part = slice(m * rows, (m + 1) * rows)
        value = (low_ref[part, :] + low_received[part, :].astype(jnp.float32)) * 0.5
        target[0:rows, :] = value.astype(target.dtype)
        if m > 0:
            target[rows : rows + MASS_ROWS, :] = block
            target[rows + MASS_ROWS :, :] = mains[m - 1][...]


def fold(low, low_received, mass, mains):
    chips = len(mains) + 1
    rows = low.shape[0] // chips
    return pl.pallas_call(
        functools.partial(fold_kernel, chips=chips),
        in_specs=whole_vmem(2 + chips),
        out_specs=whole_vmem(1 + chips),
        out_shape=[
            jax.ShapeDtypeStruct((rows, LANES), jnp.float32),
            jax.ShapeDtypeStruct((8, LANES), jnp.float32),
        ]
        + [
            jax.ShapeDtypeStruct((rows + MASS_ROWS + main.shape[0], LANES), jnp.bfloat16)
            for main in mains
        ],
        compiler_params=pltpu.CompilerParams(vmem_limit_bytes=16 * MIB),
        name="fold",
    )(low, low_received, mass, *mains)


def merge_kernel(own, own_low, mass, *refs):
    received, (keep, to_core, mass_out) = refs[:-3], refs[-3:]
    core = own_half()
    low_rows = own_low.shape[0]
    low_half = low_rows // 2
    head = low_rows + MASS_ROWS
    half = own.shape[0] // 2
    total_mass = mass[0:1, :]
    for ref in received:
        total_mass = total_mass + joined_mass(ref[low_rows:head, :])
    mass_out[...] = jnp.broadcast_to(total_mass, mass_out.shape)
    for target, place in ((to_core, 1 - core), (keep, core)):
        start = pl.multiple_of(place * half, half)
        total = own[pl.ds(start, half), :]
        for ref in received:
            total = total + ref[pl.ds(head + start, half), :].astype(jnp.float32)
        where = pl.ds(pl.multiple_of(place * low_half, low_half), low_half)
        low = own_low[where, :]
        for ref in received:
            low = low + ref[where, :].astype(jnp.float32)
        target[...] = jnp.concatenate(
            [low[0:LOW_TILES], total[0 : half // 2], low[LOW_TILES:], total[half // 2 :]], axis=0
        ).astype(target.dtype)


def merge(own, own_low, mass, received):
    rows = (own.shape[0] + own_low.shape[0]) // 2
    return pl.pallas_call(
        merge_kernel,
        in_specs=whole_vmem(3 + len(received)),
        out_specs=whole_vmem(3),
        out_shape=[
            jax.ShapeDtypeStruct((rows, LANES), jnp.float32),
            jax.ShapeDtypeStruct((rows, LANES), jnp.bfloat16),
            jax.ShapeDtypeStruct((8, LANES), jnp.float32),
        ],
        compiler_params=pltpu.CompilerParams(vmem_limit_bytes=16 * MIB),
        name="merge",
    )(own, own_low, mass, *received)


def finish_kernel(own, received, mass, out, mass_out, *, scale, mass_scale):
    core = own_half()
    mass_out[...] = mass[0, :CLASSES] * mass_scale
    for step in range(own.shape[0] // BLOCK):
        rows = slice(step * BLOCK, (step + 1) * BLOCK)
        own_rows = pl.ds(pl.multiple_of((2 * step + core) * BLOCK, BLOCK), BLOCK)
        other_rows = pl.ds(pl.multiple_of((2 * step + 1 - core) * BLOCK, BLOCK), BLOCK)
        out[own_rows, :] = own[rows, :] * scale
        out[other_rows, :] = received[rows, :].astype(jnp.float32) * scale


def finish(own, received, mass, scale, mass_scale):
    return pl.pallas_call(
        functools.partial(finish_kernel, scale=scale, mass_scale=mass_scale),
        in_specs=whole_vmem(3),
        out_specs=whole_vmem(2),
        out_shape=[
            jax.ShapeDtypeStruct((2 * own.shape[0], LANES), jnp.float32),
            jax.ShapeDtypeStruct((CLASSES,), jnp.float32),
        ],
        compiler_params=pltpu.CompilerParams(vmem_limit_bytes=16 * MIB),
        name="finish",
    )(own, received, mass)


def local(
    images, noise_precision, assigned_class, class_refs, interp_index, interp_frac, shift_grid
):
    dev_count = lax.axis_size("particle")
    slots = dev_count // 2
    chips = slots // 2
    parts, width = images.shape
    to_core, table, index, frac = project_other(class_refs, interp_index, interp_frac, images)
    images_received = exchange(to_core, 1)
    own, own_images = project_own(table, index, frac, images)
    pair = pair_rows(own, images_received)
    others = chip_order(chips)[1:]
    pairs = [pair] + [exchange(pair, 4 * m) for m in others]
    group = chips // 2
    first, cos_table, sin_table = correlate(
        own_images, images_received, pairs[:group], shift_grid=shift_grid
    )
    passes = [first]
    for start in range(group, chips, group):
        passes += correlate(
            own_images,
            images_received,
            pairs[start : start + group],
            tables=(cos_table, sin_table),
        )
    mine = collect(
        passes,
        noise_precision.reshape(1, parts),
        assigned_class.reshape(1, parts),
        shift_grid.shape[0] * 2 * group,
    )
    weights, low, low_send, mass = posterior(
        mine, exchange(mine, 1), own_images, images_received, cos_table, sin_table, slots
    )
    low_from_half = exchange(low_send, 2)
    sums = backproject(weights, own_images, images_received, cos_table, sin_table, slots)
    folded = fold(low, low_from_half, mass, sums[1:])
    chip_sums = [exchange(send, 4 * m) for m, send in zip(others, folded[2:])]
    chip_sums = chip_sums[:1] + chip_sums[:0:-1]
    keep, send, mass = merge(sums[0], folded[0], folded[1], chip_sums)
    back, class_mass = finish(
        keep, exchange(send, 1), mass, 1.0 / math.sqrt(parts), CLASSES / (parts * dev_count)
    )
    return back.reshape(1, width), class_mass


def solution(mesh):
    in_specs = (
        P(("groups", "particle"), None),
        P(("groups", "particle")),
        P(("groups", "particle")),
        P("groups", None, None, None),
        P("particle", None),
        P("particle", None),
        P(),
    )
    out_specs = (P(("groups", "particle"), None), P("groups"))
    return jax.shard_map(local, mesh=mesh, in_specs=in_specs, out_specs=out_specs, check_vma=False)
```

```python
import functools
import math

import jax
import jax.numpy as jnp
from jax import lax
from jax.experimental import pallas as pl
from jax.experimental.pallas import tpu as pltpu
from jax.sharding import PartitionSpec as P

KY = 128
BOX = 256
CLASSES = 8
LOWK = 16
LANES = 128
PRIOR_REWARD = 1.0
MASS_ROWS = 16
BLOCK = 8
PROJECT_CHUNK = 256
LOW_TILES = LOWK * KY // LANES // 2
MIB = 1 << 20


def exchange(value, mask):
    pairs = [(source, source ^ mask) for source in range(lax.axis_size("particle"))]
    return lax.ppermute(value, "particle", pairs)


def in_hbm(value):
    return pltpu.with_memory_space_constraint(value, pltpu.HBM)


def whole_vmem(count):
    return [pl.BlockSpec(memory_space=pltpu.VMEM)] * count


def own_half():
    return lax.axis_index("particle") % 2


def tree_select(values, masks):
    for mask in masks:
        values = [
            jnp.where(mask, values[i + 1], values[i]) if i + 1 < len(values) else values[i]
            for i in range(0, len(values), 2)
        ]
    return values[0]


def project_half(table, index_ref, frac_ref, half, blended):
    pixels = index_ref.shape[1]
    highs = table.shape[1]
    groups = table.shape[0] // 16
    stride = 8 * groups
    chunk = PROJECT_CHUNK
    tiles = chunk // LANES
    per_block = BLOCK // tiles
    half_tiles = pixels // (2 * LANES)

    def body(step, carry):
        block = 2 * (step // per_block) + half
        where = pl.ds(pl.multiple_of((block * per_block + step % per_block) * chunk, chunk), chunk)
        index = index_ref[:, where]
        frac = frac_ref[:, where]
        high = index >> 7
        low = index & (LANES - 1)
        group = (low * 147) >> 10
        first = low - 7 * group
        high_ids = lax.broadcasted_iota(jnp.int32, (highs, chunk), 0)
        one_hot = jnp.where(high_ids == high, 1.0, 0.0).astype(jnp.bfloat16)
        rows = jnp.dot(table[...], one_hot, preferred_element_type=jnp.float32)
        group = jnp.broadcast_to(group, (8, chunk))
        masks = [(group & (1 << bit)) != 0 for bit in range((groups - 1).bit_length())]
        ids = lax.broadcasted_iota(jnp.int32, (8, chunk), 0)
        weight = jnp.where(ids == first, 1.0 - frac, jnp.where(ids == first + 1, frac, 0.0))
        for comp in range(2):
            start = comp * stride
            picked = tree_select([rows[start + 8 * g : start + 8 * g + 8] for g in range(groups)], masks)
            value = jnp.sum(picked * weight, axis=0, keepdims=True)
            for k in range(tiles):
                row = comp * half_tiles + step * tiles + k
                blended[pl.ds(row, 1), :] = value[:, k * LANES : (k + 1) * LANES]
        return carry

    lax.fori_loop(0, half_tiles // tiles, body, 0, unroll=8)


def image_copies(images_hbm, target, sems, first, half, pixels):
    chunk = BLOCK * LANES
    blocks = pixels // (2 * chunk)
    copies = []
    for comp in range(2):
        for step in range(blocks):
            source = pl.multiple_of(comp * pixels + (2 * step + half) * chunk, chunk)
            dest = (comp * blocks + step) * chunk
            copies.append(
                pltpu.make_async_copy(
                    images_hbm.at[:, pl.ds(source, chunk)],
                    target.at[:, pl.ds(dest, chunk)],
                    sems.at[first + len(copies)],
                )
            )
    return copies


def project_other_kernel(
    table_hbm, index_hbm, frac_hbm, images_hbm,
    out_ref, table, index_ref, frac_ref, table_in, flat, wide, blended, sems
):
    device = lax.axis_index("particle")
    row_count = lax.axis_size("particle") // 2
    half_set = device // 2 % 2
    class_id = (2 * (device // 4) + device % 2) // (row_count // CLASSES)
    copies = [
        pltpu.make_async_copy(
            table_hbm.at[pl.ds(half_set, 1), pl.ds(class_id, 1)], table_in, sems.at[0]
        ),
        pltpu.make_async_copy(index_hbm, index_ref, sems.at[1]),
        pltpu.make_async_copy(frac_hbm, frac_ref, sems.at[2]),
    ]
    pixels = index_ref.shape[1]
    copies += image_copies(images_hbm, out_ref, sems, 3, 1 - own_half(), pixels)
    for copy in copies[:3]:
        copy.start()
    copies[0].wait()
    for copy in copies[3:]:
        copy.start()
    highs = flat.shape[1]
    groups = table.shape[0] // 16

    def unfold(step, carry):
        piece = table_in[0, 0, :, pl.ds(step * 8 * LANES, 8 * LANES)].astype(jnp.float32)
        for k in range(8):
            for comp in range(2):
                flat[comp, pl.ds(step * 8 + k, 1), :] = piece[comp : comp + 1, k * LANES : (k + 1) * LANES]
        return carry

    lax.fori_loop(0, highs // 8, unfold, 0, unroll=4)
    picked = []
    for comp in range(2):
        turned = flat[comp].T
        wide[0:LANES, :] = turned
        wide[LANES : LANES + 8, :] = pltpu.roll(turned[0:8], highs - 1, 1)
        picked += [wide[7 * g : 7 * g + 8, :] for g in range(groups)]
    for pair in range(groups):
        table[16 * pair : 16 * (pair + 1), :] = jnp.concatenate(
            picked[2 * pair : 2 * pair + 2], axis=0
        ).astype(jnp.bfloat16)
    copies[1].wait()
    copies[2].wait()
    project_half(table, index_ref, frac_ref, 1 - own_half(), blended)
    parts = out_ref.shape[0]
    for k in range(blended.shape[0] // parts):
        out_ref[:, pixels + k * LANES : pixels + (k + 1) * LANES] = blended[
            k * parts : (k + 1) * parts, :
        ].astype(jnp.bfloat16)
    for copy in copies[3:]:
        copy.wait()


def project_other(class_refs, interp_index, interp_frac, images):
    vox = class_refs.shape[3]
    pixels = interp_index.shape[1]
    highs = vox // LANES
    half_rows = pixels // LANES
    groups = -(-LANES // 7)
    parts = images.shape[0]
    copies = 3 + pixels // (BLOCK * LANES)
    return pl.pallas_call(
        project_other_kernel,
        in_specs=[pl.BlockSpec(memory_space=pltpu.HBM)] * 4,
        out_specs=whole_vmem(4),
        out_shape=[
            jax.ShapeDtypeStruct((parts, pixels + half_rows * LANES // parts), jnp.bfloat16),
            jax.ShapeDtypeStruct((16 * groups, highs), jnp.bfloat16),
            jax.ShapeDtypeStruct((1, pixels), jnp.int32),
            jax.ShapeDtypeStruct((1, pixels), jnp.float32),
        ],
        scratch_shapes=[
            pltpu.VMEM((1, 1, 2, vox), jnp.bfloat16),
            pltpu.VMEM((2, highs, LANES), jnp.float32),
            pltpu.VMEM((LANES + 8, highs), jnp.float32),
            pltpu.VMEM((half_rows, LANES), jnp.float32),
            pltpu.SemaphoreType.DMA((copies,)),
        ],
        compiler_params=pltpu.CompilerParams(vmem_limit_bytes=16 * MIB),
        name="project_other",
    )(*(in_hbm(value) for value in (class_refs, interp_index, interp_frac, images)))


def project_own_kernel(table, index_ref, frac_ref, images_hbm, out_ref, own_images, blended, sems):
    copies = image_copies(images_hbm, own_images, sems, 0, own_half(), index_ref.shape[1])
    for copy in copies:
        copy.start()
    project_half(table, index_ref, frac_ref, own_half(), blended)
    out_ref[...] = blended[...].astype(jnp.bfloat16)
    for copy in copies:
        copy.wait()


def project_own(table, index, frac, images):
    pixels = index.shape[1]
    half_rows = pixels // LANES
    return pl.pallas_call(
        project_own_kernel,
        in_specs=whole_vmem(3) + [pl.BlockSpec(memory_space=pltpu.HBM)],
        out_specs=whole_vmem(2),
        out_shape=[
            jax.ShapeDtypeStruct((half_rows, LANES), jnp.bfloat16),
            jax.ShapeDtypeStruct((images.shape[0], pixels), jnp.bfloat16),
        ],
        scratch_shapes=[
            pltpu.VMEM((half_rows, LANES), jnp.float32),
            pltpu.SemaphoreType.DMA((pixels // (BLOCK * LANES),)),
        ],
        compiler_params=pltpu.CompilerParams(vmem_limit_bytes=16 * MIB),
        cost_estimate=pl.CostEstimate(flops=2000000000, bytes_accessed=8000000, transcendentals=0),
        name="project_own",
    )(table, index, frac, in_hbm(images))


def pair_kernel(own, other, out_ref):
    count = own.shape[0]
    parts, width = other.shape
    tiles = count // parts
    core = own_half()
    out_ref[pl.ds(pl.multiple_of(core * count, count), count), :] = own[...]
    for k in range(tiles):
        lanes = slice(width - (tiles - k) * LANES, width - (tiles - k - 1) * LANES)
        rows = pl.ds(pl.multiple_of((1 - core) * count + k * parts, parts), parts)
        out_ref[rows, :] = other[:, lanes]


def pair_rows(own, other):
    return pl.pallas_call(
        pair_kernel,
        in_specs=whole_vmem(2),
        out_specs=pl.BlockSpec(memory_space=pltpu.VMEM),
        out_shape=jax.ShapeDtypeStruct((2 * own.shape[0], LANES), own.dtype),
        compiler_params=pltpu.CompilerParams(vmem_limit_bytes=16 * MIB),
        name="pair_rows",
    )(own, other)


def chip_order(chips):
    return [0] + list(range(chips - 1, 0, -1))


def slot_orientation(device, slot, slots):
    return 2 * ((device // 4) ^ chip_order(slots // 2)[slot // 2]) + slot % 2


def split_mass(mass_row):
    ids = lax.broadcasted_iota(jnp.int32, (MASS_ROWS, LANES), 0)
    upper = mass_row.astype(jnp.bfloat16).astype(jnp.float32)
    lower = mass_row - upper
    return jnp.where(ids == 0, upper, jnp.where(ids == 1, lower, 0.0)).astype(jnp.bfloat16)


def joined_mass(block):
    return jnp.sum(block.astype(jnp.float32), axis=0, keepdims=True)


def fill_tables(shift_ref, cos_ref, sin_ref):
    shifts, width = cos_ref.shape
    grid_x = shift_ref[:, 0:1]
    grid_y = shift_ref[:, 1:2]
    lane = lax.broadcasted_iota(jnp.int32, (shifts, LANES), 1)
    freq_x = (lane // BLOCK) * (2 * BLOCK) + own_half() * BLOCK + lane % BLOCK
    turn_x = (freq_x * grid_x) & (BOX - 1)
    turn_y = ((lane - KY // 2) * grid_y) & (BOX - 1)
    angle_x = turn_x.astype(jnp.float32) * (2.0 * math.pi / BOX)
    angle_y = turn_y.astype(jnp.float32) * (2.0 * math.pi / BOX)
    cos_x, sin_x = jnp.cos(angle_x), jnp.sin(angle_x)
    cos_y, sin_y = jnp.cos(angle_y), jnp.sin(angle_y)
    for j in range(width // LANES):
        where = slice(j * LANES, (j + 1) * LANES)
        cos_j, sin_j = cos_x[:, j : j + 1], sin_x[:, j : j + 1]
        cos_ref[:, where] = cos_j * cos_y - sin_j * sin_y
        sin_ref[:, where] = sin_j * cos_y + cos_j * sin_y


def correlate_first_kernel(shift_ref, own_images, other_images, *refs, chunk):
    pair_refs, (out_ref, cos_ref, sin_ref, proj) = refs[:-4], refs[-4:]
    fill_tables(shift_ref, cos_ref, sin_ref)
    correlate_kernel(
        cos_ref, sin_ref, own_images, other_images, *pair_refs, out_ref, proj, chunk=chunk
    )


def correlate_kernel(cos_ref, sin_ref, own_images, other_images, *refs, chunk):
    pair_refs, (out_ref, proj) = refs[:-2], refs[-2:]
    shifts = cos_ref.shape[0]
    parts = own_images.shape[0]
    slots = 2 * len(pair_refs)
    width = own_images.shape[1] // 2
    tiles = width // LANES
    per_row = 2 * tiles
    combos = shifts * slots
    for slot in range(slots):
        place = slice(slot % 2 * per_row, (slot % 2 + 1) * per_row)
        row = pair_refs[slot // 2][place, :].astype(jnp.float32)
        proj[slot * per_row : (slot + 1) * per_row, :] = row
        out_ref[combos + slot : combos + slot + 1, :] = jnp.sum(row * row, axis=0, keepdims=True)

    chunk_tiles = chunk // LANES
    contract_lanes = (((1,), (1,)), ((), ()))

    def body(step, total):
        first = step * chunk_tiles
        where = pl.ds(pl.multiple_of(step * chunk, chunk), chunk)
        imag_where = pl.ds(pl.multiple_of(width + step * chunk, chunk), chunk)
        cos_part, sin_part = cos_ref[:, where], sin_ref[:, where]
        reals, imags = [], []
        for slot in range(slots):
            start = slot * per_row + first
            real = jnp.concatenate(
                [proj[pl.ds(start + k, 1), :] for k in range(chunk_tiles)], axis=1
            )
            imag = jnp.concatenate(
                [proj[pl.ds(start + tiles + k, 1), :] for k in range(chunk_tiles)], axis=1
            )
            reals.append(real * cos_part - imag * sin_part)
            imags.append(real * sin_part + imag * cos_part)
        turned_real = jnp.concatenate(reals, axis=0).astype(jnp.bfloat16)
        turned_imag = jnp.concatenate(imags, axis=0).astype(jnp.bfloat16)
        image_real = jnp.concatenate([own_images[:, where], other_images[:, where]], axis=0)
        image_imag = jnp.concatenate([own_images[:, imag_where], other_images[:, imag_where]], axis=0)
        total = total + lax.dot_general(
            image_real, turned_real, contract_lanes, preferred_element_type=jnp.float32
        )
        return total + lax.dot_general(
            image_imag, turned_imag, contract_lanes, preferred_element_type=jnp.float32
        )

    total = lax.fori_loop(
        0, width // chunk, body, jnp.zeros((2 * parts, combos), jnp.float32), unroll=2
    )
    out_ref[0:combos, :] = jnp.zeros((combos, LANES), jnp.float32)
    out_ref[0:combos, 0 : 2 * parts] = total.T


def correlate(own_images, other_images, pairs, shift_grid=None, tables=None):
    slots = 2 * len(pairs)
    width = own_images.shape[1] // 2
    shifts = shift_grid.shape[0] if tables is None else tables[0].shape[0]
    first = (shift_grid,) if tables is None else tuple(tables)
    table = jax.ShapeDtypeStruct((shifts, width), jnp.float32)
    outs = [jax.ShapeDtypeStruct((shifts * slots + slots, LANES), jnp.float32)]
    outs += [table, table] if tables is None else []
    kernel = correlate_first_kernel if tables is None else correlate_kernel
    return pl.pallas_call(
        functools.partial(kernel, chunk=2048),
        in_specs=whole_vmem(len(first) + 2 + len(pairs)),
        out_specs=whole_vmem(len(outs)),
        out_shape=outs,
        scratch_shapes=[pltpu.VMEM((slots * 2 * width // LANES, LANES), jnp.float32)],
        compiler_params=pltpu.CompilerParams(vmem_limit_bytes=(14 + slots) * MIB),
        cost_estimate=pl.CostEstimate(flops=1000000000, bytes_accessed=4000000, transcendentals=0),
        name="correlate",
    )(*first, own_images, other_images, *pairs)


def collect_kernel(*refs, combos):
    parts_refs, (precision_ref, assigned_ref, out_ref) = refs[:-3], refs[-3:]
    count = len(parts_refs)
    slots = parts_refs[0].shape[0] - combos
    parts = precision_ref.shape[1]
    for index, ref in enumerate(parts_refs):
        out_ref[index * combos : (index + 1) * combos, :] = ref[0:combos, :]
        power = count * combos + index * slots
        out_ref[power : power + slots, :] = ref[combos:, :]
    rest = count * (combos + slots)
    out_ref[rest:, :] = jnp.zeros((8, LANES), jnp.float32)
    out_ref[rest : rest + 1, 0:parts] = precision_ref[...]
    out_ref[rest + 1 : rest + 2, 0:parts] = assigned_ref[...].astype(jnp.float32)


def collect(passes, precision, assigned, combos):
    rows = len(passes) * passes[0].shape[0] + 8
    return pl.pallas_call(
        functools.partial(collect_kernel, combos=combos),
        in_specs=whole_vmem(2 + len(passes)),
        out_specs=pl.BlockSpec(memory_space=pltpu.VMEM),
        out_shape=jax.ShapeDtypeStruct((rows, LANES), jnp.float32),
        compiler_params=pltpu.CompilerParams(vmem_limit_bytes=16 * MIB),
        name="collect",
    )(*passes, precision, assigned)


def rotate_back(weights, own_images, other_images, cos_ref, sin_ref, where, imag_where, slots):
    image_real = jnp.concatenate([own_images[:, where], other_images[:, where]], axis=0)
    image_imag = jnp.concatenate([own_images[:, imag_where], other_images[:, imag_where]], axis=0)
    from_real = jnp.dot(weights, image_real, preferred_element_type=jnp.float32)
    from_imag = jnp.dot(weights, image_imag, preferred_element_type=jnp.float32)
    real = imag = None
    for s in range(cos_ref.shape[0]):
        cos_s, sin_s = cos_ref[s : s + 1, where], sin_ref[s : s + 1, where]
        part_real = from_real[s * slots : (s + 1) * slots]
        part_imag = from_imag[s * slots : (s + 1) * slots]
        real_s = part_real * cos_s + part_imag * sin_s
        imag_s = part_imag * cos_s - part_real * sin_s
        real = real_s if real is None else real + real_s
        imag = imag_s if imag is None else imag + imag_s
    return real, imag


def posterior_kernel(
    mine, received, own_images, other_images, cos_ref, sin_ref,
    weight_ref, low_ref, low_send, own_mass, ordered, *, slots
):
    device = lax.axis_index("particle")
    shifts, width = cos_ref.shape
    parts = own_images.shape[0]
    combos = shifts * slots
    theirs = received[...]
    lane = lax.broadcasted_iota(jnp.int32, theirs.shape, 1)
    swapped = jnp.where(
        lane < parts, pltpu.roll(theirs, LANES - parts, 1), pltpu.roll(theirs, parts, 1)
    )
    joint = mine[...] + swapped
    power = jnp.sum(
        mine[combos : combos + slots, :] + received[combos : combos + slots, :], axis=1, keepdims=True
    )
    precision = joint[combos + slots : combos + slots + 1]
    assigned = joint[combos + slots + 1 : combos + slots + 2].astype(jnp.int32)
    likelihood_scale = 1.0 / math.sqrt(4 * width)
    classes = [slot_orientation(device, slot, slots) // (slots // CLASSES) for slot in range(slots)]
    logits = []
    for slot in range(slots):
        match = (assigned == classes[slot]).astype(jnp.float32) * PRIOR_REWARD
        part = joint[slot * shifts : (slot + 1) * shifts]
        logits.append(precision * (part - 0.5 * power[slot : slot + 1]) * likelihood_scale + match)
    peak = jnp.max(functools.reduce(jnp.maximum, logits), axis=0, keepdims=True)
    terms = [jnp.exp(value - peak) for value in logits]
    norm = jnp.sum(functools.reduce(jnp.add, terms), axis=0, keepdims=True)
    counted = lax.broadcasted_iota(jnp.int32, (1, LANES), 1) < 2 * parts
    class_lane = lax.broadcasted_iota(jnp.int32, (1, LANES), 1)
    mass_row = jnp.zeros((1, LANES), jnp.float32)
    for slot in range(slots):
        value = terms[slot] / norm
        ordered[slot * shifts : (slot + 1) * shifts, :] = value
        share = jnp.where(counted, jnp.sum(value, axis=0, keepdims=True) * precision, 0.0)
        share = jnp.sum(share, axis=1, keepdims=True)
        mass_row = mass_row + jnp.where(class_lane == classes[slot], share, 0.0)
    weights = jnp.concatenate(
        [ordered[pl.ds(s, slots, stride=shifts), :] for s in range(shifts)], axis=0
    )
    weights = weights[:, 0 : 2 * parts].astype(jnp.bfloat16)
    weight_ref[...] = weights
    own_mass[...] = jnp.broadcast_to(mass_row, own_mass.shape)

    low = LOW_TILES * LANES
    real, imag = rotate_back(
        weights, own_images, other_images, cos_ref, sin_ref, slice(0, low), slice(width, width + low), slots
    )
    for k in range(LOW_TILES):
        piece = slice(k * LANES, (k + 1) * LANES)
        low_ref[pl.ds(k, slots, stride=2 * LOW_TILES), :] = real[:, piece]
        low_ref[pl.ds(LOW_TILES + k, slots, stride=2 * LOW_TILES), :] = imag[:, piece]
    low_body = low_ref.shape[0]
    low_send[0:low_body, :] = low_ref[...].astype(jnp.bfloat16)
    low_send[low_body:, :] = split_mass(mass_row)


def posterior(mine, received, own_images, other_images, cos_table, sin_table, slots):
    shifts = cos_table.shape[0]
    low = slots * 2 * LOW_TILES
    return pl.pallas_call(
        functools.partial(posterior_kernel, slots=slots),
        in_specs=whole_vmem(6),
        out_specs=whole_vmem(4),
        out_shape=[
            jax.ShapeDtypeStruct((shifts * slots, 2 * own_images.shape[0]), jnp.bfloat16),
            jax.ShapeDtypeStruct((low, LANES), jnp.float32),
            jax.ShapeDtypeStruct((low + MASS_ROWS, LANES), jnp.bfloat16),
            jax.ShapeDtypeStruct((8, LANES), jnp.float32),
        ],
        scratch_shapes=[pltpu.VMEM((shifts * slots, LANES), jnp.float32)],
        compiler_params=pltpu.CompilerParams(vmem_limit_bytes=(14 + slots // 2) * MIB),
        name="posterior",
    )(mine, received, own_images, other_images, cos_table, sin_table)


def backproject_kernel(
    weight_ref, own_images, other_images, cos_ref, sin_ref, own, *refs, slots, chunk, unroll
):
    sends, sums = refs[:-1], refs[-1]
    width = cos_ref.shape[1]
    tiles = width // LANES - LOW_TILES
    per_row = 2 * tiles
    chunk_tiles = chunk // LANES
    weights = weight_ref[...]

    def body(step, carry):
        first = step * chunk_tiles
        start = pl.multiple_of((LOW_TILES + first) * LANES, LOW_TILES * LANES)
        where = pl.ds(start, chunk)
        imag_where = pl.ds(pl.multiple_of(width + start, LOW_TILES * LANES), chunk)
        real, imag = rotate_back(
            weights, own_images, other_images, cos_ref, sin_ref, where, imag_where, slots
        )
        for k in range(chunk_tiles):
            piece = slice(k * LANES, (k + 1) * LANES)
            sums[pl.ds(first + k, slots, stride=per_row), :] = real[:, piece]
            sums[pl.ds(tiles + first + k, slots, stride=per_row), :] = imag[:, piece]
        return carry

    lax.fori_loop(0, tiles // chunk_tiles, body, 0, unroll=unroll)
    own[...] = sums[0 : 2 * per_row, :]
    for m, send in enumerate(sends, start=1):
        send[...] = sums[2 * m * per_row : 2 * (m + 1) * per_row, :].astype(jnp.bfloat16)


def backproject(weights, own_images, other_images, cos_table, sin_table, slots):
    width = cos_table.shape[1]
    rows = 2 * 2 * (width // LANES - LOW_TILES)
    chips = slots // 2
    return pl.pallas_call(
        functools.partial(
            backproject_kernel, slots=slots, chunk=LOW_TILES * LANES, unroll=7 if slots <= 8 else 1
        ),
        in_specs=whole_vmem(5),
        out_specs=whole_vmem(chips),
        out_shape=[jax.ShapeDtypeStruct((rows, LANES), jnp.float32)]
        + [jax.ShapeDtypeStruct((rows, LANES), jnp.bfloat16)] * (chips - 1),
        scratch_shapes=[pltpu.VMEM((chips * rows, LANES), jnp.float32)],
        compiler_params=pltpu.CompilerParams(vmem_limit_bytes=(14 + slots // 2) * MIB),
        cost_estimate=pl.CostEstimate(flops=2000000000, bytes_accessed=8000000, transcendentals=0),
        name="backproject",
    )(weights, own_images, other_images, cos_table, sin_table)


def fold_kernel(low_ref, low_received, mass, *refs, chips):
    mains, (own, own_mass), sends = refs[: chips - 2], refs[chips - 2 : chips], refs[chips:]
    rows = own.shape[0]
    low_body = low_ref.shape[0]
    total_mass = mass[0:1, :] + joined_mass(low_received[low_body:, :])
    block = split_mass(total_mass)
    own_mass[...] = jnp.broadcast_to(total_mass, own_mass.shape)
    for m, target in enumerate((own,) + tuple(sends)):
        part = slice(m * rows, (m + 1) * rows)
        value = (low_ref[part, :] + low_received[part, :].astype(jnp.float32)) * 0.5
        target[0:rows, :] = value.astype(target.dtype)
        if m > 0:
            target[rows : rows + MASS_ROWS, :] = block
        if m > 1:
            target[rows + MASS_ROWS :, :] = mains[m - 2][...]


def fold(low, low_received, mass, mains):
    chips = len(mains) + 2
    rows = low.shape[0] // chips
    head = rows + MASS_ROWS
    return pl.pallas_call(
        functools.partial(fold_kernel, chips=chips),
        in_specs=whole_vmem(1 + chips),
        out_specs=whole_vmem(1 + chips),
        out_shape=[
            jax.ShapeDtypeStruct((rows, LANES), jnp.float32),
            jax.ShapeDtypeStruct((8, LANES), jnp.float32),
            jax.ShapeDtypeStruct((head, LANES), jnp.bfloat16),
        ]
        + [jax.ShapeDtypeStruct((head + main.shape[0], LANES), jnp.bfloat16) for main in mains],
        compiler_params=pltpu.CompilerParams(vmem_limit_bytes=16 * MIB),
        cost_estimate=pl.CostEstimate(flops=4000000000, bytes_accessed=16000000, transcendentals=0),
        name="fold",
    )(low, low_received, mass, *mains)


def add_far_kernel(own, received, out):
    out[...] = own[...] + received[...].astype(jnp.float32)


def add_far(own, received):
    return pl.pallas_call(
        add_far_kernel,
        in_specs=whole_vmem(2),
        out_specs=pl.BlockSpec(memory_space=pltpu.VMEM),
        out_shape=jax.ShapeDtypeStruct(own.shape, jnp.float32),
        compiler_params=pltpu.CompilerParams(vmem_limit_bytes=16 * MIB),
        cost_estimate=pl.CostEstimate(flops=1000000000, bytes_accessed=4000000, transcendentals=0),
        name="add_far",
    )(own, received)


def merge_kernel(own, own_low, mass, *refs):
    received, (keep, to_core, mass_out) = refs[:-3], refs[-3:]
    core = own_half()
    low_rows = own_low.shape[0]
    low_half = low_rows // 2
    head = low_rows + MASS_ROWS
    half = own.shape[0] // 2
    total_mass = mass[0:1, :]
    for ref in received:
        total_mass = total_mass + joined_mass(ref[low_rows:head, :])
    mass_out[...] = jnp.broadcast_to(total_mass, mass_out.shape)
    for target, place in ((to_core, 1 - core), (keep, core)):
        start = pl.multiple_of(place * half, half)
        total = own[pl.ds(start, half), :]
        for ref in received[:-1]:
            total = total + ref[pl.ds(head + start, half), :].astype(jnp.float32)
        where = pl.ds(pl.multiple_of(place * low_half, low_half), low_half)
        low = own_low[where, :]
        for ref in received:
            low = low + ref[where, :].astype(jnp.float32)
        target[...] = jnp.concatenate(
            [low[0:LOW_TILES], total[0 : half // 2], low[LOW_TILES:], total[half // 2 :]], axis=0
        ).astype(target.dtype)


def merge(own, own_low, mass, received):
    rows = (own.shape[0] + own_low.shape[0]) // 2
    return pl.pallas_call(
        merge_kernel,
        in_specs=whole_vmem(3 + len(received)),
        out_specs=whole_vmem(3),
        out_shape=[
            jax.ShapeDtypeStruct((rows, LANES), jnp.float32),
            jax.ShapeDtypeStruct((rows, LANES), jnp.bfloat16),
            jax.ShapeDtypeStruct((8, LANES), jnp.float32),
        ],
        compiler_params=pltpu.CompilerParams(vmem_limit_bytes=16 * MIB),
        name="merge",
    )(own, own_low, mass, *received)


def finish_kernel(own, received, mass, out, mass_out, *, scale, mass_scale):
    core = own_half()
    mass_out[...] = mass[0, :CLASSES] * mass_scale
    for step in range(own.shape[0] // BLOCK):
        rows = slice(step * BLOCK, (step + 1) * BLOCK)
        own_rows = pl.ds(pl.multiple_of((2 * step + core) * BLOCK, BLOCK), BLOCK)
        other_rows = pl.ds(pl.multiple_of((2 * step + 1 - core) * BLOCK, BLOCK), BLOCK)
        out[own_rows, :] = own[rows, :] * scale
        out[other_rows, :] = received[rows, :].astype(jnp.float32) * scale


def finish(own, received, mass, scale, mass_scale):
    return pl.pallas_call(
        functools.partial(finish_kernel, scale=scale, mass_scale=mass_scale),
        in_specs=whole_vmem(3),
        out_specs=whole_vmem(2),
        out_shape=[
            jax.ShapeDtypeStruct((2 * own.shape[0], LANES), jnp.float32),
            jax.ShapeDtypeStruct((CLASSES,), jnp.float32),
        ],
        compiler_params=pltpu.CompilerParams(vmem_limit_bytes=16 * MIB),
        name="finish",
    )(own, received, mass)


def local(
    images, noise_precision, assigned_class, class_refs, interp_index, interp_frac, shift_grid
):
    dev_count = lax.axis_size("particle")
    slots = dev_count // 2
    chips = slots // 2
    parts, width = images.shape
    to_core, table, index, frac = project_other(class_refs, interp_index, interp_frac, images)
    images_received = exchange(to_core, 1)
    own, own_images = project_own(table, index, frac, images)
    pair = pair_rows(own, images_received)
    others = chip_order(chips)[1:]
    pairs = [pair] + [exchange(pair, 4 * m) for m in others]
    group = chips // 2
    first, cos_table, sin_table = correlate(
        own_images, images_received, pairs[:group], shift_grid=shift_grid
    )
    passes = [first]
    for start in range(group, chips, group):
        passes += correlate(
            own_images,
            images_received,
            pairs[start : start + group],
            tables=(cos_table, sin_table),
        )
    mine = collect(
        passes,
        noise_precision.reshape(1, parts),
        assigned_class.reshape(1, parts),
        shift_grid.shape[0] * 2 * group,
    )
    weights, low, low_send, mass = posterior(
        mine, exchange(mine, 1), own_images, images_received, cos_table, sin_table, slots
    )
    low_from_half = exchange(low_send, 2)
    sums = backproject(weights, own_images, images_received, cos_table, sin_table, slots)
    far_sum = add_far(sums[0], exchange(sums[1], 4 * others[0]))
    folded = fold(low, low_from_half, mass, sums[2:])
    received = [exchange(send, 4 * m) for m, send in zip(others[1:], folded[3:])]
    received.append(exchange(folded[2], 4 * others[0]))
    keep, send, mass = merge(far_sum, folded[0], folded[1], received)
    back, class_mass = finish(
        keep, exchange(send, 1), mass, 1.0 / math.sqrt(parts), CLASSES / (parts * dev_count)
    )
    return back.reshape(1, width), class_mass


def solution(mesh):
    in_specs = (
        P(("groups", "particle"), None),
        P(("groups", "particle")),
        P(("groups", "particle")),
        P("groups", None, None, None),
        P("particle", None),
        P("particle", None),
        P(),
    )
    out_specs = (P(("groups", "particle"), None), P("groups"))
    return jax.shard_map(local, mesh=mesh, in_specs=in_specs, out_specs=out_specs, check_vma=False)
```

```python
import functools
import math

import jax
import jax.numpy as jnp
from jax import lax
from jax.experimental import pallas as pl
from jax.experimental.pallas import tpu as pltpu
from jax.sharding import PartitionSpec as P

KY = 128
BOX = 256
CLASSES = 8
LOWK = 16
LANES = 128
PRIOR_REWARD = 1.0
MASS_ROWS = 16
BLOCK = 8
PROJECT_CHUNK = 256
LOW_TILES = LOWK * KY // LANES // 2
MIB = 1 << 20


def exchange(value, mask):
    pairs = [(source, source ^ mask) for source in range(lax.axis_size("particle"))]
    return lax.ppermute(value, "particle", pairs)


def in_hbm(value):
    return pltpu.with_memory_space_constraint(value, pltpu.HBM)


def whole_vmem(count):
    return [pl.BlockSpec(memory_space=pltpu.VMEM)] * count


def own_half():
    return lax.axis_index("particle") % 2


def tree_select(values, masks):
    for mask in masks:
        values = [
            jnp.where(mask, values[i + 1], values[i]) if i + 1 < len(values) else values[i]
            for i in range(0, len(values), 2)
        ]
    return values[0]


def project_half(table, index_ref, frac_ref, half, blended):
    pixels = index_ref.shape[1]
    highs = table.shape[1]
    groups = table.shape[0] // 16
    stride = 8 * groups
    chunk = PROJECT_CHUNK
    tiles = chunk // LANES
    per_block = BLOCK // tiles
    half_tiles = pixels // (2 * LANES)

    def body(step, carry):
        block = 2 * (step // per_block) + half
        where = pl.ds(pl.multiple_of((block * per_block + step % per_block) * chunk, chunk), chunk)
        index = index_ref[:, where]
        frac = frac_ref[:, where]
        high = index >> 7
        low = index & (LANES - 1)
        group = (low * 147) >> 10
        first = low - 7 * group
        high_ids = lax.broadcasted_iota(jnp.int32, (highs, chunk), 0)
        one_hot = jnp.where(high_ids == high, 1.0, 0.0).astype(jnp.bfloat16)
        rows = jnp.dot(table[...], one_hot, preferred_element_type=jnp.float32)
        group = jnp.broadcast_to(group, (8, chunk))
        masks = [(group & (1 << bit)) != 0 for bit in range((groups - 1).bit_length())]
        ids = lax.broadcasted_iota(jnp.int32, (8, chunk), 0)
        weight = jnp.where(ids == first, 1.0 - frac, jnp.where(ids == first + 1, frac, 0.0))
        for comp in range(2):
            start = comp * stride
            picked = tree_select([rows[start + 8 * g : start + 8 * g + 8] for g in range(groups)], masks)
            value = jnp.sum(picked * weight, axis=0, keepdims=True)
            for k in range(tiles):
                row = comp * half_tiles + step * tiles + k
                blended[pl.ds(row, 1), :] = value[:, k * LANES : (k + 1) * LANES]
        return carry

    lax.fori_loop(0, half_tiles // tiles, body, 0, unroll=8)


def image_copies(images_hbm, target, sems, first, half, pixels):
    chunk = BLOCK * LANES
    blocks = pixels // (2 * chunk)
    copies = []
    for comp in range(2):
        for step in range(blocks):
            source = pl.multiple_of(comp * pixels + (2 * step + half) * chunk, chunk)
            dest = (comp * blocks + step) * chunk
            copies.append(
                pltpu.make_async_copy(
                    images_hbm.at[:, pl.ds(source, chunk)],
                    target.at[:, pl.ds(dest, chunk)],
                    sems.at[first + len(copies)],
                )
            )
    return copies


def project_other_kernel(
    table_hbm, index_hbm, frac_hbm, images_hbm,
    out_ref, table, index_ref, frac_ref, table_in, flat, wide, blended, sems
):
    device = lax.axis_index("particle")
    row_count = lax.axis_size("particle") // 2
    half_set = device // 2 % 2
    class_id = (2 * (device // 4) + device % 2) // (row_count // CLASSES)
    copies = [
        pltpu.make_async_copy(
            table_hbm.at[pl.ds(half_set, 1), pl.ds(class_id, 1)], table_in, sems.at[0]
        ),
        pltpu.make_async_copy(index_hbm, index_ref, sems.at[1]),
        pltpu.make_async_copy(frac_hbm, frac_ref, sems.at[2]),
    ]
    pixels = index_ref.shape[1]
    copies += image_copies(images_hbm, out_ref, sems, 3, 1 - own_half(), pixels)
    for copy in copies[:3]:
        copy.start()
    copies[0].wait()
    for copy in copies[3:]:
        copy.start()
    highs = flat.shape[1]
    groups = table.shape[0] // 16

    def unfold(step, carry):
        piece = table_in[0, 0, :, pl.ds(step * 8 * LANES, 8 * LANES)].astype(jnp.float32)
        for k in range(8):
            for comp in range(2):
                flat[comp, pl.ds(step * 8 + k, 1), :] = piece[comp : comp + 1, k * LANES : (k + 1) * LANES]
        return carry

    lax.fori_loop(0, highs // 8, unfold, 0, unroll=16)
    picked = []
    for comp in range(2):
        turned = flat[comp].T
        wide[0:LANES, :] = turned
        wide[LANES : LANES + 8, :] = pltpu.roll(turned[0:8], highs - 1, 1)
        picked += [wide[7 * g : 7 * g + 8, :] for g in range(groups)]
    for pair in range(groups):
        table[16 * pair : 16 * (pair + 1), :] = jnp.concatenate(
            picked[2 * pair : 2 * pair + 2], axis=0
        ).astype(jnp.bfloat16)
    copies[1].wait()
    copies[2].wait()
    project_half(table, index_ref, frac_ref, 1 - own_half(), blended)
    parts = out_ref.shape[0]
    for k in range(blended.shape[0] // parts):
        out_ref[:, pixels + k * LANES : pixels + (k + 1) * LANES] = blended[
            k * parts : (k + 1) * parts, :
        ].astype(jnp.bfloat16)
    for copy in copies[3:]:
        copy.wait()


def project_other(class_refs, interp_index, interp_frac, images):
    vox = class_refs.shape[3]
    pixels = interp_index.shape[1]
    highs = vox // LANES
    half_rows = pixels // LANES
    groups = -(-LANES // 7)
    parts = images.shape[0]
    copies = 3 + pixels // (BLOCK * LANES)
    return pl.pallas_call(
        project_other_kernel,
        in_specs=[pl.BlockSpec(memory_space=pltpu.HBM)] * 4,
        out_specs=whole_vmem(4),
        out_shape=[
            jax.ShapeDtypeStruct((parts, pixels + half_rows * LANES // parts), jnp.bfloat16),
            jax.ShapeDtypeStruct((16 * groups, highs), jnp.bfloat16),
            jax.ShapeDtypeStruct((1, pixels), jnp.int32),
            jax.ShapeDtypeStruct((1, pixels), jnp.float32),
        ],
        scratch_shapes=[
            pltpu.VMEM((1, 1, 2, vox), jnp.bfloat16),
            pltpu.VMEM((2, highs, LANES), jnp.float32),
            pltpu.VMEM((LANES + 8, highs), jnp.float32),
            pltpu.VMEM((half_rows, LANES), jnp.float32),
            pltpu.SemaphoreType.DMA((copies,)),
        ],
        compiler_params=pltpu.CompilerParams(vmem_limit_bytes=16 * MIB),
        name="project_other",
    )(*(in_hbm(value) for value in (class_refs, interp_index, interp_frac, images)))


def project_own_kernel(table, index_ref, frac_ref, images_hbm, out_ref, own_images, blended, sems):
    copies = image_copies(images_hbm, own_images, sems, 0, own_half(), index_ref.shape[1])
    for copy in copies:
        copy.start()
    project_half(table, index_ref, frac_ref, own_half(), blended)
    out_ref[...] = blended[...].astype(jnp.bfloat16)
    for copy in copies:
        copy.wait()


def project_own(table, index, frac, images):
    pixels = index.shape[1]
    half_rows = pixels // LANES
    return pl.pallas_call(
        project_own_kernel,
        in_specs=whole_vmem(3) + [pl.BlockSpec(memory_space=pltpu.HBM)],
        out_specs=whole_vmem(2),
        out_shape=[
            jax.ShapeDtypeStruct((half_rows, LANES), jnp.bfloat16),
            jax.ShapeDtypeStruct((images.shape[0], pixels), jnp.bfloat16),
        ],
        scratch_shapes=[
            pltpu.VMEM((half_rows, LANES), jnp.float32),
            pltpu.SemaphoreType.DMA((pixels // (BLOCK * LANES),)),
        ],
        compiler_params=pltpu.CompilerParams(vmem_limit_bytes=16 * MIB),
        cost_estimate=pl.CostEstimate(flops=2000000000, bytes_accessed=8000000, transcendentals=0),
        name="project_own",
    )(table, index, frac, in_hbm(images))


def pair_kernel(own, other, out_ref):
    count = own.shape[0]
    parts, width = other.shape
    tiles = count // parts
    core = own_half()
    out_ref[pl.ds(pl.multiple_of(core * count, count), count), :] = own[...]
    for k in range(tiles):
        lanes = slice(width - (tiles - k) * LANES, width - (tiles - k - 1) * LANES)
        rows = pl.ds(pl.multiple_of((1 - core) * count + k * parts, parts), parts)
        out_ref[rows, :] = other[:, lanes]


def pair_rows(own, other):
    return pl.pallas_call(
        pair_kernel,
        in_specs=whole_vmem(2),
        out_specs=pl.BlockSpec(memory_space=pltpu.VMEM),
        out_shape=jax.ShapeDtypeStruct((2 * own.shape[0], LANES), own.dtype),
        compiler_params=pltpu.CompilerParams(vmem_limit_bytes=16 * MIB),
        name="pair_rows",
    )(own, other)


def chip_order(chips):
    return [0, chips - 1] + list(range(1, chips - 1))


def slot_orientation(device, slot, slots):
    return 2 * ((device // 4) ^ chip_order(slots // 2)[slot // 2]) + slot % 2


def split_mass(mass_row):
    ids = lax.broadcasted_iota(jnp.int32, (MASS_ROWS, LANES), 0)
    upper = mass_row.astype(jnp.bfloat16).astype(jnp.float32)
    lower = mass_row - upper
    return jnp.where(ids == 0, upper, jnp.where(ids == 1, lower, 0.0)).astype(jnp.bfloat16)


def joined_mass(block):
    return jnp.sum(block.astype(jnp.float32), axis=0, keepdims=True)


def fill_tables(shift_ref, cos_ref, sin_ref):
    shifts, width = cos_ref.shape
    same = lax.broadcasted_iota(jnp.int32, (shifts, shifts), 0) == lax.broadcasted_iota(
        jnp.int32, (shifts, shifts), 1
    )
    grid_x, grid_y = (
        jnp.sum(
            jnp.where(same, shift_ref[axis : axis + 1, :].astype(jnp.float32), 0.0),
            axis=1,
            keepdims=True,
        ).astype(jnp.int32)
        for axis in range(2)
    )
    lane = lax.broadcasted_iota(jnp.int32, (shifts, LANES), 1)
    freq_x = (lane // BLOCK) * (2 * BLOCK) + own_half() * BLOCK + lane % BLOCK
    turn_x = (freq_x * grid_x) & (BOX - 1)
    turn_y = ((lane - KY // 2) * grid_y) & (BOX - 1)
    angle_x = turn_x.astype(jnp.float32) * (2.0 * math.pi / BOX)
    angle_y = turn_y.astype(jnp.float32) * (2.0 * math.pi / BOX)
    cos_x, sin_x = jnp.cos(angle_x), jnp.sin(angle_x)
    cos_y, sin_y = jnp.cos(angle_y), jnp.sin(angle_y)
    for j in range(width // LANES):
        where = slice(j * LANES, (j + 1) * LANES)
        cos_j, sin_j = cos_x[:, j : j + 1], sin_x[:, j : j + 1]
        cos_ref[:, where] = cos_j * cos_y - sin_j * sin_y
        sin_ref[:, where] = sin_j * cos_y + cos_j * sin_y


def correlate_first_kernel(shift_ref, own_images, other_images, *refs, chunk):
    pair_refs, (out_ref, cos_ref, sin_ref, proj) = refs[:-4], refs[-4:]
    fill_tables(shift_ref, cos_ref, sin_ref)
    correlate_kernel(
        cos_ref, sin_ref, own_images, other_images, *pair_refs, out_ref, proj, chunk=chunk
    )


def correlate_kernel(cos_ref, sin_ref, own_images, other_images, *refs, chunk):
    pair_refs, (out_ref, proj) = refs[:-2], refs[-2:]
    shifts = cos_ref.shape[0]
    parts = own_images.shape[0]
    slots = 2 * len(pair_refs)
    width = own_images.shape[1] // 2
    tiles = width // LANES
    per_row = 2 * tiles
    combos = shifts * slots
    for slot in range(slots):
        place = slice(slot % 2 * per_row, (slot % 2 + 1) * per_row)
        row = pair_refs[slot // 2][place, :].astype(jnp.float32)
        proj[slot * per_row : (slot + 1) * per_row, :] = row
        out_ref[combos + slot : combos + slot + 1, :] = jnp.sum(row * row, axis=0, keepdims=True)

    chunk_tiles = chunk // LANES
    contract_lanes = (((1,), (1,)), ((), ()))

    def body(step, total):
        first = step * chunk_tiles
        where = pl.ds(pl.multiple_of(step * chunk, chunk), chunk)
        imag_where = pl.ds(pl.multiple_of(width + step * chunk, chunk), chunk)
        cos_part, sin_part = cos_ref[:, where], sin_ref[:, where]
        reals, imags = [], []
        for slot in range(slots):
            start = slot * per_row + first
            real = jnp.concatenate(
                [proj[pl.ds(start + k, 1), :] for k in range(chunk_tiles)], axis=1
            )
            imag = jnp.concatenate(
                [proj[pl.ds(start + tiles + k, 1), :] for k in range(chunk_tiles)], axis=1
            )
            reals.append(real * cos_part - imag * sin_part)
            imags.append(real * sin_part + imag * cos_part)
        turned_real = jnp.concatenate(reals, axis=0).astype(jnp.bfloat16)
        turned_imag = jnp.concatenate(imags, axis=0).astype(jnp.bfloat16)
        image_real = jnp.concatenate([own_images[:, where], other_images[:, where]], axis=0)
        image_imag = jnp.concatenate([own_images[:, imag_where], other_images[:, imag_where]], axis=0)
        total = total + lax.dot_general(
            turned_real, image_real, contract_lanes, preferred_element_type=jnp.float32
        )
        return total + lax.dot_general(
            turned_imag, image_imag, contract_lanes, preferred_element_type=jnp.float32
        )

    total = lax.fori_loop(
        0, width // chunk, body, jnp.zeros((combos, 2 * parts), jnp.float32), unroll=2
    )
    out_ref[0:combos, :] = jnp.zeros((combos, LANES), jnp.float32)
    out_ref[0:combos, 0 : 2 * parts] = total


def correlate(own_images, other_images, pairs, shift_grid=None, tables=None):
    slots = 2 * len(pairs)
    width = own_images.shape[1] // 2
    shifts = shift_grid.shape[0] if tables is None else tables[0].shape[0]
    first = (shift_grid.T,) if tables is None else tuple(tables)
    table = jax.ShapeDtypeStruct((shifts, width), jnp.float32)
    outs = [jax.ShapeDtypeStruct((shifts * slots + slots, LANES), jnp.float32)]
    outs += [table, table] if tables is None else []
    kernel = correlate_first_kernel if tables is None else correlate_kernel
    return pl.pallas_call(
        functools.partial(kernel, chunk=4096),
        in_specs=whole_vmem(len(first) + 2 + len(pairs)),
        out_specs=whole_vmem(len(outs)),
        out_shape=outs,
        scratch_shapes=[pltpu.VMEM((slots * 2 * width // LANES, LANES), jnp.float32)],
        compiler_params=pltpu.CompilerParams(vmem_limit_bytes=(14 + slots) * MIB),
        cost_estimate=pl.CostEstimate(flops=1000000000, bytes_accessed=4000000, transcendentals=0),
        name="correlate",
    )(*first, own_images, other_images, *pairs)


def collect_kernel(*refs, combos):
    parts_refs, (precision_ref, assigned_ref, out_ref) = refs[:-3], refs[-3:]
    count = len(parts_refs)
    slots = parts_refs[0].shape[0] - combos
    parts = precision_ref.shape[1]
    for index, ref in enumerate(parts_refs):
        out_ref[index * combos : (index + 1) * combos, :] = ref[0:combos, :]
        power = count * combos + index * slots
        out_ref[power : power + slots, :] = ref[combos:, :]
    rest = count * (combos + slots)
    out_ref[rest:, :] = jnp.zeros((8, LANES), jnp.float32)
    out_ref[rest : rest + 1, 0:parts] = precision_ref[...]
    out_ref[rest + 1 : rest + 2, 0:parts] = assigned_ref[...].astype(jnp.float32)


def collect(passes, precision, assigned, combos):
    rows = len(passes) * passes[0].shape[0] + 8
    return pl.pallas_call(
        functools.partial(collect_kernel, combos=combos),
        in_specs=whole_vmem(2 + len(passes)),
        out_specs=pl.BlockSpec(memory_space=pltpu.VMEM),
        out_shape=jax.ShapeDtypeStruct((rows, LANES), jnp.float32),
        compiler_params=pltpu.CompilerParams(vmem_limit_bytes=16 * MIB),
        name="collect",
    )(*passes, precision, assigned)


def rotate_back(weights, own_images, other_images, cos_ref, sin_ref, where, imag_where, slots):
    image_real = jnp.concatenate([own_images[:, where], other_images[:, where]], axis=0)
    image_imag = jnp.concatenate([own_images[:, imag_where], other_images[:, imag_where]], axis=0)
    from_real = jnp.dot(weights, image_real, preferred_element_type=jnp.float32)
    from_imag = jnp.dot(weights, image_imag, preferred_element_type=jnp.float32)
    real = imag = None
    for s in range(cos_ref.shape[0]):
        cos_s, sin_s = cos_ref[s : s + 1, where], sin_ref[s : s + 1, where]
        part_real = from_real[s * slots : (s + 1) * slots]
        part_imag = from_imag[s * slots : (s + 1) * slots]
        real_s = part_real * cos_s + part_imag * sin_s
        imag_s = part_imag * cos_s - part_real * sin_s
        real = real_s if real is None else real + real_s
        imag = imag_s if imag is None else imag + imag_s
    return real, imag


def posterior_kernel(
    mine, received, own_images, other_images, cos_ref, sin_ref,
    weight_ref, low_ref, low_send, own_mass, ordered, *, slots
):
    device = lax.axis_index("particle")
    shifts, width = cos_ref.shape
    parts = own_images.shape[0]
    combos = shifts * slots
    theirs = received[...]
    lane = lax.broadcasted_iota(jnp.int32, theirs.shape, 1)
    swapped = jnp.where(
        lane < parts, pltpu.roll(theirs, LANES - parts, 1), pltpu.roll(theirs, parts, 1)
    )
    joint = mine[...] + swapped
    power = jnp.sum(
        mine[combos : combos + slots, :] + received[combos : combos + slots, :], axis=1, keepdims=True
    )
    precision = joint[combos + slots : combos + slots + 1]
    assigned = joint[combos + slots + 1 : combos + slots + 2].astype(jnp.int32)
    likelihood_scale = 1.0 / math.sqrt(4 * width)
    classes = [slot_orientation(device, slot, slots) // (slots // CLASSES) for slot in range(slots)]
    logits = []
    for slot in range(slots):
        match = (assigned == classes[slot]).astype(jnp.float32) * PRIOR_REWARD
        part = joint[slot * shifts : (slot + 1) * shifts]
        logits.append(precision * (part - 0.5 * power[slot : slot + 1]) * likelihood_scale + match)
    peak = jnp.max(functools.reduce(jnp.maximum, logits), axis=0, keepdims=True)
    terms = [jnp.exp(value - peak) for value in logits]
    norm = jnp.sum(functools.reduce(jnp.add, terms), axis=0, keepdims=True)
    counted = lax.broadcasted_iota(jnp.int32, (1, LANES), 1) < 2 * parts
    class_lane = lax.broadcasted_iota(jnp.int32, (1, LANES), 1)
    mass_row = jnp.zeros((1, LANES), jnp.float32)
    for slot in range(slots):
        value = terms[slot] / norm
        ordered[slot * shifts : (slot + 1) * shifts, :] = value
        share = jnp.where(counted, jnp.sum(value, axis=0, keepdims=True) * precision, 0.0)
        share = jnp.sum(share, axis=1, keepdims=True)
        mass_row = mass_row + jnp.where(class_lane == classes[slot], share, 0.0)
    weights = jnp.concatenate(
        [ordered[pl.ds(s, slots, stride=shifts), :] for s in range(shifts)], axis=0
    )
    weights = weights[:, 0 : 2 * parts].astype(jnp.bfloat16)
    weight_ref[...] = weights
    own_mass[...] = jnp.broadcast_to(mass_row, own_mass.shape)

    low = LOW_TILES * LANES
    real, imag = rotate_back(
        weights, own_images, other_images, cos_ref, sin_ref, slice(0, low), slice(width, width + low), slots
    )
    for k in range(LOW_TILES):
        piece = slice(k * LANES, (k + 1) * LANES)
        low_ref[pl.ds(k, slots, stride=2 * LOW_TILES), :] = real[:, piece]
        low_ref[pl.ds(LOW_TILES + k, slots, stride=2 * LOW_TILES), :] = imag[:, piece]
    low_body = low_ref.shape[0]
    low_send[0:low_body, :] = low_ref[...].astype(jnp.bfloat16)
    low_send[low_body:, :] = split_mass(mass_row)


def posterior(mine, received, own_images, other_images, cos_table, sin_table, slots):
    shifts = cos_table.shape[0]
    low = slots * 2 * LOW_TILES
    return pl.pallas_call(
        functools.partial(posterior_kernel, slots=slots),
        in_specs=whole_vmem(6),
        out_specs=whole_vmem(4),
        out_shape=[
            jax.ShapeDtypeStruct((shifts * slots, 2 * own_images.shape[0]), jnp.bfloat16),
            jax.ShapeDtypeStruct((low, LANES), jnp.float32),
            jax.ShapeDtypeStruct((low + MASS_ROWS, LANES), jnp.bfloat16),
            jax.ShapeDtypeStruct((8, LANES), jnp.float32),
        ],
        scratch_shapes=[pltpu.VMEM((shifts * slots, LANES), jnp.float32)],
        compiler_params=pltpu.CompilerParams(vmem_limit_bytes=(14 + slots // 2) * MIB),
        name="posterior",
    )(mine, received, own_images, other_images, cos_table, sin_table)


def backproject_kernel(
    weight_ref, own_images, other_images, cos_ref, sin_ref, own, *refs, slots, chunk, unroll
):
    sends, sums = refs[:-1], refs[-1]
    width = cos_ref.shape[1]
    tiles = width // LANES - LOW_TILES
    per_row = 2 * tiles
    chunk_tiles = chunk // LANES
    weights = weight_ref[...]

    def body(step, carry):
        first = step * chunk_tiles
        start = pl.multiple_of((LOW_TILES + first) * LANES, LOW_TILES * LANES)
        where = pl.ds(start, chunk)
        imag_where = pl.ds(pl.multiple_of(width + start, LOW_TILES * LANES), chunk)
        real, imag = rotate_back(
            weights, own_images, other_images, cos_ref, sin_ref, where, imag_where, slots
        )
        for k in range(chunk_tiles):
            piece = slice(k * LANES, (k + 1) * LANES)
            sums[pl.ds(first + k, slots, stride=per_row), :] = real[:, piece]
            sums[pl.ds(tiles + first + k, slots, stride=per_row), :] = imag[:, piece]
        return carry

    lax.fori_loop(0, tiles // chunk_tiles, body, 0, unroll=unroll)
    own[...] = sums[0 : 2 * per_row, :]
    for m, send in enumerate(sends, start=1):
        send[...] = sums[2 * m * per_row : 2 * (m + 1) * per_row, :].astype(jnp.bfloat16)


def backproject(weights, own_images, other_images, cos_table, sin_table, slots):
    width = cos_table.shape[1]
    rows = 2 * 2 * (width // LANES - LOW_TILES)
    chips = slots // 2
    return pl.pallas_call(
        functools.partial(
            backproject_kernel, slots=slots, chunk=LOW_TILES * LANES, unroll=7 if slots <= 8 else 1
        ),
        in_specs=whole_vmem(5),
        out_specs=whole_vmem(chips),
        out_shape=[jax.ShapeDtypeStruct((rows, LANES), jnp.float32)]
        + [jax.ShapeDtypeStruct((rows, LANES), jnp.bfloat16)] * (chips - 1),
        scratch_shapes=[pltpu.VMEM((chips * rows, LANES), jnp.float32)],
        compiler_params=pltpu.CompilerParams(vmem_limit_bytes=(14 + slots // 2) * MIB),
        cost_estimate=pl.CostEstimate(flops=2000000000, bytes_accessed=8000000, transcendentals=0),
        name="backproject",
    )(weights, own_images, other_images, cos_table, sin_table)


def fold_kernel(low_ref, low_received, mass, *refs, chips):
    mains, (own, own_mass), sends = refs[: chips - 1], refs[chips - 1 : chips + 1], refs[chips + 1 :]
    rows = own.shape[0]
    low_body = low_ref.shape[0]
    total_mass = mass[0:1, :] + joined_mass(low_received[low_body:, :])
    block = split_mass(total_mass)
    own_mass[...] = jnp.broadcast_to(total_mass, own_mass.shape)
    for m, target in enumerate((own,) + tuple(sends)):
        part = slice(m * rows, (m + 1) * rows)
        value = (low_ref[part, :] + low_received[part, :].astype(jnp.float32)) * 0.5
        target[0:rows, :] = value.astype(target.dtype)
        if m > 0:
            target[rows : rows + MASS_ROWS, :] = block
            target[rows + MASS_ROWS :, :] = mains[m - 1][...]


def fold(low, low_received, mass, mains):
    chips = len(mains) + 1
    rows = low.shape[0] // chips
    return pl.pallas_call(
        functools.partial(fold_kernel, chips=chips),
        in_specs=whole_vmem(2 + chips),
        out_specs=whole_vmem(1 + chips),
        out_shape=[
            jax.ShapeDtypeStruct((rows, LANES), jnp.float32),
            jax.ShapeDtypeStruct((8, LANES), jnp.float32),
        ]
        + [
            jax.ShapeDtypeStruct((rows + MASS_ROWS + main.shape[0], LANES), jnp.bfloat16)
            for main in mains
        ],
        compiler_params=pltpu.CompilerParams(vmem_limit_bytes=16 * MIB),
        name="fold",
    )(low, low_received, mass, *mains)


def merge_kernel(own, own_low, mass, *refs):
    received, (keep, to_core, mass_out) = refs[:-3], refs[-3:]
    core = own_half()
    low_rows = own_low.shape[0]
    low_half = low_rows // 2
    head = low_rows + MASS_ROWS
    half = own.shape[0] // 2
    total_mass = mass[0:1, :]
    for ref in received:
        total_mass = total_mass + joined_mass(ref[low_rows:head, :])
    mass_out[...] = jnp.broadcast_to(total_mass, mass_out.shape)
    for target, place in ((to_core, 1 - core), (keep, core)):
        start = pl.multiple_of(place * half, half)
        total = own[pl.ds(start, half), :]
        for ref in received:
            total = total + ref[pl.ds(head + start, half), :].astype(jnp.float32)
        where = pl.ds(pl.multiple_of(place * low_half, low_half), low_half)
        low = own_low[where, :]
        for ref in received:
            low = low + ref[where, :].astype(jnp.float32)
        target[...] = jnp.concatenate(
            [low[0:LOW_TILES], total[0 : half // 2], low[LOW_TILES:], total[half // 2 :]], axis=0
        ).astype(target.dtype)


def merge(own, own_low, mass, received):
    rows = (own.shape[0] + own_low.shape[0]) // 2
    return pl.pallas_call(
        merge_kernel,
        in_specs=whole_vmem(3 + len(received)),
        out_specs=whole_vmem(3),
        out_shape=[
            jax.ShapeDtypeStruct((rows, LANES), jnp.float32),
            jax.ShapeDtypeStruct((rows, LANES), jnp.bfloat16),
            jax.ShapeDtypeStruct((8, LANES), jnp.float32),
        ],
        compiler_params=pltpu.CompilerParams(vmem_limit_bytes=16 * MIB),
        name="merge",
    )(own, own_low, mass, *received)


def finish_kernel(own, received, mass, out, mass_out, *, scale, mass_scale):
    core = own_half()
    mass_out[...] = mass[0, :CLASSES] * mass_scale
    for step in range(own.shape[0] // BLOCK):
        rows = slice(step * BLOCK, (step + 1) * BLOCK)
        own_rows = pl.ds(pl.multiple_of((2 * step + core) * BLOCK, BLOCK), BLOCK)
        other_rows = pl.ds(pl.multiple_of((2 * step + 1 - core) * BLOCK, BLOCK), BLOCK)
        out[own_rows, :] = own[rows, :] * scale
        out[other_rows, :] = received[rows, :].astype(jnp.float32) * scale


def finish(own, received, mass, scale, mass_scale):
    return pl.pallas_call(
        functools.partial(finish_kernel, scale=scale, mass_scale=mass_scale),
        in_specs=whole_vmem(3),
        out_specs=whole_vmem(2),
        out_shape=[
            jax.ShapeDtypeStruct((2 * own.shape[0], LANES), jnp.float32),
            jax.ShapeDtypeStruct((CLASSES,), jnp.float32),
        ],
        compiler_params=pltpu.CompilerParams(vmem_limit_bytes=16 * MIB),
        name="finish",
    )(own, received, mass)


def local(
    images, noise_precision, assigned_class, class_refs, interp_index, interp_frac, shift_grid
):
    dev_count = lax.axis_size("particle")
    slots = dev_count // 2
    chips = slots // 2
    parts, width = images.shape
    to_core, table, index, frac = project_other(class_refs, interp_index, interp_frac, images)
    images_received = exchange(to_core, 1)
    own, own_images = project_own(table, index, frac, images)
    pair = pair_rows(own, images_received)
    others = chip_order(chips)[1:]
    pairs = [pair] + [exchange(pair, 4 * m) for m in others]
    group = chips // 2
    first, cos_table, sin_table = correlate(
        own_images, images_received, pairs[:group], shift_grid=shift_grid
    )
    passes = [first]
    for start in range(group, chips, group):
        passes += correlate(
            own_images,
            images_received,
            pairs[start : start + group],
            tables=(cos_table, sin_table),
        )
    mine = collect(
        passes,
        noise_precision.reshape(1, parts),
        assigned_class.reshape(1, parts),
        shift_grid.shape[0] * 2 * group,
    )
    weights, low, low_send, mass = posterior(
        mine, exchange(mine, 1), own_images, images_received, cos_table, sin_table, slots
    )
    low_from_half = exchange(low_send, 2)
    sums = backproject(weights, own_images, images_received, cos_table, sin_table, slots)
    folded = fold(low, low_from_half, mass, sums[1:])
    chip_sums = [exchange(send, 4 * m) for m, send in zip(others, folded[2:])]
    keep, send, mass = merge(sums[0], folded[0], folded[1], chip_sums)
    back, class_mass = finish(
        keep, exchange(send, 1), mass, 1.0 / math.sqrt(parts), CLASSES / (parts * dev_count)
    )
    return back.reshape(1, width), class_mass


def solution(mesh):
    in_specs = (
        P(("groups", "particle"), None),
        P(("groups", "particle")),
        P(("groups", "particle")),
        P("groups", None, None, None),
        P("particle", None),
        P("particle", None),
        P(),
    )
    out_specs = (P(("groups", "particle"), None), P("groups"))
    return jax.shard_map(local, mesh=mesh, in_specs=in_specs, out_specs=out_specs, check_vma=False)
```

```python
import functools
import math

import jax
import jax.numpy as jnp
from jax import lax
from jax.experimental import pallas as pl
from jax.experimental.pallas import tpu as pltpu
from jax.sharding import PartitionSpec as P

KY = 128
BOX = 256
CLASSES = 8
LOWK = 16
LANES = 128
PRIOR_REWARD = 1.0
MASS_ROWS = 16
BLOCK = 8
PROJECT_CHUNK = 512
LOW_TILES = LOWK * KY // LANES // 2
MIB = 1 << 20


def exchange(value, mask):
    pairs = [(source, source ^ mask) for source in range(lax.axis_size("particle"))]
    return lax.ppermute(value, "particle", pairs)


def in_hbm(value):
    return pltpu.with_memory_space_constraint(value, pltpu.HBM)


def whole_vmem(count):
    return [pl.BlockSpec(memory_space=pltpu.VMEM)] * count


def own_half():
    return lax.axis_index("particle") % 2


def tree_select(values, masks):
    for mask in masks:
        values = [
            jnp.where(mask, values[i + 1], values[i]) if i + 1 < len(values) else values[i]
            for i in range(0, len(values), 2)
        ]
    return values[0]


def project_half(table, index_ref, frac_ref, half, blended):
    pixels = index_ref.shape[1]
    highs = table.shape[1]
    groups = table.shape[0] // 16
    stride = 8 * groups
    chunk = PROJECT_CHUNK
    tiles = chunk // LANES
    per_block = BLOCK // tiles
    half_tiles = pixels // (2 * LANES)

    def body(step, carry):
        block = 2 * (step // per_block) + half
        where = pl.ds(pl.multiple_of((block * per_block + step % per_block) * chunk, chunk), chunk)
        index = index_ref[:, where]
        frac = frac_ref[:, where]
        high = index >> 7
        low = index & (LANES - 1)
        group = (low * 147) >> 10
        first = low - 7 * group
        high_ids = lax.broadcasted_iota(jnp.int32, (highs, chunk), 0)
        one_hot = jnp.where(high_ids == high, 1.0, 0.0).astype(jnp.bfloat16)
        rows = jnp.dot(table[...], one_hot, preferred_element_type=jnp.float32)
        group = jnp.broadcast_to(group, (8, chunk))
        masks = [(group & (1 << bit)) != 0 for bit in range((groups - 1).bit_length())]
        ids = lax.broadcasted_iota(jnp.int32, (8, chunk), 0)
        weight = jnp.where(ids == first, 1.0 - frac, jnp.where(ids == first + 1, frac, 0.0))
        for comp in range(2):
            start = comp * stride
            picked = tree_select([rows[start + 8 * g : start + 8 * g + 8] for g in range(groups)], masks)
            value = jnp.sum(picked * weight, axis=0, keepdims=True)
            for k in range(tiles):
                row = comp * half_tiles + step * tiles + k
                blended[pl.ds(row, 1), :] = value[:, k * LANES : (k + 1) * LANES]
        return carry

    lax.fori_loop(0, half_tiles // tiles, body, 0, unroll=16)


def image_copies(images_hbm, target, sems, first, half, pixels):
    chunk = BLOCK * LANES
    blocks = pixels // (2 * chunk)
    copies = []
    for comp in range(2):
        for step in range(blocks):
            source = pl.multiple_of(comp * pixels + (2 * step + half) * chunk, chunk)
            dest = (comp * blocks + step) * chunk
            copies.append(
                pltpu.make_async_copy(
                    images_hbm.at[:, pl.ds(source, chunk)],
                    target.at[:, pl.ds(dest, chunk)],
                    sems.at[first + len(copies)],
                )
            )
    return copies


def project_other_kernel(
    table_hbm, index_hbm, frac_hbm, images_hbm,
    out_ref, table, index_ref, frac_ref, table_in, flat, wide, blended, sems
):
    device = lax.axis_index("particle")
    row_count = lax.axis_size("particle") // 2
    half_set = device // 2 % 2
    class_id = (2 * (device // 4) + device % 2) // (row_count // CLASSES)
    copies = [
        pltpu.make_async_copy(
            table_hbm.at[pl.ds(half_set, 1), pl.ds(class_id, 1)], table_in, sems.at[0]
        ),
        pltpu.make_async_copy(index_hbm, index_ref, sems.at[1]),
        pltpu.make_async_copy(frac_hbm, frac_ref, sems.at[2]),
    ]
    pixels = index_ref.shape[1]
    copies += image_copies(images_hbm, out_ref, sems, 3, 1 - own_half(), pixels)
    for copy in copies[:3]:
        copy.start()
    copies[0].wait()
    for copy in copies[3:]:
        copy.start()
    highs = flat.shape[1]
    groups = table.shape[0] // 16

    def unfold(step, carry):
        piece = table_in[0, 0, :, pl.ds(step * 8 * LANES, 8 * LANES)].astype(jnp.float32)
        for k in range(8):
            for comp in range(2):
                flat[comp, pl.ds(step * 8 + k, 1), :] = piece[comp : comp + 1, k * LANES : (k + 1) * LANES]
        return carry

    lax.fori_loop(0, highs // 8, unfold, 0, unroll=16)
    picked = []
    for comp in range(2):
        turned = flat[comp].T
        wide[0:LANES, :] = turned
        wide[LANES : LANES + 8, :] = pltpu.roll(turned[0:8], highs - 1, 1)
        picked += [wide[7 * g : 7 * g + 8, :] for g in range(groups)]
    for pair in range(groups):
        table[16 * pair : 16 * (pair + 1), :] = jnp.concatenate(
            picked[2 * pair : 2 * pair + 2], axis=0
        ).astype(jnp.bfloat16)
    copies[1].wait()
    copies[2].wait()
    project_half(table, index_ref, frac_ref, 1 - own_half(), blended)
    parts = out_ref.shape[0]
    for k in range(blended.shape[0] // parts):
        out_ref[:, pixels + k * LANES : pixels + (k + 1) * LANES] = blended[
            k * parts : (k + 1) * parts, :
        ].astype(jnp.bfloat16)
    for copy in copies[3:]:
        copy.wait()


def project_other(class_refs, interp_index, interp_frac, images):
    vox = class_refs.shape[3]
    pixels = interp_index.shape[1]
    highs = vox // LANES
    half_rows = pixels // LANES
    groups = -(-LANES // 7)
    parts = images.shape[0]
    copies = 3 + pixels // (BLOCK * LANES)
    return pl.pallas_call(
        project_other_kernel,
        in_specs=[pl.BlockSpec(memory_space=pltpu.HBM)] * 4,
        out_specs=whole_vmem(4),
        out_shape=[
            jax.ShapeDtypeStruct((parts, pixels + half_rows * LANES // parts), jnp.bfloat16),
            jax.ShapeDtypeStruct((16 * groups, highs), jnp.bfloat16),
            jax.ShapeDtypeStruct((1, pixels), jnp.int32),
            jax.ShapeDtypeStruct((1, pixels), jnp.float32),
        ],
        scratch_shapes=[
            pltpu.VMEM((1, 1, 2, vox), jnp.bfloat16),
            pltpu.VMEM((2, highs, LANES), jnp.float32),
            pltpu.VMEM((LANES + 8, highs), jnp.float32),
            pltpu.VMEM((half_rows, LANES), jnp.float32),
            pltpu.SemaphoreType.DMA((copies,)),
        ],
        compiler_params=pltpu.CompilerParams(vmem_limit_bytes=16 * MIB),
        name="project_other",
    )(*(in_hbm(value) for value in (class_refs, interp_index, interp_frac, images)))


def project_own_kernel(table, index_ref, frac_ref, images_hbm, out_ref, own_images, blended, sems):
    copies = image_copies(images_hbm, own_images, sems, 0, own_half(), index_ref.shape[1])
    for copy in copies:
        copy.start()
    project_half(table, index_ref, frac_ref, own_half(), blended)
    out_ref[...] = blended[...].astype(jnp.bfloat16)
    for copy in copies:
        copy.wait()


def project_own(table, index, frac, images):
    pixels = index.shape[1]
    half_rows = pixels // LANES
    return pl.pallas_call(
        project_own_kernel,
        in_specs=whole_vmem(3) + [pl.BlockSpec(memory_space=pltpu.HBM)],
        out_specs=whole_vmem(2),
        out_shape=[
            jax.ShapeDtypeStruct((half_rows, LANES), jnp.bfloat16),
            jax.ShapeDtypeStruct((images.shape[0], pixels), jnp.bfloat16),
        ],
        scratch_shapes=[
            pltpu.VMEM((half_rows, LANES), jnp.float32),
            pltpu.SemaphoreType.DMA((pixels // (BLOCK * LANES),)),
        ],
        compiler_params=pltpu.CompilerParams(vmem_limit_bytes=16 * MIB),
        cost_estimate=pl.CostEstimate(flops=2000000000, bytes_accessed=8000000, transcendentals=0),
        name="project_own",
    )(table, index, frac, in_hbm(images))


def pair_kernel(own, other, out_ref):
    count = own.shape[0]
    parts, width = other.shape
    tiles = count // parts
    core = own_half()
    out_ref[pl.ds(pl.multiple_of(core * count, count), count), :] = own[...]
    for k in range(tiles):
        lanes = slice(width - (tiles - k) * LANES, width - (tiles - k - 1) * LANES)
        rows = pl.ds(pl.multiple_of((1 - core) * count + k * parts, parts), parts)
        out_ref[rows, :] = other[:, lanes]


def pair_rows(own, other):
    return pl.pallas_call(
        pair_kernel,
        in_specs=whole_vmem(2),
        out_specs=pl.BlockSpec(memory_space=pltpu.VMEM),
        out_shape=jax.ShapeDtypeStruct((2 * own.shape[0], LANES), own.dtype),
        compiler_params=pltpu.CompilerParams(vmem_limit_bytes=16 * MIB),
        name="pair_rows",
    )(own, other)


def chip_order(chips):
    return [0, chips - 1] + list(range(1, chips - 1))


def slot_orientation(device, slot, slots):
    return 2 * ((device // 4) ^ chip_order(slots // 2)[slot // 2]) + slot % 2


def split_mass(mass_row):
    ids = lax.broadcasted_iota(jnp.int32, (MASS_ROWS, LANES), 0)
    upper = mass_row.astype(jnp.bfloat16).astype(jnp.float32)
    lower = mass_row - upper
    return jnp.where(ids == 0, upper, jnp.where(ids == 1, lower, 0.0)).astype(jnp.bfloat16)


def joined_mass(block):
    return jnp.sum(block.astype(jnp.float32), axis=0, keepdims=True)


def fill_tables(shift_ref, cos_ref, sin_ref):
    shifts, width = cos_ref.shape
    same = lax.broadcasted_iota(jnp.int32, (shifts, shifts), 0) == lax.broadcasted_iota(
        jnp.int32, (shifts, shifts), 1
    )
    grid_x, grid_y = (
        jnp.sum(
            jnp.where(same, shift_ref[axis : axis + 1, :].astype(jnp.float32), 0.0),
            axis=1,
            keepdims=True,
        ).astype(jnp.int32)
        for axis in range(2)
    )
    lane = lax.broadcasted_iota(jnp.int32, (shifts, LANES), 1)
    freq_x = (lane // BLOCK) * (2 * BLOCK) + own_half() * BLOCK + lane % BLOCK
    turn_x = (freq_x * grid_x) & (BOX - 1)
    turn_y = ((lane - KY // 2) * grid_y) & (BOX - 1)
    angle_x = turn_x.astype(jnp.float32) * (2.0 * math.pi / BOX)
    angle_y = turn_y.astype(jnp.float32) * (2.0 * math.pi / BOX)
    cos_x, sin_x = jnp.cos(angle_x), jnp.sin(angle_x)
    cos_y, sin_y = jnp.cos(angle_y), jnp.sin(angle_y)
    for j in range(width // LANES):
        where = slice(j * LANES, (j + 1) * LANES)
        cos_j, sin_j = cos_x[:, j : j + 1], sin_x[:, j : j + 1]
        cos_ref[:, where] = cos_j * cos_y - sin_j * sin_y
        sin_ref[:, where] = sin_j * cos_y + cos_j * sin_y


def correlate_first_kernel(shift_ref, own_images, other_images, *refs, chunk):
    pair_refs, (out_ref, cos_ref, sin_ref, proj) = refs[:-4], refs[-4:]
    fill_tables(shift_ref, cos_ref, sin_ref)
    correlate_kernel(
        cos_ref, sin_ref, own_images, other_images, *pair_refs, out_ref, proj, chunk=chunk
    )


def correlate_kernel(cos_ref, sin_ref, own_images, other_images, *refs, chunk):
    pair_refs, (out_ref, proj) = refs[:-2], refs[-2:]
    shifts = cos_ref.shape[0]
    parts = own_images.shape[0]
    slots = 2 * len(pair_refs)
    width = own_images.shape[1] // 2
    tiles = width // LANES
    per_row = 2 * tiles
    combos = shifts * slots
    for slot in range(slots):
        place = slice(slot % 2 * per_row, (slot % 2 + 1) * per_row)
        row = pair_refs[slot // 2][place, :].astype(jnp.float32)
        proj[slot * per_row : (slot + 1) * per_row, :] = row
        out_ref[combos + slot : combos + slot + 1, :] = jnp.sum(row * row, axis=0, keepdims=True)

    chunk_tiles = chunk // LANES
    contract_lanes = (((1,), (1,)), ((), ()))

    def body(step, total):
        first = step * chunk_tiles
        where = pl.ds(pl.multiple_of(step * chunk, chunk), chunk)
        imag_where = pl.ds(pl.multiple_of(width + step * chunk, chunk), chunk)
        cos_part, sin_part = cos_ref[:, where], sin_ref[:, where]
        reals, imags = [], []
        for slot in range(slots):
            start = slot * per_row + first
            real = jnp.concatenate(
                [proj[pl.ds(start + k, 1), :] for k in range(chunk_tiles)], axis=1
            )
            imag = jnp.concatenate(
                [proj[pl.ds(start + tiles + k, 1), :] for k in range(chunk_tiles)], axis=1
            )
            reals.append(real * cos_part - imag * sin_part)
            imags.append(real * sin_part + imag * cos_part)
        turned_real = jnp.concatenate(reals, axis=0).astype(jnp.bfloat16)
        turned_imag = jnp.concatenate(imags, axis=0).astype(jnp.bfloat16)
        image_real = jnp.concatenate([own_images[:, where], other_images[:, where]], axis=0)
        image_imag = jnp.concatenate([own_images[:, imag_where], other_images[:, imag_where]], axis=0)
        total = total + lax.dot_general(
            turned_real, image_real, contract_lanes, preferred_element_type=jnp.float32
        )
        return total + lax.dot_general(
            turned_imag, image_imag, contract_lanes, preferred_element_type=jnp.float32
        )

    total = lax.fori_loop(
        0, width // chunk, body, jnp.zeros((combos, 2 * parts), jnp.float32), unroll=2
    )
    out_ref[0:combos, :] = jnp.zeros((combos, LANES), jnp.float32)
    out_ref[0:combos, 0 : 2 * parts] = total


def correlate(own_images, other_images, pairs, shift_grid=None, tables=None):
    slots = 2 * len(pairs)
    width = own_images.shape[1] // 2
    shifts = shift_grid.shape[0] if tables is None else tables[0].shape[0]
    first = (shift_grid.T,) if tables is None else tuple(tables)
    table = jax.ShapeDtypeStruct((shifts, width), jnp.float32)
    outs = [jax.ShapeDtypeStruct((shifts * slots + slots, LANES), jnp.float32)]
    outs += [table, table] if tables is None else []
    kernel = correlate_first_kernel if tables is None else correlate_kernel
    return pl.pallas_call(
        functools.partial(kernel, chunk=4096),
        in_specs=whole_vmem(len(first) + 2 + len(pairs)),
        out_specs=whole_vmem(len(outs)),
        out_shape=outs,
        scratch_shapes=[pltpu.VMEM((slots * 2 * width // LANES, LANES), jnp.float32)],
        compiler_params=pltpu.CompilerParams(vmem_limit_bytes=(14 + slots) * MIB),
        cost_estimate=pl.CostEstimate(flops=1000000000, bytes_accessed=4000000, transcendentals=0),
        name="correlate",
    )(*first, own_images, other_images, *pairs)


def collect_kernel(*refs, combos):
    parts_refs, (precision_ref, assigned_ref, out_ref) = refs[:-3], refs[-3:]
    count = len(parts_refs)
    slots = parts_refs[0].shape[0] - combos
    parts = precision_ref.shape[1]
    for index, ref in enumerate(parts_refs):
        out_ref[index * combos : (index + 1) * combos, :] = ref[0:combos, :]
        power = count * combos + index * slots
        out_ref[power : power + slots, :] = ref[combos:, :]
    rest = count * (combos + slots)
    out_ref[rest:, :] = jnp.zeros((8, LANES), jnp.float32)
    out_ref[rest : rest + 1, 0:parts] = precision_ref[...]
    out_ref[rest + 1 : rest + 2, 0:parts] = assigned_ref[...].astype(jnp.float32)


def collect(passes, precision, assigned, combos):
    rows = len(passes) * passes[0].shape[0] + 8
    return pl.pallas_call(
        functools.partial(collect_kernel, combos=combos),
        in_specs=whole_vmem(2 + len(passes)),
        out_specs=pl.BlockSpec(memory_space=pltpu.VMEM),
        out_shape=jax.ShapeDtypeStruct((rows, LANES), jnp.float32),
        compiler_params=pltpu.CompilerParams(vmem_limit_bytes=16 * MIB),
        name="collect",
    )(*passes, precision, assigned)


def rotate_back(weights, own_images, other_images, cos_ref, sin_ref, where, imag_where, slots):
    image_real = jnp.concatenate([own_images[:, where], other_images[:, where]], axis=0)
    image_imag = jnp.concatenate([own_images[:, imag_where], other_images[:, imag_where]], axis=0)
    from_real = jnp.dot(weights, image_real, preferred_element_type=jnp.float32)
    from_imag = jnp.dot(weights, image_imag, preferred_element_type=jnp.float32)
    real = imag = None
    for s in range(cos_ref.shape[0]):
        cos_s, sin_s = cos_ref[s : s + 1, where], sin_ref[s : s + 1, where]
        part_real = from_real[s * slots : (s + 1) * slots]
        part_imag = from_imag[s * slots : (s + 1) * slots]
        real_s = part_real * cos_s + part_imag * sin_s
        imag_s = part_imag * cos_s - part_real * sin_s
        real = real_s if real is None else real + real_s
        imag = imag_s if imag is None else imag + imag_s
    return real, imag


def posterior_kernel(
    mine, received, own_images, other_images, cos_ref, sin_ref,
    weight_ref, low_ref, low_send, own_mass, ordered, *, slots
):
    device = lax.axis_index("particle")
    shifts, width = cos_ref.shape
    parts = own_images.shape[0]
    combos = shifts * slots
    theirs = received[...]
    lane = lax.broadcasted_iota(jnp.int32, theirs.shape, 1)
    swapped = jnp.where(
        lane < parts, pltpu.roll(theirs, LANES - parts, 1), pltpu.roll(theirs, parts, 1)
    )
    joint = mine[...] + swapped
    power = jnp.sum(
        mine[combos : combos + slots, :] + received[combos : combos + slots, :], axis=1, keepdims=True
    )
    precision = joint[combos + slots : combos + slots + 1]
    assigned = joint[combos + slots + 1 : combos + slots + 2].astype(jnp.int32)
    likelihood_scale = 1.0 / math.sqrt(4 * width)
    classes = [slot_orientation(device, slot, slots) // (slots // CLASSES) for slot in range(slots)]
    logits = []
    for slot in range(slots):
        match = (assigned == classes[slot]).astype(jnp.float32) * PRIOR_REWARD
        part = joint[slot * shifts : (slot + 1) * shifts]
        logits.append(precision * (part - 0.5 * power[slot : slot + 1]) * likelihood_scale + match)
    peak = jnp.max(functools.reduce(jnp.maximum, logits), axis=0, keepdims=True)
    terms = [jnp.exp(value - peak) for value in logits]
    norm = jnp.sum(functools.reduce(jnp.add, terms), axis=0, keepdims=True)
    counted = lax.broadcasted_iota(jnp.int32, (1, LANES), 1) < 2 * parts
    class_lane = lax.broadcasted_iota(jnp.int32, (1, LANES), 1)
    mass_row = jnp.zeros((1, LANES), jnp.float32)
    for slot in range(slots):
        value = terms[slot] / norm
        ordered[slot * shifts : (slot + 1) * shifts, :] = value
        share = jnp.where(counted, jnp.sum(value, axis=0, keepdims=True) * precision, 0.0)
        share = jnp.sum(share, axis=1, keepdims=True)
        mass_row = mass_row + jnp.where(class_lane == classes[slot], share, 0.0)
    weights = jnp.concatenate(
        [ordered[pl.ds(s, slots, stride=shifts), :] for s in range(shifts)], axis=0
    )
    weights = weights[:, 0 : 2 * parts].astype(jnp.bfloat16)
    weight_ref[...] = weights
    own_mass[...] = jnp.broadcast_to(mass_row, own_mass.shape)

    low = LOW_TILES * LANES
    real, imag = rotate_back(
        weights, own_images, other_images, cos_ref, sin_ref, slice(0, low), slice(width, width + low), slots
    )
    for k in range(LOW_TILES):
        piece = slice(k * LANES, (k + 1) * LANES)
        low_ref[pl.ds(k, slots, stride=2 * LOW_TILES), :] = real[:, piece]
        low_ref[pl.ds(LOW_TILES + k, slots, stride=2 * LOW_TILES), :] = imag[:, piece]
    low_body = low_ref.shape[0]
    low_send[0:low_body, :] = low_ref[...].astype(jnp.bfloat16)
    low_send[low_body:, :] = split_mass(mass_row)


def posterior(mine, received, own_images, other_images, cos_table, sin_table, slots):
    shifts = cos_table.shape[0]
    low = slots * 2 * LOW_TILES
    return pl.pallas_call(
        functools.partial(posterior_kernel, slots=slots),
        in_specs=whole_vmem(6),
        out_specs=whole_vmem(4),
        out_shape=[
            jax.ShapeDtypeStruct((shifts * slots, 2 * own_images.shape[0]), jnp.bfloat16),
            jax.ShapeDtypeStruct((low, LANES), jnp.float32),
            jax.ShapeDtypeStruct((low + MASS_ROWS, LANES), jnp.bfloat16),
            jax.ShapeDtypeStruct((8, LANES), jnp.float32),
        ],
        scratch_shapes=[pltpu.VMEM((shifts * slots, LANES), jnp.float32)],
        compiler_params=pltpu.CompilerParams(vmem_limit_bytes=(14 + slots // 2) * MIB),
        name="posterior",
    )(mine, received, own_images, other_images, cos_table, sin_table)


def backproject_kernel(
    weight_ref, own_images, other_images, cos_ref, sin_ref, own, *refs, slots, chunk, unroll
):
    sends, sums = refs[:-1], refs[-1]
    width = cos_ref.shape[1]
    tiles = width // LANES - LOW_TILES
    per_row = 2 * tiles
    chunk_tiles = chunk // LANES
    weights = weight_ref[...]

    def body(step, carry):
        first = step * chunk_tiles
        start = pl.multiple_of((LOW_TILES + first) * LANES, LOW_TILES * LANES)
        where = pl.ds(start, chunk)
        imag_where = pl.ds(pl.multiple_of(width + start, LOW_TILES * LANES), chunk)
        real, imag = rotate_back(
            weights, own_images, other_images, cos_ref, sin_ref, where, imag_where, slots
        )
        for k in range(chunk_tiles):
            piece = slice(k * LANES, (k + 1) * LANES)
            sums[pl.ds(first + k, slots, stride=per_row), :] = real[:, piece]
            sums[pl.ds(tiles + first + k, slots, stride=per_row), :] = imag[:, piece]
        return carry

    lax.fori_loop(0, tiles // chunk_tiles, body, 0, unroll=unroll)
    own[...] = sums[0 : 2 * per_row, :]
    for m, send in enumerate(sends, start=1):
        send[...] = sums[2 * m * per_row : 2 * (m + 1) * per_row, :].astype(jnp.bfloat16)


def backproject(weights, own_images, other_images, cos_table, sin_table, slots):
    width = cos_table.shape[1]
    rows = 2 * 2 * (width // LANES - LOW_TILES)
    chips = slots // 2
    return pl.pallas_call(
        functools.partial(
            backproject_kernel, slots=slots, chunk=LOW_TILES * LANES, unroll=7 if slots <= 8 else 1
        ),
        in_specs=whole_vmem(5),
        out_specs=whole_vmem(chips),
        out_shape=[jax.ShapeDtypeStruct((rows, LANES), jnp.float32)]
        + [jax.ShapeDtypeStruct((rows, LANES), jnp.bfloat16)] * (chips - 1),
        scratch_shapes=[pltpu.VMEM((chips * rows, LANES), jnp.float32)],
        compiler_params=pltpu.CompilerParams(vmem_limit_bytes=(14 + slots // 2) * MIB),
        cost_estimate=pl.CostEstimate(flops=2000000000, bytes_accessed=8000000, transcendentals=0),
        name="backproject",
    )(weights, own_images, other_images, cos_table, sin_table)


def fold_kernel(low_ref, low_received, mass, *refs, chips):
    mains, (own, own_mass), sends = refs[: chips - 1], refs[chips - 1 : chips + 1], refs[chips + 1 :]
    rows = own.shape[0]
    low_body = low_ref.shape[0]
    total_mass = mass[0:1, :] + joined_mass(low_received[low_body:, :])
    block = split_mass(total_mass)
    own_mass[...] = jnp.broadcast_to(total_mass, own_mass.shape)
    for m, target in enumerate((own,) + tuple(sends)):
        part = slice(m * rows, (m + 1) * rows)
        value = (low_ref[part, :] + low_received[part, :].astype(jnp.float32)) * 0.5
        target[0:rows, :] = value.astype(target.dtype)
        if m > 0:
            target[rows : rows + MASS_ROWS, :] = block
            target[rows + MASS_ROWS :, :] = mains[m - 1][...]


def fold(low, low_received, mass, mains):
    chips = len(mains) + 1
    rows = low.shape[0] // chips
    return pl.pallas_call(
        functools.partial(fold_kernel, chips=chips),
        in_specs=whole_vmem(2 + chips),
        out_specs=whole_vmem(1 + chips),
        out_shape=[
            jax.ShapeDtypeStruct((rows, LANES), jnp.float32),
            jax.ShapeDtypeStruct((8, LANES), jnp.float32),
        ]
        + [
            jax.ShapeDtypeStruct((rows + MASS_ROWS + main.shape[0], LANES), jnp.bfloat16)
            for main in mains
        ],
        compiler_params=pltpu.CompilerParams(vmem_limit_bytes=16 * MIB),
        name="fold",
    )(low, low_received, mass, *mains)


def merge_kernel(own, own_low, mass, *refs):
    received, (keep, to_core, mass_out) = refs[:-3], refs[-3:]
    core = own_half()
    low_rows = own_low.shape[0]
    low_half = low_rows // 2
    head = low_rows + MASS_ROWS
    half = own.shape[0] // 2
    total_mass = mass[0:1, :]
    for ref in received:
        total_mass = total_mass + joined_mass(ref[low_rows:head, :])
    mass_out[...] = jnp.broadcast_to(total_mass, mass_out.shape)
    for target, place in ((to_core, 1 - core), (keep, core)):
        start = pl.multiple_of(place * half, half)
        total = own[pl.ds(start, half), :]
        for ref in received:
            total = total + ref[pl.ds(head + start, half), :].astype(jnp.float32)
        where = pl.ds(pl.multiple_of(place * low_half, low_half), low_half)
        low = own_low[where, :]
        for ref in received:
            low = low + ref[where, :].astype(jnp.float32)
        target[...] = jnp.concatenate(
            [low[0:LOW_TILES], total[0 : half // 2], low[LOW_TILES:], total[half // 2 :]], axis=0
        ).astype(target.dtype)


def merge(own, own_low, mass, received):
    rows = (own.shape[0] + own_low.shape[0]) // 2
    return pl.pallas_call(
        merge_kernel,
        in_specs=whole_vmem(3 + len(received)),
        out_specs=whole_vmem(3),
        out_shape=[
            jax.ShapeDtypeStruct((rows, LANES), jnp.float32),
            jax.ShapeDtypeStruct((rows, LANES), jnp.bfloat16),
            jax.ShapeDtypeStruct((8, LANES), jnp.float32),
        ],
        compiler_params=pltpu.CompilerParams(vmem_limit_bytes=16 * MIB),
        name="merge",
    )(own, own_low, mass, *received)


def finish_kernel(own, received, mass, out, mass_out, *, scale, mass_scale):
    core = own_half()
    mass_out[...] = mass[0, :CLASSES] * mass_scale
    for step in range(own.shape[0] // BLOCK):
        rows = slice(step * BLOCK, (step + 1) * BLOCK)
        own_rows = pl.ds(pl.multiple_of((2 * step + core) * BLOCK, BLOCK), BLOCK)
        other_rows = pl.ds(pl.multiple_of((2 * step + 1 - core) * BLOCK, BLOCK), BLOCK)
        out[own_rows, :] = own[rows, :] * scale
        out[other_rows, :] = received[rows, :].astype(jnp.float32) * scale


def finish(own, received, mass, scale, mass_scale):
    return pl.pallas_call(
        functools.partial(finish_kernel, scale=scale, mass_scale=mass_scale),
        in_specs=whole_vmem(3),
        out_specs=whole_vmem(2),
        out_shape=[
            jax.ShapeDtypeStruct((2 * own.shape[0], LANES), jnp.float32),
            jax.ShapeDtypeStruct((CLASSES,), jnp.float32),
        ],
        compiler_params=pltpu.CompilerParams(vmem_limit_bytes=16 * MIB),
        name="finish",
    )(own, received, mass)


def local(
    images, noise_precision, assigned_class, class_refs, interp_index, interp_frac, shift_grid
):
    dev_count = lax.axis_size("particle")
    slots = dev_count // 2
    chips = slots // 2
    parts, width = images.shape
    to_core, table, index, frac = project_other(class_refs, interp_index, interp_frac, images)
    images_received = exchange(to_core, 1)
    own, own_images = project_own(table, index, frac, images)
    pair = pair_rows(own, images_received)
    others = chip_order(chips)[1:]
    pairs = [pair] + [exchange(pair, 4 * m) for m in others]
    group = chips // 2
    first, cos_table, sin_table = correlate(
        own_images, images_received, pairs[:group], shift_grid=shift_grid
    )
    passes = [first]
    for start in range(group, chips, group):
        passes += correlate(
            own_images,
            images_received,
            pairs[start : start + group],
            tables=(cos_table, sin_table),
        )
    mine = collect(
        passes,
        noise_precision.reshape(1, parts),
        assigned_class.reshape(1, parts),
        shift_grid.shape[0] * 2 * group,
    )
    weights, low, low_send, mass = posterior(
        mine, exchange(mine, 1), own_images, images_received, cos_table, sin_table, slots
    )
    low_from_half = exchange(low_send, 2)
    sums = backproject(weights, own_images, images_received, cos_table, sin_table, slots)
    folded = fold(low, low_from_half, mass, sums[1:])
    chip_sums = [exchange(send, 4 * m) for m, send in zip(others, folded[2:])]
    keep, send, mass = merge(sums[0], folded[0], folded[1], chip_sums)
    back, class_mass = finish(
        keep, exchange(send, 1), mass, 1.0 / math.sqrt(parts), CLASSES / (parts * dev_count)
    )
    return back.reshape(1, width), class_mass


def solution(mesh):
    in_specs = (
        P(("groups", "particle"), None),
        P(("groups", "particle")),
        P(("groups", "particle")),
        P("groups", None, None, None),
        P("particle", None),
        P("particle", None),
        P(),
    )
    out_specs = (P(("groups", "particle"), None), P("groups"))
    return jax.shard_map(local, mesh=mesh, in_specs=in_specs, out_specs=out_specs, check_vma=False)
```

```python
import functools
import math

import jax
import jax.numpy as jnp
from jax import lax
from jax.experimental import pallas as pl
from jax.experimental.pallas import tpu as pltpu
from jax.sharding import PartitionSpec as P

KY = 128
BOX = 256
CLASSES = 8
LOWK = 16
LANES = 128
PRIOR_REWARD = 1.0
MASS_ROWS = 16
BLOCK = 8
PROJECT_CHUNK = 256
LOW_TILES = LOWK * KY // LANES // 2
MIB = 1 << 20


def exchange(value, mask):
    pairs = [(source, source ^ mask) for source in range(lax.axis_size("particle"))]
    return lax.ppermute(value, "particle", pairs)


def in_hbm(value):
    return pltpu.with_memory_space_constraint(value, pltpu.HBM)


def whole_vmem(count):
    return [pl.BlockSpec(memory_space=pltpu.VMEM)] * count


def own_half():
    return lax.axis_index("particle") % 2


def tree_select(values, masks):
    for mask in masks:
        values = [
            jnp.where(mask, values[i + 1], values[i]) if i + 1 < len(values) else values[i]
            for i in range(0, len(values), 2)
        ]
    return values[0]


def project_half(table, index_ref, frac_ref, half, blended):
    pixels = index_ref.shape[1]
    highs = table.shape[1]
    groups = table.shape[0] // 16
    stride = 8 * groups
    chunk = PROJECT_CHUNK
    tiles = chunk // LANES
    per_block = BLOCK // tiles
    half_tiles = pixels // (2 * LANES)

    def body(step, carry):
        block = 2 * (step // per_block) + half
        where = pl.ds(pl.multiple_of((block * per_block + step % per_block) * chunk, chunk), chunk)
        index = index_ref[:, where]
        frac = frac_ref[:, where]
        high = index >> 7
        low = index & (LANES - 1)
        group = (low * 147) >> 10
        first = low - 7 * group
        high_ids = lax.broadcasted_iota(jnp.int32, (highs, chunk), 0)
        one_hot = jnp.where(high_ids == high, 1.0, 0.0).astype(jnp.bfloat16)
        rows = jnp.dot(table[...], one_hot, preferred_element_type=jnp.float32)
        group = jnp.broadcast_to(group, (8, chunk))
        masks = [(group & (1 << bit)) != 0 for bit in range((groups - 1).bit_length())]
        ids = lax.broadcasted_iota(jnp.int32, (8, chunk), 0)
        weight = jnp.where(ids == first, 1.0 - frac, jnp.where(ids == first + 1, frac, 0.0))
        for comp in range(2):
            start = comp * stride
            picked = tree_select([rows[start + 8 * g : start + 8 * g + 8] for g in range(groups)], masks)
            value = jnp.sum(picked * weight, axis=0, keepdims=True)
            for k in range(tiles):
                row = comp * half_tiles + step * tiles + k
                blended[pl.ds(row, 1), :] = value[:, k * LANES : (k + 1) * LANES]
        return carry

    lax.fori_loop(0, half_tiles // tiles, body, 0, unroll=4)


def image_copies(images_hbm, target, sems, first, half, pixels):
    chunk = BLOCK * LANES
    blocks = pixels // (2 * chunk)
    copies = []
    for comp in range(2):
        for step in range(blocks):
            source = pl.multiple_of(comp * pixels + (2 * step + half) * chunk, chunk)
            dest = (comp * blocks + step) * chunk
            copies.append(
                pltpu.make_async_copy(
                    images_hbm.at[:, pl.ds(source, chunk)],
                    target.at[:, pl.ds(dest, chunk)],
                    sems.at[first + len(copies)],
                )
            )
    return copies


def project_other_kernel(
    table_hbm, index_hbm, frac_hbm, images_hbm,
    out_ref, table, index_ref, frac_ref, table_in, flat, wide, blended, sems
):
    device = lax.axis_index("particle")
    row_count = lax.axis_size("particle") // 2
    half_set = device // 2 % 2
    class_id = (2 * (device // 4) + device % 2) // (row_count // CLASSES)
    copies = [
        pltpu.make_async_copy(
            table_hbm.at[pl.ds(half_set, 1), pl.ds(class_id, 1)], table_in, sems.at[0]
        ),
        pltpu.make_async_copy(index_hbm, index_ref, sems.at[1]),
        pltpu.make_async_copy(frac_hbm, frac_ref, sems.at[2]),
    ]
    pixels = index_ref.shape[1]
    copies += image_copies(images_hbm, out_ref, sems, 3, 1 - own_half(), pixels)
    for copy in copies[:3]:
        copy.start()
    copies[0].wait()
    for copy in copies[3:]:
        copy.start()
    highs = flat.shape[1]
    groups = table.shape[0] // 16

    def unfold(step, carry):
        piece = table_in[0, 0, :, pl.ds(step * 8 * LANES, 8 * LANES)].astype(jnp.float32)
        for k in range(8):
            for comp in range(2):
                flat[comp, pl.ds(step * 8 + k, 1), :] = piece[comp : comp + 1, k * LANES : (k + 1) * LANES]
        return carry

    lax.fori_loop(0, highs // 8, unfold, 0, unroll=16)
    picked = []
    for comp in range(2):
        turned = flat[comp].T
        wide[0:LANES, :] = turned
        wide[LANES : LANES + 8, :] = pltpu.roll(turned[0:8], highs - 1, 1)
        picked += [wide[7 * g : 7 * g + 8, :] for g in range(groups)]
    for pair in range(groups):
        table[16 * pair : 16 * (pair + 1), :] = jnp.concatenate(
            picked[2 * pair : 2 * pair + 2], axis=0
        ).astype(jnp.bfloat16)
    copies[1].wait()
    copies[2].wait()
    project_half(table, index_ref, frac_ref, 1 - own_half(), blended)
    parts = out_ref.shape[0]
    for k in range(blended.shape[0] // parts):
        out_ref[:, pixels + k * LANES : pixels + (k + 1) * LANES] = blended[
            k * parts : (k + 1) * parts, :
        ].astype(jnp.bfloat16)
    for copy in copies[3:]:
        copy.wait()


def project_other(class_refs, interp_index, interp_frac, images):
    vox = class_refs.shape[3]
    pixels = interp_index.shape[1]
    highs = vox // LANES
    half_rows = pixels // LANES
    groups = -(-LANES // 7)
    parts = images.shape[0]
    copies = 3 + pixels // (BLOCK * LANES)
    return pl.pallas_call(
        project_other_kernel,
        in_specs=[pl.BlockSpec(memory_space=pltpu.HBM)] * 4,
        out_specs=whole_vmem(4),
        out_shape=[
            jax.ShapeDtypeStruct((parts, pixels + half_rows * LANES // parts), jnp.bfloat16),
            jax.ShapeDtypeStruct((16 * groups, highs), jnp.bfloat16),
            jax.ShapeDtypeStruct((1, pixels), jnp.int32),
            jax.ShapeDtypeStruct((1, pixels), jnp.float32),
        ],
        scratch_shapes=[
            pltpu.VMEM((1, 1, 2, vox), jnp.bfloat16),
            pltpu.VMEM((2, highs, LANES), jnp.float32),
            pltpu.VMEM((LANES + 8, highs), jnp.float32),
            pltpu.VMEM((half_rows, LANES), jnp.float32),
            pltpu.SemaphoreType.DMA((copies,)),
        ],
        compiler_params=pltpu.CompilerParams(vmem_limit_bytes=16 * MIB),
        name="project_other",
    )(*(in_hbm(value) for value in (class_refs, interp_index, interp_frac, images)))


def project_own_kernel(table, index_ref, frac_ref, images_hbm, out_ref, own_images, blended, sems):
    copies = image_copies(images_hbm, own_images, sems, 0, own_half(), index_ref.shape[1])
    for copy in copies:
        copy.start()
    project_half(table, index_ref, frac_ref, own_half(), blended)
    out_ref[...] = blended[...].astype(jnp.bfloat16)
    for copy in copies:
        copy.wait()


def project_own(table, index, frac, images):
    pixels = index.shape[1]
    half_rows = pixels // LANES
    return pl.pallas_call(
        project_own_kernel,
        in_specs=whole_vmem(3) + [pl.BlockSpec(memory_space=pltpu.HBM)],
        out_specs=whole_vmem(2),
        out_shape=[
            jax.ShapeDtypeStruct((half_rows, LANES), jnp.bfloat16),
            jax.ShapeDtypeStruct((images.shape[0], pixels), jnp.bfloat16),
        ],
        scratch_shapes=[
            pltpu.VMEM((half_rows, LANES), jnp.float32),
            pltpu.SemaphoreType.DMA((pixels // (BLOCK * LANES),)),
        ],
        compiler_params=pltpu.CompilerParams(vmem_limit_bytes=16 * MIB),
        cost_estimate=pl.CostEstimate(flops=2000000000, bytes_accessed=8000000, transcendentals=0),
        name="project_own",
    )(table, index, frac, in_hbm(images))


def pair_kernel(own, other, out_ref):
    count = own.shape[0]
    parts, width = other.shape
    tiles = count // parts
    core = own_half()
    out_ref[pl.ds(pl.multiple_of(core * count, count), count), :] = own[...]
    for k in range(tiles):
        lanes = slice(width - (tiles - k) * LANES, width - (tiles - k - 1) * LANES)
        rows = pl.ds(pl.multiple_of((1 - core) * count + k * parts, parts), parts)
        out_ref[rows, :] = other[:, lanes]


def pair_rows(own, other):
    return pl.pallas_call(
        pair_kernel,
        in_specs=whole_vmem(2),
        out_specs=pl.BlockSpec(memory_space=pltpu.VMEM),
        out_shape=jax.ShapeDtypeStruct((2 * own.shape[0], LANES), own.dtype),
        compiler_params=pltpu.CompilerParams(vmem_limit_bytes=16 * MIB),
        name="pair_rows",
    )(own, other)


def chip_order(chips):
    return [0, chips - 1] + list(range(1, chips - 1))


def slot_orientation(device, slot, slots):
    return 2 * ((device // 4) ^ chip_order(slots // 2)[slot // 2]) + slot % 2


def split_mass(mass_row):
    ids = lax.broadcasted_iota(jnp.int32, (MASS_ROWS, LANES), 0)
    upper = mass_row.astype(jnp.bfloat16).astype(jnp.float32)
    lower = mass_row - upper
    return jnp.where(ids == 0, upper, jnp.where(ids == 1, lower, 0.0)).astype(jnp.bfloat16)


def joined_mass(block):
    return jnp.sum(block.astype(jnp.float32), axis=0, keepdims=True)


def fill_tables(shift_ref, cos_ref, sin_ref):
    shifts, width = cos_ref.shape
    same = lax.broadcasted_iota(jnp.int32, (shifts, shifts), 0) == lax.broadcasted_iota(
        jnp.int32, (shifts, shifts), 1
    )
    grid_x, grid_y = (
        jnp.sum(
            jnp.where(same, shift_ref[axis : axis + 1, :].astype(jnp.float32), 0.0),
            axis=1,
            keepdims=True,
        ).astype(jnp.int32)
        for axis in range(2)
    )
    lane = lax.broadcasted_iota(jnp.int32, (shifts, LANES), 1)
    freq_x = (lane // BLOCK) * (2 * BLOCK) + own_half() * BLOCK + lane % BLOCK
    turn_x = (freq_x * grid_x) & (BOX - 1)
    turn_y = ((lane - KY // 2) * grid_y) & (BOX - 1)
    angle_x = turn_x.astype(jnp.float32) * (2.0 * math.pi / BOX)
    angle_y = turn_y.astype(jnp.float32) * (2.0 * math.pi / BOX)
    cos_x, sin_x = jnp.cos(angle_x), jnp.sin(angle_x)
    cos_y, sin_y = jnp.cos(angle_y), jnp.sin(angle_y)
    for j in range(width // LANES):
        where = slice(j * LANES, (j + 1) * LANES)
        cos_j, sin_j = cos_x[:, j : j + 1], sin_x[:, j : j + 1]
        cos_ref[:, where] = cos_j * cos_y - sin_j * sin_y
        sin_ref[:, where] = sin_j * cos_y + cos_j * sin_y


def correlate_first_kernel(shift_ref, own_images, other_images, *refs, chunk):
    pair_refs, (out_ref, cos_ref, sin_ref, proj) = refs[:-4], refs[-4:]
    fill_tables(shift_ref, cos_ref, sin_ref)
    correlate_kernel(
        cos_ref, sin_ref, own_images, other_images, *pair_refs, out_ref, proj, chunk=chunk
    )


def correlate_kernel(cos_ref, sin_ref, own_images, other_images, *refs, chunk):
    pair_refs, (out_ref, proj) = refs[:-2], refs[-2:]
    shifts = cos_ref.shape[0]
    parts = own_images.shape[0]
    slots = 2 * len(pair_refs)
    width = own_images.shape[1] // 2
    tiles = width // LANES
    per_row = 2 * tiles
    combos = shifts * slots
    for slot in range(slots):
        place = slice(slot % 2 * per_row, (slot % 2 + 1) * per_row)
        row = pair_refs[slot // 2][place, :].astype(jnp.float32)
        proj[slot * per_row : (slot + 1) * per_row, :] = row
        out_ref[combos + slot : combos + slot + 1, :] = jnp.sum(row * row, axis=0, keepdims=True)

    chunk_tiles = chunk // LANES
    contract_lanes = (((1,), (1,)), ((), ()))

    def body(step, total):
        first = step * chunk_tiles
        where = pl.ds(pl.multiple_of(step * chunk, chunk), chunk)
        imag_where = pl.ds(pl.multiple_of(width + step * chunk, chunk), chunk)
        cos_part, sin_part = cos_ref[:, where], sin_ref[:, where]
        reals, imags = [], []
        for slot in range(slots):
            start = slot * per_row + first
            real = jnp.concatenate(
                [proj[pl.ds(start + k, 1), :] for k in range(chunk_tiles)], axis=1
            )
            imag = jnp.concatenate(
                [proj[pl.ds(start + tiles + k, 1), :] for k in range(chunk_tiles)], axis=1
            )
            reals.append(real * cos_part - imag * sin_part)
            imags.append(real * sin_part + imag * cos_part)
        turned_real = jnp.concatenate(reals, axis=0).astype(jnp.bfloat16)
        turned_imag = jnp.concatenate(imags, axis=0).astype(jnp.bfloat16)
        image_real = jnp.concatenate([own_images[:, where], other_images[:, where]], axis=0)
        image_imag = jnp.concatenate([own_images[:, imag_where], other_images[:, imag_where]], axis=0)
        total = total + lax.dot_general(
            turned_real, image_real, contract_lanes, preferred_element_type=jnp.float32
        )
        return total + lax.dot_general(
            turned_imag, image_imag, contract_lanes, preferred_element_type=jnp.float32
        )

    total = lax.fori_loop(
        0, width // chunk, body, jnp.zeros((combos, 2 * parts), jnp.float32), unroll=2
    )
    out_ref[0:combos, :] = jnp.zeros((combos, LANES), jnp.float32)
    out_ref[0:combos, 0 : 2 * parts] = total


def correlate(own_images, other_images, pairs, shift_grid=None, tables=None):
    slots = 2 * len(pairs)
    width = own_images.shape[1] // 2
    shifts = shift_grid.shape[0] if tables is None else tables[0].shape[0]
    first = (shift_grid.T,) if tables is None else tuple(tables)
    table = jax.ShapeDtypeStruct((shifts, width), jnp.float32)
    outs = [jax.ShapeDtypeStruct((shifts * slots + slots, LANES), jnp.float32)]
    outs += [table, table] if tables is None else []
    kernel = correlate_first_kernel if tables is None else correlate_kernel
    return pl.pallas_call(
        functools.partial(kernel, chunk=4096),
        in_specs=whole_vmem(len(first) + 2 + len(pairs)),
        out_specs=whole_vmem(len(outs)),
        out_shape=outs,
        scratch_shapes=[pltpu.VMEM((slots * 2 * width // LANES, LANES), jnp.float32)],
        compiler_params=pltpu.CompilerParams(vmem_limit_bytes=(14 + slots) * MIB),
        cost_estimate=pl.CostEstimate(flops=1000000000, bytes_accessed=4000000, transcendentals=0),
        name="correlate",
    )(*first, own_images, other_images, *pairs)


def collect_kernel(*refs, combos):
    parts_refs, (precision_ref, assigned_ref, out_ref) = refs[:-3], refs[-3:]
    count = len(parts_refs)
    slots = parts_refs[0].shape[0] - combos
    parts = precision_ref.shape[1]
    for index, ref in enumerate(parts_refs):
        out_ref[index * combos : (index + 1) * combos, :] = ref[0:combos, :]
        power = count * combos + index * slots
        out_ref[power : power + slots, :] = ref[combos:, :]
    rest = count * (combos + slots)
    out_ref[rest:, :] = jnp.zeros((8, LANES), jnp.float32)
    out_ref[rest : rest + 1, 0:parts] = precision_ref[...]
    out_ref[rest + 1 : rest + 2, 0:parts] = assigned_ref[...].astype(jnp.float32)


def collect(passes, precision, assigned, combos):
    rows = len(passes) * passes[0].shape[0] + 8
    return pl.pallas_call(
        functools.partial(collect_kernel, combos=combos),
        in_specs=whole_vmem(2 + len(passes)),
        out_specs=pl.BlockSpec(memory_space=pltpu.VMEM),
        out_shape=jax.ShapeDtypeStruct((rows, LANES), jnp.float32),
        compiler_params=pltpu.CompilerParams(vmem_limit_bytes=16 * MIB),
        name="collect",
    )(*passes, precision, assigned)


def rotate_back(weights, own_images, other_images, cos_ref, sin_ref, where, imag_where, slots):
    image_real = jnp.concatenate([own_images[:, where], other_images[:, where]], axis=0)
    image_imag = jnp.concatenate([own_images[:, imag_where], other_images[:, imag_where]], axis=0)
    from_real = jnp.dot(weights, image_real, preferred_element_type=jnp.float32)
    from_imag = jnp.dot(weights, image_imag, preferred_element_type=jnp.float32)
    real = imag = None
    for s in range(cos_ref.shape[0]):
        cos_s, sin_s = cos_ref[s : s + 1, where], sin_ref[s : s + 1, where]
        part_real = from_real[s * slots : (s + 1) * slots]
        part_imag = from_imag[s * slots : (s + 1) * slots]
        real_s = part_real * cos_s + part_imag * sin_s
        imag_s = part_imag * cos_s - part_real * sin_s
        real = real_s if real is None else real + real_s
        imag = imag_s if imag is None else imag + imag_s
    return real, imag


def posterior_kernel(
    mine, received, own_images, other_images, cos_ref, sin_ref,
    weight_ref, low_ref, low_send, own_mass, ordered, *, slots
):
    device = lax.axis_index("particle")
    shifts, width = cos_ref.shape
    parts = own_images.shape[0]
    combos = shifts * slots
    theirs = received[...]
    lane = lax.broadcasted_iota(jnp.int32, theirs.shape, 1)
    swapped = jnp.where(
        lane < parts, pltpu.roll(theirs, LANES - parts, 1), pltpu.roll(theirs, parts, 1)
    )
    joint = mine[...] + swapped
    power = jnp.sum(
        mine[combos : combos + slots, :] + received[combos : combos + slots, :], axis=1, keepdims=True
    )
    precision = joint[combos + slots : combos + slots + 1]
    assigned = joint[combos + slots + 1 : combos + slots + 2].astype(jnp.int32)
    likelihood_scale = 1.0 / math.sqrt(4 * width)
    classes = [slot_orientation(device, slot, slots) // (slots // CLASSES) for slot in range(slots)]
    logits = []
    for slot in range(slots):
        match = (assigned == classes[slot]).astype(jnp.float32) * PRIOR_REWARD
        part = joint[slot * shifts : (slot + 1) * shifts]
        logits.append(precision * (part - 0.5 * power[slot : slot + 1]) * likelihood_scale + match)
    peak = jnp.max(functools.reduce(jnp.maximum, logits), axis=0, keepdims=True)
    terms = [jnp.exp(value - peak) for value in logits]
    norm = jnp.sum(functools.reduce(jnp.add, terms), axis=0, keepdims=True)
    counted = lax.broadcasted_iota(jnp.int32, (1, LANES), 1) < 2 * parts
    class_lane = lax.broadcasted_iota(jnp.int32, (1, LANES), 1)
    mass_row = jnp.zeros((1, LANES), jnp.float32)
    for slot in range(slots):
        value = terms[slot] / norm
        ordered[slot * shifts : (slot + 1) * shifts, :] = value
        share = jnp.where(counted, jnp.sum(value, axis=0, keepdims=True) * precision, 0.0)
        share = jnp.sum(share, axis=1, keepdims=True)
        mass_row = mass_row + jnp.where(class_lane == classes[slot], share, 0.0)
    weights = jnp.concatenate(
        [ordered[pl.ds(s, slots, stride=shifts), :] for s in range(shifts)], axis=0
    )
    weights = weights[:, 0 : 2 * parts].astype(jnp.bfloat16)
    weight_ref[...] = weights
    own_mass[...] = jnp.broadcast_to(mass_row, own_mass.shape)

    low = LOW_TILES * LANES
    real, imag = rotate_back(
        weights, own_images, other_images, cos_ref, sin_ref, slice(0, low), slice(width, width + low), slots
    )
    for k in range(LOW_TILES):
        piece = slice(k * LANES, (k + 1) * LANES)
        low_ref[pl.ds(k, slots, stride=2 * LOW_TILES), :] = real[:, piece]
        low_ref[pl.ds(LOW_TILES + k, slots, stride=2 * LOW_TILES), :] = imag[:, piece]
    low_body = low_ref.shape[0]
    low_send[0:low_body, :] = low_ref[...].astype(jnp.bfloat16)
    low_send[low_body:, :] = split_mass(mass_row)


def posterior(mine, received, own_images, other_images, cos_table, sin_table, slots):
    shifts = cos_table.shape[0]
    low = slots * 2 * LOW_TILES
    return pl.pallas_call(
        functools.partial(posterior_kernel, slots=slots),
        in_specs=whole_vmem(6),
        out_specs=whole_vmem(4),
        out_shape=[
            jax.ShapeDtypeStruct((shifts * slots, 2 * own_images.shape[0]), jnp.bfloat16),
            jax.ShapeDtypeStruct((low, LANES), jnp.float32),
            jax.ShapeDtypeStruct((low + MASS_ROWS, LANES), jnp.bfloat16),
            jax.ShapeDtypeStruct((8, LANES), jnp.float32),
        ],
        scratch_shapes=[pltpu.VMEM((shifts * slots, LANES), jnp.float32)],
        compiler_params=pltpu.CompilerParams(vmem_limit_bytes=(14 + slots // 2) * MIB),
        name="posterior",
    )(mine, received, own_images, other_images, cos_table, sin_table)


def backproject_kernel(
    weight_ref, own_images, other_images, cos_ref, sin_ref, own, *refs, slots, chunk, unroll
):
    sends, sums = refs[:-1], refs[-1]
    width = cos_ref.shape[1]
    tiles = width // LANES - LOW_TILES
    per_row = 2 * tiles
    chunk_tiles = chunk // LANES
    weights = weight_ref[...]

    def body(step, carry):
        first = step * chunk_tiles
        start = pl.multiple_of((LOW_TILES + first) * LANES, LOW_TILES * LANES)
        where = pl.ds(start, chunk)
        imag_where = pl.ds(pl.multiple_of(width + start, LOW_TILES * LANES), chunk)
        real, imag = rotate_back(
            weights, own_images, other_images, cos_ref, sin_ref, where, imag_where, slots
        )
        for k in range(chunk_tiles):
            piece = slice(k * LANES, (k + 1) * LANES)
            sums[pl.ds(first + k, slots, stride=per_row), :] = real[:, piece]
            sums[pl.ds(tiles + first + k, slots, stride=per_row), :] = imag[:, piece]
        return carry

    lax.fori_loop(0, tiles // chunk_tiles, body, 0, unroll=unroll)
    own[...] = sums[0 : 2 * per_row, :]
    for m, send in enumerate(sends, start=1):
        send[...] = sums[2 * m * per_row : 2 * (m + 1) * per_row, :].astype(jnp.bfloat16)


def backproject(weights, own_images, other_images, cos_table, sin_table, slots):
    width = cos_table.shape[1]
    rows = 2 * 2 * (width // LANES - LOW_TILES)
    chips = slots // 2
    return pl.pallas_call(
        functools.partial(
            backproject_kernel, slots=slots, chunk=LOW_TILES * LANES, unroll=7 if slots <= 8 else 1
        ),
        in_specs=whole_vmem(5),
        out_specs=whole_vmem(chips),
        out_shape=[jax.ShapeDtypeStruct((rows, LANES), jnp.float32)]
        + [jax.ShapeDtypeStruct((rows, LANES), jnp.bfloat16)] * (chips - 1),
        scratch_shapes=[pltpu.VMEM((chips * rows, LANES), jnp.float32)],
        compiler_params=pltpu.CompilerParams(vmem_limit_bytes=(14 + slots // 2) * MIB),
        cost_estimate=pl.CostEstimate(flops=2000000000, bytes_accessed=8000000, transcendentals=0),
        name="backproject",
    )(weights, own_images, other_images, cos_table, sin_table)


def fold_kernel(low_ref, low_received, mass, *refs, chips):
    mains, (own, own_mass), sends = refs[: chips - 1], refs[chips - 1 : chips + 1], refs[chips + 1 :]
    rows = own.shape[0]
    low_body = low_ref.shape[0]
    total_mass = mass[0:1, :] + joined_mass(low_received[low_body:, :])
    block = split_mass(total_mass)
    own_mass[...] = jnp.broadcast_to(total_mass, own_mass.shape)
    for m, target in enumerate((own,) + tuple(sends)):
        part = slice(m * rows, (m + 1) * rows)
        value = (low_ref[part, :] + low_received[part, :].astype(jnp.float32)) * 0.5
        target[0:rows, :] = value.astype(target.dtype)
        if m > 0:
            target[rows : rows + MASS_ROWS, :] = block
            target[rows + MASS_ROWS :, :] = mains[m - 1][...]


def fold(low, low_received, mass, mains):
    chips = len(mains) + 1
    rows = low.shape[0] // chips
    return pl.pallas_call(
        functools.partial(fold_kernel, chips=chips),
        in_specs=whole_vmem(2 + chips),
        out_specs=whole_vmem(1 + chips),
        out_shape=[
            jax.ShapeDtypeStruct((rows, LANES), jnp.float32),
            jax.ShapeDtypeStruct((8, LANES), jnp.float32),
        ]
        + [
            jax.ShapeDtypeStruct((rows + MASS_ROWS + main.shape[0], LANES), jnp.bfloat16)
            for main in mains
        ],
        compiler_params=pltpu.CompilerParams(vmem_limit_bytes=16 * MIB),
        name="fold",
    )(low, low_received, mass, *mains)


def merge_kernel(own, own_low, mass, *refs):
    received, (keep, to_core, mass_out) = refs[:-3], refs[-3:]
    core = own_half()
    low_rows = own_low.shape[0]
    low_half = low_rows // 2
    head = low_rows + MASS_ROWS
    half = own.shape[0] // 2
    total_mass = mass[0:1, :]
    for ref in received:
        total_mass = total_mass + joined_mass(ref[low_rows:head, :])
    mass_out[...] = jnp.broadcast_to(total_mass, mass_out.shape)
    for target, place in ((to_core, 1 - core), (keep, core)):
        start = pl.multiple_of(place * half, half)
        total = own[pl.ds(start, half), :]
        for ref in received:
            total = total + ref[pl.ds(head + start, half), :].astype(jnp.float32)
        where = pl.ds(pl.multiple_of(place * low_half, low_half), low_half)
        low = own_low[where, :]
        for ref in received:
            low = low + ref[where, :].astype(jnp.float32)
        target[...] = jnp.concatenate(
            [low[0:LOW_TILES], total[0 : half // 2], low[LOW_TILES:], total[half // 2 :]], axis=0
        ).astype(target.dtype)


def merge(own, own_low, mass, received):
    rows = (own.shape[0] + own_low.shape[0]) // 2
    return pl.pallas_call(
        merge_kernel,
        in_specs=whole_vmem(3 + len(received)),
        out_specs=whole_vmem(3),
        out_shape=[
            jax.ShapeDtypeStruct((rows, LANES), jnp.float32),
            jax.ShapeDtypeStruct((rows, LANES), jnp.bfloat16),
            jax.ShapeDtypeStruct((8, LANES), jnp.float32),
        ],
        compiler_params=pltpu.CompilerParams(vmem_limit_bytes=16 * MIB),
        name="merge",
    )(own, own_low, mass, *received)


def finish_kernel(own, received, mass, out, mass_out, *, scale, mass_scale):
    core = own_half()
    mass_out[...] = mass[0, :CLASSES] * mass_scale
    for step in range(own.shape[0] // BLOCK):
        rows = slice(step * BLOCK, (step + 1) * BLOCK)
        own_rows = pl.ds(pl.multiple_of((2 * step + core) * BLOCK, BLOCK), BLOCK)
        other_rows = pl.ds(pl.multiple_of((2 * step + 1 - core) * BLOCK, BLOCK), BLOCK)
        out[own_rows, :] = own[rows, :] * scale
        out[other_rows, :] = received[rows, :].astype(jnp.float32) * scale


def finish(own, received, mass, scale, mass_scale):
    return pl.pallas_call(
        functools.partial(finish_kernel, scale=scale, mass_scale=mass_scale),
        in_specs=whole_vmem(3),
        out_specs=whole_vmem(2),
        out_shape=[
            jax.ShapeDtypeStruct((2 * own.shape[0], LANES), jnp.float32),
            jax.ShapeDtypeStruct((CLASSES,), jnp.float32),
        ],
        compiler_params=pltpu.CompilerParams(vmem_limit_bytes=16 * MIB),
        name="finish",
    )(own, received, mass)


def local(
    images, noise_precision, assigned_class, class_refs, interp_index, interp_frac, shift_grid
):
    dev_count = lax.axis_size("particle")
    slots = dev_count // 2
    chips = slots // 2
    parts, width = images.shape
    to_core, table, index, frac = project_other(class_refs, interp_index, interp_frac, images)
    images_received = exchange(to_core, 1)
    own, own_images = project_own(table, index, frac, images)
    pair = pair_rows(own, images_received)
    others = chip_order(chips)[1:]
    pairs = [pair] + [exchange(pair, 4 * m) for m in others]
    group = chips // 2
    first, cos_table, sin_table = correlate(
        own_images, images_received, pairs[:group], shift_grid=shift_grid
    )
    passes = [first]
    for start in range(group, chips, group):
        passes += correlate(
            own_images,
            images_received,
            pairs[start : start + group],
            tables=(cos_table, sin_table),
        )
    mine = collect(
        passes,
        noise_precision.reshape(1, parts),
        assigned_class.reshape(1, parts),
        shift_grid.shape[0] * 2 * group,
    )
    weights, low, low_send, mass = posterior(
        mine, exchange(mine, 1), own_images, images_received, cos_table, sin_table, slots
    )
    low_from_half = exchange(low_send, 2)
    sums = backproject(weights, own_images, images_received, cos_table, sin_table, slots)
    folded = fold(low, low_from_half, mass, sums[1:])
    chip_sums = [exchange(send, 4 * m) for m, send in zip(others, folded[2:])]
    keep, send, mass = merge(sums[0], folded[0], folded[1], chip_sums)
    back, class_mass = finish(
        keep, exchange(send, 1), mass, 1.0 / math.sqrt(parts), CLASSES / (parts * dev_count)
    )
    return back.reshape(1, width), class_mass


def solution(mesh):
    in_specs = (
        P(("groups", "particle"), None),
        P(("groups", "particle")),
        P(("groups", "particle")),
        P("groups", None, None, None),
        P("particle", None),
        P("particle", None),
        P(),
    )
    out_specs = (P(("groups", "particle"), None), P("groups"))
    return jax.shard_map(local, mesh=mesh, in_specs=in_specs, out_specs=out_specs, check_vma=False)
```

```python
import functools
import math

import jax
import jax.numpy as jnp
from jax import lax
from jax.experimental import pallas as pl
from jax.experimental.pallas import tpu as pltpu
from jax.sharding import PartitionSpec as P

KY = 128
BOX = 256
CLASSES = 8
LOWK = 16
LANES = 128
PRIOR_REWARD = 1.0
MASS_ROWS = 16
BLOCK = 8
PROJECT_CHUNK = 256
LOW_TILES = LOWK * KY // LANES // 2
MIB = 1 << 20


def exchange(value, mask):
    pairs = [(source, source ^ mask) for source in range(lax.axis_size("particle"))]
    return lax.ppermute(value, "particle", pairs)


def in_hbm(value):
    return pltpu.with_memory_space_constraint(value, pltpu.HBM)


def whole_vmem(count):
    return [pl.BlockSpec(memory_space=pltpu.VMEM)] * count


def own_half():
    return lax.axis_index("particle") % 2


def tree_select(values, masks):
    for mask in masks:
        values = [
            jnp.where(mask, values[i + 1], values[i]) if i + 1 < len(values) else values[i]
            for i in range(0, len(values), 2)
        ]
    return values[0]


def project_half(table, index_ref, frac_ref, half, blended):
    pixels = index_ref.shape[1]
    highs = table.shape[1]
    groups = table.shape[0] // 16
    stride = 8 * groups
    chunk = PROJECT_CHUNK
    tiles = chunk // LANES
    per_block = BLOCK // tiles
    half_tiles = pixels // (2 * LANES)

    def body(step, carry):
        block = 2 * (step // per_block) + half
        where = pl.ds(pl.multiple_of((block * per_block + step % per_block) * chunk, chunk), chunk)
        index = index_ref[:, where]
        frac = frac_ref[:, where]
        high = index >> 7
        low = index & (LANES - 1)
        group = (low * 147) >> 10
        first = low - 7 * group
        high_ids = lax.broadcasted_iota(jnp.int32, (highs, chunk), 0)
        one_hot = jnp.where(high_ids == high, 1.0, 0.0).astype(jnp.bfloat16)
        rows = jnp.dot(table[...], one_hot, preferred_element_type=jnp.float32)
        group = jnp.broadcast_to(group, (8, chunk))
        masks = [(group & (1 << bit)) != 0 for bit in range((groups - 1).bit_length())]
        ids = lax.broadcasted_iota(jnp.int32, (8, chunk), 0)
        weight = jnp.where(ids == first, 1.0 - frac, jnp.where(ids == first + 1, frac, 0.0))
        for comp in range(2):
            start = comp * stride
            picked = tree_select([rows[start + 8 * g : start + 8 * g + 8] for g in range(groups)], masks)
            value = jnp.sum(picked * weight, axis=0, keepdims=True)
            for k in range(tiles):
                row = comp * half_tiles + step * tiles + k
                blended[pl.ds(row, 1), :] = value[:, k * LANES : (k + 1) * LANES]
        return carry

    lax.fori_loop(0, half_tiles // tiles, body, 0, unroll=8)


def image_copies(images_hbm, target, sems, first, half, pixels):
    chunk = BLOCK * LANES
    blocks = pixels // (2 * chunk)
    copies = []
    for comp in range(2):
        for step in range(blocks):
            source = pl.multiple_of(comp * pixels + (2 * step + half) * chunk, chunk)
            dest = (comp * blocks + step) * chunk
            copies.append(
                pltpu.make_async_copy(
                    images_hbm.at[:, pl.ds(source, chunk)],
                    target.at[:, pl.ds(dest, chunk)],
                    sems.at[first + len(copies)],
                )
            )
    return copies


def project_other_kernel(
    table_hbm, index_hbm, frac_hbm, images_hbm,
    out_ref, table, index_ref, frac_ref, table_in, flat, wide, blended, sems
):
    device = lax.axis_index("particle")
    row_count = lax.axis_size("particle") // 2
    half_set = device // 2 % 2
    class_id = (2 * (device // 4) + device % 2) // (row_count // CLASSES)
    copies = [
        pltpu.make_async_copy(
            table_hbm.at[pl.ds(half_set, 1), pl.ds(class_id, 1)], table_in, sems.at[0]
        ),
        pltpu.make_async_copy(index_hbm, index_ref, sems.at[1]),
        pltpu.make_async_copy(frac_hbm, frac_ref, sems.at[2]),
    ]
    pixels = index_ref.shape[1]
    copies += image_copies(images_hbm, out_ref, sems, 3, 1 - own_half(), pixels)
    for copy in copies[:3]:
        copy.start()
    copies[0].wait()
    for copy in copies[3:]:
        copy.start()
    highs = flat.shape[1]
    groups = table.shape[0] // 16

    def unfold(step, carry):
        piece = table_in[0, 0, :, pl.ds(step * 8 * LANES, 8 * LANES)].astype(jnp.float32)
        for k in range(8):
            for comp in range(2):
                flat[comp, pl.ds(step * 8 + k, 1), :] = piece[comp : comp + 1, k * LANES : (k + 1) * LANES]
        return carry

    lax.fori_loop(0, highs // 8, unfold, 0, unroll=16)
    picked = []
    for comp in range(2):
        turned = flat[comp].T
        wide[0:LANES, :] = turned
        wide[LANES : LANES + 8, :] = pltpu.roll(turned[0:8], highs - 1, 1)
        picked += [wide[7 * g : 7 * g + 8, :] for g in range(groups)]
    for pair in range(groups):
        table[16 * pair : 16 * (pair + 1), :] = jnp.concatenate(
            picked[2 * pair : 2 * pair + 2], axis=0
        ).astype(jnp.bfloat16)
    copies[1].wait()
    copies[2].wait()
    project_half(table, index_ref, frac_ref, 1 - own_half(), blended)
    parts = out_ref.shape[0]
    for k in range(blended.shape[0] // parts):
        out_ref[:, pixels + k * LANES : pixels + (k + 1) * LANES] = blended[
            k * parts : (k + 1) * parts, :
        ].astype(jnp.bfloat16)
    for copy in copies[3:]:
        copy.wait()


def project_other(class_refs, interp_index, interp_frac, images):
    vox = class_refs.shape[3]
    pixels = interp_index.shape[1]
    highs = vox // LANES
    half_rows = pixels // LANES
    groups = -(-LANES // 7)
    parts = images.shape[0]
    copies = 3 + pixels // (BLOCK * LANES)
    return pl.pallas_call(
        project_other_kernel,
        in_specs=[pl.BlockSpec(memory_space=pltpu.HBM)] * 4,
        out_specs=whole_vmem(4),
        out_shape=[
            jax.ShapeDtypeStruct((parts, pixels + half_rows * LANES // parts), jnp.bfloat16),
            jax.ShapeDtypeStruct((16 * groups, highs), jnp.bfloat16),
            jax.ShapeDtypeStruct((1, pixels), jnp.int32),
            jax.ShapeDtypeStruct((1, pixels), jnp.float32),
        ],
        scratch_shapes=[
            pltpu.VMEM((1, 1, 2, vox), jnp.bfloat16),
            pltpu.VMEM((2, highs, LANES), jnp.float32),
            pltpu.VMEM((LANES + 8, highs), jnp.float32),
            pltpu.VMEM((half_rows, LANES), jnp.float32),
            pltpu.SemaphoreType.DMA((copies,)),
        ],
        compiler_params=pltpu.CompilerParams(vmem_limit_bytes=16 * MIB),
        name="project_other",
    )(*(in_hbm(value) for value in (class_refs, interp_index, interp_frac, images)))


def project_own_kernel(table, index_ref, frac_ref, images_hbm, out_ref, own_images, blended, sems):
    copies = image_copies(images_hbm, own_images, sems, 0, own_half(), index_ref.shape[1])
    for copy in copies:
        copy.start()
    project_half(table, index_ref, frac_ref, own_half(), blended)
    out_ref[...] = blended[...].astype(jnp.bfloat16)
    for copy in copies:
        copy.wait()


def project_own(table, index, frac, images):
    pixels = index.shape[1]
    half_rows = pixels // LANES
    return pl.pallas_call(
        project_own_kernel,
        in_specs=whole_vmem(3) + [pl.BlockSpec(memory_space=pltpu.HBM)],
        out_specs=whole_vmem(2),
        out_shape=[
            jax.ShapeDtypeStruct((half_rows, LANES), jnp.bfloat16),
            jax.ShapeDtypeStruct((images.shape[0], pixels), jnp.bfloat16),
        ],
        scratch_shapes=[
            pltpu.VMEM((half_rows, LANES), jnp.float32),
            pltpu.SemaphoreType.DMA((pixels // (BLOCK * LANES),)),
        ],
        compiler_params=pltpu.CompilerParams(vmem_limit_bytes=16 * MIB),
        cost_estimate=pl.CostEstimate(flops=2000000000, bytes_accessed=8000000, transcendentals=0),
        name="project_own",
    )(table, index, frac, in_hbm(images))


def pair_kernel(own, other, out_ref):
    count = own.shape[0]
    parts, width = other.shape
    tiles = count // parts
    core = own_half()
    out_ref[pl.ds(pl.multiple_of(core * count, count), count), :] = own[...]
    for k in range(tiles):
        lanes = slice(width - (tiles - k) * LANES, width - (tiles - k - 1) * LANES)
        rows = pl.ds(pl.multiple_of((1 - core) * count + k * parts, parts), parts)
        out_ref[rows, :] = other[:, lanes]


def pair_rows(own, other):
    return pl.pallas_call(
        pair_kernel,
        in_specs=whole_vmem(2),
        out_specs=pl.BlockSpec(memory_space=pltpu.VMEM),
        out_shape=jax.ShapeDtypeStruct((2 * own.shape[0], LANES), own.dtype),
        compiler_params=pltpu.CompilerParams(vmem_limit_bytes=16 * MIB),
        name="pair_rows",
    )(own, other)


def chip_order(chips):
    return [0, chips // 2] + [m for m in range(1, chips) if m != chips // 2]


def slot_orientation(device, slot, slots):
    return 2 * ((device // 4) ^ chip_order(slots // 2)[slot // 2]) + slot % 2


def split_mass(mass_row):
    ids = lax.broadcasted_iota(jnp.int32, (MASS_ROWS, LANES), 0)
    upper = mass_row.astype(jnp.bfloat16).astype(jnp.float32)
    lower = mass_row - upper
    return jnp.where(ids == 0, upper, jnp.where(ids == 1, lower, 0.0)).astype(jnp.bfloat16)


def joined_mass(block):
    return jnp.sum(block.astype(jnp.float32), axis=0, keepdims=True)


def fill_tables(shift_ref, cos_ref, sin_ref):
    shifts, width = cos_ref.shape
    same = lax.broadcasted_iota(jnp.int32, (shifts, shifts), 0) == lax.broadcasted_iota(
        jnp.int32, (shifts, shifts), 1
    )
    grid_x, grid_y = (
        jnp.sum(
            jnp.where(same, shift_ref[axis : axis + 1, :].astype(jnp.float32), 0.0),
            axis=1,
            keepdims=True,
        ).astype(jnp.int32)
        for axis in range(2)
    )
    lane = lax.broadcasted_iota(jnp.int32, (shifts, LANES), 1)
    freq_x = (lane // BLOCK) * (2 * BLOCK) + own_half() * BLOCK + lane % BLOCK
    turn_x = (freq_x * grid_x) & (BOX - 1)
    turn_y = ((lane - KY // 2) * grid_y) & (BOX - 1)
    angle_x = turn_x.astype(jnp.float32) * (2.0 * math.pi / BOX)
    angle_y = turn_y.astype(jnp.float32) * (2.0 * math.pi / BOX)
    cos_x, sin_x = jnp.cos(angle_x), jnp.sin(angle_x)
    cos_y, sin_y = jnp.cos(angle_y), jnp.sin(angle_y)
    for j in range(width // LANES):
        where = slice(j * LANES, (j + 1) * LANES)
        cos_j, sin_j = cos_x[:, j : j + 1], sin_x[:, j : j + 1]
        cos_ref[:, where] = cos_j * cos_y - sin_j * sin_y
        sin_ref[:, where] = sin_j * cos_y + cos_j * sin_y


def correlate_first_kernel(shift_ref, own_images, other_images, *refs, chunk):
    pair_refs, (out_ref, cos_ref, sin_ref, proj) = refs[:-4], refs[-4:]
    fill_tables(shift_ref, cos_ref, sin_ref)
    correlate_kernel(
        cos_ref, sin_ref, own_images, other_images, *pair_refs, out_ref, proj, chunk=chunk
    )


def correlate_kernel(cos_ref, sin_ref, own_images, other_images, *refs, chunk):
    pair_refs, (out_ref, proj) = refs[:-2], refs[-2:]
    shifts = cos_ref.shape[0]
    parts = own_images.shape[0]
    slots = 2 * len(pair_refs)
    width = own_images.shape[1] // 2
    tiles = width // LANES
    per_row = 2 * tiles
    combos = shifts * slots
    for slot in range(slots):
        place = slice(slot % 2 * per_row, (slot % 2 + 1) * per_row)
        row = pair_refs[slot // 2][place, :].astype(jnp.float32)
        proj[slot * per_row : (slot + 1) * per_row, :] = row
        out_ref[combos + slot : combos + slot + 1, :] = jnp.sum(row * row, axis=0, keepdims=True)

    chunk_tiles = chunk // LANES
    contract_lanes = (((1,), (1,)), ((), ()))

    def body(step, total):
        first = step * chunk_tiles
        where = pl.ds(pl.multiple_of(step * chunk, chunk), chunk)
        imag_where = pl.ds(pl.multiple_of(width + step * chunk, chunk), chunk)
        cos_part, sin_part = cos_ref[:, where], sin_ref[:, where]
        reals, imags = [], []
        for slot in range(slots):
            start = slot * per_row + first
            real = jnp.concatenate(
                [proj[pl.ds(start + k, 1), :] for k in range(chunk_tiles)], axis=1
            )
            imag = jnp.concatenate(
                [proj[pl.ds(start + tiles + k, 1), :] for k in range(chunk_tiles)], axis=1
            )
            reals.append(real * cos_part - imag * sin_part)
            imags.append(real * sin_part + imag * cos_part)
        turned_real = jnp.concatenate(reals, axis=0).astype(jnp.bfloat16)
        turned_imag = jnp.concatenate(imags, axis=0).astype(jnp.bfloat16)
        image_real = jnp.concatenate([own_images[:, where], other_images[:, where]], axis=0)
        image_imag = jnp.concatenate([own_images[:, imag_where], other_images[:, imag_where]], axis=0)
        total = total + lax.dot_general(
            turned_real, image_real, contract_lanes, preferred_element_type=jnp.float32
        )
        return total + lax.dot_general(
            turned_imag, image_imag, contract_lanes, preferred_element_type=jnp.float32
        )

    total = lax.fori_loop(
        0, width // chunk, body, jnp.zeros((combos, 2 * parts), jnp.float32), unroll=2
    )
    out_ref[0:combos, :] = jnp.zeros((combos, LANES), jnp.float32)
    out_ref[0:combos, 0 : 2 * parts] = total


def correlate(own_images, other_images, pairs, shift_grid=None, tables=None):
    slots = 2 * len(pairs)
    width = own_images.shape[1] // 2
    shifts = shift_grid.shape[0] if tables is None else tables[0].shape[0]
    first = (shift_grid.T,) if tables is None else tuple(tables)
    table = jax.ShapeDtypeStruct((shifts, width), jnp.float32)
    outs = [jax.ShapeDtypeStruct((shifts * slots + slots, LANES), jnp.float32)]
    outs += [table, table] if tables is None else []
    kernel = correlate_first_kernel if tables is None else correlate_kernel
    return pl.pallas_call(
        functools.partial(kernel, chunk=4096),
        in_specs=whole_vmem(len(first) + 2 + len(pairs)),
        out_specs=whole_vmem(len(outs)),
        out_shape=outs,
        scratch_shapes=[pltpu.VMEM((slots * 2 * width // LANES, LANES), jnp.float32)],
        compiler_params=pltpu.CompilerParams(vmem_limit_bytes=(14 + slots) * MIB),
        cost_estimate=pl.CostEstimate(flops=1000000000, bytes_accessed=4000000, transcendentals=0),
        name="correlate",
    )(*first, own_images, other_images, *pairs)


def collect_kernel(*refs, combos):
    parts_refs, (precision_ref, assigned_ref, out_ref) = refs[:-3], refs[-3:]
    count = len(parts_refs)
    slots = parts_refs[0].shape[0] - combos
    parts = precision_ref.shape[1]
    for index, ref in enumerate(parts_refs):
        out_ref[index * combos : (index + 1) * combos, :] = ref[0:combos, :]
        power = count * combos + index * slots
        out_ref[power : power + slots, :] = ref[combos:, :]
    rest = count * (combos + slots)
    out_ref[rest:, :] = jnp.zeros((8, LANES), jnp.float32)
    out_ref[rest : rest + 1, 0:parts] = precision_ref[...]
    out_ref[rest + 1 : rest + 2, 0:parts] = assigned_ref[...].astype(jnp.float32)


def collect(passes, precision, assigned, combos):
    rows = len(passes) * passes[0].shape[0] + 8
    return pl.pallas_call(
        functools.partial(collect_kernel, combos=combos),
        in_specs=whole_vmem(2 + len(passes)),
        out_specs=pl.BlockSpec(memory_space=pltpu.VMEM),
        out_shape=jax.ShapeDtypeStruct((rows, LANES), jnp.float32),
        compiler_params=pltpu.CompilerParams(vmem_limit_bytes=16 * MIB),
        name="collect",
    )(*passes, precision, assigned)


def rotate_back(weights, own_images, other_images, cos_ref, sin_ref, where, imag_where, slots):
    image_real = jnp.concatenate([own_images[:, where], other_images[:, where]], axis=0)
    image_imag = jnp.concatenate([own_images[:, imag_where], other_images[:, imag_where]], axis=0)
    from_real = jnp.dot(weights, image_real, preferred_element_type=jnp.float32)
    from_imag = jnp.dot(weights, image_imag, preferred_element_type=jnp.float32)
    real = imag = None
    for s in range(cos_ref.shape[0]):
        cos_s, sin_s = cos_ref[s : s + 1, where], sin_ref[s : s + 1, where]
        part_real = from_real[s * slots : (s + 1) * slots]
        part_imag = from_imag[s * slots : (s + 1) * slots]
        real_s = part_real * cos_s + part_imag * sin_s
        imag_s = part_imag * cos_s - part_real * sin_s
        real = real_s if real is None else real + real_s
        imag = imag_s if imag is None else imag + imag_s
    return real, imag


def posterior_kernel(
    mine, received, own_images, other_images, cos_ref, sin_ref,
    weight_ref, low_ref, low_send, own_mass, ordered, *, slots
):
    device = lax.axis_index("particle")
    shifts, width = cos_ref.shape
    parts = own_images.shape[0]
    combos = shifts * slots
    theirs = received[...]
    lane = lax.broadcasted_iota(jnp.int32, theirs.shape, 1)
    swapped = jnp.where(
        lane < parts, pltpu.roll(theirs, LANES - parts, 1), pltpu.roll(theirs, parts, 1)
    )
    joint = mine[...] + swapped
    power = jnp.sum(
        mine[combos : combos + slots, :] + received[combos : combos + slots, :], axis=1, keepdims=True
    )
    precision = joint[combos + slots : combos + slots + 1]
    assigned = joint[combos + slots + 1 : combos + slots + 2].astype(jnp.int32)
    likelihood_scale = 1.0 / math.sqrt(4 * width)
    classes = [slot_orientation(device, slot, slots) // (slots // CLASSES) for slot in range(slots)]
    logits = []
    for slot in range(slots):
        match = (assigned == classes[slot]).astype(jnp.float32) * PRIOR_REWARD
        part = joint[slot * shifts : (slot + 1) * shifts]
        logits.append(precision * (part - 0.5 * power[slot : slot + 1]) * likelihood_scale + match)
    peak = jnp.max(functools.reduce(jnp.maximum, logits), axis=0, keepdims=True)
    terms = [jnp.exp(value - peak) for value in logits]
    norm = jnp.sum(functools.reduce(jnp.add, terms), axis=0, keepdims=True)
    counted = lax.broadcasted_iota(jnp.int32, (1, LANES), 1) < 2 * parts
    class_lane = lax.broadcasted_iota(jnp.int32, (1, LANES), 1)
    mass_row = jnp.zeros((1, LANES), jnp.float32)
    for slot in range(slots):
        value = terms[slot] / norm
        ordered[slot * shifts : (slot + 1) * shifts, :] = value
        share = jnp.where(counted, jnp.sum(value, axis=0, keepdims=True) * precision, 0.0)
        share = jnp.sum(share, axis=1, keepdims=True)
        mass_row = mass_row + jnp.where(class_lane == classes[slot], share, 0.0)
    weights = jnp.concatenate(
        [ordered[pl.ds(s, slots, stride=shifts), :] for s in range(shifts)], axis=0
    )
    weights = weights[:, 0 : 2 * parts].astype(jnp.bfloat16)
    weight_ref[...] = weights
    own_mass[...] = jnp.broadcast_to(mass_row, own_mass.shape)

    low = LOW_TILES * LANES
    real, imag = rotate_back(
        weights, own_images, other_images, cos_ref, sin_ref, slice(0, low), slice(width, width + low), slots
    )
    for k in range(LOW_TILES):
        piece = slice(k * LANES, (k + 1) * LANES)
        low_ref[pl.ds(k, slots, stride=2 * LOW_TILES), :] = real[:, piece]
        low_ref[pl.ds(LOW_TILES + k, slots, stride=2 * LOW_TILES), :] = imag[:, piece]
    low_body = low_ref.shape[0]
    low_send[0:low_body, :] = low_ref[...].astype(jnp.bfloat16)
    low_send[low_body:, :] = split_mass(mass_row)


def posterior(mine, received, own_images, other_images, cos_table, sin_table, slots):
    shifts = cos_table.shape[0]
    low = slots * 2 * LOW_TILES
    return pl.pallas_call(
        functools.partial(posterior_kernel, slots=slots),
        in_specs=whole_vmem(6),
        out_specs=whole_vmem(4),
        out_shape=[
            jax.ShapeDtypeStruct((shifts * slots, 2 * own_images.shape[0]), jnp.bfloat16),
            jax.ShapeDtypeStruct((low, LANES), jnp.float32),
            jax.ShapeDtypeStruct((low + MASS_ROWS, LANES), jnp.bfloat16),
            jax.ShapeDtypeStruct((8, LANES), jnp.float32),
        ],
        scratch_shapes=[pltpu.VMEM((shifts * slots, LANES), jnp.float32)],
        compiler_params=pltpu.CompilerParams(vmem_limit_bytes=(14 + slots // 2) * MIB),
        name="posterior",
    )(mine, received, own_images, other_images, cos_table, sin_table)


def backproject_kernel(
    weight_ref, own_images, other_images, cos_ref, sin_ref, own, *refs, slots, chunk, unroll
):
    sends, sums = refs[:-1], refs[-1]
    width = cos_ref.shape[1]
    tiles = width // LANES - LOW_TILES
    per_row = 2 * tiles
    chunk_tiles = chunk // LANES
    weights = weight_ref[...]

    def body(step, carry):
        first = step * chunk_tiles
        start = pl.multiple_of((LOW_TILES + first) * LANES, LOW_TILES * LANES)
        where = pl.ds(start, chunk)
        imag_where = pl.ds(pl.multiple_of(width + start, LOW_TILES * LANES), chunk)
        real, imag = rotate_back(
            weights, own_images, other_images, cos_ref, sin_ref, where, imag_where, slots
        )
        for k in range(chunk_tiles):
            piece = slice(k * LANES, (k + 1) * LANES)
            sums[pl.ds(first + k, slots, stride=per_row), :] = real[:, piece]
            sums[pl.ds(tiles + first + k, slots, stride=per_row), :] = imag[:, piece]
        return carry

    lax.fori_loop(0, tiles // chunk_tiles, body, 0, unroll=unroll)
    own[...] = sums[0 : 2 * per_row, :]
    for m, send in enumerate(sends, start=1):
        send[...] = sums[2 * m * per_row : 2 * (m + 1) * per_row, :].astype(jnp.bfloat16)


def backproject(weights, own_images, other_images, cos_table, sin_table, slots):
    width = cos_table.shape[1]
    rows = 2 * 2 * (width // LANES - LOW_TILES)
    chips = slots // 2
    return pl.pallas_call(
        functools.partial(
            backproject_kernel, slots=slots, chunk=LOW_TILES * LANES, unroll=7 if slots <= 8 else 1
        ),
        in_specs=whole_vmem(5),
        out_specs=whole_vmem(chips),
        out_shape=[jax.ShapeDtypeStruct((rows, LANES), jnp.float32)]
        + [jax.ShapeDtypeStruct((rows, LANES), jnp.bfloat16)] * (chips - 1),
        scratch_shapes=[pltpu.VMEM((chips * rows, LANES), jnp.float32)],
        compiler_params=pltpu.CompilerParams(vmem_limit_bytes=(14 + slots // 2) * MIB),
        cost_estimate=pl.CostEstimate(flops=2000000000, bytes_accessed=8000000, transcendentals=0),
        name="backproject",
    )(weights, own_images, other_images, cos_table, sin_table)


def fold_kernel(low_ref, low_received, mass, *refs, chips):
    mains, (own, own_mass), sends = refs[: chips - 1], refs[chips - 1 : chips + 1], refs[chips + 1 :]
    rows = own.shape[0]
    low_body = low_ref.shape[0]
    total_mass = mass[0:1, :] + joined_mass(low_received[low_body:, :])
    block = split_mass(total_mass)
    own_mass[...] = jnp.broadcast_to(total_mass, own_mass.shape)
    for m, target in enumerate((own,) + tuple(sends)):
        part = slice(m * rows, (m + 1) * rows)
        value = (low_ref[part, :] + low_received[part, :].astype(jnp.float32)) * 0.5
        target[0:rows, :] = value.astype(target.dtype)
        if m > 0:
            target[rows : rows + MASS_ROWS, :] = block
            target[rows + MASS_ROWS :, :] = mains[m - 1][...]


def fold(low, low_received, mass, mains):
    chips = len(mains) + 1
    rows = low.shape[0] // chips
    return pl.pallas_call(
        functools.partial(fold_kernel, chips=chips),
        in_specs=whole_vmem(2 + chips),
        out_specs=whole_vmem(1 + chips),
        out_shape=[
            jax.ShapeDtypeStruct((rows, LANES), jnp.float32),
            jax.ShapeDtypeStruct((8, LANES), jnp.float32),
        ]
        + [
            jax.ShapeDtypeStruct((rows + MASS_ROWS + main.shape[0], LANES), jnp.bfloat16)
            for main in mains
        ],
        compiler_params=pltpu.CompilerParams(vmem_limit_bytes=16 * MIB),
        name="fold",
    )(low, low_received, mass, *mains)


def merge_kernel(own, own_low, mass, *refs):
    received, (keep, to_core, mass_out) = refs[:-3], refs[-3:]
    core = own_half()
    low_rows = own_low.shape[0]
    low_half = low_rows // 2
    head = low_rows + MASS_ROWS
    half = own.shape[0] // 2
    total_mass = mass[0:1, :]
    for ref in received:
        total_mass = total_mass + joined_mass(ref[low_rows:head, :])
    mass_out[...] = jnp.broadcast_to(total_mass, mass_out.shape)
    for target, place in ((to_core, 1 - core), (keep, core)):
        start = pl.multiple_of(place * half, half)
        total = own[pl.ds(start, half), :]
        for ref in received:
            total = total + ref[pl.ds(head + start, half), :].astype(jnp.float32)
        where = pl.ds(pl.multiple_of(place * low_half, low_half), low_half)
        low = own_low[where, :]
        for ref in received:
            low = low + ref[where, :].astype(jnp.float32)
        target[...] = jnp.concatenate(
            [low[0:LOW_TILES], total[0 : half // 2], low[LOW_TILES:], total[half // 2 :]], axis=0
        ).astype(target.dtype)


def merge(own, own_low, mass, received):
    rows = (own.shape[0] + own_low.shape[0]) // 2
    return pl.pallas_call(
        merge_kernel,
        in_specs=whole_vmem(3 + len(received)),
        out_specs=whole_vmem(3),
        out_shape=[
            jax.ShapeDtypeStruct((rows, LANES), jnp.float32),
            jax.ShapeDtypeStruct((rows, LANES), jnp.bfloat16),
            jax.ShapeDtypeStruct((8, LANES), jnp.float32),
        ],
        compiler_params=pltpu.CompilerParams(vmem_limit_bytes=16 * MIB),
        name="merge",
    )(own, own_low, mass, *received)


def finish_kernel(own, received, mass, out, mass_out, *, scale, mass_scale):
    core = own_half()
    mass_out[...] = mass[0, :CLASSES] * mass_scale
    for step in range(own.shape[0] // BLOCK):
        rows = slice(step * BLOCK, (step + 1) * BLOCK)
        own_rows = pl.ds(pl.multiple_of((2 * step + core) * BLOCK, BLOCK), BLOCK)
        other_rows = pl.ds(pl.multiple_of((2 * step + 1 - core) * BLOCK, BLOCK), BLOCK)
        out[own_rows, :] = own[rows, :] * scale
        out[other_rows, :] = received[rows, :].astype(jnp.float32) * scale


def finish(own, received, mass, scale, mass_scale):
    return pl.pallas_call(
        functools.partial(finish_kernel, scale=scale, mass_scale=mass_scale),
        in_specs=whole_vmem(3),
        out_specs=whole_vmem(2),
        out_shape=[
            jax.ShapeDtypeStruct((2 * own.shape[0], LANES), jnp.float32),
            jax.ShapeDtypeStruct((CLASSES,), jnp.float32),
        ],
        compiler_params=pltpu.CompilerParams(vmem_limit_bytes=16 * MIB),
        name="finish",
    )(own, received, mass)


def local(
    images, noise_precision, assigned_class, class_refs, interp_index, interp_frac, shift_grid
):
    dev_count = lax.axis_size("particle")
    slots = dev_count // 2
    chips = slots // 2
    parts, width = images.shape
    to_core, table, index, frac = project_other(class_refs, interp_index, interp_frac, images)
    images_received = exchange(to_core, 1)
    own, own_images = project_own(table, index, frac, images)
    pair = pair_rows(own, images_received)
    others = chip_order(chips)[1:]
    pairs = [pair] + [exchange(pair, 4 * m) for m in others]
    group = chips // 2
    first, cos_table, sin_table = correlate(
        own_images, images_received, pairs[:group], shift_grid=shift_grid
    )
    passes = [first]
    for start in range(group, chips, group):
        passes += correlate(
            own_images,
            images_received,
            pairs[start : start + group],
            tables=(cos_table, sin_table),
        )
    mine = collect(
        passes,
        noise_precision.reshape(1, parts),
        assigned_class.reshape(1, parts),
        shift_grid.shape[0] * 2 * group,
    )
    weights, low, low_send, mass = posterior(
        mine, exchange(mine, 1), own_images, images_received, cos_table, sin_table, slots
    )
    low_from_half = exchange(low_send, 2)
    sums = backproject(weights, own_images, images_received, cos_table, sin_table, slots)
    folded = fold(low, low_from_half, mass, sums[1:])
    chip_sums = [exchange(send, 4 * m) for m, send in zip(others, folded[2:])][::-1]
    keep, send, mass = merge(sums[0], folded[0], folded[1], chip_sums)
    back, class_mass = finish(
        keep, exchange(send, 1), mass, 1.0 / math.sqrt(parts), CLASSES / (parts * dev_count)
    )
    return back.reshape(1, width), class_mass


def solution(mesh):
    in_specs = (
        P(("groups", "particle"), None),
        P(("groups", "particle")),
        P(("groups", "particle")),
        P("groups", None, None, None),
        P("particle", None),
        P("particle", None),
        P(),
    )
    out_specs = (P(("groups", "particle"), None), P("groups"))
    return jax.shard_map(local, mesh=mesh, in_specs=in_specs, out_specs=out_specs, check_vma=False)
```

```python
import functools
import math

import jax
import jax.numpy as jnp
from jax import lax
from jax.experimental import pallas as pl
from jax.experimental.pallas import tpu as pltpu
from jax.sharding import PartitionSpec as P

KY = 128
BOX = 256
CLASSES = 8
LOWK = 16
LANES = 128
PRIOR_REWARD = 1.0
MASS_ROWS = 16
BLOCK = 8
PROJECT_CHUNK = 256
LOW_TILES = LOWK * KY // LANES // 2
MIB = 1 << 20


def exchange(value, mask):
    pairs = [(source, source ^ mask) for source in range(lax.axis_size("particle"))]
    return lax.ppermute(value, "particle", pairs)


def in_hbm(value):
    return pltpu.with_memory_space_constraint(value, pltpu.HBM)


def whole_vmem(count):
    return [pl.BlockSpec(memory_space=pltpu.VMEM)] * count


def own_half():
    return lax.axis_index("particle") % 2


def tree_select(values, masks):
    for mask in masks:
        values = [
            jnp.where(mask, values[i + 1], values[i]) if i + 1 < len(values) else values[i]
            for i in range(0, len(values), 2)
        ]
    return values[0]


def project_half(table, index_ref, frac_ref, half, blended):
    pixels = index_ref.shape[1]
    highs = table.shape[1]
    groups = table.shape[0] // 16
    stride = 8 * groups
    chunk = PROJECT_CHUNK
    tiles = chunk // LANES
    per_block = BLOCK // tiles
    half_tiles = pixels // (2 * LANES)

    def body(step, carry):
        block = 2 * (step // per_block) + half
        where = pl.ds(pl.multiple_of((block * per_block + step % per_block) * chunk, chunk), chunk)
        index = index_ref[:, where]
        frac = frac_ref[:, where]
        high = index >> 7
        low = index & (LANES - 1)
        group = (low * 147) >> 10
        first = low - 7 * group
        high_ids = lax.broadcasted_iota(jnp.int32, (highs, chunk), 0)
        one_hot = jnp.where(high_ids == high, 1.0, 0.0).astype(jnp.bfloat16)
        rows = jnp.dot(table[...], one_hot, preferred_element_type=jnp.float32)
        group = jnp.broadcast_to(group, (8, chunk))
        masks = [(group & (1 << bit)) != 0 for bit in range((groups - 1).bit_length())]
        ids = lax.broadcasted_iota(jnp.int32, (8, chunk), 0)
        weight = jnp.where(ids == first, 1.0 - frac, jnp.where(ids == first + 1, frac, 0.0))
        for comp in range(2):
            start = comp * stride
            picked = tree_select([rows[start + 8 * g : start + 8 * g + 8] for g in range(groups)], masks)
            value = jnp.sum(picked * weight, axis=0, keepdims=True)
            for k in range(tiles):
                row = comp * half_tiles + step * tiles + k
                blended[pl.ds(row, 1), :] = value[:, k * LANES : (k + 1) * LANES]
        return carry

    lax.fori_loop(0, half_tiles // tiles, body, 0, unroll=8)


def image_copies(images_hbm, target, sems, first, half, pixels):
    chunk = BLOCK * LANES
    blocks = pixels // (2 * chunk)
    copies = []
    for comp in range(2):
        for step in range(blocks):
            source = pl.multiple_of(comp * pixels + (2 * step + half) * chunk, chunk)
            dest = (comp * blocks + step) * chunk
            copies.append(
                pltpu.make_async_copy(
                    images_hbm.at[:, pl.ds(source, chunk)],
                    target.at[:, pl.ds(dest, chunk)],
                    sems.at[first + len(copies)],
                )
            )
    return copies


def project_other_kernel(
    table_hbm, index_hbm, frac_hbm, images_hbm,
    out_ref, table, index_ref, frac_ref, table_in, flat, wide, blended, sems
):
    device = lax.axis_index("particle")
    row_count = lax.axis_size("particle") // 2
    half_set = device // 2 % 2
    class_id = (2 * (device // 4) + device % 2) // (row_count // CLASSES)
    copies = [
        pltpu.make_async_copy(
            table_hbm.at[pl.ds(half_set, 1), pl.ds(class_id, 1)], table_in, sems.at[0]
        ),
        pltpu.make_async_copy(index_hbm, index_ref, sems.at[1]),
        pltpu.make_async_copy(frac_hbm, frac_ref, sems.at[2]),
    ]
    pixels = index_ref.shape[1]
    copies += image_copies(images_hbm, out_ref, sems, 3, 1 - own_half(), pixels)
    for copy in copies[:3]:
        copy.start()
    copies[0].wait()
    for copy in copies[3:]:
        copy.start()
    highs = flat.shape[1]
    groups = table.shape[0] // 16

    def unfold(step, carry):
        piece = table_in[0, 0, :, pl.ds(step * 8 * LANES, 8 * LANES)].astype(jnp.float32)
        for k in range(8):
            for comp in range(2):
                flat[comp, pl.ds(step * 8 + k, 1), :] = piece[comp : comp + 1, k * LANES : (k + 1) * LANES]
        return carry

    lax.fori_loop(0, highs // 8, unfold, 0, unroll=16)
    picked = []
    for comp in range(2):
        turned = flat[comp].T
        wide[0:LANES, :] = turned
        wide[LANES : LANES + 8, :] = pltpu.roll(turned[0:8], highs - 1, 1)
        picked += [wide[7 * g : 7 * g + 8, :] for g in range(groups)]
    for pair in range(groups):
        table[16 * pair : 16 * (pair + 1), :] = jnp.concatenate(
            picked[2 * pair : 2 * pair + 2], axis=0
        ).astype(jnp.bfloat16)
    copies[1].wait()
    copies[2].wait()
    project_half(table, index_ref, frac_ref, 1 - own_half(), blended)
    parts = out_ref.shape[0]
    for k in range(blended.shape[0] // parts):
        out_ref[:, pixels + k * LANES : pixels + (k + 1) * LANES] = blended[
            k * parts : (k + 1) * parts, :
        ].astype(jnp.bfloat16)
    for copy in copies[3:]:
        copy.wait()


def project_other(class_refs, interp_index, interp_frac, images):
    vox = class_refs.shape[3]
    pixels = interp_index.shape[1]
    highs = vox // LANES
    half_rows = pixels // LANES
    groups = -(-LANES // 7)
    parts = images.shape[0]
    copies = 3 + pixels // (BLOCK * LANES)
    return pl.pallas_call(
        project_other_kernel,
        in_specs=[pl.BlockSpec(memory_space=pltpu.HBM)] * 4,
        out_specs=whole_vmem(4),
        out_shape=[
            jax.ShapeDtypeStruct((parts, pixels + half_rows * LANES // parts), jnp.bfloat16),
            jax.ShapeDtypeStruct((16 * groups, highs), jnp.bfloat16),
            jax.ShapeDtypeStruct((1, pixels), jnp.int32),
            jax.ShapeDtypeStruct((1, pixels), jnp.float32),
        ],
        scratch_shapes=[
            pltpu.VMEM((1, 1, 2, vox), jnp.bfloat16),
            pltpu.VMEM((2, highs, LANES), jnp.float32),
            pltpu.VMEM((LANES + 8, highs), jnp.float32),
            pltpu.VMEM((half_rows, LANES), jnp.float32),
            pltpu.SemaphoreType.DMA((copies,)),
        ],
        compiler_params=pltpu.CompilerParams(vmem_limit_bytes=16 * MIB),
        name="project_other",
    )(*(in_hbm(value) for value in (class_refs, interp_index, interp_frac, images)))


def project_own_kernel(table, index_ref, frac_ref, images_hbm, out_ref, own_images, blended, sems):
    copies = image_copies(images_hbm, own_images, sems, 0, own_half(), index_ref.shape[1])
    for copy in copies:
        copy.start()
    project_half(table, index_ref, frac_ref, own_half(), blended)
    out_ref[...] = blended[...].astype(jnp.bfloat16)
    for copy in copies:
        copy.wait()


def project_own(table, index, frac, images):
    pixels = index.shape[1]
    half_rows = pixels // LANES
    return pl.pallas_call(
        project_own_kernel,
        in_specs=whole_vmem(3) + [pl.BlockSpec(memory_space=pltpu.HBM)],
        out_specs=whole_vmem(2),
        out_shape=[
            jax.ShapeDtypeStruct((half_rows, LANES), jnp.bfloat16),
            jax.ShapeDtypeStruct((images.shape[0], pixels), jnp.bfloat16),
        ],
        scratch_shapes=[
            pltpu.VMEM((half_rows, LANES), jnp.float32),
            pltpu.SemaphoreType.DMA((pixels // (BLOCK * LANES),)),
        ],
        compiler_params=pltpu.CompilerParams(vmem_limit_bytes=16 * MIB),
        cost_estimate=pl.CostEstimate(flops=2000000000, bytes_accessed=8000000, transcendentals=0),
        name="project_own",
    )(table, index, frac, in_hbm(images))


def pair_kernel(own, other, out_ref):
    count = own.shape[0]
    parts, width = other.shape
    tiles = count // parts
    core = own_half()
    out_ref[pl.ds(pl.multiple_of(core * count, count), count), :] = own[...]
    for k in range(tiles):
        lanes = slice(width - (tiles - k) * LANES, width - (tiles - k - 1) * LANES)
        rows = pl.ds(pl.multiple_of((1 - core) * count + k * parts, parts), parts)
        out_ref[rows, :] = other[:, lanes]


def pair_rows(own, other):
    return pl.pallas_call(
        pair_kernel,
        in_specs=whole_vmem(2),
        out_specs=pl.BlockSpec(memory_space=pltpu.VMEM),
        out_shape=jax.ShapeDtypeStruct((2 * own.shape[0], LANES), own.dtype),
        compiler_params=pltpu.CompilerParams(vmem_limit_bytes=16 * MIB),
        name="pair_rows",
    )(own, other)


def chip_order(chips):
    return [0, chips - 1] + list(range(1, chips - 1))


def slot_orientation(device, slot, slots):
    return 2 * ((device // 4) ^ chip_order(slots // 2)[slot // 2]) + slot % 2


def split_mass(mass_row):
    ids = lax.broadcasted_iota(jnp.int32, (MASS_ROWS, LANES), 0)
    upper = mass_row.astype(jnp.bfloat16).astype(jnp.float32)
    lower = mass_row - upper
    return jnp.where(ids == 0, upper, jnp.where(ids == 1, lower, 0.0)).astype(jnp.bfloat16)


def joined_mass(block):
    return jnp.sum(block.astype(jnp.float32), axis=0, keepdims=True)


def fill_tables(shift_ref, cos_ref, sin_ref):
    shifts, width = cos_ref.shape
    same = lax.broadcasted_iota(jnp.int32, (shifts, shifts), 0) == lax.broadcasted_iota(
        jnp.int32, (shifts, shifts), 1
    )
    grid_x, grid_y = (
        jnp.sum(
            jnp.where(same, shift_ref[axis : axis + 1, :].astype(jnp.float32), 0.0),
            axis=1,
            keepdims=True,
        ).astype(jnp.int32)
        for axis in range(2)
    )
    lane = lax.broadcasted_iota(jnp.int32, (shifts, LANES), 1)
    freq_x = (lane // BLOCK) * (2 * BLOCK) + own_half() * BLOCK + lane % BLOCK
    turn_x = (freq_x * grid_x) & (BOX - 1)
    turn_y = ((lane - KY // 2) * grid_y) & (BOX - 1)
    angle_x = turn_x.astype(jnp.float32) * (2.0 * math.pi / BOX)
    angle_y = turn_y.astype(jnp.float32) * (2.0 * math.pi / BOX)
    cos_x, sin_x = jnp.cos(angle_x), jnp.sin(angle_x)
    cos_y, sin_y = jnp.cos(angle_y), jnp.sin(angle_y)
    for j in range(width // LANES):
        where = slice(j * LANES, (j + 1) * LANES)
        cos_j, sin_j = cos_x[:, j : j + 1], sin_x[:, j : j + 1]
        cos_ref[:, where] = cos_j * cos_y - sin_j * sin_y
        sin_ref[:, where] = sin_j * cos_y + cos_j * sin_y


def correlate_first_kernel(shift_ref, own_images, other_images, *refs, chunk):
    pair_refs, (out_ref, cos_ref, sin_ref, proj) = refs[:-4], refs[-4:]
    fill_tables(shift_ref, cos_ref, sin_ref)
    correlate_kernel(
        cos_ref, sin_ref, own_images, other_images, *pair_refs, out_ref, proj, chunk=chunk
    )


def correlate_kernel(cos_ref, sin_ref, own_images, other_images, *refs, chunk):
    pair_refs, (out_ref, proj) = refs[:-2], refs[-2:]
    shifts = cos_ref.shape[0]
    parts = own_images.shape[0]
    slots = 2 * len(pair_refs)
    width = own_images.shape[1] // 2
    tiles = width // LANES
    per_row = 2 * tiles
    combos = shifts * slots
    for slot in range(slots):
        place = slice(slot % 2 * per_row, (slot % 2 + 1) * per_row)
        row = pair_refs[slot // 2][place, :].astype(jnp.float32)
        proj[slot * per_row : (slot + 1) * per_row, :] = row
        out_ref[combos + slot : combos + slot + 1, :] = jnp.sum(row * row, axis=0, keepdims=True)

    chunk_tiles = chunk // LANES
    contract_lanes = (((1,), (1,)), ((), ()))

    def body(step, total):
        first = step * chunk_tiles
        where = pl.ds(pl.multiple_of(step * chunk, chunk), chunk)
        imag_where = pl.ds(pl.multiple_of(width + step * chunk, chunk), chunk)
        cos_part, sin_part = cos_ref[:, where], sin_ref[:, where]
        reals, imags = [], []
        for slot in range(slots):
            start = slot * per_row + first
            real = jnp.concatenate(
                [proj[pl.ds(start + k, 1), :] for k in range(chunk_tiles)], axis=1
            )
            imag = jnp.concatenate(
                [proj[pl.ds(start + tiles + k, 1), :] for k in range(chunk_tiles)], axis=1
            )
            reals.append(real * cos_part - imag * sin_part)
            imags.append(real * sin_part + imag * cos_part)
        turned_real = jnp.concatenate(reals, axis=0).astype(jnp.bfloat16)
        turned_imag = jnp.concatenate(imags, axis=0).astype(jnp.bfloat16)
        image_real = jnp.concatenate([own_images[:, where], other_images[:, where]], axis=0)
        image_imag = jnp.concatenate([own_images[:, imag_where], other_images[:, imag_where]], axis=0)
        total = total + lax.dot_general(
            turned_real, image_real, contract_lanes, preferred_element_type=jnp.float32
        )
        return total + lax.dot_general(
            turned_imag, image_imag, contract_lanes, preferred_element_type=jnp.float32
        )

    total = lax.fori_loop(
        0, width // chunk, body, jnp.zeros((combos, 2 * parts), jnp.float32), unroll=2
    )
    out_ref[0:combos, :] = jnp.zeros((combos, LANES), jnp.float32)
    out_ref[0:combos, 0 : 2 * parts] = total


def correlate(own_images, other_images, pairs, shift_grid=None, tables=None):
    slots = 2 * len(pairs)
    width = own_images.shape[1] // 2
    shifts = shift_grid.shape[0] if tables is None else tables[0].shape[0]
    first = (shift_grid.T,) if tables is None else tuple(tables)
    table = jax.ShapeDtypeStruct((shifts, width), jnp.float32)
    outs = [jax.ShapeDtypeStruct((shifts * slots + slots, LANES), jnp.float32)]
    outs += [table, table] if tables is None else []
    kernel = correlate_first_kernel if tables is None else correlate_kernel
    return pl.pallas_call(
        functools.partial(kernel, chunk=4096),
        in_specs=whole_vmem(len(first) + 2 + len(pairs)),
        out_specs=whole_vmem(len(outs)),
        out_shape=outs,
        scratch_shapes=[pltpu.VMEM((slots * 2 * width // LANES, LANES), jnp.float32)],
        compiler_params=pltpu.CompilerParams(vmem_limit_bytes=(14 + slots) * MIB),
        cost_estimate=pl.CostEstimate(flops=1000000000, bytes_accessed=4000000, transcendentals=0),
        name="correlate",
    )(*first, own_images, other_images, *pairs)


def collect_kernel(*refs, combos):
    parts_refs, (precision_ref, assigned_ref, out_ref) = refs[:-3], refs[-3:]
    count = len(parts_refs)
    slots = parts_refs[0].shape[0] - combos
    parts = precision_ref.shape[1]
    for index, ref in enumerate(parts_refs):
        out_ref[index * combos : (index + 1) * combos, :] = ref[0:combos, :]
        power = count * combos + index * slots
        out_ref[power : power + slots, :] = ref[combos:, :]
    rest = count * (combos + slots)
    out_ref[rest:, :] = jnp.zeros((8, LANES), jnp.float32)
    out_ref[rest : rest + 1, 0:parts] = precision_ref[...]
    out_ref[rest + 1 : rest + 2, 0:parts] = assigned_ref[...].astype(jnp.float32)


def collect(passes, precision, assigned, combos):
    rows = len(passes) * passes[0].shape[0] + 8
    return pl.pallas_call(
        functools.partial(collect_kernel, combos=combos),
        in_specs=whole_vmem(2 + len(passes)),
        out_specs=pl.BlockSpec(memory_space=pltpu.VMEM),
        out_shape=jax.ShapeDtypeStruct((rows, LANES), jnp.float32),
        compiler_params=pltpu.CompilerParams(vmem_limit_bytes=16 * MIB),
        name="collect",
    )(*passes, precision, assigned)


def rotate_back(weights, own_images, other_images, cos_ref, sin_ref, where, imag_where, slots):
    image_real = jnp.concatenate([own_images[:, where], other_images[:, where]], axis=0)
    image_imag = jnp.concatenate([own_images[:, imag_where], other_images[:, imag_where]], axis=0)
    from_real = jnp.dot(weights, image_real, preferred_element_type=jnp.float32)
    from_imag = jnp.dot(weights, image_imag, preferred_element_type=jnp.float32)
    real = imag = None
    for s in range(cos_ref.shape[0]):
        cos_s, sin_s = cos_ref[s : s + 1, where], sin_ref[s : s + 1, where]
        part_real = from_real[s * slots : (s + 1) * slots]
        part_imag = from_imag[s * slots : (s + 1) * slots]
        real_s = part_real * cos_s + part_imag * sin_s
        imag_s = part_imag * cos_s - part_real * sin_s
        real = real_s if real is None else real + real_s
        imag = imag_s if imag is None else imag + imag_s
    return real, imag


def posterior_kernel(
    mine, received, own_images, other_images, cos_ref, sin_ref,
    weight_ref, low_ref, low_send, own_mass, ordered, *, slots
):
    device = lax.axis_index("particle")
    shifts, width = cos_ref.shape
    parts = own_images.shape[0]
    combos = shifts * slots
    theirs = received[...]
    lane = lax.broadcasted_iota(jnp.int32, theirs.shape, 1)
    swapped = jnp.where(
        lane < parts, pltpu.roll(theirs, LANES - parts, 1), pltpu.roll(theirs, parts, 1)
    )
    joint = mine[...] + swapped
    power = jnp.sum(
        mine[combos : combos + slots, :] + received[combos : combos + slots, :], axis=1, keepdims=True
    )
    precision = joint[combos + slots : combos + slots + 1]
    assigned = joint[combos + slots + 1 : combos + slots + 2].astype(jnp.int32)
    likelihood_scale = 1.0 / math.sqrt(4 * width)
    classes = [slot_orientation(device, slot, slots) // (slots // CLASSES) for slot in range(slots)]
    logits = []
    for slot in range(slots):
        match = (assigned == classes[slot]).astype(jnp.float32) * PRIOR_REWARD
        part = joint[slot * shifts : (slot + 1) * shifts]
        logits.append(precision * (part - 0.5 * power[slot : slot + 1]) * likelihood_scale + match)
    peak = jnp.max(functools.reduce(jnp.maximum, logits), axis=0, keepdims=True)
    terms = [jnp.exp(value - peak) for value in logits]
    norm = jnp.sum(functools.reduce(jnp.add, terms), axis=0, keepdims=True)
    counted = lax.broadcasted_iota(jnp.int32, (1, LANES), 1) < 2 * parts
    class_lane = lax.broadcasted_iota(jnp.int32, (1, LANES), 1)
    mass_row = jnp.zeros((1, LANES), jnp.float32)
    for slot in range(slots):
        value = terms[slot] / norm
        ordered[slot * shifts : (slot + 1) * shifts, :] = value
        share = jnp.where(counted, jnp.sum(value, axis=0, keepdims=True) * precision, 0.0)
        share = jnp.sum(share, axis=1, keepdims=True)
        mass_row = mass_row + jnp.where(class_lane == classes[slot], share, 0.0)
    weights = jnp.concatenate(
        [ordered[pl.ds(s, slots, stride=shifts), :] for s in range(shifts)], axis=0
    )
    weights = weights[:, 0 : 2 * parts].astype(jnp.bfloat16)
    weight_ref[...] = weights
    own_mass[...] = jnp.broadcast_to(mass_row, own_mass.shape)

    low = LOW_TILES * LANES
    real, imag = rotate_back(
        weights, own_images, other_images, cos_ref, sin_ref, slice(0, low), slice(width, width + low), slots
    )
    for k in range(LOW_TILES):
        piece = slice(k * LANES, (k + 1) * LANES)
        low_ref[pl.ds(k, slots, stride=2 * LOW_TILES), :] = real[:, piece]
        low_ref[pl.ds(LOW_TILES + k, slots, stride=2 * LOW_TILES), :] = imag[:, piece]
    low_body = low_ref.shape[0]
    low_send[0:low_body, :] = low_ref[...].astype(jnp.bfloat16)
    low_send[low_body:, :] = split_mass(mass_row)


def posterior(mine, received, own_images, other_images, cos_table, sin_table, slots):
    shifts = cos_table.shape[0]
    low = slots * 2 * LOW_TILES
    return pl.pallas_call(
        functools.partial(posterior_kernel, slots=slots),
        in_specs=whole_vmem(6),
        out_specs=whole_vmem(4),
        out_shape=[
            jax.ShapeDtypeStruct((shifts * slots, 2 * own_images.shape[0]), jnp.bfloat16),
            jax.ShapeDtypeStruct((low, LANES), jnp.float32),
            jax.ShapeDtypeStruct((low + MASS_ROWS, LANES), jnp.bfloat16),
            jax.ShapeDtypeStruct((8, LANES), jnp.float32),
        ],
        scratch_shapes=[pltpu.VMEM((shifts * slots, LANES), jnp.float32)],
        compiler_params=pltpu.CompilerParams(vmem_limit_bytes=(14 + slots // 2) * MIB),
        name="posterior",
    )(mine, received, own_images, other_images, cos_table, sin_table)


def backproject_kernel(
    weight_ref, own_images, other_images, cos_ref, sin_ref, own, *refs, slots, chunk, unroll
):
    sends, sums = refs[:-1], refs[-1]
    width = cos_ref.shape[1]
    tiles = width // LANES - LOW_TILES
    per_row = 2 * tiles
    chunk_tiles = chunk // LANES
    weights = weight_ref[...]

    def body(step, carry):
        first = step * chunk_tiles
        start = pl.multiple_of((LOW_TILES + first) * LANES, LOW_TILES * LANES)
        where = pl.ds(start, chunk)
        imag_where = pl.ds(pl.multiple_of(width + start, LOW_TILES * LANES), chunk)
        real, imag = rotate_back(
            weights, own_images, other_images, cos_ref, sin_ref, where, imag_where, slots
        )
        for k in range(chunk_tiles):
            piece = slice(k * LANES, (k + 1) * LANES)
            sums[pl.ds(first + k, slots, stride=per_row), :] = real[:, piece]
            sums[pl.ds(tiles + first + k, slots, stride=per_row), :] = imag[:, piece]
        return carry

    lax.fori_loop(0, tiles // chunk_tiles, body, 0, unroll=unroll)
    own[...] = sums[0 : 2 * per_row, :]
    for m, send in enumerate(sends, start=1):
        send[...] = sums[2 * m * per_row : 2 * (m + 1) * per_row, :].astype(jnp.bfloat16)


def backproject(weights, own_images, other_images, cos_table, sin_table, slots):
    width = cos_table.shape[1]
    rows = 2 * 2 * (width // LANES - LOW_TILES)
    chips = slots // 2
    return pl.pallas_call(
        functools.partial(
            backproject_kernel, slots=slots, chunk=LOW_TILES * LANES, unroll=7 if slots <= 8 else 1
        ),
        in_specs=whole_vmem(5),
        out_specs=whole_vmem(chips),
        out_shape=[jax.ShapeDtypeStruct((rows, LANES), jnp.float32)]
        + [jax.ShapeDtypeStruct((rows, LANES), jnp.bfloat16)] * (chips - 1),
        scratch_shapes=[pltpu.VMEM((chips * rows, LANES), jnp.float32)],
        compiler_params=pltpu.CompilerParams(vmem_limit_bytes=(14 + slots // 2) * MIB),
        cost_estimate=pl.CostEstimate(flops=2000000000, bytes_accessed=8000000, transcendentals=0),
        name="backproject",
    )(weights, own_images, other_images, cos_table, sin_table)


def fold_kernel(low_ref, low_received, mass, *refs, chips):
    mains, (own, own_mass), sends = refs[: chips - 1], refs[chips - 1 : chips + 1], refs[chips + 1 :]
    rows = own.shape[0]
    low_body = low_ref.shape[0]
    total_mass = mass[0:1, :] + joined_mass(low_received[low_body:, :])
    block = split_mass(total_mass)
    own_mass[...] = jnp.broadcast_to(total_mass, own_mass.shape)
    for m, target in enumerate((own,) + tuple(sends)):
        part = slice(m * rows, (m + 1) * rows)
        value = (low_ref[part, :] + low_received[part, :].astype(jnp.float32)) * 0.5
        target[0:rows, :] = value.astype(target.dtype)
        if m > 0:
            target[rows : rows + MASS_ROWS, :] = block
            target[rows + MASS_ROWS :, :] = mains[m - 1][...]


def fold(low, low_received, mass, mains):
    chips = len(mains) + 1
    rows = low.shape[0] // chips
    return pl.pallas_call(
        functools.partial(fold_kernel, chips=chips),
        in_specs=whole_vmem(2 + chips),
        out_specs=whole_vmem(1 + chips),
        out_shape=[
            jax.ShapeDtypeStruct((rows, LANES), jnp.float32),
            jax.ShapeDtypeStruct((8, LANES), jnp.float32),
        ]
        + [
            jax.ShapeDtypeStruct((rows + MASS_ROWS + main.shape[0], LANES), jnp.bfloat16)
            for main in mains
        ],
        compiler_params=pltpu.CompilerParams(vmem_limit_bytes=16 * MIB),
        name="fold",
    )(low, low_received, mass, *mains)


def merge_kernel(own, own_low, mass, *refs):
    received, (keep, to_core, mass_out) = refs[:-3], refs[-3:]
    core = own_half()
    low_rows = own_low.shape[0]
    low_half = low_rows // 2
    head = low_rows + MASS_ROWS
    half = own.shape[0] // 2
    total_mass = mass[0:1, :]
    for ref in received:
        total_mass = total_mass + joined_mass(ref[low_rows:head, :])
    mass_out[...] = jnp.broadcast_to(total_mass, mass_out.shape)
    for target, place in ((to_core, 1 - core), (keep, core)):
        start = pl.multiple_of(place * half, half)
        total = own[pl.ds(start, half), :]
        for ref in received:
            total = total + ref[pl.ds(head + start, half), :].astype(jnp.float32)
        where = pl.ds(pl.multiple_of(place * low_half, low_half), low_half)
        low = own_low[where, :]
        for ref in received:
            low = low + ref[where, :].astype(jnp.float32)
        target[...] = jnp.concatenate(
            [low[0:LOW_TILES], total[0 : half // 2], low[LOW_TILES:], total[half // 2 :]], axis=0
        ).astype(target.dtype)


def merge(own, own_low, mass, received):
    rows = (own.shape[0] + own_low.shape[0]) // 2
    return pl.pallas_call(
        merge_kernel,
        in_specs=whole_vmem(3 + len(received)),
        out_specs=whole_vmem(3),
        out_shape=[
            jax.ShapeDtypeStruct((rows, LANES), jnp.float32),
            jax.ShapeDtypeStruct((rows, LANES), jnp.bfloat16),
            jax.ShapeDtypeStruct((8, LANES), jnp.float32),
        ],
        compiler_params=pltpu.CompilerParams(vmem_limit_bytes=16 * MIB),
        name="merge",
    )(own, own_low, mass, *received)


def finish_kernel(own, received, mass, out, mass_out, *, scale, mass_scale):
    core = own_half()
    mass_out[...] = mass[0, :CLASSES] * mass_scale
    for step in range(own.shape[0] // BLOCK):
        rows = slice(step * BLOCK, (step + 1) * BLOCK)
        own_rows = pl.ds(pl.multiple_of((2 * step + core) * BLOCK, BLOCK), BLOCK)
        other_rows = pl.ds(pl.multiple_of((2 * step + 1 - core) * BLOCK, BLOCK), BLOCK)
        out[own_rows, :] = own[rows, :] * scale
        out[other_rows, :] = received[rows, :].astype(jnp.float32) * scale


def finish(own, received, mass, scale, mass_scale):
    return pl.pallas_call(
        functools.partial(finish_kernel, scale=scale, mass_scale=mass_scale),
        in_specs=whole_vmem(3),
        out_specs=whole_vmem(2),
        out_shape=[
            jax.ShapeDtypeStruct((2 * own.shape[0], LANES), jnp.float32),
            jax.ShapeDtypeStruct((CLASSES,), jnp.float32),
        ],
        compiler_params=pltpu.CompilerParams(vmem_limit_bytes=16 * MIB),
        name="finish",
    )(own, received, mass)


def local(
    images, noise_precision, assigned_class, class_refs, interp_index, interp_frac, shift_grid
):
    dev_count = lax.axis_size("particle")
    slots = dev_count // 2
    chips = slots // 2
    parts, width = images.shape
    to_core, table, index, frac = project_other(class_refs, interp_index, interp_frac, images)
    images_received = exchange(to_core, 1)
    own, own_images = project_own(table, index, frac, images)
    pair = pair_rows(own, images_received)
    others = chip_order(chips)[1:]
    pairs = [pair] + [exchange(pair, 4 * m) for m in others]
    group = chips // 2
    first, cos_table, sin_table = correlate(
        own_images, images_received, pairs[:group], shift_grid=shift_grid
    )
    passes = [first]
    for start in range(group, chips, group):
        passes += correlate(
            own_images,
            images_received,
            pairs[start : start + group],
            tables=(cos_table, sin_table),
        )
    mine = collect(
        passes,
        noise_precision.reshape(1, parts),
        assigned_class.reshape(1, parts),
        shift_grid.shape[0] * 2 * group,
    )
    weights, low, low_send, mass = posterior(
        mine, exchange(mine, 1), own_images, images_received, cos_table, sin_table, slots
    )
    low_from_half = exchange(low_send, 2)
    sums = backproject(weights, own_images, images_received, cos_table, sin_table, slots)
    folded = fold(low, low_from_half, mass, sums[1:])
    chip_sums = [exchange(send, 4 * m) for m, send in zip(others, folded[2:])][::-1]
    keep, send, mass = merge(sums[0], folded[0], folded[1], chip_sums)
    back, class_mass = finish(
        keep, exchange(send, 1), mass, 1.0 / math.sqrt(parts), CLASSES / (parts * dev_count)
    )
    return back.reshape(1, width), class_mass


def solution(mesh):
    in_specs = (
        P(("groups", "particle"), None),
        P(("groups", "particle")),
        P(("groups", "particle")),
        P("groups", None, None, None),
        P("particle", None),
        P("particle", None),
        P(),
    )
    out_specs = (P(("groups", "particle"), None), P("groups"))
    return jax.shard_map(local, mesh=mesh, in_specs=in_specs, out_specs=out_specs, check_vma=False)
```
